256 devices in a mesh: dp: 32 (over y, z), item: 8 (over x, core).
Axes of the slice: x: 4, y: 4, z: 8, core: 2. Of those that a mesh axis runs over, the one named last changes fastest.
Arguments:
- table: bfloat16 [16384, 1024], P('item'), may hold values from -0.5 to 0.5
- w_uvqk: bfloat16 [1024, 4, 1024], P(None, None, 'item'), may hold values from -0.1875 to 0.1875
- w_out: bfloat16 [1024, 1024], P('item'), may hold values from -0.1875 to 0.1875
- history: int32 [32, 1024], P('dp'), may hold values from 0 to 16383
- lengths: int32 [32], P('dp'), may hold values from 1 to 1024, 16384 in all
- candidates: int32 [32, 512], P('dp'), may hold values from 0 to 16383
- counts: int32 [32], P('dp'), may hold values from 128 to 512, as said below
- actions: int32 [32, 1024], P('dp'), may hold values from 0 to 511, as said below
- targets: float32 [32, 1024], P('dp'), may hold values from -6 to 6
Outputs:
- loss: float32 [], replicated
- grad_uvqk: float32 [1024, 4, 1024], P('dp', None, 'item')
- grad_out: float32 [1024, 1024], P('item', 'dp')
- grad_table: float32 [16384, 1024], P('item', 'dp')
The draws below stay inside these ranges and needn't reach their ends.
Inputs may be any that keep to these rules, and one draw needn't show every extreme that they name: `counts`: every user has at least 128 live candidates and some user has all 512. `actions`: each action is below its user's count.
All inputs are finite; a program needn't handle non-finite values. No bound on the sum of `lengths` on one device may be relied on, other than what follows from the above.
Results may differ from the reference program's by a relative error of at most 0.023.
Values may be sent and summed in bfloat16 or wider, within the bound.
No kernel may reach another device: no remote copies, remote signals or barrier semaphores. Data moves between devices by JAX's collectives and lax.ppermute only.
A program may use at most 128 MiB of HBM per device.

```python
import math
import jax
import jax.numpy as jnp
import numpy as np
from jax import lax

D = 1024
HEADS = 8
HD = 128
SEQ = 1024
CAND = 512
USERS = 32
ITEMS = 16384
N_DP = 32
N_ITEM = 8


def shared_counts(key):
    lower = jax.random.randint(jax.random.fold_in(key, 11), (USERS,), CAND // 4, CAND + 1)
    chosen = jax.random.randint(jax.random.fold_in(key, 12), (), 0, USERS)
    return jnp.where(jnp.arange(USERS) == chosen, CAND, lower).astype(jnp.int32)


def draw_counts(key, part):
    return shared_counts(key)


def draw_actions(key, part):
    counts = shared_counts(key)
    key = jax.random.fold_in(key, 5)
    raw = jax.random.randint(key, (USERS, SEQ), 0, 1 << 20)
    return (raw % counts[:, None]).astype(jnp.int32)


def draw_table(key, part):
    key = jax.random.fold_in(key, 7)
    values = 0.05 * jax.random.normal(jax.random.fold_in(key, 1), (ITEMS, D), jnp.float32)
    return jnp.clip(values, -0.3, 0.3).astype(jnp.bfloat16)


def plant(result, rng, least, top_value):
    extent = result.shape
    spot = [jax.random.randint(jax.random.fold_in(rng, axis), (), 0, extent[axis]) for axis in range(len(extent))]
    result = result.at[tuple(spot)].set(least)
    longest = extent.index(max(extent))
    spot[longest] = (spot[longest] + 1) % extent[longest]
    return result.at[tuple(spot)].set(top_value)


def shard_levels(key, dims, shards, least, largest):
    factor_of, own = 1.0, jax.random.fold_in(key, 6)
    for dim, parts in shards:
        draws = jnp.exp(jax.random.uniform(jax.random.fold_in(own, dim), (parts,), jnp.float32, least / len(shards), largest / len(shards)))
        factor_of = factor_of * jnp.repeat(draws, dims[dim] // parts).reshape([-1 if axis == dim else 1 for axis in range(len(dims))])
    return factor_of


def rank_bounds(number_of, lean):
    weights = [(1 << 20) // math.isqrt(standing ** lean) + 1 for standing in range(1, number_of + 1)]
    scale = 1 + sum(weights) // (1 << 30)
    return np.cumsum(np.array([max(1, weight // scale) for weight in weights]))


def ranked(own_key, shape, amount, slope):
    grid = rank_bounds(amount, slope)
    pick = jax.random.randint(jax.random.fold_in(own_key, 1), shape, 0, int(grid[amount - 1]))
    standing = jnp.searchsorted(jnp.asarray(grid, jnp.int32), pick, side="right")
    return jax.random.permutation(jax.random.fold_in(own_key, 2), amount)[standing].astype(jnp.int32)


def split_up(amount, total, reach, skew):
    loads = [(1 << 20) // math.isqrt(grade ** skew) + 1 for grade in range(2, amount + 1)]
    rest, holding = total - reach - (amount - 1), [1] * (amount - 1)
    while rest > 0:
        movable = [i for i in range(amount - 1) if holding[i] < reach]
        mass, remaining = sum([loads[i] for i in movable]), rest
        for i in movable:
            more = min(reach - holding[i], max(1, remaining * loads[i] // mass), rest)
            holding[i] = holding[i] + more
            rest = rest - more
    return np.array([reach] + holding)


def ragged(rng, number_of, total, most, slope):
    if number_of == 2:
        one = jax.random.randint(rng, (), max(1, total - most), min(most, total - 1) + 1)
        return jnp.stack([one, total - one])
    sizes = jnp.asarray(split_up(number_of, total, most, slope), jnp.int32)
    twos = (number_of - 1) // 2
    giver, sink = sizes[1:1 + 2 * twos:2], sizes[2:2 + 2 * twos:2]
    slack = jnp.minimum(giver - 1, most - sink)
    moved = jax.random.randint(jax.random.fold_in(rng, 1), (twos,), 0, 1 << 20) % (slack + 1)
    sizes = sizes.at[1:1 + 2 * twos:2].set(giver - moved).at[2:2 + 2 * twos:2].set(sink + moved)
    return sizes[jax.random.permutation(jax.random.fold_in(rng, 2), number_of)]


def bell_draw(rng, extent, width, most, cuts=(), held_as=jnp.bfloat16):
    entries = jax.random.normal(rng, extent, jnp.float32) * width
    if len(cuts) > 0:
        entries = shard_levels(rng, extent, cuts, -0.22, 0.18) * entries
    return jnp.clip(entries, min=-most, max=most).astype(held_as)


def setup_inputs(seed: int = 0) -> dict:
    key_list = jax.random.split(jax.random.key(seed), 10)
    table = draw_table(jax.random.fold_in(key_list[9], 71), 0)
    w_uvqk = bell_draw(key_list[1], (D, 4, D), D ** -0.5, 0.1875, ((2, 8),))
    w_out = bell_draw(key_list[2], (D, D), D ** -0.5, 0.1875, ((0, 8),))
    history = plant(ranked(key_list[3], (USERS, SEQ), ITEMS, 2), jax.random.fold_in(key_list[3], 3), 0, ITEMS - 1).astype(jnp.int32)
    lengths = ragged(key_list[4], USERS, N_DP * SEQ // 2, SEQ, 2).astype(jnp.int32)
    candidates = plant(jax.random.randint(key_list[5], (USERS, CAND), 0, ITEMS), jax.random.fold_in(key_list[5], 1), 0, ITEMS - 1).astype(jnp.int32)
    counts = draw_counts(jax.random.fold_in(key_list[9], 71), 0)
    actions = draw_actions(jax.random.fold_in(key_list[9], 71), 0)
    targets = bell_draw(key_list[8], (USERS, SEQ), 1.0, 6.0, ((0, 32),), jnp.float32)
    return {"table": table, "w_uvqk": w_uvqk, "w_out": w_out, "history": history, "lengths": lengths, "candidates": candidates, "counts": counts, "actions": actions, "targets": targets}


CQL_WEIGHT = 0.5

def silu_slope(value):
    sigma = jax.nn.sigmoid(value)
    return sigma * (1.0 + value * (1.0 - sigma))

def rounded(value):
    return lax.optimization_barrier(value.astype(jnp.bfloat16)).astype(jnp.float32)

def one_user(table, w_uvqk, w_out, hist, length, cand, count, action, target):
    rows = jnp.take(table, hist, axis=0)
    rows_f = rows.astype(jnp.float32)
    scale = lax.rsqrt(lax.optimization_barrier(jnp.mean(rows_f * rows_f, axis=-1, keepdims=True)) + 1e-06)
    normed_f = rows_f * scale
    normed = normed_f.astype(jnp.bfloat16)
    flat_w = w_uvqk.reshape(D, 4 * D)
    pre = jnp.dot(normed, flat_w, preferred_element_type=jnp.float32)
    act = rounded(jax.nn.silu(pre)).reshape(SEQ, 4, HEADS, HD)
    gate_u, values, queries, keys = (act[:, 0], act[:, 1], act[:, 2], act[:, 3])
    places = jnp.arange(SEQ, dtype=jnp.int32)
    allowed = (places[None, :] <= places[:, None]) & (places[None, :] < length)
    weight = allowed.astype(jnp.float32) / length.astype(jnp.float32)
    logits = jnp.einsum('thd,shd->hts', queries, keys) * HD ** (-0.5)
    attn = rounded(jax.nn.silu(logits) * weight)
    mixed = jnp.einsum('hts,shd->thd', attn, values).reshape(SEQ, D)
    center = lax.optimization_barrier(jnp.mean(mixed, axis=-1, keepdims=True))
    rstd = lax.rsqrt(lax.optimization_barrier(jnp.mean(mixed * mixed, axis=-1, keepdims=True)) - center * center + 1e-05)
    normo = (mixed - center) * rstd
    u_flat = gate_u.reshape(SEQ, D)
    gated = (normo * u_flat).astype(jnp.bfloat16)
    hidden = (rows_f + jnp.dot(gated, w_out, preferred_element_type=jnp.float32)).astype(jnp.bfloat16)
    crows = jnp.take(table, cand, axis=0)
    scores = jnp.dot(hidden, crows.T, preferred_element_type=jnp.float32)
    slots = jnp.arange(CAND, dtype=jnp.int32)
    valid = slots[None, :] < count
    masked = jnp.where(valid, scores, -jnp.inf)
    top = lax.optimization_barrier(jnp.max(masked, axis=-1, keepdims=True))
    expo = jnp.exp(masked - top)
    total = lax.optimization_barrier(jnp.sum(expo, axis=-1, keepdims=True))
    lse = top[:, 0] + jnp.log(total[:, 0])
    soft = expo / total
    onehot = (slots[None, :] == action[:, None]).astype(jnp.float32)
    taken = lax.optimization_barrier(jnp.sum(scores * onehot, axis=-1))
    live = (places < length).astype(jnp.float32) / SEQ
    miss = taken - target
    loss = jnp.sum(live * (CQL_WEIGHT * (lse - taken) + 0.5 * miss * miss))
    dscore = rounded(live[:, None] * (CQL_WEIGHT * soft + (miss - CQL_WEIGHT)[:, None] * onehot))
    dhidden = rounded(jnp.dot(dscore, crows.astype(jnp.float32)))
    block = SEQ // N_ITEM
    pieces = jnp.einsum('nbc,nbd->ncd', dscore.reshape(N_ITEM, block, CAND), hidden.astype(jnp.float32).reshape(N_ITEM, block, D))
    dcand = lax.optimization_barrier(jnp.sum(rounded(pieces), axis=0))
    out_f = w_out.astype(jnp.float32)
    dgated = jnp.dot(dhidden, out_f.T)
    grad_out = jnp.dot(gated.astype(jnp.float32).T, dhidden)
    du = dgated * normo
    dnormo = dgated * u_flat
    first = lax.optimization_barrier(jnp.mean(dnormo, axis=-1, keepdims=True))
    second = lax.optimization_barrier(jnp.mean(dnormo * normo, axis=-1, keepdims=True))
    dmixed = rounded(rstd * (dnormo - first - normo * second)).reshape(SEQ, HEADS, HD)
    dattn = jnp.einsum('thd,shd->hts', dmixed, values)
    dvalues = jnp.einsum('hts,thd->shd', attn, dmixed)
    dlogits = rounded(dattn * weight * silu_slope(logits) * HD ** (-0.5))
    dqueries = jnp.einsum('hts,shd->thd', dlogits, keys)
    dkeys = jnp.einsum('hts,thd->shd', dlogits, queries)
    dact = jnp.stack([du.reshape(SEQ, HEADS, HD), dvalues, dqueries, dkeys], axis=1).reshape(SEQ, 4 * D)
    dpre = (dact * silu_slope(pre)).astype(jnp.bfloat16)
    grad_in = jnp.dot(normed.T, dpre, preferred_element_type=jnp.float32)
    group = HEADS // N_ITEM * HD
    dgroups = jnp.einsum('skne,dkne->nsd', dpre.astype(jnp.float32).reshape(SEQ, 4, N_ITEM, group), w_uvqk.astype(jnp.float32).reshape(D, 4, N_ITEM, group))
    dnormed = lax.optimization_barrier(jnp.sum(rounded(dgroups), axis=0))
    drows = dhidden + scale * (dnormed - normed_f * lax.optimization_barrier(jnp.mean(dnormed * normed_f, axis=-1, keepdims=True)))
    return (loss, grad_in.reshape(D, 4, D), grad_out, drows, dcand)

def reference(table, w_uvqk, w_out, history, lengths, candidates, counts, actions, targets):

    def advance(carry, user):
        loss, grad_in, grad_out, grad_table = carry
        hist, length, cand, count, action, target = user
        terms = one_user(table, w_uvqk, w_out, hist, length, cand, count, action, target)
        grad_table = grad_table.at[hist].add(terms[3]).at[cand].add(terms[4])
        return ((loss + terms[0], grad_in + terms[1], grad_out + terms[2], grad_table), None)
    start = (jnp.zeros((), jnp.float32), jnp.zeros((D, 4, D), jnp.float32), jnp.zeros((D, D), jnp.float32), jnp.zeros((ITEMS, D), jnp.float32))
    final, unused = lax.scan(advance, start, (history, lengths, candidates, counts, actions, targets))
    return (final[0], final[1], final[2], final[3])
```

```python
import jax
import jax.numpy as jnp
from jax import lax
from jax.experimental import pallas as pl
from jax.experimental.pallas import tpu as pltpu
from jax.sharding import Mesh, PartitionSpec as P

HD = 128
NX, NC, NY, NZ = 4, 2, 4, 8
CQL_WEIGHT = 0.5
BF = jnp.bfloat16
F32 = jnp.float32


def silu_slope(value):
    sigma = jax.nn.sigmoid(value)
    return sigma * (1.0 + value * (1.0 - sigma))


def swap_x(value, k):
    return lax.ppermute(value, "x", [(i, i ^ k) for i in range(NX)])


def swap_core(value):
    return lax.ppermute(value, "c", [(0, 1), (1, 0)])


def flip_if(bit, value, axis):
    return jnp.where(bit == 1, jnp.flip(value, axis), value)


def relative_items(value):
    x, c = lax.axis_index("x"), lax.axis_index("c")
    parts = value.reshape((2, 2, 2) + value.shape[1:])
    parts = flip_if(x // 2, parts, 0)
    parts = flip_if(x % 2, parts, 1)
    parts = flip_if(c, parts, 2)
    return jnp.moveaxis(parts, 2, 0).reshape(value.shape)


def reduce_blocks(other, own):
    return (own.astype(F32) + swap_core(other).astype(F32)).astype(BF)


def reduce_line(blocks):
    got = [swap_x(blocks[k], k) for k in range(1, NX)]
    total = blocks[0].astype(F32)
    for part in got:
        total = total + part.astype(F32)
    return total


def gather_item(block):
    line = jnp.concatenate([block] + [swap_x(block, k) for k in range(1, NX)], axis=0)
    return jnp.concatenate([line, swap_core(line)], axis=0)


def exchange_item(blocks):
    own, other = blocks[:NX], swap_core(blocks[NX:])
    got = [jnp.stack([own[0], other[0]])]
    for k in range(1, NX):
        got.append(swap_x(jnp.stack([own[k], other[k]]), k))
    return [got[k][0] for k in range(NX)] + [got[k][1] for k in range(NX)]


def pack_kernel(rows_ref, out_ref):
    count = rows_ref.shape[0] // 4
    for d in range(out_ref.shape[0]):
        out_ref[d] = jnp.concatenate(
            [rows_ref[g * count : (g + 1) * count, 32 * d : 32 * d + 32] for g in range(4)], axis=1
        )


def scatter_kernel(ids_ref, place_ref, data_ref, out_ref, rows_ref, acc_ref):
    users = 32
    slots = data_ref.shape[0] // users
    total = acc_ref.shape[0]
    chunk = 512

    def clear(i, carry):
        acc_ref[pl.ds(pl.multiple_of(i * chunk, chunk), chunk), :] = jnp.zeros((chunk, 128), F32)
        return carry

    lax.fori_loop(0, total // chunk, clear, 0)
    rows_ref[...] = data_ref[...].astype(F32)
    lane = lax.broadcasted_iota(jnp.int32, (1, 128), 1) // 32
    masks = [lane == g for g in range(4)]

    def user(u, carry):
        base = u * (4 * slots)

        def step(i, inner):
            for j in range(8):
                p = i * 8 + j
                row = rows_ref[pl.ds(u * slots + p, 1), :]
                ids = [ids_ref[base + g * slots + p] for g in range(4)]
                held = [acc_ref[pl.ds(ids[g], 1), :] for g in range(4)]
                for g in range(4):
                    pltpu.store(acc_ref.at[pl.ds(ids[g], 1), :], held[g] + row, mask=masks[g])
            return inner

        return lax.fori_loop(0, slots // 8, step, carry)

    lax.fori_loop(0, users, user, 0)
    x, c = place_ref[0], place_ref[1]
    wide = lax.broadcasted_iota(jnp.int32, (512, 128), 1) // 32
    for cc in range(2):
        for k in range(4):
            item = 2 * jnp.bitwise_xor(x, k) + jnp.bitwise_xor(c, cc)
            result = jnp.zeros((512, 128), F32)
            for q in range(4):
                part = acc_ref[pl.ds(pl.multiple_of(item * 2048 + q * 512, 512), 512), :]
                part = part + pltpu.roll(part, 64, 1)
                part = part + pltpu.roll(part, 32, 1)
                result = jnp.where(wide == q, part, result)
            out_ref[cc * 4 + k] = result.astype(BF)


def unpack_kernel(a_ref, b_ref, c_ref, d_ref, out_ref):
    total = (
        a_ref[...].astype(F32)
        + b_ref[...].astype(F32)
        + c_ref[...].astype(F32)
        + d_ref[...].astype(F32)
    )
    turned = total.T
    for q in range(4):
        out_ref[:, q * 512 : (q + 1) * 512] = turned[32 * q : 32 * q + 32, :]


def whole(count, smem=0):
    specs = [pl.BlockSpec(memory_space=pltpu.SMEM)] * smem
    return specs + [pl.BlockSpec(memory_space=pltpu.VMEM)] * count


def on_device(table, w_uvqk, w_out, history, lengths, candidates, counts, actions, targets):
    rows_total, width = table.shape
    seq = history.shape[1]
    ncand = candidates.shape[1]
    parts = NX * NC
    block = seq // parts
    cblock = ncand // parts
    x, c = lax.axis_index("x"), lax.axis_index("c")
    owner = 2 * x + c
    first_row = owner * rows_total
    local_w = w_uvqk.reshape(width, -1)
    length = lengths[0]

    w_out_all = gather_item(w_out)

    history_rel = relative_items(history[0].reshape(parts, block)).reshape(-1)
    cand_rel = relative_items(candidates[0].reshape(parts, cblock)).reshape(-1)
    own_ids = jnp.concatenate(
        [
            lax.dynamic_slice_in_dim(history[0], owner * block, block, 0),
            lax.dynamic_slice_in_dim(candidates[0], owner * cblock, cblock, 0),
        ]
    )

    ids = own_ids[None]
    for axis, size in (("z", NZ), ("y", NY)):
        step = 1
        while step < size:
            got = lax.ppermute(ids, axis, [(i, i ^ step) for i in range(size)])
            ids = jnp.concatenate([ids, got], axis=0)
            step *= 2
    y, z = lax.axis_index("y"), lax.axis_index("z")
    ids = ids.reshape(2, 2, 2, 2, 2, -1)
    for bit, axis in ((y // 2, 0), (y % 2, 1), (z // 4, 2), (z // 2 % 2, 3), (z % 2, 4)):
        ids = flip_if(bit, ids, axis)
    all_ids = ids.reshape(-1)

    def pick(wanted):
        local = wanted - first_row
        mine = (local >= 0) & (local < rows_total)
        found = jnp.take(table, jnp.clip(local, 0, rows_total - 1), axis=0)
        return jnp.where(mine[:, None], found, jnp.zeros((), BF))

    def fetch(wanted, size):
        half = NX * size
        other = pick(wanted[half:]).reshape(NX, size, width)
        own = pick(wanted[:half]).reshape(NX, size, width)
        return reduce_line(reduce_blocks(other, own))

    rows_f = fetch(history_rel, block)
    scale = lax.rsqrt(jnp.mean(rows_f * rows_f, axis=-1, keepdims=True) + 1e-06)
    normed_f = rows_f * scale
    normed = gather_item(normed_f.astype(BF))
    crows = gather_item(fetch(cand_rel, cblock).astype(BF))

    pre = jnp.dot(normed, local_w, preferred_element_type=F32)
    act = jax.nn.silu(pre).astype(BF)
    gate_u, values, queries, keys = (act[:, HD * i : HD * i + HD] for i in range(4))
    gate_all = exchange_item(gate_u.reshape(parts, block, HD))
    places = (
        relative_items(jnp.arange(parts, dtype=jnp.int32))[:, None] * block
        + jnp.arange(block, dtype=jnp.int32)[None, :]
    ).reshape(-1)
    allowed = (places[None, :] <= places[:, None]) & (places[None, :] < length)
    weight = allowed.astype(F32) / length.astype(F32)
    logits = jnp.einsum("td,sd->ts", queries, keys, preferred_element_type=F32) * HD ** (-0.5)
    attn = (jax.nn.silu(logits) * weight).astype(BF)
    mixed_own = jnp.dot(attn, values, preferred_element_type=F32)

    mixed = jnp.concatenate(exchange_item(mixed_own.reshape(parts, block, HD)), axis=1)
    u_flat = jnp.concatenate(gate_all, axis=1).astype(F32)
    center = jnp.mean(mixed, axis=-1, keepdims=True)
    rstd = lax.rsqrt(jnp.mean(mixed * mixed, axis=-1, keepdims=True) - center * center + 1e-05)
    normo = (mixed - center) * rstd
    gated = (normo * u_flat).astype(BF)
    hidden = (rows_f + jnp.dot(gated, w_out_all, preferred_element_type=F32)).astype(BF)

    scores = jnp.einsum("td,cd->tc", hidden, crows, preferred_element_type=F32)
    slots = (
        relative_items(jnp.arange(parts, dtype=jnp.int32))[:, None] * cblock
        + jnp.arange(cblock, dtype=jnp.int32)[None, :]
    ).reshape(-1)
    valid = slots[None, :] < counts[0]
    masked = jnp.where(valid, scores, -jnp.inf)
    top = jnp.max(masked, axis=-1, keepdims=True)
    expo = jnp.exp(masked - top)
    total = jnp.sum(expo, axis=-1, keepdims=True)
    lse = top[:, 0] + jnp.log(total[:, 0])
    soft = expo / total
    begin = owner * block
    action_block = lax.dynamic_slice_in_dim(actions[0], begin, block, 0)
    target_block = lax.dynamic_slice_in_dim(targets[0], begin, block, 0)
    onehot = (slots[None, :] == action_block[:, None]).astype(F32)
    taken = jnp.sum(scores * onehot, axis=-1)
    block_places = begin + jnp.arange(block, dtype=jnp.int32)
    live = (block_places < length).astype(F32) / seq
    miss = taken - target_block
    loss = jnp.sum(live * (CQL_WEIGHT * (lse - taken) + 0.5 * miss * miss)).reshape(1, 1)
    dscore = (live[:, None] * (CQL_WEIGHT * soft + (miss - CQL_WEIGHT)[:, None] * onehot)).astype(BF)
    dhidden = jnp.dot(dscore, crows, preferred_element_type=F32).astype(BF)

    dgated = jnp.einsum("td,ed->te", dhidden, w_out_all, preferred_element_type=F32)
    du = dgated * normo
    dnormo = dgated * u_flat
    first = jnp.mean(dnormo, axis=-1, keepdims=True)
    second = jnp.mean(dnormo * normo, axis=-1, keepdims=True)
    dmixed_all = (rstd * (dnormo - first - normo * second)).astype(BF)
    back = jnp.concatenate(
        [
            jnp.moveaxis(dmixed_all.reshape(block, parts, HD), 1, 0),
            jnp.moveaxis(du.astype(BF).reshape(block, parts, HD), 1, 0),
        ],
        axis=2,
    )
    back = jnp.concatenate(exchange_item(back), axis=0)
    dmixed, du_own = back[:, :HD], back[:, HD:].astype(F32)

    half = NX * cblock
    dcand_other = jnp.einsum("tc,td->cd", dscore[:, half:], hidden, preferred_element_type=F32)
    dcand_own = jnp.einsum("tc,td->cd", dscore[:, :half], hidden, preferred_element_type=F32)
    dcand = reduce_line(
        reduce_blocks(
            dcand_other.astype(BF).reshape(NX, cblock, width), dcand_own.astype(BF).reshape(NX, cblock, width)
        )
    )
    half = NX * HD
    gout_other = jnp.einsum("td,te->de", dhidden, gated[:, half:], preferred_element_type=F32)
    gout_own = jnp.einsum("td,te->de", dhidden, gated[:, :half], preferred_element_type=F32)
    gout = reduce_blocks(gout_other.astype(BF), gout_own.astype(BF))
    gout = reduce_line([gout[:, HD * k : HD * k + HD] for k in range(NX)])

    for axis, size in (("c", NC), ("x", NX), ("z", NZ), ("y", NY)):
        step = 1
        while step < size:
            loss = loss + lax.ppermute(loss, axis, [(i, i ^ step) for i in range(size)])
            step *= 2

    dattn = jnp.einsum("td,sd->ts", dmixed, values, preferred_element_type=F32)
    dvalues = jnp.einsum("ts,td->sd", attn, dmixed, preferred_element_type=F32)
    dlogits = (dattn * weight * silu_slope(logits) * HD ** (-0.5)).astype(BF)
    dqueries = jnp.einsum("ts,sd->td", dlogits, keys, preferred_element_type=F32)
    dkeys = jnp.einsum("ts,td->sd", dlogits, queries, preferred_element_type=F32)
    dact = jnp.concatenate([du_own, dvalues, dqueries, dkeys], axis=1)
    dpre = (dact * silu_slope(pre)).astype(BF)

    half = NX * block
    part_other = jnp.einsum("sk,dk->sd", dpre[half:], local_w, preferred_element_type=F32)
    part_own = jnp.einsum("sk,dk->sd", dpre[:half], local_w, preferred_element_type=F32)
    dnormed = reduce_line(
        reduce_blocks(
            part_other.astype(BF).reshape(NX, block, width), part_own.astype(BF).reshape(NX, block, width)
        )
    )

    dw_in = jnp.einsum("sd,sk->dk", normed, dpre, preferred_element_type=F32)
    grads = jnp.concatenate([dw_in.astype(BF), gout.astype(BF)], axis=1)
    grads = grads.reshape(NY, NZ * 32, -1)
    grads = lax.psum_scatter(grads, "y", scatter_dimension=0, tiled=False)
    grads = lax.psum_scatter(grads, "z", scatter_dimension=0, tiled=True).astype(F32)
    grad_in = grads[:, : 4 * HD].reshape(-1, 4, HD)
    grad_proj = grads[:, 4 * HD :].T

    drows = dhidden.astype(F32) + scale * (
        dnormed - normed_f * jnp.mean(dnormed * normed_f, axis=-1, keepdims=True)
    )
    sparse = jnp.concatenate([drows.astype(BF), dcand.astype(BF)], axis=0)
    users = NY * NZ
    count = sparse.shape[0] // 4
    packed = pl.pallas_call(
        pack_kernel,
        out_shape=jax.ShapeDtypeStruct((users, count, 128), BF),
        in_specs=whole(1),
        out_specs=whole(1)[0],
        name="pack",
    )(sparse)
    arrived = lax.all_to_all(packed, ("y", "z"), 0, 0).reshape(users * count, 128)
    per_item = pl.pallas_call(
        scatter_kernel,
        out_shape=jax.ShapeDtypeStruct((parts, 512, 128), BF),
        in_specs=whole(1, smem=2),
        out_specs=whole(1)[0],
        scratch_shapes=[
            pltpu.VMEM((users * count, 128), F32),
            pltpu.VMEM((parts * rows_total, 128), F32),
        ],
        compiler_params=pltpu.CompilerParams(vmem_limit_bytes=40 * 1024 * 1024),
        name="scatter",
    )(all_ids, jnp.stack([x, c]).astype(jnp.int32), arrived)
    mine = reduce_blocks(per_item[NX:], per_item[:NX])
    pieces = [mine[0]] + [swap_x(mine[k], k) for k in range(1, NX)]
    shard_t = pl.pallas_call(
        unpack_kernel,
        out_shape=jax.ShapeDtypeStruct((32, rows_total), F32),
        in_specs=whole(4),
        out_specs=whole(1)[0],
        name="unpack",
    )(*pieces)
    return (loss[0, 0], grad_in, grad_proj, shard_t.T)


def solution(mesh):
    fine = Mesh(mesh.devices.reshape(NY, NZ, NX, NC), ("y", "z", "x", "c"))
    dp, item = ("y", "z"), ("x", "c")
    placed = (
        P(item, None),
        P(None, None, item),
        P(item, None),
        P(dp, None),
        P(dp),
        P(dp, None),
        P(dp),
        P(dp, None),
        P(dp, None),
    )
    return jax.shard_map(
        on_device,
        mesh=fine,
        in_specs=placed,
        out_specs=(P(), P(dp, None, item), P(item, dp), P(item, dp)),
        check_vma=False,
    )
```

```python
import jax
import jax.numpy as jnp
from jax import lax
from jax.experimental import pallas as pl
from jax.experimental.pallas import tpu as pltpu
from jax.sharding import Mesh, PartitionSpec as P

HD = 128
NX, NC, NY, NZ = 4, 2, 4, 8
CQL_WEIGHT = 0.5
BF = jnp.bfloat16
F32 = jnp.float32


def silu_slope(value):
    sigma = jax.nn.sigmoid(value)
    return sigma * (1.0 + value * (1.0 - sigma))


def swap_x(value, k):
    return lax.ppermute(value, "x", [(i, i ^ k) for i in range(NX)])


def swap_core(value):
    return lax.ppermute(value, "c", [(0, 1), (1, 0)])


def flip_if(bit, value, axis):
    return jnp.where(bit == 1, jnp.flip(value, axis), value)


def relative_items(value):
    x, c = lax.axis_index("x"), lax.axis_index("c")
    parts = value.reshape((2, 2, 2) + value.shape[1:])
    parts = flip_if(x // 2, parts, 0)
    parts = flip_if(x % 2, parts, 1)
    parts = flip_if(c, parts, 2)
    return jnp.moveaxis(parts, 2, 0).reshape(value.shape)


def reduce_blocks(other, own):
    return (own.astype(F32) + swap_core(other).astype(F32)).astype(BF)


def reduce_line(blocks):
    got = [swap_x(blocks[k], k) for k in range(1, NX)]
    total = blocks[0].astype(F32)
    for part in got:
        total = total + part.astype(F32)
    return total


def gather_item(block):
    line = jnp.concatenate([block] + [swap_x(block, k) for k in range(1, NX)], axis=0)
    return jnp.concatenate([line, swap_core(line)], axis=0)


def exchange_item(blocks):
    own, other = blocks[:NX], swap_core(blocks[NX:])
    got = [jnp.stack([own[0], other[0]])]
    for k in range(1, NX):
        got.append(swap_x(jnp.stack([own[k], other[k]]), k))
    return [got[k][0] for k in range(NX)] + [got[k][1] for k in range(NX)]


def after(value, *others):
    return lax.optimization_barrier((value,) + others)[0]


def pack_kernel(weights_ref, events_ref, cands_ref, meta_ref, out_ref):
    for d in range(out_ref.shape[0]):
        for h in range(4):
            out_ref[d, 32 * h : 32 * h + 32, :] = weights_ref[
                32 * d : 32 * d + 32, 128 * h : 128 * h + 128
            ]
        out_ref[d, 128:160, :] = jnp.concatenate(
            [events_ref[32 * g : 32 * g + 32, 32 * d : 32 * d + 32] for g in range(4)], axis=1
        )
        out_ref[d, 160:176, :] = jnp.concatenate(
            [cands_ref[16 * g : 16 * g + 16, 32 * d : 32 * d + 32] for g in range(4)], axis=1
        )
        out_ref[d, 176:192, :] = meta_ref[...]


def scatter_kernel(ids_ref, place_ref, data_ref, out_ref, rows_ref, acc_ref):
    users = data_ref.shape[0]
    total = acc_ref.shape[0]
    chunk = 512
    x, c = place_ref[0], place_ref[1]
    owner = 2 * x + c

    def clear(i, carry):
        acc_ref[pl.ds(pl.multiple_of(i * chunk, chunk), chunk), :] = jnp.zeros((chunk, 128), F32)
        return carry

    lax.fori_loop(0, total // chunk, clear, 0)
    for u in range(users):
        rows_ref[48 * u : 48 * u + 48, :] = data_ref[u, 128:176, :].astype(F32)
    lane = lax.broadcasted_iota(jnp.int32, (1, 128), 1) // 32
    masks = [lane == g for g in range(4)]

    def add(first_id, pitch, first_row, count):
        def step(i, carry):
            for j in range(4):
                p = i * 4 + j
                row = rows_ref[pl.ds(first_row + p, 1), :]
                ids = [ids_ref[first_id + g * pitch + p] for g in range(4)]
                held = [acc_ref[pl.ds(ids[g], 1), :] for g in range(4)]
                for g in range(4):
                    pltpu.store(acc_ref.at[pl.ds(ids[g], 1), :], held[g] + row, mask=masks[g])
            return carry

        lax.fori_loop(0, (count + 3) // 4, step, 0)

    def user(u, carry):
        base = u * 256
        events = jnp.clip((ids_ref[base + 192] - owner + 31) // 32, 0, 32)
        cands = jnp.clip((ids_ref[base + 193] - owner + 31) // 32, 0, 16)
        add(base, 32, u * 48, events)
        add(base + 128, 16, u * 48 + 32, cands)
        return carry

    lax.fori_loop(0, users, user, 0)
    wide = lax.broadcasted_iota(jnp.int32, (512, 128), 1) // 32
    for cc in range(2):
        for k in range(4):
            item = 2 * jnp.bitwise_xor(x, k) + jnp.bitwise_xor(c, cc)
            result = jnp.zeros((512, 128), F32)
            for q in range(4):
                part = acc_ref[pl.ds(pl.multiple_of(item * 2048 + q * 512, 512), 512), :]
                part = part + pltpu.roll(part, 64, 1)
                part = part + pltpu.roll(part, 32, 1)
                result = jnp.where(wide == q, part, result)
            out_ref[cc * 4 + k] = result.astype(BF)


def unpack_kernel(a_ref, b_ref, c_ref, d_ref, out_ref):
    total = (
        a_ref[...].astype(F32)
        + b_ref[...].astype(F32)
        + c_ref[...].astype(F32)
        + d_ref[...].astype(F32)
    )
    turned = total.T
    for q in range(4):
        out_ref[:, q * 512 : (q + 1) * 512] = turned[32 * q : 32 * q + 32, :]


def whole(count, smem=0):
    specs = [pl.BlockSpec(memory_space=pltpu.SMEM)] * smem
    return specs + [pl.BlockSpec(memory_space=pltpu.VMEM)] * count


def on_device(table, w_uvqk, w_out, history, lengths, candidates, counts, actions, targets):
    rows_total, width = table.shape
    seq = history.shape[1]
    ncand = candidates.shape[1]
    users = NY * NZ
    parts = NX * NC
    block = seq // parts
    cblock = ncand // parts
    x, c = lax.axis_index("x"), lax.axis_index("c")
    owner = 2 * x + c
    first_row = owner * rows_total
    local_w = w_uvqk.reshape(width, -1)
    length = lengths[0]

    def deal(values):
        return jnp.moveaxis(values.reshape(-1, 4, parts), 2, 0).swapaxes(1, 2).reshape(parts, -1)

    def own_of(values):
        return lax.dynamic_index_in_dim(values, owner, 0, keepdims=False)

    w_out_all = gather_item(w_out)

    history_all, cand_all = deal(history[0]), deal(candidates[0])
    history_rel = relative_items(history_all).reshape(-1)
    cand_rel = relative_items(cand_all).reshape(-1)
    places_all = deal(jnp.arange(seq, dtype=jnp.int32))
    slots_all = deal(jnp.arange(ncand, dtype=jnp.int32))

    def pick(wanted):
        local = wanted - first_row
        rows = jnp.arange(rows_total, dtype=jnp.int32)
        hot = (local[:, None] == rows[None, :]).astype(BF)
        return jnp.dot(hot, table, preferred_element_type=F32).astype(BF)

    def line_of(wanted, size):
        half = NX * size
        other = pick(wanted[half:]).reshape(NX, size, width)
        own = pick(wanted[:half]).reshape(NX, size, width)
        return reduce_blocks(other, own)

    row_line = line_of(history_rel, block)
    rows_f = reduce_line(row_line)
    scale = lax.rsqrt(jnp.mean(rows_f * rows_f, axis=-1, keepdims=True) + 1e-06)
    normed_f = rows_f * scale
    normed = gather_item(normed_f.astype(BF))
    cand_line = line_of(after(cand_rel, row_line), cblock)
    crows = gather_item(reduce_line(after(cand_line, normed_f)).astype(BF))

    pre = jnp.dot(normed, local_w, preferred_element_type=F32)
    act = jax.nn.silu(pre).astype(BF)
    gate_u, values, queries, keys = (act[:, HD * i : HD * i + HD] for i in range(4))
    places = relative_items(places_all).reshape(-1)
    allowed = (places[None, :] <= places[:, None]) & (places[None, :] < length)
    weight = allowed.astype(F32) / length.astype(F32)
    logits = jnp.einsum("td,sd->ts", queries, keys, preferred_element_type=F32) * HD ** (-0.5)
    attn = (jax.nn.silu(logits) * weight).astype(BF)
    mixed_own = jnp.dot(attn, values, preferred_element_type=F32)
    mixed_top = mixed_own.astype(BF)
    mixed_rest = (mixed_own - mixed_top.astype(F32)).astype(BF)
    sent = jnp.concatenate([mixed_top, mixed_rest, gate_u], axis=1).reshape(parts, block, 3 * HD)
    sent = exchange_item(sent)

    mixed = jnp.concatenate(
        [part[:, :HD].astype(F32) + part[:, HD : 2 * HD].astype(F32) for part in sent], axis=1
    )
    u_flat = jnp.concatenate([part[:, 2 * HD :] for part in sent], axis=1).astype(F32)
    center = jnp.mean(mixed, axis=-1, keepdims=True)
    rstd = lax.rsqrt(jnp.mean(mixed * mixed, axis=-1, keepdims=True) - center * center + 1e-05)
    normo = (mixed - center) * rstd
    gated = (normo * u_flat).astype(BF)
    hidden = (rows_f + jnp.dot(gated, w_out_all, preferred_element_type=F32)).astype(BF)

    scores = jnp.einsum("td,cd->tc", hidden, crows, preferred_element_type=F32)
    slots = relative_items(slots_all).reshape(-1)
    valid = slots[None, :] < counts[0]
    masked = jnp.where(valid, scores, -jnp.inf)
    top = jnp.max(masked, axis=-1, keepdims=True)
    expo = jnp.exp(masked - top)
    total = jnp.sum(expo, axis=-1, keepdims=True)
    lse = top[:, 0] + jnp.log(total[:, 0])
    soft = expo / total
    action_block = own_of(deal(actions[0]))
    target_block = own_of(deal(targets[0]))
    onehot = (slots[None, :] == action_block[:, None]).astype(F32)
    taken = jnp.sum(scores * onehot, axis=-1)
    live = (own_of(places_all) < length).astype(F32) / seq
    miss = taken - target_block
    loss = jnp.sum(live * (CQL_WEIGHT * (lse - taken) + 0.5 * miss * miss)).reshape(1, 1)
    dscore = (live[:, None] * (CQL_WEIGHT * soft + (miss - CQL_WEIGHT)[:, None] * onehot)).astype(BF)
    dhidden = jnp.dot(dscore, crows, preferred_element_type=F32).astype(BF)

    dgated = jnp.einsum("td,ed->te", dhidden, w_out_all, preferred_element_type=F32)
    du = dgated * normo
    dnormo = dgated * u_flat
    first = jnp.mean(dnormo, axis=-1, keepdims=True)
    second = jnp.mean(dnormo * normo, axis=-1, keepdims=True)
    dmixed_all = (rstd * (dnormo - first - normo * second)).astype(BF)
    du = du.astype(BF)
    back = jnp.stack(
        [
            jnp.concatenate([dmixed_all[:, HD * i : HD * i + HD], du[:, HD * i : HD * i + HD]], axis=1)
            for i in range(parts)
        ]
    )
    dscore_b, dhidden_b, back = lax.optimization_barrier((dscore, dhidden, back))
    back = jnp.concatenate(exchange_item(back), axis=0)
    dmixed, du_own = back[:, :HD], back[:, HD:].astype(F32)

    half = NX * cblock
    dcand_other = jnp.einsum("tc,td->cd", dscore_b[:, half:], hidden, preferred_element_type=F32)
    dcand_own = jnp.einsum("tc,td->cd", dscore_b[:, :half], hidden, preferred_element_type=F32)
    dcand = reduce_line(
        reduce_blocks(
            dcand_other.astype(BF).reshape(NX, cblock, width), dcand_own.astype(BF).reshape(NX, cblock, width)
        )
    ).astype(BF)
    gout = jnp.einsum("td,te->de", dhidden_b, gated, preferred_element_type=F32).astype(BF)
    gout = lax.psum_scatter(gout.reshape(NY, -1, width), "y", scatter_dimension=0, tiled=False)
    for axis, k in (("c", 1), ("x", 1), ("x", 2)):
        size = NC if axis == "c" else NX
        loss = loss + lax.ppermute(loss, axis, [(i, i ^ k) for i in range(size)])

    dattn = jnp.einsum("td,sd->ts", dmixed, values, preferred_element_type=F32)
    dvalues = jnp.einsum("ts,td->sd", attn, dmixed, preferred_element_type=F32)
    dlogits = (dattn * weight * silu_slope(logits) * HD ** (-0.5)).astype(BF)
    dqueries = jnp.einsum("ts,sd->td", dlogits, keys, preferred_element_type=F32)
    dkeys = jnp.einsum("ts,td->sd", dlogits, queries, preferred_element_type=F32)
    dact = jnp.concatenate([du_own, dvalues, dqueries, dkeys], axis=1)
    dpre = (dact * silu_slope(pre)).astype(BF)
    dpre = after(dpre, dcand)

    half = NX * block
    part_other = jnp.einsum("sk,dk->sd", dpre[half:], local_w, preferred_element_type=F32)
    part_own = jnp.einsum("sk,dk->sd", dpre[:half], local_w, preferred_element_type=F32)
    dnormed_line = reduce_blocks(
        part_other.astype(BF).reshape(NX, block, width), part_own.astype(BF).reshape(NX, block, width)
    )
    dnormed = reduce_line(dnormed_line)
    dw_in = jnp.einsum("sd,sk->dk", normed, dpre, preferred_element_type=F32).astype(BF)

    drows = dhidden.astype(F32) + scale * (
        dnormed - normed_f * jnp.mean(dnormed * normed_f, axis=-1, keepdims=True)
    )
    drows = drows.astype(BF)
    gout = lax.psum_scatter(after(gout, drows), "z", scatter_dimension=0, tiled=True)

    ids = jnp.concatenate(
        [
            own_of(history_all),
            own_of(cand_all),
            lengths,
            counts,
            jnp.zeros((62,), jnp.int32),
        ]
    ).reshape(2, 128)
    loss_top = loss.astype(BF).astype(F32)
    loss_mid = (loss - loss_top).astype(BF).astype(F32)
    loss_low = loss - loss_top - loss_mid
    loss_row = jnp.concatenate([loss_top, loss_mid, loss_low, jnp.zeros((1, 125), F32)], axis=1)
    meta = jnp.concatenate(
        [(ids // 128).astype(BF), (ids % 128).astype(BF), loss_row.astype(BF), jnp.zeros((11, 128), BF)]
    )
    packed = pl.pallas_call(
        pack_kernel,
        out_shape=jax.ShapeDtypeStruct((users, 192, 128), BF),
        in_specs=whole(4),
        out_specs=whole(1)[0],
        name="pack",
    )(dw_in, drows, dcand, meta)
    arrived = lax.all_to_all(packed, ("y", "z"), 0, 0)
    got = arrived[:, 176:181].astype(F32)
    all_ids = (got[:, 0:2] * 128.0 + got[:, 2:4]).astype(jnp.int32).reshape(-1)
    per_item = pl.pallas_call(
        scatter_kernel,
        out_shape=jax.ShapeDtypeStruct((parts, 512, 128), BF),
        in_specs=whole(1, smem=2),
        out_specs=whole(1)[0],
        scratch_shapes=[
            pltpu.VMEM((users * 48, 128), F32),
            pltpu.VMEM((parts * rows_total, 128), F32),
        ],
        compiler_params=pltpu.CompilerParams(vmem_limit_bytes=40 * 1024 * 1024),
        name="scatter",
    )(all_ids, jnp.stack([x, c]).astype(jnp.int32), arrived)
    mine = reduce_blocks(per_item[NX:], per_item[:NX])
    pieces = [mine[0]] + [swap_x(mine[k], k) for k in range(1, NX)]
    shard_t = pl.pallas_call(
        unpack_kernel,
        out_shape=jax.ShapeDtypeStruct((32, rows_total), F32),
        in_specs=whole(4),
        out_specs=whole(1)[0],
        name="unpack",
    )(*pieces)

    loss = jnp.sum(got[:, 4, 0:3])
    late = after(arrived, per_item)
    grad_in = jnp.sum(late[:, :128].astype(F32), axis=0).reshape(4, 32, HD).swapaxes(0, 1)
    half = NX * HD
    gout = gout[:, :half].astype(F32) + swap_core(gout[:, half:]).astype(F32)
    gout = gout.astype(BF)
    grad_proj = reduce_line([gout[:, HD * k : HD * k + HD] for k in range(NX)])
    return (loss, grad_in, grad_proj.T, shard_t.T)


def solution(mesh):
    fine = Mesh(mesh.devices.reshape(NY, NZ, NX, NC), ("y", "z", "x", "c"))
    dp, item = ("y", "z"), ("x", "c")
    placed = (
        P(item, None),
        P(None, None, item),
        P(item, None),
        P(dp, None),
        P(dp),
        P(dp, None),
        P(dp),
        P(dp, None),
        P(dp, None),
    )
    return jax.shard_map(
        on_device,
        mesh=fine,
        in_specs=placed,
        out_specs=(P(), P(dp, None, item), P(item, dp), P(item, dp)),
        check_vma=False,
    )
```

```python
import jax
import jax.numpy as jnp
from jax import lax
from jax.experimental import pallas as pl
from jax.experimental.pallas import tpu as pltpu
from jax.sharding import Mesh, PartitionSpec as P

HD = 128
NX, NC, NY, NZ = 4, 2, 4, 8
CQL_WEIGHT = 0.5
BF = jnp.bfloat16
F32 = jnp.float32


def silu_slope(value):
    sigma = jax.nn.sigmoid(value)
    return sigma * (1.0 + value * (1.0 - sigma))


def swap_x(value, k):
    return lax.ppermute(value, "x", [(i, i ^ k) for i in range(NX)])


def swap_core(value):
    return lax.ppermute(value, "c", [(0, 1), (1, 0)])


def flip_if(bit, value, axis):
    return jnp.where(bit == 1, jnp.flip(value, axis), value)


def relative_items(value):
    x, c = lax.axis_index("x"), lax.axis_index("c")
    parts = value.reshape((2, 2, 2) + value.shape[1:])
    parts = flip_if(x // 2, parts, 0)
    parts = flip_if(x % 2, parts, 1)
    parts = flip_if(c, parts, 2)
    return jnp.moveaxis(parts, 2, 0).reshape(value.shape)


def reduce_blocks(other, own):
    return (own.astype(F32) + swap_core(other).astype(F32)).astype(BF)


def reduce_line(blocks):
    got = [swap_x(blocks[k], k) for k in range(1, NX)]
    total = blocks[0].astype(F32)
    for part in got:
        total = total + part.astype(F32)
    return total


def exchange_item(blocks):
    own, other = blocks[:NX], swap_core(blocks[NX:])
    got = [jnp.stack([own[0], other[0]])]
    for k in range(1, NX):
        got.append(swap_x(jnp.stack([own[k], other[k]]), k))
    return [got[k][0] for k in range(NX)] + [got[k][1] for k in range(NX)]


def after(value, *others):
    return lax.optimization_barrier((value,) + others)[0]


def pick_kernel(ids_ref, table_ref, out_ref, hot_ref):
    @pl.when(pl.program_id(0) == 0)
    def _():
        chunk = 256
        for i in range(hot_ref.shape[1] // chunk):
            rows = lax.broadcasted_iota(jnp.int32, (hot_ref.shape[0], chunk), 1) + i * chunk
            hot_ref[:, i * chunk : (i + 1) * chunk] = (ids_ref[...] == rows).astype(F32).astype(BF)

    out_ref[...] = jnp.dot(hot_ref[...], table_ref[...], preferred_element_type=F32).astype(BF)


def pack_kernel(events_ref, cands_ref, meta_ref, out_ref):
    for d in range(out_ref.shape[0]):
        out_ref[d, 0:32, :] = jnp.concatenate(
            [events_ref[32 * g : 32 * g + 32, 32 * d : 32 * d + 32] for g in range(4)], axis=1
        )
        out_ref[d, 32:48, :] = jnp.concatenate(
            [cands_ref[16 * g : 16 * g + 16, 32 * d : 32 * d + 32] for g in range(4)], axis=1
        )
        out_ref[d, 48:64, :] = meta_ref[...]


def scatter_kernel(ids_ref, place_ref, data_ref, out_ref, rows_ref, acc_ref):
    users = data_ref.shape[0]
    total = acc_ref.shape[0]
    chunk = 512
    x, c = place_ref[0], place_ref[1]
    owner = 2 * x + c

    def clear(i, carry):
        acc_ref[pl.ds(pl.multiple_of(i * chunk, chunk), chunk), :] = jnp.zeros((chunk, 128), F32)
        return carry

    lax.fori_loop(0, total // chunk, clear, 0)
    for u in range(users):
        rows_ref[48 * u : 48 * u + 48, :] = data_ref[u, 0:48, :].astype(F32)
    lane = lax.broadcasted_iota(jnp.int32, (1, 128), 1) // 32
    masks = [lane == g for g in range(4)]

    def add(first_id, pitch, first_row, count):
        def step(i, carry):
            for j in range(4):
                p = i * 4 + j
                row = rows_ref[pl.ds(first_row + p, 1), :]
                ids = [ids_ref[first_id + g * pitch + p] for g in range(4)]
                held = [acc_ref[pl.ds(ids[g], 1), :] for g in range(4)]
                for g in range(4):
                    pltpu.store(acc_ref.at[pl.ds(ids[g], 1), :], held[g] + row, mask=masks[g])
            return carry

        lax.fori_loop(0, (count + 3) // 4, step, 0)

    def user(u, carry):
        base = u * 256
        events = jnp.clip((ids_ref[base + 192] - owner + 31) // 32, 0, 32)
        cands = jnp.clip((ids_ref[base + 193] - owner + 31) // 32, 0, 16)
        add(base, 32, u * 48, events)
        add(base + 128, 16, u * 48 + 32, cands)
        return carry

    lax.fori_loop(0, users, user, 0)
    wide = lax.broadcasted_iota(jnp.int32, (512, 128), 1) // 32
    for cc in range(2):
        for k in range(4):
            item = 2 * jnp.bitwise_xor(x, k) + jnp.bitwise_xor(c, cc)
            result = jnp.zeros((512, 128), F32)
            for q in range(4):
                part = acc_ref[pl.ds(pl.multiple_of(item * 2048 + q * 512, 512), 512), :]
                part = part + pltpu.roll(part, 64, 1)
                part = part + pltpu.roll(part, 32, 1)
                result = jnp.where(wide == q, part, result)
            out_ref[cc * 4 + k] = result.astype(BF)


def unpack_kernel(own_ref, proj_ref, b_ref, c_ref, d_ref, out_ref, proj_out_ref):
    total = own_ref[...].astype(F32)
    proj = proj_ref[...].astype(F32)
    for ref in (b_ref, c_ref, d_ref):
        total = total + ref[:512, :].astype(F32)
        proj = proj + ref[512:, :].astype(F32)
    proj_out_ref[...] = proj
    turned = total.T
    for q in range(4):
        out_ref[:, q * 512 : (q + 1) * 512] = turned[32 * q : 32 * q + 32, :]


def whole(count, smem=0):
    specs = [pl.BlockSpec(memory_space=pltpu.SMEM)] * smem
    return specs + [pl.BlockSpec(memory_space=pltpu.VMEM)] * count


def on_device(table, w_uvqk, w_out, history, lengths, candidates, counts, actions, targets):
    rows_total, width = table.shape
    seq = history.shape[1]
    ncand = candidates.shape[1]
    users = NY * NZ
    parts = NX * NC
    block = seq // parts
    cblock = ncand // parts
    x, c = lax.axis_index("x"), lax.axis_index("c")
    owner = 2 * x + c
    first_row = owner * rows_total
    local_w = w_uvqk.reshape(width, -1)
    length = lengths[0]

    def deal(values):
        return jnp.moveaxis(values.reshape(-1, 4, parts), 2, 0).swapaxes(1, 2).reshape(parts, -1)

    def own_of(values):
        return lax.dynamic_index_in_dim(values, owner, 0, keepdims=False)

    def from_items(values, size, flip):
        return [
            lax.dynamic_slice_in_dim(
                values, (2 * jnp.bitwise_xor(x, k) + jnp.bitwise_xor(c, flip)) * size, size, 0
            )
            for k in range(NX)
        ]

    w_out_all = lax.all_gather(w_out, ("x", "c"), axis=0, tiled=True)
    w_out_all = jnp.concatenate(from_items(w_out_all, HD, 0) + from_items(w_out_all, HD, 1), axis=0)

    history_all, cand_all = deal(history[0]), deal(candidates[0])
    places_all = deal(jnp.arange(seq, dtype=jnp.int32))
    slots = deal(jnp.arange(ncand, dtype=jnp.int32)).reshape(-1)
    wanted = relative_items(jnp.concatenate([history_all, cand_all], axis=1)) - first_row
    wanted = wanted.reshape(NC, NX * (block + cblock), 1)

    def pick(local):
        size, cols = local.shape[0], 256
        return pl.pallas_call(
            pick_kernel,
            out_shape=jax.ShapeDtypeStruct((size, width), BF),
            grid=(width // cols,),
            in_specs=[
                pl.BlockSpec((size, 1), lambda i: (0, 0)),
                pl.BlockSpec((rows_total, cols), lambda i: (0, i)),
            ],
            out_specs=pl.BlockSpec((size, cols), lambda i: (0, i)),
            scratch_shapes=[pltpu.VMEM((size, rows_total), BF)],
            compiler_params=pltpu.CompilerParams(vmem_limit_bytes=24 * 1024 * 1024),
            name="pick",
        )(local, table).reshape(NX, block + cblock, width)

    fetched = reduce_line(reduce_blocks(pick(wanted[1]), pick(wanted[0])))
    rows_f, crow_own = fetched[:block], fetched[block:].astype(BF)
    scale = lax.rsqrt(jnp.mean(rows_f * rows_f, axis=-1, keepdims=True) + 1e-06)
    normed_f = rows_f * scale
    normed = normed_f.astype(BF)
    line = jnp.concatenate([normed] + [swap_x(normed, k) for k in range(1, NX)], axis=0)
    normed = jnp.concatenate([line, swap_core(line)], axis=0)
    crows = lax.all_gather(after(crow_own, line), ("x", "c"), axis=0, tiled=True)

    pre = jnp.dot(normed, local_w, preferred_element_type=F32)
    act = jax.nn.silu(pre).astype(BF)
    gate_u, values, queries, keys = (act[:, HD * i : HD * i + HD] for i in range(4))
    places = relative_items(places_all).reshape(-1)
    allowed = (places[None, :] <= places[:, None]) & (places[None, :] < length)
    weight = allowed.astype(F32) / length.astype(F32)
    logits = jnp.einsum("td,sd->ts", queries, keys, preferred_element_type=F32) * HD ** (-0.5)
    attn = (jax.nn.silu(logits) * weight).astype(BF)
    mixed_own = jnp.dot(attn, values, preferred_element_type=F32)
    mixed_top = mixed_own.astype(BF)
    mixed_rest = (mixed_own - mixed_top.astype(F32)).astype(BF)
    sent = jnp.concatenate([mixed_top, mixed_rest, gate_u], axis=1).reshape(parts, block, 3 * HD)
    sent = exchange_item(sent)

    mixed = jnp.concatenate(
        [part[:, :HD].astype(F32) + part[:, HD : 2 * HD].astype(F32) for part in sent], axis=1
    )
    u_flat = jnp.concatenate([part[:, 2 * HD :] for part in sent], axis=1).astype(F32)
    center = jnp.mean(mixed, axis=-1, keepdims=True)
    rstd = lax.rsqrt(jnp.mean(mixed * mixed, axis=-1, keepdims=True) - center * center + 1e-05)
    normo = (mixed - center) * rstd
    gated = (normo * u_flat).astype(BF)
    hidden = (rows_f + jnp.dot(gated, w_out_all, preferred_element_type=F32)).astype(BF)

    scores = jnp.einsum("td,cd->tc", hidden, crows, preferred_element_type=F32)
    valid = slots[None, :] < counts[0]
    masked = jnp.where(valid, scores, -jnp.inf)
    top = jnp.max(masked, axis=-1, keepdims=True)
    expo = jnp.exp(masked - top)
    total = jnp.sum(expo, axis=-1, keepdims=True)
    lse = top[:, 0] + jnp.log(total[:, 0])
    soft = expo / total
    action_block = own_of(deal(after(actions[0], act)))
    target_block = own_of(deal(after(targets[0], act)))
    onehot = (slots[None, :] == action_block[:, None]).astype(F32)
    taken = jnp.sum(scores * onehot, axis=-1)
    live = (own_of(places_all) < length).astype(F32) / seq
    miss = taken - target_block
    loss = jnp.sum(live * (CQL_WEIGHT * (lse - taken) + 0.5 * miss * miss)).reshape(1, 1)
    dscore = (live[:, None] * (CQL_WEIGHT * soft + (miss - CQL_WEIGHT)[:, None] * onehot)).astype(BF)
    dhidden = jnp.dot(dscore, crows, preferred_element_type=F32).astype(BF)

    dgated = jnp.einsum("td,ed->te", dhidden, w_out_all, preferred_element_type=F32)
    du = dgated * normo
    dnormo = dgated * u_flat
    first = jnp.mean(dnormo, axis=-1, keepdims=True)
    second = jnp.mean(dnormo * normo, axis=-1, keepdims=True)
    dmixed_all = (rstd * (dnormo - first - normo * second)).astype(BF)
    du = du.astype(BF)
    loss_top = loss.astype(BF).astype(F32)
    loss_mid = (loss - loss_top).astype(BF).astype(F32)
    loss_low = loss - loss_top - loss_mid
    loss_row = jnp.concatenate([loss_top, loss_mid, loss_low], axis=1).astype(BF)
    loss_rows = jnp.pad(loss_row, ((0, 15), (0, 2 * HD - 3)))
    back = jnp.stack(
        [
            jnp.concatenate(
                [
                    jnp.concatenate(
                        [dmixed_all[:, HD * i : HD * i + HD], du[:, HD * i : HD * i + HD]], axis=1
                    ),
                    loss_rows,
                ],
                axis=0,
            )
            for i in range(parts)
        ]
    )
    dscore_b, dhidden_b, back = lax.optimization_barrier((dscore, dhidden, back))
    back_other = swap_core(back[NX:])
    dcand = jnp.einsum("tc,td->cd", dscore_b, hidden, preferred_element_type=F32).astype(BF)
    dcand_other = swap_core(jnp.stack(from_items(dcand, cblock, 1)))
    dcand_line = [
        (part.astype(F32) + dcand_other[k].astype(F32)).astype(BF)
        for k, part in enumerate(from_items(dcand, cblock, 0))
    ]
    size = block + 16
    joint = [
        jnp.concatenate(
            [back[k], back_other[k]] + [dcand_line[k][:, 256 * i : 256 * i + 256] for i in range(4)], axis=0
        )
        for k in range(1, NX)
    ]
    joint = [swap_x(part, k + 1) for k, part in enumerate(joint)]
    firsts = [back[0]] + [part[:size] for part in joint]
    seconds = [back_other[0]] + [part[size : 2 * size] for part in joint]
    back_all = jnp.concatenate([part[:block] for part in firsts + seconds], axis=0)
    dmixed, du_own = back_all[:, :HD], back_all[:, HD:].astype(F32)
    loss = sum(jnp.sum(part[block : block + 1, :3].astype(F32)) for part in firsts + seconds)
    dcand = dcand_line[0].astype(F32)
    for part in joint:
        pieces = [part[2 * size + cblock * i : 2 * size + cblock * (i + 1)] for i in range(4)]
        dcand = dcand + jnp.concatenate(pieces, axis=1).astype(F32)
    dcand = dcand.astype(BF)

    half = NX * HD
    gout_other = jnp.einsum("td,te->de", dhidden_b, gated[:, half:], preferred_element_type=F32)
    gout_own = jnp.einsum("td,te->de", dhidden_b, gated[:, :half], preferred_element_type=F32)
    gout = reduce_blocks(gout_other.astype(BF), gout_own.astype(BF))
    gout = lax.psum_scatter(gout.reshape(NY, -1, half), "y", scatter_dimension=0, tiled=False)

    dattn = jnp.einsum("td,sd->ts", dmixed, values, preferred_element_type=F32)
    dvalues = jnp.einsum("ts,td->sd", attn, dmixed, preferred_element_type=F32)
    dlogits = (dattn * weight * silu_slope(logits) * HD ** (-0.5)).astype(BF)
    dqueries = jnp.einsum("ts,sd->td", dlogits, keys, preferred_element_type=F32)
    dkeys = jnp.einsum("ts,td->sd", dlogits, queries, preferred_element_type=F32)
    dact = jnp.concatenate([du_own, dvalues, dqueries, dkeys], axis=1)
    dpre = (dact * silu_slope(pre)).astype(BF)

    near = NX * block
    part_other = jnp.einsum("sk,dk->sd", dpre[near:], local_w, preferred_element_type=F32)
    part_own = jnp.einsum("sk,dk->sd", dpre[:near], local_w, preferred_element_type=F32)
    dnormed_line = reduce_blocks(
        part_other.astype(BF).reshape(NX, block, width), part_own.astype(BF).reshape(NX, block, width)
    )
    dnormed = reduce_line(dnormed_line)
    dw_in = jnp.einsum("sd,sk->dk", normed, dpre, preferred_element_type=F32).astype(BF)
    dw_in = lax.psum_scatter(dw_in.reshape(NY, -1, 4 * HD), "y", scatter_dimension=0, tiled=False)
    grads = jnp.concatenate([gout, dw_in], axis=1)
    grads = lax.psum_scatter(grads, "z", scatter_dimension=0, tiled=True)

    drows = dhidden.astype(F32) + scale * (
        dnormed - normed_f * jnp.mean(dnormed * normed_f, axis=-1, keepdims=True)
    )
    drows = drows.astype(BF)

    ids = jnp.concatenate(
        [
            own_of(history_all),
            own_of(cand_all),
            lengths,
            counts,
            jnp.zeros((62,), jnp.int32),
        ]
    ).reshape(2, 128)
    loss = loss.reshape(1, 1)
    loss_top = loss.astype(BF).astype(F32)
    loss_mid = (loss - loss_top).astype(BF).astype(F32)
    loss_low = loss - loss_top - loss_mid
    loss_row = jnp.concatenate([loss_top, loss_mid, loss_low, jnp.zeros((1, 125), F32)], axis=1)
    meta = jnp.concatenate(
        [(ids // 128).astype(BF), (ids % 128).astype(BF), loss_row.astype(BF), jnp.zeros((11, 128), BF)]
    )
    packed = pl.pallas_call(
        pack_kernel,
        out_shape=jax.ShapeDtypeStruct((users, 64, 128), BF),
        in_specs=whole(3),
        out_specs=whole(1)[0],
        name="pack",
    )(drows, dcand, meta)
    arrived = lax.all_to_all(packed, ("y", "z"), 0, 0)
    got = arrived[:, 48:53].astype(F32)
    all_ids = (got[:, 0:2] * 128.0 + got[:, 2:4]).astype(jnp.int32).reshape(-1)
    per_item = pl.pallas_call(
        scatter_kernel,
        out_shape=jax.ShapeDtypeStruct((parts, 512, 128), BF),
        in_specs=whole(1, smem=2),
        out_specs=whole(1)[0],
        scratch_shapes=[
            pltpu.VMEM((users * 48, 128), F32),
            pltpu.VMEM((parts * rows_total, 128), F32),
        ],
        compiler_params=pltpu.CompilerParams(vmem_limit_bytes=40 * 1024 * 1024),
        name="scatter",
    )(all_ids, jnp.stack([x, c]).astype(jnp.int32), arrived)
    mine = reduce_blocks(per_item[NX:], per_item[:NX])
    grad_in = grads[:, half:].astype(F32).reshape(-1, 4, HD)
    proj = [grads[:, HD * k : HD * k + HD] for k in range(NX)]
    pieces = [swap_x(jnp.concatenate([mine[k], proj[k]], axis=0), k) for k in range(1, NX)]
    shard_t, proj_t = pl.pallas_call(
        unpack_kernel,
        out_shape=(
            jax.ShapeDtypeStruct((32, rows_total), F32),
            jax.ShapeDtypeStruct((32, HD), F32),
        ),
        in_specs=whole(5),
        out_specs=(whole(1)[0], whole(1)[0]),
        name="unpack",
    )(mine[0], proj[0], *pieces)

    loss = jnp.sum(got[:, 4, 0:3])
    return (loss, grad_in, proj_t.T, shard_t.T)


def solution(mesh):
    fine = Mesh(mesh.devices.reshape(NY, NZ, NX, NC), ("y", "z", "x", "c"))
    dp, item = ("y", "z"), ("x", "c")
    placed = (
        P(item, None),
        P(None, None, item),
        P(item, None),
        P(dp, None),
        P(dp),
        P(dp, None),
        P(dp),
        P(dp, None),
        P(dp, None),
    )
    return jax.shard_map(
        on_device,
        mesh=fine,
        in_specs=placed,
        out_specs=(P(), P(dp, None, item), P(item, dp), P(item, dp)),
        check_vma=False,
    )
```

```python
import jax
import jax.numpy as jnp
from jax import lax
from jax.experimental import pallas as pl
from jax.experimental.pallas import tpu as pltpu
from jax.sharding import Mesh, PartitionSpec as P

HD = 128
NX, NC, NY, NZ = 4, 2, 4, 8
CQL_WEIGHT = 0.5
BF = jnp.bfloat16
F32 = jnp.float32


def swap_x(value, k):
    return lax.ppermute(value, "x", [(i, i ^ k) for i in range(NX)])


def swap_core(value):
    return lax.ppermute(value, "c", [(0, 1), (1, 0)])


def flip_if(bit, value, axis):
    return jnp.where(bit == 1, jnp.flip(value, axis), value)


def relative_items(value):
    x, c = lax.axis_index("x"), lax.axis_index("c")
    parts = value.reshape((2, 2, 2) + value.shape[1:])
    parts = flip_if(x // 2, parts, 0)
    parts = flip_if(x % 2, parts, 1)
    parts = flip_if(c, parts, 2)
    return jnp.moveaxis(parts, 2, 0).reshape(value.shape)


def after(value, *others):
    return lax.optimization_barrier((value,) + others)[0]


def pick_kernel(ids_ref, table_ref, out_ref, hot_ref):
    @pl.when(pl.program_id(0) == 0)
    def _():
        chunk = 256
        for i in range(hot_ref.shape[1] // chunk):
            rows = lax.broadcasted_iota(jnp.int32, (hot_ref.shape[0], chunk), 1) + i * chunk
            hot_ref[:, i * chunk : (i + 1) * chunk] = (ids_ref[...] == rows).astype(F32).astype(BF)

    out_ref[...] = jnp.dot(hot_ref[...], table_ref[...], preferred_element_type=F32).astype(BF)


def pair_kernel(a_ref, b_ref, *outs):
    for k, out in enumerate(outs):
        out[...] = (a_ref[k].astype(F32) + b_ref[k].astype(F32)).astype(BF)


def norm_kernel(a_ref, b_ref, c_ref, d_ref, rows_ref, normed_ref, crow_ref):
    refs = (a_ref, b_ref, c_ref, d_ref)
    block = rows_ref.shape[0]
    rows = sum(ref[:block, :].astype(F32) for ref in refs)
    rows_ref[...] = rows
    scale = lax.rsqrt(jnp.mean(rows * rows, axis=-1, keepdims=True) + 1e-06)
    normed_ref[...] = (rows * scale).astype(BF)
    crow_ref[...] = sum(ref[block:, :].astype(F32) for ref in refs).astype(BF)


def item_of(place_ref, b):
    return 2 * jnp.bitwise_xor(place_ref[0], b % NX) + jnp.bitwise_xor(place_ref[1], b // NX)


def places_of(place_ref, shape, axis, first=0):
    row = lax.broadcasted_iota(jnp.int32, shape, axis) + first
    line = jnp.bitwise_and(row, 511)
    item = 2 * jnp.bitwise_xor(place_ref[0], line // 128) + jnp.bitwise_xor(place_ref[1], row // 512)
    inside = jnp.bitwise_and(row, 127)
    return 32 * jnp.bitwise_and(inside, 31) + 8 * (inside // 32) + item


def attend_kernel(place_ref, b0, b1, b2, b3, b4, b5, b6, b7, w_ref, normed_ref, pre_ref, act_ref, sent_ref):
    for b, ref in enumerate((b0, b1, b2, b3, b4, b5, b6, b7)):
        normed_ref[128 * b : 128 * b + 128, :] = ref[...]
    seq = normed_ref.shape[0]
    for i in range(0, seq, 256):
        pre = jnp.dot(normed_ref[i : i + 256, :], w_ref[...], preferred_element_type=F32)
        pre_ref[i : i + 256, :] = pre
        act_ref[i : i + 256, :] = (pre * jax.nn.sigmoid(pre)).astype(BF)
    length = place_ref[2]
    inverse = 1.0 / jnp.full((1, 1), length, jnp.int32).astype(F32)
    cols = places_of(place_ref, (1, seq), 1)
    cols = jnp.where(cols < length, cols, seq)
    for i in range(0, seq, 256):
        queries = act_ref[i : i + 256, 2 * HD : 3 * HD]
        logits = lax.dot_general(
            queries, act_ref[:, 3 * HD :], (((1,), (1,)), ((), ())), preferred_element_type=F32
        ) * HD ** (-0.5)
        rows = places_of(place_ref, (256, 1), 0, i)
        attn = jnp.where(cols <= rows, logits * jax.nn.sigmoid(logits) * inverse, 0.0).astype(BF)
        mixed = jnp.dot(attn, act_ref[:, HD : 2 * HD], preferred_element_type=F32)
        top = mixed.astype(BF)
        rest = (mixed - top.astype(F32)).astype(BF)
        for h in range(2):
            b = i // 128 + h
            item = item_of(place_ref, b)
            sent_ref[item, :, 0:HD] = top[128 * h : 128 * h + 128, :]
            sent_ref[item, :, HD : 2 * HD] = rest[128 * h : 128 * h + 128, :]
            sent_ref[item, :, 2 * HD :] = act_ref[128 * b : 128 * b + 128, 0:HD]


def split_loss(value, shape, row):
    value = jnp.broadcast_to(value, shape)
    top = value.astype(BF).astype(F32)
    middle = (value - top).astype(BF).astype(F32)
    low = value - top - middle
    lane = lax.broadcasted_iota(jnp.int32, shape, 1)
    picked = jnp.where(lane == 0, top, jnp.where(lane == 1, middle, jnp.where(lane == 2, low, 0.0)))
    return jnp.where(lax.broadcasted_iota(jnp.int32, shape, 0) == row, picked, 0.0).astype(BF)


def event_kernel(
    place_ref, sent_ref, rows_ref, w0, w1, w2, w3, w4, w5, w6, w7, crows_ref, action_ref, target_ref,
    back_ref, dhidden_ref, cand_own_ref, cand_other_ref, out_own_ref, out_other_ref, dcand_ref,
):
    weights = (w0, w1, w2, w3, w4, w5, w6, w7)
    owner = 2 * place_ref[0] + place_ref[1]
    length, count = place_ref[2], place_ref[3]
    block, width = rows_ref.shape
    seq = block * len(weights)
    items = [item_of(place_ref, b) for b in range(len(weights))]
    mixed = jnp.concatenate(
        [sent_ref[i, :, 0:HD].astype(F32) + sent_ref[i, :, HD : 2 * HD].astype(F32) for i in items], axis=1
    )
    gate = jnp.concatenate([sent_ref[i, :, 2 * HD :] for i in items], axis=1).astype(F32)
    center = jnp.mean(mixed, axis=-1, keepdims=True)
    rstd = lax.rsqrt(jnp.mean(mixed * mixed, axis=-1, keepdims=True) - center * center + 1e-05)
    normo = (mixed - center) * rstd
    gated = (normo * gate).astype(BF)
    out = rows_ref[...]
    for b, ref in enumerate(weights):
        out = out + jnp.dot(gated[:, HD * b : HD * b + HD], ref[...], preferred_element_type=F32)
    hidden = out.astype(BF)
    crows = crows_ref[...]
    scores = lax.dot_general(hidden, crows, (((1,), (1,)), ((), ())), preferred_element_type=F32)
    col = lax.broadcasted_iota(jnp.int32, (1, crows.shape[0]), 1)
    inside = jnp.bitwise_and(col, 63)
    slots = 32 * jnp.bitwise_and(inside, 15) + 8 * (inside // 16) + col // 64
    masked = jnp.where(slots < count, scores, -jnp.inf)
    top = jnp.max(masked, axis=-1, keepdims=True)
    expo = jnp.exp(masked - top)
    total = jnp.sum(expo, axis=-1, keepdims=True)
    soft = expo / total
    lse = top + jnp.log(total)
    onehot = (slots == action_ref[...]).astype(F32)
    taken = jnp.sum(scores * onehot, axis=-1, keepdims=True)
    row = lax.broadcasted_iota(jnp.int32, (block, 1), 0)
    places = 32 * jnp.bitwise_and(row, 31) + 8 * (row // 32) + owner
    live = jnp.where(places < length, 1.0 / seq, 0.0)
    miss = taken - target_ref[...]
    loss = jnp.sum(live * (CQL_WEIGHT * (lse - taken) + 0.5 * miss * miss), axis=0, keepdims=True)
    loss = split_loss(loss, (16, 2 * HD), 0)
    dscore = (live * (CQL_WEIGHT * soft + (miss - CQL_WEIGHT) * onehot)).astype(BF)
    dhidden = jnp.dot(dscore, crows, preferred_element_type=F32).astype(BF)
    dhidden_ref[...] = dhidden
    dgated = jnp.concatenate(
        [
            lax.dot_general(dhidden, ref[...], (((1,), (1,)), ((), ())), preferred_element_type=F32)
            for ref in weights
        ],
        axis=1,
    )
    dnormo = dgated * gate
    first = jnp.mean(dnormo, axis=-1, keepdims=True)
    second = jnp.mean(dnormo * normo, axis=-1, keepdims=True)
    dmixed = (rstd * (dnormo - first - normo * second)).astype(BF)
    du = (dgated * normo).astype(BF)
    for b, i in enumerate(items):
        back_ref[i, 0:block, 0:HD] = dmixed[:, HD * b : HD * b + HD]
        back_ref[i, 0:block, HD:] = du[:, HD * b : HD * b + HD]
        back_ref[i, block:, :] = loss
    turned = (((0,), (0,)), ((), ()))
    half = NX * HD
    out_other_ref[...] = lax.dot_general(
        dhidden, gated[:, half:], turned, preferred_element_type=F32
    ).astype(BF)
    out_own_ref[...] = lax.dot_general(
        dhidden, gated[:, :half], turned, preferred_element_type=F32
    ).astype(BF)
    dcand_ref[...] = lax.dot_general(dscore, hidden, turned, preferred_element_type=F32).astype(BF)
    size = cand_own_ref.shape[1]
    for k in range(NX):
        cand_own_ref[k] = dcand_ref[pl.ds(pl.multiple_of(items[k] * size, size), size), :]
        cand_other_ref[k] = dcand_ref[pl.ds(pl.multiple_of(items[NX + k] * size, size), size), :]


def backward_kernel(
    place_ref, back_ref, act_ref, pre_ref, w_ref, cand_ref, dpre_ref, part_ref, loss_ref,
    dm_ref, du_ref, dq_ref,
):
    seq = act_ref.shape[0]
    loss = jnp.zeros((16, 2 * HD), F32)
    for b in range(8):
        item = item_of(place_ref, b)
        dm_ref[128 * b : 128 * b + 128, :] = back_ref[item, 0:128, 0:HD]
        du_ref[128 * b : 128 * b + 128, :] = back_ref[item, 0:128, HD:]
        loss = loss + back_ref[item, 128:144, :].astype(F32)
    loss = jnp.sum(jnp.sum(loss, axis=1, keepdims=True), axis=0, keepdims=True)
    loss_ref[...] = split_loss(loss, (16, 128), 4)
    length = place_ref[2]
    inverse = 1.0 / jnp.full((1, 1), length, jnp.int32).astype(F32)
    cols = places_of(place_ref, (1, seq), 1)
    across = (((1,), (1,)), ((), ()))
    dq_ref[...] = jnp.zeros(dq_ref.shape, F32)

    def slope(value, sigma):
        return sigma * (1.0 + value * (1.0 - sigma))

    for i in range(0, seq, 256):
        keys = act_ref[i : i + 256, 3 * HD :]
        logits = lax.dot_general(
            keys, act_ref[:, 2 * HD : 3 * HD], across, preferred_element_type=F32
        ) * HD ** (-0.5)
        rows = places_of(place_ref, (256, 1), 0, i)
        rows = jnp.where(rows < length, rows, seq)
        allowed = rows <= cols
        sigma = jax.nn.sigmoid(logits)
        attn = jnp.where(allowed, logits * sigma * inverse, 0.0).astype(BF)
        dattn = lax.dot_general(
            act_ref[i : i + 256, HD : 2 * HD], dm_ref[...], across, preferred_element_type=F32
        )
        dlogits = jnp.where(
            allowed, dattn * inverse * slope(logits, sigma) * HD ** (-0.5), 0.0
        ).astype(BF)
        dvalues = jnp.dot(attn, dm_ref[...], preferred_element_type=F32)
        dkeys = jnp.dot(dlogits, act_ref[:, 2 * HD : 3 * HD], preferred_element_type=F32)
        dq_ref[...] += lax.dot_general(
            dlogits, keys, (((0,), (0,)), ((), ())), preferred_element_type=F32
        )
        for j, grad in ((1, dvalues), (3, dkeys)):
            pre = pre_ref[i : i + 256, HD * j : HD * j + HD]
            dpre_ref[i : i + 256, HD * j : HD * j + HD] = (
                grad * slope(pre, jax.nn.sigmoid(pre))
            ).astype(BF)
    for j, ref in ((0, du_ref), (2, dq_ref)):
        pre = pre_ref[:, HD * j : HD * j + HD]
        dpre_ref[:, HD * j : HD * j + HD] = (
            ref[...].astype(F32) * slope(pre, jax.nn.sigmoid(pre))
        ).astype(BF)
    part_rows(part_ref, dpre_ref, w_ref, cand_ref, NX * 128)


def part_rows(part_ref, dpre_ref, w_ref, cand_ref, first):
    across = (((1,), (1,)), ((), ()))
    for h in range(2):
        part = lax.dot_general(
            dpre_ref[first + 256 * h : first + 256 * h + 256, :],
            w_ref[...],
            across,
            preferred_element_type=F32,
        ).astype(BF)
        part_ref[2 * h, 0:128, :] = part[:128, :]
        part_ref[2 * h + 1, 0:128, :] = part[128:, :]
    for k in range(NX):
        part_ref[k, 128:, :] = cand_ref[k]


def weight_kernel(dpre_ref, w_ref, cand_ref, normed_ref, part_ref, dw_ref):
    part_rows(part_ref, dpre_ref, w_ref, cand_ref, 0)
    dw_ref[...] = lax.dot_general(
        normed_ref[...], dpre_ref[...], (((0,), (0,)), ((), ())), preferred_element_type=F32
    ).astype(BF)


def pack_kernel(a_ref, b_ref, c_ref, d_ref, rows_ref, dhidden_ref, meta_ref, loss_ref, out_ref):
    refs = (a_ref, b_ref, c_ref, d_ref)
    block = rows_ref.shape[0]
    dnormed = sum(ref[:block, :].astype(F32) for ref in refs)
    rows = rows_ref[...]
    scale = lax.rsqrt(jnp.mean(rows * rows, axis=-1, keepdims=True) + 1e-06)
    normed = rows * scale
    drows = dhidden_ref[...].astype(F32) + scale * (
        dnormed - normed * jnp.mean(dnormed * normed, axis=-1, keepdims=True)
    )
    drows = drows.astype(BF)
    dcand = sum(ref[block:, :].astype(F32) for ref in refs).astype(BF)
    meta = (meta_ref[...].astype(F32) + loss_ref[...].astype(F32)).astype(BF)
    for d in range(out_ref.shape[0]):
        out_ref[d, 0:32, :] = jnp.concatenate(
            [drows[32 * g : 32 * g + 32, 32 * d : 32 * d + 32] for g in range(4)], axis=1
        )
        out_ref[d, 32:48, :] = jnp.concatenate(
            [dcand[16 * g : 16 * g + 16, 32 * d : 32 * d + 32] for g in range(4)], axis=1
        )
        out_ref[d, 48:64, :] = meta


def scatter_kernel(ids_ref, place_ref, data_ref, own_ref, other_ref, rows_ref, acc_ref):
    users = data_ref.shape[0]
    total = acc_ref.shape[0]
    chunk = 512
    x, c = place_ref[0], place_ref[1]
    owner = 2 * x + c

    def clear(i, carry):
        acc_ref[pl.ds(pl.multiple_of(i * chunk, chunk), chunk), :] = jnp.zeros((chunk, 128), F32)
        return carry

    lax.fori_loop(0, total // chunk, clear, 0)
    for u in range(users):
        rows_ref[48 * u : 48 * u + 48, :] = data_ref[u, 0:48, :].astype(F32)
    lane = lax.broadcasted_iota(jnp.int32, (1, 128), 1) // 32
    masks = [lane == g for g in range(4)]

    def add(first_id, pitch, first_row, count):
        def step(i, carry):
            for j in range(4):
                p = i * 4 + j
                row = rows_ref[pl.ds(first_row + p, 1), :]
                ids = [ids_ref[first_id + g * pitch + p] for g in range(4)]
                held = [acc_ref[pl.ds(ids[g], 1), :] for g in range(4)]
                for g in range(4):
                    pltpu.store(acc_ref.at[pl.ds(ids[g], 1), :], held[g] + row, mask=masks[g])
            return carry

        lax.fori_loop(0, (count + 3) // 4, step, 0)

    def user(u, carry):
        base = u * 256
        events = jnp.clip((ids_ref[base + 192] - owner + 31) // 32, 0, 32)
        cands = jnp.clip((ids_ref[base + 193] - owner + 31) // 32, 0, 16)
        add(base, 32, u * 48, events)
        add(base + 128, 16, u * 48 + 32, cands)
        return carry

    lax.fori_loop(0, users, user, 0)
    wide = lax.broadcasted_iota(jnp.int32, (512, 128), 1) // 32
    for cc in range(2):
        for k in range(4):
            item = item_of(place_ref, cc * NX + k)
            result = jnp.zeros((512, 128), F32)
            for q in range(4):
                part = acc_ref[pl.ds(pl.multiple_of(item * 2048 + q * 512, 512), 512), :]
                part = part + pltpu.roll(part, 64, 1)
                part = part + pltpu.roll(part, 32, 1)
                result = jnp.where(wide == q, part, result)
            (own_ref, other_ref)[cc][k] = result.astype(BF)


def final_pair_kernel(a_ref, b_ref, grads_ref, *outs):
    for k, out in enumerate(outs):
        out[:512, :] = (a_ref[k].astype(F32) + b_ref[k].astype(F32)).astype(BF)
        out[512:, :] = grads_ref[:, HD * k : HD * k + HD]


def unpack_kernel(a_ref, b_ref, c_ref, d_ref, grads_ref, out_ref, proj_ref, in_ref):
    refs = (a_ref, b_ref, c_ref, d_ref)
    proj_ref[...] = sum(ref[512:, :].astype(F32) for ref in refs)
    turned = sum(ref[:512, :].astype(F32) for ref in refs).T
    for q in range(4):
        out_ref[:, q * 512 : (q + 1) * 512] = turned[32 * q : 32 * q + 32, :]
    in_ref[...] = grads_ref[:, NX * HD :].astype(F32)


def call(kernel, name, outs, *args, smem=0, scratch=(), limit=32):
    outs = tuple(jax.ShapeDtypeStruct(shape, dtype) for shape, dtype in outs)
    specs = whole(len(outs))
    return pl.pallas_call(
        kernel,
        out_shape=outs if len(outs) > 1 else outs[0],
        in_specs=whole(len(args) - smem, smem),
        out_specs=tuple(specs) if len(outs) > 1 else specs[0],
        scratch_shapes=list(scratch),
        compiler_params=pltpu.CompilerParams(vmem_limit_bytes=limit * 1024 * 1024),
        name=name,
    )(*args)


def whole(count, smem=0):
    specs = [pl.BlockSpec(memory_space=pltpu.SMEM)] * smem
    return specs + [pl.BlockSpec(memory_space=pltpu.VMEM)] * count


def on_device(table, w_uvqk, w_out, history, lengths, candidates, counts, actions, targets):
    rows_total, width = table.shape
    seq = history.shape[1]
    ncand = candidates.shape[1]
    users = NY * NZ
    parts = NX * NC
    block = seq // parts
    cblock = ncand // parts
    x, c = lax.axis_index("x"), lax.axis_index("c")
    owner = 2 * x + c
    first_row = owner * rows_total
    local_w = w_uvqk.reshape(width, -1)
    length = lengths[0]

    def deal(values):
        return jnp.moveaxis(values.reshape(-1, 4, parts), 2, 0).swapaxes(1, 2).reshape(parts, -1)

    def own_of(values):
        return lax.dynamic_index_in_dim(values, owner, 0, keepdims=False)

    place = jnp.stack([x, c, length, counts[0]]).astype(jnp.int32)

    def spread(own):
        line = [own] + [swap_x(own, k) for k in range(1, NX)]
        return line + [swap_core(part) for part in line]

    weights_out = spread(w_out)

    history_all, cand_all = deal(history[0]), deal(candidates[0])
    wanted = relative_items(jnp.concatenate([history_all, cand_all], axis=1)) - first_row
    wanted = wanted.reshape(NC, NX * (block + cblock), 1)

    def pick(local):
        size, cols = local.shape[0], 256
        return pl.pallas_call(
            pick_kernel,
            out_shape=jax.ShapeDtypeStruct((size, width), BF),
            grid=(width // cols,),
            in_specs=[
                pl.BlockSpec((size, 1), lambda i: (0, 0)),
                pl.BlockSpec((rows_total, cols), lambda i: (0, i)),
            ],
            out_specs=pl.BlockSpec((size, cols), lambda i: (0, i)),
            scratch_shapes=[pltpu.VMEM((size, rows_total), BF)],
            compiler_params=pltpu.CompilerParams(vmem_limit_bytes=24 * 1024 * 1024),
            name="pick",
        )(local, table).reshape(NX, block + cblock, width)

    size = block + cblock
    line = call(
        pair_kernel, "pair", [((size, width), BF)] * NX, swap_core(pick(wanted[1])), pick(wanted[0])
    )
    line = [line[0]] + [swap_x(line[k], k) for k in range(1, NX)]
    rows_f, normed, crow = call(
        norm_kernel,
        "norm",
        [((block, width), F32), ((block, width), BF), ((cblock, width), BF)],
        *line,
    )
    spread_rows = spread(normed)
    crows = lax.all_gather(after(crow, spread_rows[3]), ("x", "c"), axis=0, tiled=True)
    normed, pre, act, sent = call(
        attend_kernel,
        "attend",
        [((seq, width), BF), ((seq, 4 * HD), F32), ((seq, 4 * HD), BF), ((parts, block, 3 * HD), BF)],
        place,
        *spread_rows,
        local_w,
        smem=1,
    )
    sent = lax.all_to_all(sent, ("x", "c"), 0, 0)

    half = NX * HD
    back, dhidden, cand_own, cand_other, out_own, out_other = call(
        event_kernel,
        "event",
        [
            ((parts, block + 16, 2 * HD), BF),
            ((block, width), BF),
            ((NX, cblock, width), BF),
            ((NX, cblock, width), BF),
            ((width, half), BF),
            ((width, half), BF),
        ],
        place,
        sent,
        rows_f,
        *weights_out,
        crows,
        own_of(deal(actions[0])).reshape(block, 1),
        own_of(deal(targets[0])).reshape(block, 1),
        smem=1,
        scratch=[pltpu.VMEM((ncand, width), BF)],
    )
    back = lax.all_to_all(back, ("x", "c"), 0, 0)
    gout = (out_own.astype(F32) + swap_core(out_other).astype(F32)).astype(BF)
    gout = lax.psum_scatter(gout.reshape(NY, -1, half), "y", scatter_dimension=0, tiled=False)

    dpre, part_other, loss_meta = call(
        backward_kernel,
        "backward",
        [((seq, 4 * HD), BF), ((NX, size, width), BF), ((16, 128), BF)],
        place,
        back,
        act,
        pre,
        local_w,
        cand_other,
        smem=1,
        scratch=[
            pltpu.VMEM((seq, HD), BF),
            pltpu.VMEM((seq, HD), BF),
            pltpu.VMEM((seq, HD), F32),
        ],
    )
    part_own, dw_in = call(
        weight_kernel,
        "weight",
        [((NX, size, width), BF), ((width, 4 * HD), BF)],
        dpre,
        local_w,
        cand_own,
        normed,
    )
    line = call(pair_kernel, "pair", [((size, width), BF)] * NX, swap_core(part_other), part_own)
    line = [line[0]] + [swap_x(line[k], k) for k in range(1, NX)]
    dw_in, gout = lax.optimization_barrier((dw_in, gout))
    dw_in = lax.psum_scatter(dw_in.reshape(NY, -1, 4 * HD), "y", scatter_dimension=0, tiled=False)
    grads = jnp.concatenate([gout, dw_in], axis=1)
    grads = lax.psum_scatter(grads, "z", scatter_dimension=0, tiled=True)

    ids = jnp.concatenate(
        [
            own_of(history_all),
            own_of(cand_all),
            lengths,
            counts,
            jnp.zeros((62,), jnp.int32),
        ]
    ).reshape(2, 128)
    meta = jnp.concatenate([(ids // 128).astype(BF), (ids % 128).astype(BF), jnp.zeros((12, 128), BF)])
    packed = call(
        pack_kernel,
        "pack",
        [((users, 64, 128), BF)],
        *line,
        rows_f,
        dhidden,
        meta,
        loss_meta,
    )
    arrived = lax.all_to_all(packed, ("y", "z"), 0, 0)
    got = arrived[:, 48:53].astype(F32)
    all_ids = (got[:, 0:2] * 128.0 + got[:, 2:4]).astype(jnp.int32).reshape(-1)
    own, other = call(
        scatter_kernel,
        "scatter",
        [((NX, 512, 128), BF)] * 2,
        all_ids,
        place,
        arrived,
        smem=2,
        scratch=[
            pltpu.VMEM((users * 48, 128), F32),
            pltpu.VMEM((parts * rows_total, 128), F32),
        ],
        limit=40,
    )
    line = call(
        final_pair_kernel, "final_pair", [((512 + 32, 128), BF)] * NX, swap_core(other), own, grads
    )
    line = [line[0]] + [swap_x(line[k], k) for k in range(1, NX)]
    shard_t, proj_t, grad_in = call(
        unpack_kernel,
        "unpack",
        [((32, rows_total), F32), ((32, HD), F32), ((32, 4 * HD), F32)],
        *line,
        grads,
    )
    grad_in = grad_in.reshape(-1, 4, HD)
    loss = jnp.sum(got[:, 4, 0:3])
    return (loss, grad_in, proj_t.T, shard_t.T)


def solution(mesh):
    fine = Mesh(mesh.devices.reshape(NY, NZ, NX, NC), ("y", "z", "x", "c"))
    dp, item = ("y", "z"), ("x", "c")
    placed = (
        P(item, None),
        P(None, None, item),
        P(item, None),
        P(dp, None),
        P(dp),
        P(dp, None),
        P(dp),
        P(dp, None),
        P(dp, None),
    )
    return jax.shard_map(
        on_device,
        mesh=fine,
        in_specs=placed,
        out_specs=(P(), P(dp, None, item), P(item, dp), P(item, dp)),
        check_vma=False,
    )
```

```python
import functools

import jax
import jax.numpy as jnp
from jax import lax
from jax.experimental import pallas as pl
from jax.experimental.pallas import tpu as pltpu
from jax.sharding import Mesh, PartitionSpec as P

HD = 128
NX, NC, NY, NZ = 4, 2, 4, 8
CQL_WEIGHT = 0.5
BF = jnp.bfloat16
F32 = jnp.float32


def swap_x(value, k):
    return lax.ppermute(value, "x", [(i, i ^ k) for i in range(NX)])


def swap_core(value):
    return lax.ppermute(value, "c", [(0, 1), (1, 0)])


def event_slots(item, shape, axis):
    row = lax.broadcasted_iota(jnp.int32, shape, axis)
    return 32 * jnp.bitwise_and(row, 31) + 8 * (row // 32) + item


def cand_slots(item, shape, axis):
    row = lax.broadcasted_iota(jnp.int32, shape, axis)
    return 32 * jnp.bitwise_and(row, 15) + 8 * (row // 16) + item


def chosen(values, slots):
    cols = lax.broadcasted_iota(jnp.int32, (1, values.shape[1]), 1)
    return jnp.sum(jnp.where(cols == slots, values.astype(F32), 0.0), axis=1, keepdims=True)


def pick_kernel(half, place_ref, history_ref, cand_ref, table_ref, out_ref, rows_ref, hot_ref, sems):
    pieces = 4
    total = rows_ref.shape[0]
    step = total // pieces
    copies = [
        pltpu.make_async_copy(
            table_ref.at[pl.ds(i * step, step), :], rows_ref.at[pl.ds(i * step, step), :], sems.at[i]
        )
        for i in range(pieces)
    ]
    for copy in copies:
        copy.start()
    first_row = (2 * place_ref[0] + place_ref[1]) * total
    size = out_ref.shape[1]
    for k in range(NX):
        item = item_of(place_ref, half * NX + k)
        events = chosen(history_ref[...], event_slots(item, (128, 1), 0))
        cands = chosen(cand_ref[...], cand_slots(item, (size - 128, 1), 0))
        for first, ids in ((0, events), (128, cands)):
            local = ids.astype(jnp.int32) - first_row
            count = ids.shape[0]
            for i in range(0, total, 512):
                cols = lax.broadcasted_iota(jnp.int32, (1, 512), 1) + i
                hot_ref[size * k + first : size * k + first + count, i : i + 512] = (
                    (local == cols).astype(F32).astype(BF)
                )
    for copy in copies:
        copy.wait()
    for i in range(0, out_ref.shape[2], 256):
        found = jnp.dot(hot_ref[...], rows_ref[:, i : i + 256], preferred_element_type=F32).astype(BF)
        for k in range(NX):
            out_ref[k, :, i : i + 256] = found[size * k : size * k + size, :]


def pair_kernel(a_ref, b_ref, *outs):
    for k, out in enumerate(outs):
        out[...] = (a_ref[k].astype(F32) + b_ref[k].astype(F32)).astype(BF)


def norm_kernel(a_ref, b_ref, c_ref, d_ref, rows_ref, normed_ref, crow_ref):
    refs = (a_ref, b_ref, c_ref, d_ref)
    block = rows_ref.shape[0]
    rows = sum(ref[:block, :].astype(F32) for ref in refs)
    rows_ref[...] = rows
    scale = lax.rsqrt(jnp.mean(rows * rows, axis=-1, keepdims=True) + 1e-06)
    normed_ref[...] = (rows * scale).astype(BF)
    crow_ref[...] = sum(ref[block:, :].astype(F32) for ref in refs).astype(BF)


def item_of(place_ref, b):
    return 2 * jnp.bitwise_xor(place_ref[0], b % NX) + jnp.bitwise_xor(place_ref[1], b // NX)


def places_of(place_ref, shape, axis, first=0):
    row = lax.broadcasted_iota(jnp.int32, shape, axis) + first
    line = jnp.bitwise_and(row, 511)
    item = 2 * jnp.bitwise_xor(place_ref[0], line // 128) + jnp.bitwise_xor(place_ref[1], row // 512)
    inside = jnp.bitwise_and(row, 127)
    return 32 * jnp.bitwise_and(inside, 31) + 8 * (inside // 32) + item


def attend_kernel(place_ref, b0, b1, b2, b3, b4, b5, b6, b7, w_ref, normed_ref, pre_ref, act_ref, sent_ref):
    for b, ref in enumerate((b0, b1, b2, b3, b4, b5, b6, b7)):
        normed_ref[128 * b : 128 * b + 128, :] = ref[...]
    seq = normed_ref.shape[0]
    for i in range(0, seq, 256):
        pre = jnp.dot(normed_ref[i : i + 256, :], w_ref[...], preferred_element_type=F32)
        pre_ref[i : i + 256, :] = pre
        act_ref[i : i + 256, :] = (pre * jax.nn.sigmoid(pre)).astype(BF)
    length = place_ref[2]
    inverse = 1.0 / jnp.full((1, 1), length, jnp.int32).astype(F32)
    cols = places_of(place_ref, (1, seq), 1)
    cols = jnp.where(cols < length, cols, seq)
    for i in range(0, seq, 256):
        queries = act_ref[i : i + 256, 2 * HD : 3 * HD]
        logits = lax.dot_general(
            queries, act_ref[:, 3 * HD :], (((1,), (1,)), ((), ())), preferred_element_type=F32
        ) * HD ** (-0.5)
        rows = places_of(place_ref, (256, 1), 0, i)
        attn = jnp.where(cols <= rows, logits * jax.nn.sigmoid(logits) * inverse, 0.0).astype(BF)
        mixed = jnp.dot(attn, act_ref[:, HD : 2 * HD], preferred_element_type=F32)
        top = mixed.astype(BF)
        rest = (mixed - top.astype(F32)).astype(BF)
        for h in range(2):
            b = i // 128 + h
            item = item_of(place_ref, b)
            sent_ref[item, :, 0:HD] = top[128 * h : 128 * h + 128, :]
            sent_ref[item, :, HD : 2 * HD] = rest[128 * h : 128 * h + 128, :]
            sent_ref[item, :, 2 * HD :] = act_ref[128 * b : 128 * b + 128, 0:HD]


def split_loss(value, shape, row):
    value = jnp.broadcast_to(value, shape)
    top = value.astype(BF).astype(F32)
    middle = (value - top).astype(BF).astype(F32)
    low = value - top - middle
    lane = lax.broadcasted_iota(jnp.int32, shape, 1)
    picked = jnp.where(lane == 0, top, jnp.where(lane == 1, middle, jnp.where(lane == 2, low, 0.0)))
    return jnp.where(lax.broadcasted_iota(jnp.int32, shape, 0) == row, picked, 0.0).astype(BF)


def event_kernel(
    place_ref, sent_ref, rows_ref, w0, w1, w2, w3, w4, w5, w6, w7, crows_ref, action_ref, target_ref,
    back_ref, dhidden_ref, cand_own_ref, cand_other_ref, out_own_ref, out_other_ref, dcand_ref,
):
    weights = (w0, w1, w2, w3, w4, w5, w6, w7)
    owner = 2 * place_ref[0] + place_ref[1]
    length, count = place_ref[2], place_ref[3]
    block, width = rows_ref.shape
    seq = block * len(weights)
    items = [item_of(place_ref, b) for b in range(len(weights))]
    mixed = jnp.concatenate(
        [sent_ref[i, :, 0:HD].astype(F32) + sent_ref[i, :, HD : 2 * HD].astype(F32) for i in items], axis=1
    )
    gate = jnp.concatenate([sent_ref[i, :, 2 * HD :] for i in items], axis=1).astype(F32)
    center = jnp.mean(mixed, axis=-1, keepdims=True)
    rstd = lax.rsqrt(jnp.mean(mixed * mixed, axis=-1, keepdims=True) - center * center + 1e-05)
    normo = (mixed - center) * rstd
    gated = (normo * gate).astype(BF)
    out = rows_ref[...]
    for b, ref in enumerate(weights):
        out = out + jnp.dot(gated[:, HD * b : HD * b + HD], ref[...], preferred_element_type=F32)
    hidden = out.astype(BF)
    crows = crows_ref[...]
    scores = lax.dot_general(hidden, crows, (((1,), (1,)), ((), ())), preferred_element_type=F32)
    col = lax.broadcasted_iota(jnp.int32, (1, crows.shape[0]), 1)
    inside = jnp.bitwise_and(col, 63)
    slots = 32 * jnp.bitwise_and(inside, 15) + 8 * (inside // 16) + col // 64
    masked = jnp.where(slots < count, scores, -jnp.inf)
    top = jnp.max(masked, axis=-1, keepdims=True)
    expo = jnp.exp(masked - top)
    total = jnp.sum(expo, axis=-1, keepdims=True)
    soft = expo / total
    lse = top + jnp.log(total)
    places = event_slots(owner, (block, 1), 0)
    actions = chosen(action_ref[...], places).astype(jnp.int32)
    onehot = (slots == actions).astype(F32)
    taken = jnp.sum(scores * onehot, axis=-1, keepdims=True)
    live = jnp.where(places < length, 1.0 / seq, 0.0)
    miss = taken - chosen(target_ref[...], places)
    loss = jnp.sum(live * (CQL_WEIGHT * (lse - taken) + 0.5 * miss * miss), axis=0, keepdims=True)
    loss = split_loss(loss, (16, 2 * HD), 0)
    dscore = (live * (CQL_WEIGHT * soft + (miss - CQL_WEIGHT) * onehot)).astype(BF)
    dhidden = jnp.dot(dscore, crows, preferred_element_type=F32).astype(BF)
    dhidden_ref[...] = dhidden
    dgated = jnp.concatenate(
        [
            lax.dot_general(dhidden, ref[...], (((1,), (1,)), ((), ())), preferred_element_type=F32)
            for ref in weights
        ],
        axis=1,
    )
    dnormo = dgated * gate
    first = jnp.mean(dnormo, axis=-1, keepdims=True)
    second = jnp.mean(dnormo * normo, axis=-1, keepdims=True)
    dmixed = (rstd * (dnormo - first - normo * second)).astype(BF)
    du = (dgated * normo).astype(BF)
    for b, i in enumerate(items):
        back_ref[i, 0:block, 0:HD] = dmixed[:, HD * b : HD * b + HD]
        back_ref[i, 0:block, HD:] = du[:, HD * b : HD * b + HD]
        back_ref[i, block:, :] = loss
    turned = (((0,), (0,)), ((), ()))
    half = NX * HD
    out_other_ref[...] = lax.dot_general(
        dhidden, gated[:, half:], turned, preferred_element_type=F32
    ).astype(BF)
    out_own_ref[...] = lax.dot_general(
        dhidden, gated[:, :half], turned, preferred_element_type=F32
    ).astype(BF)
    dcand_ref[...] = lax.dot_general(dscore, hidden, turned, preferred_element_type=F32).astype(BF)
    size = cand_own_ref.shape[1]
    for k in range(NX):
        cand_own_ref[k] = dcand_ref[pl.ds(pl.multiple_of(items[k] * size, size), size), :]
        cand_other_ref[k] = dcand_ref[pl.ds(pl.multiple_of(items[NX + k] * size, size), size), :]


def backward_kernel(
    place_ref, back_ref, act_ref, pre_ref, w_ref, cand_ref, dpre_ref, part_ref, loss_ref,
    dm_ref, du_ref, dq_ref,
):
    seq = act_ref.shape[0]
    loss = jnp.zeros((16, 2 * HD), F32)
    for b in range(8):
        item = item_of(place_ref, b)
        dm_ref[128 * b : 128 * b + 128, :] = back_ref[item, 0:128, 0:HD]
        du_ref[128 * b : 128 * b + 128, :] = back_ref[item, 0:128, HD:]
        loss = loss + back_ref[item, 128:144, :].astype(F32)
    loss = jnp.sum(jnp.sum(loss, axis=1, keepdims=True), axis=0, keepdims=True)
    loss_ref[...] = split_loss(loss, (16, 128), 4)
    length = place_ref[2]
    inverse = 1.0 / jnp.full((1, 1), length, jnp.int32).astype(F32)
    cols = places_of(place_ref, (1, seq), 1)
    across = (((1,), (1,)), ((), ()))
    dq_ref[...] = jnp.zeros(dq_ref.shape, F32)

    def slope(value, sigma):
        return sigma * (1.0 + value * (1.0 - sigma))

    for i in range(0, seq, 256):
        keys = act_ref[i : i + 256, 3 * HD :]
        logits = lax.dot_general(
            keys, act_ref[:, 2 * HD : 3 * HD], across, preferred_element_type=F32
        ) * HD ** (-0.5)
        rows = places_of(place_ref, (256, 1), 0, i)
        rows = jnp.where(rows < length, rows, seq)
        allowed = rows <= cols
        sigma = jax.nn.sigmoid(logits)
        attn = jnp.where(allowed, logits * sigma * inverse, 0.0).astype(BF)
        dattn = lax.dot_general(
            act_ref[i : i + 256, HD : 2 * HD], dm_ref[...], across, preferred_element_type=F32
        )
        dlogits = jnp.where(
            allowed, dattn * inverse * slope(logits, sigma) * HD ** (-0.5), 0.0
        ).astype(BF)
        dvalues = jnp.dot(attn, dm_ref[...], preferred_element_type=F32)
        dkeys = jnp.dot(dlogits, act_ref[:, 2 * HD : 3 * HD], preferred_element_type=F32)
        dq_ref[...] += lax.dot_general(
            dlogits, keys, (((0,), (0,)), ((), ())), preferred_element_type=F32
        )
        for j, grad in ((1, dvalues), (3, dkeys)):
            pre = pre_ref[i : i + 256, HD * j : HD * j + HD]
            dpre_ref[i : i + 256, HD * j : HD * j + HD] = (
                grad * slope(pre, jax.nn.sigmoid(pre))
            ).astype(BF)
    for j, ref in ((0, du_ref), (2, dq_ref)):
        pre = pre_ref[:, HD * j : HD * j + HD]
        dpre_ref[:, HD * j : HD * j + HD] = (
            ref[...].astype(F32) * slope(pre, jax.nn.sigmoid(pre))
        ).astype(BF)
    part_rows(part_ref, dpre_ref, w_ref, cand_ref, NX * 128)


def part_rows(part_ref, dpre_ref, w_ref, cand_ref, first):
    across = (((1,), (1,)), ((), ()))
    for h in range(2):
        part = lax.dot_general(
            dpre_ref[first + 256 * h : first + 256 * h + 256, :],
            w_ref[...],
            across,
            preferred_element_type=F32,
        ).astype(BF)
        part_ref[2 * h, 0:128, :] = part[:128, :]
        part_ref[2 * h + 1, 0:128, :] = part[128:, :]
    for k in range(NX):
        part_ref[k, 128:, :] = cand_ref[k]


def weight_kernel(
    place_ref, dpre_ref, w_ref, cand_ref, normed_ref, a_ref, b_ref, history_ref, cands_ref, loss_ref,
    part_ref, grads_ref, meta_ref,
):
    part_rows(part_ref, dpre_ref, w_ref, cand_ref, 0)
    half = a_ref.shape[1]
    grads_ref[:, half:] = lax.dot_general(
        normed_ref[...], dpre_ref[...], (((0,), (0,)), ((), ())), preferred_element_type=F32
    ).astype(BF)
    grads_ref[:, :half] = (a_ref[...].astype(F32) + b_ref[...].astype(F32)).astype(BF)
    owner = 2 * place_ref[0] + place_ref[1]

    def digits(values, wanted):
        row = lax.broadcasted_iota(jnp.int32, (16, values.shape[1]), 0)
        upper, lower = values // 128, jnp.bitwise_and(values, 127)
        both = jnp.where(row == 0, upper, jnp.where(row == 2, lower, 0)).astype(F32).astype(BF)
        source = lax.broadcasted_iota(jnp.int32, (values.shape[1], 128), 0)
        hot = (source == wanted).astype(F32).astype(BF)
        return jnp.dot(both, hot, preferred_element_type=F32)

    lane = lax.broadcasted_iota(jnp.int32, (16, 128), 1)
    row = lax.broadcasted_iota(jnp.int32, (16, 128), 0)
    events = digits(history_ref[...], event_slots(owner, (1, 128), 1))
    wanted = cand_slots(owner, (1, 128), 1)
    wanted = jnp.where(lax.broadcasted_iota(jnp.int32, (1, 128), 1) < 64, wanted, -1)
    cands = pltpu.roll(digits(cands_ref[...], wanted), 1, 0)
    meta = events + cands + loss_ref[...].astype(F32)
    for where, value in ((64, place_ref[2]), (65, place_ref[3])):
        for r, part in ((1, value // 128), (3, jnp.bitwise_and(value, 127))):
            part = jnp.full((16, 128), part, jnp.int32).astype(F32)
            meta = jnp.where((lane == where) & (row == r), part, meta)
    meta_ref[...] = meta.astype(BF)


def pack_kernel(a_ref, b_ref, c_ref, d_ref, rows_ref, dhidden_ref, meta_ref, out_ref):
    refs = (a_ref, b_ref, c_ref, d_ref)
    block = rows_ref.shape[0]
    dnormed = sum(ref[:block, :].astype(F32) for ref in refs)
    rows = rows_ref[...]
    scale = lax.rsqrt(jnp.mean(rows * rows, axis=-1, keepdims=True) + 1e-06)
    normed = rows * scale
    drows = dhidden_ref[...].astype(F32) + scale * (
        dnormed - normed * jnp.mean(dnormed * normed, axis=-1, keepdims=True)
    )
    drows = drows.astype(BF)
    dcand = sum(ref[block:, :].astype(F32) for ref in refs).astype(BF)
    meta = meta_ref[...]
    for d in range(out_ref.shape[0]):
        out_ref[d, 0:32, :] = jnp.concatenate(
            [drows[32 * g : 32 * g + 32, 32 * d : 32 * d + 32] for g in range(4)], axis=1
        )
        out_ref[d, 32:48, :] = jnp.concatenate(
            [dcand[16 * g : 16 * g + 16, 32 * d : 32 * d + 32] for g in range(4)], axis=1
        )
        out_ref[d, 48:64, :] = meta


def scatter_kernel(ids_ref, place_ref, data_ref, own_ref, other_ref, rows_ref, acc_ref, more_ref):
    users = data_ref.shape[0]
    total = acc_ref.shape[0]
    chunk = 512
    owner = 2 * place_ref[0] + place_ref[1]

    def clear(i, carry):
        here = pl.ds(pl.multiple_of(i * chunk, chunk), chunk)
        acc_ref[here, :] = jnp.zeros((chunk, 128), F32)
        more_ref[here, :] = jnp.zeros((chunk, 128), F32)
        return carry

    lax.fori_loop(0, total // chunk, clear, 0)
    for u in range(users):
        rows_ref[48 * u : 48 * u + 48, :] = data_ref[u, 0:48, :].astype(F32)
    lane = lax.broadcasted_iota(jnp.int32, (1, 128), 1) // 32
    masks = [lane == g for g in range(4)]

    def add(first_id, pitch, first_row, count):
        def step(i, carry):
            for j in range(2):
                work = []
                for half, ref in ((0, acc_ref), (1, more_ref)):
                    p = i * 4 + j * 2 + half
                    row = rows_ref[pl.ds(first_row + p, 1), :]
                    ids = [ids_ref[first_id + g * pitch + p] for g in range(4)]
                    work.append((ref, row, ids, [ref[pl.ds(ids[g], 1), :] for g in range(4)]))
                for ref, row, ids, held in work:
                    for g in range(4):
                        pltpu.store(ref.at[pl.ds(ids[g], 1), :], held[g] + row, mask=masks[g])
            return carry

        lax.fori_loop(0, (count + 3) // 4, step, 0)

    def user(u, carry):
        base = u * 256
        events = jnp.clip((ids_ref[base + 192] - owner + 31) // 32, 0, 32)
        cands = jnp.clip((ids_ref[base + 193] - owner + 31) // 32, 0, 16)
        add(base, 32, u * 48, events)
        add(base + 128, 16, u * 48 + 32, cands)
        return carry

    lax.fori_loop(0, users, user, 0)
    wide = lax.broadcasted_iota(jnp.int32, (512, 128), 1) // 32
    for cc in range(2):
        for k in range(4):
            item = item_of(place_ref, cc * NX + k)
            result = jnp.zeros((512, 128), F32)
            for q in range(4):
                here = pl.ds(pl.multiple_of(item * 2048 + q * 512, 512), 512)
                part = acc_ref[here, :] + more_ref[here, :]
                part = part + pltpu.roll(part, 64, 1)
                part = part + pltpu.roll(part, 32, 1)
                result = jnp.where(wide == q, part, result)
            (own_ref, other_ref)[cc][k] = result.astype(BF)


def final_pair_kernel(a_ref, b_ref, grads_ref, *outs):
    for k, out in enumerate(outs):
        out[:512, :] = (a_ref[k].astype(F32) + b_ref[k].astype(F32)).astype(BF)
        out[512:, :] = grads_ref[:, HD * k : HD * k + HD]


def unpack_kernel(a_ref, b_ref, c_ref, d_ref, grads_ref, out_ref, proj_ref, in_ref):
    refs = (a_ref, b_ref, c_ref, d_ref)
    proj_ref[...] = sum(ref[512:, :].astype(F32) for ref in refs)
    turned = sum(ref[:512, :].astype(F32) for ref in refs).T
    for q in range(4):
        out_ref[:, q * 512 : (q + 1) * 512] = turned[32 * q : 32 * q + 32, :]
    in_ref[...] = grads_ref[:, NX * HD :].astype(F32)


def call(kernel, name, outs, *args, smem=0, scratch=(), limit=32):
    outs = tuple(jax.ShapeDtypeStruct(shape, dtype) for shape, dtype in outs)
    specs = whole(len(outs))
    return pl.pallas_call(
        kernel,
        out_shape=outs if len(outs) > 1 else outs[0],
        in_specs=whole(len(args) - smem, smem),
        out_specs=tuple(specs) if len(outs) > 1 else specs[0],
        scratch_shapes=list(scratch),
        compiler_params=pltpu.CompilerParams(vmem_limit_bytes=limit * 1024 * 1024),
        name=name,
    )(*args)


def whole(count, smem=0):
    specs = [pl.BlockSpec(memory_space=pltpu.SMEM)] * smem
    return specs + [pl.BlockSpec(memory_space=pltpu.VMEM)] * count


def on_device(table, w_uvqk, w_out, history, lengths, candidates, counts, actions, targets):
    rows_total, width = table.shape
    seq = history.shape[1]
    ncand = candidates.shape[1]
    users = NY * NZ
    parts = NX * NC
    block = seq // parts
    cblock = ncand // parts
    x, c = lax.axis_index("x"), lax.axis_index("c")
    local_w = w_uvqk.reshape(width, -1)
    length = lengths[0]

    place = jnp.stack([x, c, length, counts[0]]).astype(jnp.int32)

    def along_x(own):
        return [own] + [swap_x(own, k) for k in range(1, NX)]

    size = block + cblock

    def pick(half):
        return pl.pallas_call(
            functools.partial(pick_kernel, half),
            out_shape=jax.ShapeDtypeStruct((NX, size, width), BF),
            in_specs=whole(2, smem=1) + [pl.BlockSpec(memory_space=pl.ANY)],
            out_specs=whole(1)[0],
            scratch_shapes=[
                pltpu.VMEM((rows_total, width), BF),
                pltpu.VMEM((NX * size, rows_total), BF),
                pltpu.SemaphoreType.DMA((4,)),
            ],
            compiler_params=pltpu.CompilerParams(vmem_limit_bytes=20 * 1024 * 1024),
            name="pick",
        )(place, history, candidates, table)

    picked_other = swap_core(pick(1))
    out_line = along_x(w_out)
    picked_own, *out_line = lax.optimization_barrier((pick(0), *out_line))
    weights_out = out_line + [swap_core(part) for part in out_line]
    line = call(pair_kernel, "pair", [((size, width), BF)] * NX, picked_other, picked_own, limit=8)
    line = [line[0]] + [swap_x(line[k], k) for k in range(1, NX)]
    rows_f, normed, crow = call(
        norm_kernel,
        "norm",
        [((block, width), F32), ((block, width), BF), ((cblock, width), BF)],
        *line,
        limit=8,
    )
    own_other = swap_core(normed)
    normed_line = lax.optimization_barrier(tuple(along_x(normed)) + (crow,))
    spread_rows = list(normed_line[:NX]) + [own_other] + [swap_core(part) for part in normed_line[1:NX]]
    crows = lax.all_gather(normed_line[NX], ("x", "c"), axis=0, tiled=True)
    normed, pre, act, sent = call(
        attend_kernel,
        "attend",
        [((seq, width), BF), ((seq, 4 * HD), F32), ((seq, 4 * HD), BF), ((parts, block, 3 * HD), BF)],
        place,
        *spread_rows,
        local_w,
        smem=1,
        limit=20,
    )
    sent = lax.all_to_all(sent, ("x", "c"), 0, 0)

    half = NX * HD
    back, dhidden, cand_own, cand_other, out_own, out_other = call(
        event_kernel,
        "event",
        [
            ((parts, block + 16, 2 * HD), BF),
            ((block, width), BF),
            ((NX, cblock, width), BF),
            ((NX, cblock, width), BF),
            ((width, half), BF),
            ((width, half), BF),
        ],
        place,
        sent,
        rows_f,
        *weights_out,
        crows,
        actions,
        targets,
        smem=1,
        limit=18,
        scratch=[pltpu.VMEM((ncand, width), BF)],
    )
    back = lax.all_to_all(back, ("x", "c"), 0, 0)
    out_other = swap_core(out_other)

    dpre, part_other, loss_meta = call(
        backward_kernel,
        "backward",
        [((seq, 4 * HD), BF), ((NX, size, width), BF), ((16, 128), BF)],
        place,
        back,
        act,
        pre,
        local_w,
        cand_other,
        smem=1,
        scratch=[
            pltpu.VMEM((seq, HD), BF),
            pltpu.VMEM((seq, HD), BF),
            pltpu.VMEM((seq, HD), F32),
        ],
        limit=20,
    )
    part_own, grads, meta = call(
        weight_kernel,
        "weight",
        [((NX, size, width), BF), ((width, half + 4 * HD), BF), ((16, 128), BF)],
        place,
        dpre,
        local_w,
        cand_own,
        normed,
        out_own,
        out_other,
        history,
        candidates,
        loss_meta,
        smem=1,
        limit=20,
    )
    line = call(pair_kernel, "pair", [((size, width), BF)] * NX, swap_core(part_other), part_own, limit=8)
    line = [line[0]] + [swap_x(line[k], k) for k in range(1, NX)]
    grads = lax.psum_scatter(grads.reshape(NY, -1, half + 4 * HD), "y", scatter_dimension=0, tiled=False)
    grads = lax.psum_scatter(grads, "z", scatter_dimension=0, tiled=True)

    packed = call(
        pack_kernel,
        "pack",
        [((users, 64, 128), BF)],
        *line,
        rows_f,
        dhidden,
        meta,
        limit=10,
    )
    arrived = lax.all_to_all(packed, ("y", "z"), 0, 0)
    got = arrived[:, 48:53].astype(F32)
    all_ids = (got[:, 0:2] * 128.0 + got[:, 2:4]).astype(jnp.int32).reshape(-1)
    own, other = call(
        scatter_kernel,
        "scatter",
        [((NX, 512, 128), BF)] * 2,
        all_ids,
        place,
        arrived,
        smem=2,
        scratch=[
            pltpu.VMEM((users * 48, 128), F32),
            pltpu.VMEM((parts * rows_total, 128), F32),
            pltpu.VMEM((parts * rows_total, 128), F32),
        ],
        limit=24,
    )
    line = call(
        final_pair_kernel, "final_pair", [((512 + 32, 128), BF)] * NX, swap_core(other), own, grads, limit=8
    )
    line = [line[0]] + [swap_x(line[k], k) for k in range(1, NX)]
    shard_t, proj_t, grad_in = call(
        unpack_kernel,
        "unpack",
        [((32, rows_total), F32), ((32, HD), F32), ((32, 4 * HD), F32)],
        *line,
        grads,
        limit=8,
    )
    grad_in = grad_in.reshape(-1, 4, HD)
    loss = jnp.sum(got[:, 4, 0:3])
    return (loss, grad_in, proj_t.T, shard_t.T)


def solution(mesh):
    fine = Mesh(mesh.devices.reshape(NY, NZ, NX, NC), ("y", "z", "x", "c"))
    dp, item = ("y", "z"), ("x", "c")
    placed = (
        P(item, None),
        P(None, None, item),
        P(item, None),
        P(dp, None),
        P(dp),
        P(dp, None),
        P(dp),
        P(dp, None),
        P(dp, None),
    )
    return jax.shard_map(
        on_device,
        mesh=fine,
        in_specs=placed,
        out_specs=(P(), P(dp, None, item), P(item, dp), P(item, dp)),
        check_vma=False,
    )
```

```python
import functools

import jax
import jax.numpy as jnp
from jax import lax
from jax.experimental import pallas as pl
from jax.experimental.pallas import tpu as pltpu
from jax.sharding import Mesh, PartitionSpec as P

HD = 128
NX, NC, NY, NZ = 4, 2, 4, 8
CQL_WEIGHT = 0.5
BF = jnp.bfloat16
F32 = jnp.float32


def swap_x(value, k):
    return lax.ppermute(value, "x", [(i, i ^ k) for i in range(NX)])


def swap_core(value):
    return lax.ppermute(value, "c", [(0, 1), (1, 0)])


def event_slots(item, shape, axis):
    row = lax.broadcasted_iota(jnp.int32, shape, axis)
    return 32 * jnp.bitwise_and(row, 31) + 8 * (row // 32) + item


def cand_slots(item, shape, axis):
    row = lax.broadcasted_iota(jnp.int32, shape, axis)
    return 32 * jnp.bitwise_and(row, 15) + 8 * (row // 16) + item


def chosen(values, slots):
    cols = lax.broadcasted_iota(jnp.int32, (1, values.shape[1]), 1)
    return jnp.sum(jnp.where(cols == slots, values.astype(F32), 0.0), axis=1, keepdims=True)


def pick_kernel(half, place_ref, history_ref, cand_ref, table_ref, out_ref, hot_ref):
    total = table_ref.shape[0]
    first_row = (2 * place_ref[0] + place_ref[1]) * total
    size = out_ref.shape[1]
    for k in range(NX):
        item = item_of(place_ref, half * NX + k)
        events = chosen(history_ref[...], event_slots(item, (128, 1), 0))
        cands = chosen(cand_ref[...], cand_slots(item, (size - 128, 1), 0))
        for first, ids in ((0, events), (128, cands)):
            local = ids.astype(jnp.int32) - first_row
            count = ids.shape[0]
            for i in range(0, total, 512):
                cols = lax.broadcasted_iota(jnp.int32, (1, 512), 1) + i
                hot_ref[size * k + first : size * k + first + count, i : i + 512] = (
                    (local == cols).astype(F32).astype(BF)
                )
    for i in range(0, out_ref.shape[2], 256):
        found = jnp.dot(hot_ref[...], table_ref[:, i : i + 256], preferred_element_type=F32).astype(BF)
        for k in range(NX):
            out_ref[k, :, i : i + 256] = found[size * k : size * k + size, :]


def pair_kernel(a_ref, b_ref, *outs):
    for k, out in enumerate(outs):
        out[...] = (a_ref[k].astype(F32) + b_ref[k].astype(F32)).astype(BF)


def norm_kernel(a_ref, b_ref, c_ref, d_ref, rows_ref, normed_ref, crow_ref):
    refs = (a_ref, b_ref, c_ref, d_ref)
    block = rows_ref.shape[0]
    rows = sum(ref[:block, :].astype(F32) for ref in refs)
    rows_ref[...] = rows
    scale = lax.rsqrt(jnp.mean(rows * rows, axis=-1, keepdims=True) + 1e-06)
    normed_ref[...] = (rows * scale).astype(BF)
    crow_ref[...] = sum(ref[block:, :].astype(F32) for ref in refs).astype(BF)


def item_of(place_ref, b):
    return 2 * jnp.bitwise_xor(place_ref[0], b % NX) + jnp.bitwise_xor(place_ref[1], b // NX)


def places_of(place_ref, shape, axis, first=0):
    row = lax.broadcasted_iota(jnp.int32, shape, axis) + first
    line = jnp.bitwise_and(row, 511)
    item = 2 * jnp.bitwise_xor(place_ref[0], line // 128) + jnp.bitwise_xor(place_ref[1], row // 512)
    inside = jnp.bitwise_and(row, 127)
    return 32 * jnp.bitwise_and(inside, 31) + 8 * (inside // 32) + item


def attend_kernel(
    place_ref, b0, b1, b2, b3, b4, b5, b6, b7, w_ref,
    normed_out, pre_out, act_out, sent_ref, normed_ref, pre_ref, act_ref, sems,
):
    for b, ref in enumerate((b0, b1, b2, b3, b4, b5, b6, b7)):
        normed_ref[128 * b : 128 * b + 128, :] = ref[...]
    copies = [pltpu.make_async_copy(normed_ref, normed_out, sems.at[0])]
    copies[0].start()
    seq = normed_ref.shape[0]
    for i in range(0, seq, 256):
        pre = jnp.dot(normed_ref[i : i + 256, :], w_ref[...], preferred_element_type=F32)
        pre_ref[i : i + 256, :] = pre
        act_ref[i : i + 256, :] = (pre * jax.nn.sigmoid(pre)).astype(BF)
    for i, (source, target) in enumerate(((pre_ref, pre_out), (act_ref, act_out))):
        copies.append(pltpu.make_async_copy(source, target, sems.at[i + 1]))
        copies[-1].start()
    length = place_ref[2]
    inverse = 1.0 / jnp.full((1, 1), length, jnp.int32).astype(F32)
    cols = places_of(place_ref, (1, seq), 1)
    cols = jnp.where(cols < length, cols, seq)
    for i in range(0, seq, 256):
        queries = act_ref[i : i + 256, 2 * HD : 3 * HD]
        logits = lax.dot_general(
            queries, act_ref[:, 3 * HD :], (((1,), (1,)), ((), ())), preferred_element_type=F32
        ) * HD ** (-0.5)
        rows = places_of(place_ref, (256, 1), 0, i)
        attn = jnp.where(cols <= rows, logits * jax.nn.sigmoid(logits) * inverse, 0.0).astype(BF)
        mixed = jnp.dot(attn, act_ref[:, HD : 2 * HD], preferred_element_type=F32)
        top = mixed.astype(BF)
        rest = (mixed - top.astype(F32)).astype(BF)
        for h in range(2):
            b = i // 128 + h
            item = item_of(place_ref, b)
            sent_ref[item, :, 0:HD] = top[128 * h : 128 * h + 128, :]
            sent_ref[item, :, HD : 2 * HD] = rest[128 * h : 128 * h + 128, :]
            sent_ref[item, :, 2 * HD :] = act_ref[128 * b : 128 * b + 128, 0:HD]
    for copy in copies:
        copy.wait()


def split_loss(value, shape, row):
    value = jnp.broadcast_to(value, shape)
    top = value.astype(BF).astype(F32)
    middle = (value - top).astype(BF).astype(F32)
    low = value - top - middle
    lane = lax.broadcasted_iota(jnp.int32, shape, 1)
    picked = jnp.where(lane == 0, top, jnp.where(lane == 1, middle, jnp.where(lane == 2, low, 0.0)))
    return jnp.where(lax.broadcasted_iota(jnp.int32, shape, 0) == row, picked, 0.0).astype(BF)


def event_kernel(
    place_ref, sent_ref, rows_ref, w0, w1, w2, w3, crows_ref, action_ref, target_ref,
    back_ref, dhidden_ref, cand_own_ref, cand_other_ref, out_own_ref, out_other_ref,
    dcand_ref, weight_ref, crow_ref, sems,
):
    copies = [
        pltpu.make_async_copy(
            ref.at[item_of(place_ref, b)],
            weight_ref.at[b, jnp.bitwise_xor(place_ref[4], k)],
            sems.at[NY * b + k],
        )
        for b in range(NX * NC)
        for k, ref in enumerate((w0, w1, w2, w3))
    ]
    copies.append(pltpu.make_async_copy(crows_ref, crow_ref, sems.at[NX * NC * NY]))
    for copy in copies:
        copy.start()
    owner = 2 * place_ref[0] + place_ref[1]
    length, count = place_ref[2], place_ref[3]
    block, width = rows_ref.shape
    seq = block * NX * NC
    items = [item_of(place_ref, b) for b in range(NX * NC)]
    mixed = jnp.concatenate(
        [sent_ref[i, :, 0:HD].astype(F32) + sent_ref[i, :, HD : 2 * HD].astype(F32) for i in items], axis=1
    )
    gate = jnp.concatenate([sent_ref[i, :, 2 * HD :] for i in items], axis=1).astype(F32)
    center = jnp.mean(mixed, axis=-1, keepdims=True)
    rstd = lax.rsqrt(jnp.mean(mixed * mixed, axis=-1, keepdims=True) - center * center + 1e-05)
    normo = (mixed - center) * rstd
    gated = (normo * gate).astype(BF)
    for copy in copies:
        copy.wait()
    weights = weight_ref[...].reshape(gated.shape[1], gated.shape[1])
    out = rows_ref[...] + jnp.dot(gated, weights, preferred_element_type=F32)
    hidden = out.astype(BF)
    crows = crow_ref[...]
    scores = lax.dot_general(hidden, crows, (((1,), (1,)), ((), ())), preferred_element_type=F32)
    col = lax.broadcasted_iota(jnp.int32, (1, crows.shape[0]), 1)
    inside = jnp.bitwise_and(col, 63)
    slots = 32 * jnp.bitwise_and(inside, 15) + 8 * (inside // 16) + col // 64
    masked = jnp.where(slots < count, scores, -jnp.inf)
    top = jnp.max(masked, axis=-1, keepdims=True)
    expo = jnp.exp(masked - top)
    total = jnp.sum(expo, axis=-1, keepdims=True)
    soft = expo / total
    lse = top + jnp.log(total)
    places = event_slots(owner, (block, 1), 0)
    actions = chosen(action_ref[...], places).astype(jnp.int32)
    onehot = (slots == actions).astype(F32)
    taken = jnp.sum(scores * onehot, axis=-1, keepdims=True)
    live = jnp.where(places < length, 1.0 / seq, 0.0)
    miss = taken - chosen(target_ref[...], places)
    loss = jnp.sum(live * (CQL_WEIGHT * (lse - taken) + 0.5 * miss * miss), axis=0, keepdims=True)
    loss = split_loss(loss, (16, 2 * HD), 0)
    dscore = (live * (CQL_WEIGHT * soft + (miss - CQL_WEIGHT) * onehot)).astype(BF)
    dhidden = jnp.dot(dscore, crows, preferred_element_type=F32).astype(BF)
    dhidden_ref[...] = dhidden
    dgated = lax.dot_general(
        dhidden, weights, (((1,), (1,)), ((), ())), preferred_element_type=F32
    )
    dnormo = dgated * gate
    first = jnp.mean(dnormo, axis=-1, keepdims=True)
    second = jnp.mean(dnormo * normo, axis=-1, keepdims=True)
    dmixed = (rstd * (dnormo - first - normo * second)).astype(BF)
    du = (dgated * normo).astype(BF)
    for b, i in enumerate(items):
        back_ref[i, 0:block, 0:HD] = dmixed[:, HD * b : HD * b + HD]
        back_ref[i, 0:block, HD:] = du[:, HD * b : HD * b + HD]
        back_ref[i, block:, :] = loss
    turned = (((0,), (0,)), ((), ()))
    half = NX * HD
    out_other_ref[...] = lax.dot_general(
        dhidden, gated[:, half:], turned, preferred_element_type=F32
    ).astype(BF)
    out_own_ref[...] = lax.dot_general(
        dhidden, gated[:, :half], turned, preferred_element_type=F32
    ).astype(BF)
    dcand_ref[...] = lax.dot_general(dscore, hidden, turned, preferred_element_type=F32).astype(BF)
    size = cand_own_ref.shape[1]
    for k in range(NX):
        cand_own_ref[k] = dcand_ref[pl.ds(pl.multiple_of(items[k] * size, size), size), :]
        cand_other_ref[k] = dcand_ref[pl.ds(pl.multiple_of(items[NX + k] * size, size), size), :]


def backward_kernel(
    place_ref, back_ref, act_in, pre_in, dpre_ref, far_ref, loss_ref,
    dm_ref, du_ref, dq_ref, act_ref, pre_ref, sems,
):
    copies = [
        pltpu.make_async_copy(source, target, sems.at[i])
        for i, (source, target) in enumerate(((act_in, act_ref), (pre_in, pre_ref)))
    ]
    for copy in copies:
        copy.start()
    seq = act_ref.shape[0]
    loss = jnp.zeros((16, 2 * HD), F32)
    for b in range(8):
        item = item_of(place_ref, b)
        dm_ref[128 * b : 128 * b + 128, :] = back_ref[item, 0:128, 0:HD]
        du_ref[128 * b : 128 * b + 128, :] = back_ref[item, 0:128, HD:]
        loss = loss + back_ref[item, 128:144, :].astype(F32)
    loss = jnp.sum(jnp.sum(loss, axis=1, keepdims=True), axis=0, keepdims=True)
    loss_ref[...] = split_loss(loss, (16, 128), 4)
    length = place_ref[2]
    inverse = 1.0 / jnp.full((1, 1), length, jnp.int32).astype(F32)
    cols = places_of(place_ref, (1, seq), 1)
    across = (((1,), (1,)), ((), ()))
    dq_ref[...] = jnp.zeros(dq_ref.shape, F32)

    def slope(value, sigma):
        return sigma * (1.0 + value * (1.0 - sigma))

    for copy in copies:
        copy.wait()
    for i in range(0, seq, 256):
        keys = act_ref[i : i + 256, 3 * HD :]
        logits = lax.dot_general(
            keys, act_ref[:, 2 * HD : 3 * HD], across, preferred_element_type=F32
        ) * HD ** (-0.5)
        rows = places_of(place_ref, (256, 1), 0, i)
        rows = jnp.where(rows < length, rows, seq)
        allowed = rows <= cols
        sigma = jax.nn.sigmoid(logits)
        attn = jnp.where(allowed, logits * sigma * inverse, 0.0).astype(BF)
        dattn = lax.dot_general(
            act_ref[i : i + 256, HD : 2 * HD], dm_ref[...], across, preferred_element_type=F32
        )
        dlogits = jnp.where(
            allowed, dattn * inverse * slope(logits, sigma) * HD ** (-0.5), 0.0
        ).astype(BF)
        dvalues = jnp.dot(attn, dm_ref[...], preferred_element_type=F32)
        dkeys = jnp.dot(dlogits, act_ref[:, 2 * HD : 3 * HD], preferred_element_type=F32)
        dq_ref[...] += lax.dot_general(
            dlogits, keys, (((0,), (0,)), ((), ())), preferred_element_type=F32
        )
        for j, grad in ((1, dvalues), (3, dkeys)):
            pre = pre_ref[i : i + 256, HD * j : HD * j + HD]
            dpre_ref[i : i + 256, HD * j : HD * j + HD] = (
                grad * slope(pre, jax.nn.sigmoid(pre))
            ).astype(BF)
    for j, ref in ((0, du_ref), (2, dq_ref)):
        pre = pre_ref[:, HD * j : HD * j + HD]
        dpre_ref[:, HD * j : HD * j + HD] = (
            ref[...].astype(F32) * slope(pre, jax.nn.sigmoid(pre))
        ).astype(BF)
    far_ref[...] = dpre_ref[far_ref.shape[0] :, :]


def part_kernel(dpre_ref, far_ref, w_ref, far_w_ref, cand_ref, far_cand_ref, *outs):
    across = (((1,), (1,)), ((), ()))
    for h in range(2):
        rows = slice(256 * h, 256 * h + 256)
        part = lax.dot_general(dpre_ref[rows, :], w_ref[...], across, preferred_element_type=F32)
        part = part + lax.dot_general(
            far_ref[rows, :], far_w_ref[...], across, preferred_element_type=F32
        )
        part = part.astype(BF)
        outs[2 * h][0:128, :] = part[:128, :]
        outs[2 * h + 1][0:128, :] = part[128:, :]
    for k in range(NX):
        outs[k][128:, :] = (cand_ref[k].astype(F32) + far_cand_ref[k].astype(F32)).astype(BF)


def weight_kernel(dpre_ref, normed_ref, a_ref, b_ref, grads_ref):
    half = a_ref.shape[1]
    left = (a_ref[...].astype(F32) + b_ref[...].astype(F32)).astype(BF)
    right = lax.dot_general(
        normed_ref[...], dpre_ref[...], (((0,), (0,)), ((), ())), preferred_element_type=F32
    ).astype(BF)
    for y in range(NY):
        for z in range(NZ):
            rows = slice(32 * (NZ * y + z), 32 * (NZ * y + z) + 32)
            grads_ref[z, 32 * y : 32 * y + 32, :half] = left[rows, :]
            grads_ref[z, 32 * y : 32 * y + 32, half:] = right[rows, :]


def turn_kernel(place_ref, grads_ref, *outs):
    for k, out in enumerate(outs):
        start = jnp.bitwise_xor(place_ref[4], k) * 32
        out[...] = grads_ref[pl.ds(pl.multiple_of(start, 32), 32), :]


def meta_kernel(place_ref, history_ref, cands_ref, loss_ref, meta_ref):
    owner = 2 * place_ref[0] + place_ref[1]

    def digits(values, wanted):
        row = lax.broadcasted_iota(jnp.int32, (16, values.shape[1]), 0)
        upper, lower = values // 128, jnp.bitwise_and(values, 127)
        both = jnp.where(row == 0, upper, jnp.where(row == 2, lower, 0)).astype(F32).astype(BF)
        source = lax.broadcasted_iota(jnp.int32, (values.shape[1], 128), 0)
        hot = (source == wanted).astype(F32).astype(BF)
        return jnp.dot(both, hot, preferred_element_type=F32)

    lane = lax.broadcasted_iota(jnp.int32, (16, 128), 1)
    row = lax.broadcasted_iota(jnp.int32, (16, 128), 0)
    events = digits(history_ref[...], event_slots(owner, (1, 128), 1))
    wanted = cand_slots(owner, (1, 128), 1)
    wanted = jnp.where(lax.broadcasted_iota(jnp.int32, (1, 128), 1) < 64, wanted, -1)
    cands = pltpu.roll(digits(cands_ref[...], wanted), 1, 0)
    meta = events + cands + loss_ref[...].astype(F32)
    for where, value in ((64, place_ref[2]), (65, place_ref[3])):
        for r, part in ((1, value // 128), (3, jnp.bitwise_and(value, 127))):
            part = jnp.full((16, 128), part, jnp.int32).astype(F32)
            meta = jnp.where((lane == where) & (row == r), part, meta)
    meta_ref[...] = meta.astype(BF)


def pack_kernel(a_ref, b_ref, c_ref, d_ref, rows_ref, dhidden_ref, meta_ref, out_ref):
    refs = (a_ref, b_ref, c_ref, d_ref)
    block = rows_ref.shape[0]
    dnormed = sum(ref[:block, :].astype(F32) for ref in refs)
    rows = rows_ref[...]
    scale = lax.rsqrt(jnp.mean(rows * rows, axis=-1, keepdims=True) + 1e-06)
    normed = rows * scale
    drows = dhidden_ref[...].astype(F32) + scale * (
        dnormed - normed * jnp.mean(dnormed * normed, axis=-1, keepdims=True)
    )
    drows = drows.astype(BF)
    dcand = sum(ref[block:, :].astype(F32) for ref in refs).astype(BF)
    meta = meta_ref[...]
    for d in range(out_ref.shape[0]):
        out_ref[d, 0:32, :] = jnp.concatenate(
            [drows[32 * g : 32 * g + 32, 32 * d : 32 * d + 32] for g in range(4)], axis=1
        )
        out_ref[d, 32:48, :] = jnp.concatenate(
            [dcand[16 * g : 16 * g + 16, 32 * d : 32 * d + 32] for g in range(4)], axis=1
        )
        out_ref[d, 48:64, :] = meta


def scatter_kernel(ids_ref, place_ref, data_ref, own_ref, other_ref, rows_ref, acc_ref, more_ref):
    users = data_ref.shape[0]
    total = acc_ref.shape[0]
    chunk = 512
    owner = 2 * place_ref[0] + place_ref[1]

    def clear(i, carry):
        here = pl.ds(pl.multiple_of(i * chunk, chunk), chunk)
        acc_ref[here, :] = jnp.zeros((chunk, 128), F32)
        more_ref[here, :] = jnp.zeros((chunk, 128), F32)
        return carry

    lax.fori_loop(0, total // chunk, clear, 0)
    for u in range(users):
        rows_ref[48 * u : 48 * u + 48, :] = data_ref[u, 0:48, :].astype(F32)
    lane = lax.broadcasted_iota(jnp.int32, (1, 128), 1) // 32
    masks = [lane == g for g in range(4)]

    def add(first_id, pitch, first_row, count):
        def step(i, carry):
            for j in range(2):
                work = []
                for half, ref in ((0, acc_ref), (1, more_ref)):
                    p = i * 4 + j * 2 + half
                    row = rows_ref[pl.ds(first_row + p, 1), :]
                    ids = [ids_ref[first_id + g * pitch + p] for g in range(4)]
                    work.append((ref, row, ids, [ref[pl.ds(ids[g], 1), :] for g in range(4)]))
                for ref, row, ids, held in work:
                    for g in range(4):
                        pltpu.store(ref.at[pl.ds(ids[g], 1), :], held[g] + row, mask=masks[g])
            return carry

        lax.fori_loop(0, (count + 3) // 4, step, 0)

    def user(u, carry):
        base = u * 256
        events = jnp.clip((ids_ref[base + 192] - owner + 31) // 32, 0, 32)
        cands = jnp.clip((ids_ref[base + 193] - owner + 31) // 32, 0, 16)
        add(base, 32, u * 48, events)
        add(base + 128, 16, u * 48 + 32, cands)
        return carry

    lax.fori_loop(0, users, user, 0)
    wide = lax.broadcasted_iota(jnp.int32, (512, 128), 1) // 32
    for cc in range(2):
        for k in range(4):
            item = item_of(place_ref, cc * NX + k)
            result = jnp.zeros((512, 128), F32)
            for q in range(4):
                here = pl.ds(pl.multiple_of(item * 2048 + q * 512, 512), 512)
                part = acc_ref[here, :] + more_ref[here, :]
                part = part + pltpu.roll(part, 64, 1)
                part = part + pltpu.roll(part, 32, 1)
                result = jnp.where(wide == q, part, result)
            (own_ref, other_ref)[cc][k] = result.astype(BF)


def final_pair_kernel(a_ref, b_ref, g0, g1, g2, g3, *outs):
    half = NX * HD
    proj = sum(ref[:, :half].astype(F32) for ref in (g0, g1, g2, g3)).astype(BF)
    for k, out in enumerate(outs):
        out[:512, :] = (a_ref[k].astype(F32) + b_ref[k].astype(F32)).astype(BF)
        out[512:, :] = proj[:, HD * k : HD * k + HD]


def unpack_kernel(a_ref, b_ref, c_ref, d_ref, g0, g1, g2, g3, out_ref, proj_ref, in_ref):
    refs = (a_ref, b_ref, c_ref, d_ref)
    proj_ref[...] = sum(ref[512:, :].astype(F32) for ref in refs)
    turned = sum(ref[:512, :].astype(F32) for ref in refs).T
    for q in range(4):
        out_ref[:, q * 512 : (q + 1) * 512] = turned[32 * q : 32 * q + 32, :]
    in_ref[...] = sum(ref[:, NX * HD :].astype(F32) for ref in (g0, g1, g2, g3))


def whole(count, smem=0):
    specs = [pl.BlockSpec(memory_space=pltpu.SMEM)] * smem
    return specs + [pl.BlockSpec(memory_space=pltpu.VMEM)] * count


def call(kernel, name, outs, *args, smem=0, scratch=(), limit=32, far=(), far_outs=(), cost=1.0):
    outs = tuple(jax.ShapeDtypeStruct(shape, dtype) for shape, dtype in outs)
    hbm = pl.BlockSpec(memory_space=pltpu.HBM)
    specs = [hbm if i in far_outs else whole(1)[0] for i in range(len(outs))]
    in_specs = [hbm if i in far else spec for i, spec in enumerate(whole(len(args) - smem, smem))]
    return pl.pallas_call(
        kernel,
        out_shape=outs if len(outs) > 1 else outs[0],
        in_specs=in_specs,
        out_specs=tuple(specs) if len(outs) > 1 else specs[0],
        scratch_shapes=list(scratch),
        compiler_params=pltpu.CompilerParams(vmem_limit_bytes=limit * 1024 * 1024),
        cost_estimate=pl.CostEstimate(
            flops=int(cost * 1.1e9), bytes_accessed=int(cost * 3.6e6), transcendentals=0
        ),
        name=name,
    )(*args)


def on_device(table, w_uvqk, w_out, history, lengths, candidates, counts, actions, targets):
    rows_total, width = table.shape
    seq = history.shape[1]
    ncand = candidates.shape[1]
    users = NY * NZ
    parts = NX * NC
    block = seq // parts
    cblock = ncand // parts
    x, c = lax.axis_index("x"), lax.axis_index("c")
    local_w = w_uvqk.reshape(width, -1)
    length = lengths[0]

    place = jnp.stack([x, c, length, counts[0], lax.axis_index("y")]).astype(jnp.int32)

    def along_x(own):
        return [own] + [swap_x(own, k) for k in range(1, NX)]

    def along_y(pieces):
        return [pieces[0]] + [
            lax.ppermute(pieces[k], "y", [(i, i ^ k) for i in range(NY)]) for k in range(1, NY)
        ]

    size = block + cblock

    def pick(half):
        return call(
            functools.partial(pick_kernel, half),
            "pick",
            [((NX, size, width), BF)],
            place,
            history,
            candidates,
            table,
            smem=1,
            scratch=[pltpu.VMEM((NX * size, rows_total), BF)],
            limit=20,
            cost=5.0 if half else 0.05,
        )

    picked_other = swap_core(pick(1))
    picked_own = pick(0)
    quarter = w_out.shape[0] // NY
    weights_out = lax.dynamic_slice_in_dim(w_out, lax.axis_index("y") * quarter, quarter, 0)
    weights_out = lax.all_gather(weights_out, ("x", "c"), axis=0, tiled=False)
    line = list(call(pair_kernel, "pair", [((size, width), BF)] * NX, picked_other, picked_own, limit=8))
    line = [line[0]] + [swap_x(line[k], k) for k in range(1, NX)]
    line[1], weights_out = lax.optimization_barrier((line[1], weights_out))
    weights_out = along_y([weights_out] * NY)
    rows_f, normed, crow = call(
        norm_kernel,
        "norm",
        [((block, width), F32), ((block, width), BF), ((cblock, width), BF)],
        *line,
        limit=8,
    )
    own_other = swap_core(normed)
    *normed_line, local_w = lax.optimization_barrier((*along_x(normed), crow, local_w))
    far_w = swap_core(local_w)
    spread_rows = normed_line[:NX] + [own_other] + [swap_core(part) for part in normed_line[1:NX]]
    crows = lax.all_gather(normed_line[NX], ("x", "c"), axis=0, tiled=True)
    spread_rows[NX], far_w = lax.optimization_barrier((spread_rows[NX], far_w))
    normed, pre, act, sent = call(
        attend_kernel,
        "attend",
        [((seq, width), BF), ((seq, 4 * HD), F32), ((seq, 4 * HD), BF), ((parts, block, 3 * HD), BF)],
        place,
        *spread_rows,
        local_w,
        smem=1,
        limit=20,
        far_outs=(0, 1, 2),
        scratch=[
            pltpu.VMEM((seq, width), BF),
            pltpu.VMEM((seq, 4 * HD), F32),
            pltpu.VMEM((seq, 4 * HD), BF),
            pltpu.SemaphoreType.DMA((3,)),
        ],
        cost=4.0,
    )
    sent = lax.all_to_all(sent, ("x", "c"), 0, 0)

    half = NX * HD
    back, dhidden, cand_own, cand_other, out_own, out_other = call(
        event_kernel,
        "event",
        [
            ((parts, block + 16, 2 * HD), BF),
            ((block, width), BF),
            ((NX, cblock, width), BF),
            ((NX, cblock, width), BF),
            ((width, half), BF),
            ((width, half), BF),
        ],
        place,
        sent,
        rows_f,
        *weights_out,
        crows,
        actions,
        targets,
        smem=1,
        limit=18,
        far=tuple(range(3, 8)),
        scratch=[
            pltpu.VMEM((ncand, width), BF),
            pltpu.VMEM((parts, NY, quarter, width), BF),
            pltpu.VMEM((ncand, width), BF),
            pltpu.SemaphoreType.DMA((parts * NY + 1,)),
        ],
        cost=4.0,
    )
    back = lax.all_to_all(back, ("x", "c"), 0, 0)
    out_other = swap_core(out_other)

    back, cand_other = lax.optimization_barrier((back, swap_core(cand_other)))
    dpre, dpre_far, loss_meta = call(
        backward_kernel,
        "backward",
        [((seq, 4 * HD), BF), ((seq // 2, 4 * HD), BF), ((16, 128), BF)],
        place,
        back,
        act,
        pre,
        smem=1,
        scratch=[
            pltpu.VMEM((seq, HD), BF),
            pltpu.VMEM((seq, HD), BF),
            pltpu.VMEM((seq, HD), F32),
            pltpu.VMEM((seq, 4 * HD), BF),
            pltpu.VMEM((seq, 4 * HD), F32),
            pltpu.SemaphoreType.DMA((2,)),
        ],
        limit=24,
        far=(2, 3),
        cost=6.0,
    )
    dpre_far = swap_core(dpre_far)
    grads = call(
        weight_kernel,
        "weight",
        [((NZ, width // NZ, half + 4 * HD), BF)],
        dpre,
        normed,
        out_own,
        out_other,
        limit=16,
        cost=2.5,
    )
    line = list(
        call(
            part_kernel,
            "part",
            [((size, width), BF)] * NX,
            dpre,
            dpre_far,
            local_w,
            far_w,
            cand_own,
            cand_other,
            limit=16,
            cost=2.0,
        )
    )
    grads = lax.psum_scatter(grads, "z", scatter_dimension=0, tiled=False)
    loss_meta, line[0] = lax.optimization_barrier((loss_meta, line[0]))
    meta = call(
        meta_kernel, "meta", [((16, 128), BF)], place, history, candidates, loss_meta, smem=1, limit=8
    )
    line = [line[0]] + [swap_x(line[k], k) for k in range(1, NX)]

    packed = call(
        pack_kernel,
        "pack",
        [((users, 64, 128), BF)],
        *line,
        rows_f,
        dhidden,
        meta,
        limit=10,
    )
    arrived = lax.all_to_all(packed, ("y", "z"), 0, 0)
    _, grads = lax.optimization_barrier((arrived, grads))
    grads = call(turn_kernel, "turn", [((32, half + 4 * HD), BF)] * NY, place, grads, smem=1, limit=8, cost=0.5)
    grads = along_y(list(grads))
    got = arrived[:, 48:53].astype(F32)
    all_ids = (got[:, 0:2] * 128.0 + got[:, 2:4]).astype(jnp.int32).reshape(-1)
    own, other = call(
        scatter_kernel,
        "scatter",
        [((NX, 512, 128), BF)] * 2,
        all_ids,
        place,
        arrived,
        smem=2,
        scratch=[
            pltpu.VMEM((users * 48, 128), F32),
            pltpu.VMEM((parts * rows_total, 128), F32),
            pltpu.VMEM((parts * rows_total, 128), F32),
        ],
        limit=24,
        cost=12.0,
    )
    line = call(
        final_pair_kernel, "final_pair", [((512 + 32, 128), BF)] * NX, swap_core(other), own, *grads, limit=8
    )
    line = [line[0]] + [swap_x(line[k], k) for k in range(1, NX)]
    shard_t, proj_t, grad_in = call(
        unpack_kernel,
        "unpack",
        [((32, rows_total), F32), ((32, HD), F32), ((32, 4 * HD), F32)],
        *line,
        *grads,
        limit=8,
    )
    grad_in = grad_in.reshape(-1, 4, HD)
    loss = jnp.sum(got[:, 4, 0:3])
    return (loss, grad_in, proj_t.T, shard_t.T)


def solution(mesh):
    fine = Mesh(mesh.devices.reshape(NY, NZ, NX, NC), ("y", "z", "x", "c"))
    dp, item = ("y", "z"), ("x", "c")
    placed = (
        P(item, None),
        P(None, None, item),
        P(item, None),
        P(dp, None),
        P(dp),
        P(dp, None),
        P(dp),
        P(dp, None),
        P(dp, None),
    )
    return jax.shard_map(
        on_device,
        mesh=fine,
        in_specs=placed,
        out_specs=(P(), P(dp, None, item), P(item, dp), P(item, dp)),
        check_vma=False,
    )
```

```python
import functools

import jax
import jax.numpy as jnp
from jax import lax
from jax.experimental import pallas as pl
from jax.experimental.pallas import tpu as pltpu
from jax.sharding import Mesh, PartitionSpec as P

HD = 128
NX, NC, NY, NZ = 4, 2, 4, 8
CQL_WEIGHT = 0.5
BF = jnp.bfloat16
F32 = jnp.float32


def swap_x(value, k):
    return lax.ppermute(value, "x", [(i, i ^ k) for i in range(NX)])


def swap_core(value):
    return lax.ppermute(value, "c", [(0, 1), (1, 0)])


def event_slots(item, shape, axis):
    row = lax.broadcasted_iota(jnp.int32, shape, axis)
    return 32 * jnp.bitwise_and(row, 31) + 8 * (row // 32) + item


def cand_slots(item, shape, axis):
    row = lax.broadcasted_iota(jnp.int32, shape, axis)
    return 32 * jnp.bitwise_and(row, 15) + 8 * (row // 16) + item


def chosen(values, slots):
    cols = lax.broadcasted_iota(jnp.int32, (1, values.shape[1]), 1)
    return jnp.sum(jnp.where(cols == slots, values.astype(F32), 0.0), axis=1, keepdims=True)


def pick_kernel(half, place_ref, history_ref, cand_ref, table_ref, out_ref, hot_ref):
    total = table_ref.shape[0]
    first_row = (2 * place_ref[0] + place_ref[1]) * total
    size = out_ref.shape[1]
    for k in range(NX):
        item = item_of(place_ref, half * NX + k)
        events = chosen(history_ref[...], event_slots(item, (128, 1), 0))
        cands = chosen(cand_ref[...], cand_slots(item, (size - 128, 1), 0))
        for first, ids in ((0, events), (128, cands)):
            local = ids.astype(jnp.int32) - first_row
            count = ids.shape[0]
            for i in range(0, total, 512):
                cols = lax.broadcasted_iota(jnp.int32, (1, 512), 1) + i
                hot_ref[size * k + first : size * k + first + count, i : i + 512] = (
                    (local == cols).astype(F32).astype(BF)
                )
    for i in range(0, out_ref.shape[2], 256):
        found = jnp.dot(hot_ref[...], table_ref[:, i : i + 256], preferred_element_type=F32).astype(BF)
        for k in range(NX):
            out_ref[k, :, i : i + 256] = found[size * k : size * k + size, :]


def pair_kernel(a_ref, b_ref, *outs):
    for k, out in enumerate(outs):
        out[...] = (a_ref[k].astype(F32) + b_ref[k].astype(F32)).astype(BF)


def norm_kernel(a_ref, b_ref, c_ref, d_ref, normed_ref, crow_ref):
    refs = (a_ref, b_ref, c_ref, d_ref)
    block = normed_ref.shape[0]
    rows = sum(ref[:block, :].astype(F32) for ref in refs)
    scale = lax.rsqrt(jnp.mean(rows * rows, axis=-1, keepdims=True) + 1e-06)
    normed_ref[...] = (rows * scale).astype(BF)
    crow_ref[...] = sum(ref[block:, :].astype(F32) for ref in refs).astype(BF)


def rows_kernel(a_ref, b_ref, c_ref, d_ref, rows_ref):
    block = rows_ref.shape[0]
    rows_ref[...] = sum(ref[:block, :].astype(F32) for ref in (a_ref, b_ref, c_ref, d_ref)).astype(BF)


def item_of(place_ref, b):
    return 2 * jnp.bitwise_xor(place_ref[0], b % NX) + jnp.bitwise_xor(place_ref[1], b // NX)


def places_of(place_ref, shape, axis, first=0):
    row = lax.broadcasted_iota(jnp.int32, shape, axis) + first
    line = jnp.bitwise_and(row, 511)
    item = 2 * jnp.bitwise_xor(place_ref[0], line // 128) + jnp.bitwise_xor(place_ref[1], row // 512)
    inside = jnp.bitwise_and(row, 127)
    return 32 * jnp.bitwise_and(inside, 31) + 8 * (inside // 32) + item


def attend_kernel(
    place_ref, b0, b1, b2, b3, b4, b5, b6, b7, w_ref,
    normed_out, pre_out, act_out, sent_ref, normed_ref, pre_ref, act_ref, sems,
):
    for b, ref in enumerate((b0, b1, b2, b3, b4, b5, b6, b7)):
        normed_ref[128 * b : 128 * b + 128, :] = ref[...]
    copies = [pltpu.make_async_copy(normed_ref, normed_out, sems.at[0])]
    copies[0].start()
    seq = normed_ref.shape[0]
    for i in range(0, seq, 256):
        pre = jnp.dot(normed_ref[i : i + 256, :], w_ref[...], preferred_element_type=F32)
        pre_ref[i : i + 256, :] = pre
        act_ref[i : i + 256, :] = (pre * jax.nn.sigmoid(pre)).astype(BF)
    for i, (source, target) in enumerate(((pre_ref, pre_out), (act_ref, act_out))):
        copies.append(pltpu.make_async_copy(source, target, sems.at[i + 1]))
        copies[-1].start()
    length = place_ref[2]
    inverse = 1.0 / jnp.full((1, 1), length, jnp.int32).astype(F32)
    cols = places_of(place_ref, (1, seq), 1)
    cols = jnp.where(cols < length, cols, seq)
    for i in range(0, seq, 256):
        queries = act_ref[i : i + 256, 2 * HD : 3 * HD]
        logits = lax.dot_general(
            queries, act_ref[:, 3 * HD :], (((1,), (1,)), ((), ())), preferred_element_type=F32
        ) * HD ** (-0.5)
        rows = places_of(place_ref, (256, 1), 0, i)
        attn = jnp.where(cols <= rows, logits * jax.nn.sigmoid(logits) * inverse, 0.0).astype(BF)
        mixed = jnp.dot(attn, act_ref[:, HD : 2 * HD], preferred_element_type=F32)
        top = mixed.astype(BF)
        rest = (mixed - top.astype(F32)).astype(BF)
        for h in range(2):
            b = i // 128 + h
            item = item_of(place_ref, b)
            sent_ref[item, :, 0:HD] = top[128 * h : 128 * h + 128, :]
            sent_ref[item, :, HD : 2 * HD] = rest[128 * h : 128 * h + 128, :]
            sent_ref[item, :, 2 * HD :] = act_ref[128 * b : 128 * b + 128, 0:HD]
    for copy in copies:
        copy.wait()


def split_loss(value, shape, row):
    value = jnp.broadcast_to(value, shape)
    top = value.astype(BF).astype(F32)
    middle = (value - top).astype(BF).astype(F32)
    low = value - top - middle
    lane = lax.broadcasted_iota(jnp.int32, shape, 1)
    picked = jnp.where(lane == 0, top, jnp.where(lane == 1, middle, jnp.where(lane == 2, low, 0.0)))
    return jnp.where(lax.broadcasted_iota(jnp.int32, shape, 0) == row, picked, 0.0).astype(BF)


def event_kernel(
    place_ref, sent_ref, rows_ref, w_ref, crows_ref, action_ref, target_ref,
    back_ref, dhidden_ref, cand_own_ref, cand_other_ref, out_own_ref, out_other_ref,
    dcand_ref, weight_ref, crow_ref, sems,
):
    copies = [
        pltpu.make_async_copy(
            w_ref.at[item_of(place_ref, b)], weight_ref.at[HD * b : HD * b + HD, :], sems.at[b]
        )
        for b in range(NX * NC)
    ]
    copies.append(pltpu.make_async_copy(crows_ref, crow_ref, sems.at[NX * NC]))
    for copy in copies:
        copy.start()
    owner = 2 * place_ref[0] + place_ref[1]
    length, count = place_ref[2], place_ref[3]
    block, width = rows_ref.shape
    seq = block * NX * NC
    items = [item_of(place_ref, b) for b in range(NX * NC)]
    mixed = jnp.concatenate(
        [sent_ref[i, :, 0:HD].astype(F32) + sent_ref[i, :, HD : 2 * HD].astype(F32) for i in items], axis=1
    )
    gate = jnp.concatenate([sent_ref[i, :, 2 * HD :] for i in items], axis=1).astype(F32)
    center = jnp.mean(mixed, axis=-1, keepdims=True)
    rstd = lax.rsqrt(jnp.mean(mixed * mixed, axis=-1, keepdims=True) - center * center + 1e-05)
    normo = (mixed - center) * rstd
    gated = (normo * gate).astype(BF)
    for copy in copies:
        copy.wait()
    weights = weight_ref[...]
    out = rows_ref[...].astype(F32) + jnp.dot(gated, weights, preferred_element_type=F32)
    hidden = out.astype(BF)
    crows = crow_ref[...]
    scores = lax.dot_general(hidden, crows, (((1,), (1,)), ((), ())), preferred_element_type=F32)
    col = lax.broadcasted_iota(jnp.int32, (1, crows.shape[0]), 1)
    inside = jnp.bitwise_and(col, 63)
    slots = 32 * jnp.bitwise_and(inside, 15) + 8 * (inside // 16) + col // 64
    masked = jnp.where(slots < count, scores, -jnp.inf)
    top = jnp.max(masked, axis=-1, keepdims=True)
    expo = jnp.exp(masked - top)
    total = jnp.sum(expo, axis=-1, keepdims=True)
    soft = expo / total
    lse = top + jnp.log(total)
    places = event_slots(owner, (block, 1), 0)
    actions = chosen(action_ref[...], places).astype(jnp.int32)
    onehot = (slots == actions).astype(F32)
    taken = jnp.sum(scores * onehot, axis=-1, keepdims=True)
    live = jnp.where(places < length, 1.0 / seq, 0.0)
    miss = taken - chosen(target_ref[...], places)
    loss = jnp.sum(live * (CQL_WEIGHT * (lse - taken) + 0.5 * miss * miss), axis=0, keepdims=True)
    loss = split_loss(loss, (16, 2 * HD), 0)
    dscore = (live * (CQL_WEIGHT * soft + (miss - CQL_WEIGHT) * onehot)).astype(BF)
    dhidden = jnp.dot(dscore, crows, preferred_element_type=F32).astype(BF)
    dhidden_ref[...] = dhidden
    dgated = lax.dot_general(
        dhidden, weights, (((1,), (1,)), ((), ())), preferred_element_type=F32
    )
    dnormo = dgated * gate
    first = jnp.mean(dnormo, axis=-1, keepdims=True)
    second = jnp.mean(dnormo * normo, axis=-1, keepdims=True)
    dmixed = (rstd * (dnormo - first - normo * second)).astype(BF)
    du = (dgated * normo).astype(BF)
    for b, i in enumerate(items):
        back_ref[i, 0:block, 0:HD] = dmixed[:, HD * b : HD * b + HD]
        back_ref[i, 0:block, HD:] = du[:, HD * b : HD * b + HD]
        back_ref[i, block:, :] = loss
    turned = (((0,), (0,)), ((), ()))
    half = NX * HD
    out_other_ref[...] = lax.dot_general(
        dhidden, gated[:, half:], turned, preferred_element_type=F32
    ).astype(BF)
    out_own_ref[...] = lax.dot_general(
        dhidden, gated[:, :half], turned, preferred_element_type=F32
    ).astype(BF)
    dcand_ref[...] = lax.dot_general(dscore, hidden, turned, preferred_element_type=F32).astype(BF)
    size = cand_own_ref.shape[1]
    for k in range(NX):
        cand_own_ref[k] = dcand_ref[pl.ds(pl.multiple_of(items[k] * size, size), size), :]
        cand_other_ref[k] = dcand_ref[pl.ds(pl.multiple_of(items[NX + k] * size, size), size), :]


def backward_kernel(
    place_ref, back_ref, act_in, pre_in, near_ref, far_ref, loss_ref,
    dm_ref, du_ref, dq_ref, dpre_ref, act_ref, pre_ref, sems,
):
    copies = [
        pltpu.make_async_copy(source, target, sems.at[i])
        for i, (source, target) in enumerate(((act_in, act_ref), (pre_in, pre_ref)))
    ]
    for copy in copies:
        copy.start()
    seq = act_ref.shape[0]
    loss = jnp.zeros((16, 2 * HD), F32)
    for b in range(8):
        item = item_of(place_ref, b)
        dm_ref[128 * b : 128 * b + 128, :] = back_ref[item, 0:128, 0:HD]
        du_ref[128 * b : 128 * b + 128, :] = back_ref[item, 0:128, HD:]
        loss = loss + back_ref[item, 128:144, :].astype(F32)
    loss = jnp.sum(jnp.sum(loss, axis=1, keepdims=True), axis=0, keepdims=True)
    loss_ref[...] = split_loss(loss, (16, 128), 4)
    length = place_ref[2]
    inverse = 1.0 / jnp.full((1, 1), length, jnp.int32).astype(F32)
    cols = places_of(place_ref, (1, seq), 1)
    across = (((1,), (1,)), ((), ()))
    dq_ref[...] = jnp.zeros(dq_ref.shape, F32)

    def slope(value, sigma):
        return sigma * (1.0 + value * (1.0 - sigma))

    for copy in copies:
        copy.wait()
    for i in range(0, seq, 256):
        keys = act_ref[i : i + 256, 3 * HD :]
        logits = lax.dot_general(
            keys, act_ref[:, 2 * HD : 3 * HD], across, preferred_element_type=F32
        ) * HD ** (-0.5)
        rows = places_of(place_ref, (256, 1), 0, i)
        rows = jnp.where(rows < length, rows, seq)
        allowed = rows <= cols
        sigma = jax.nn.sigmoid(logits)
        attn = jnp.where(allowed, logits * sigma * inverse, 0.0).astype(BF)
        dattn = lax.dot_general(
            act_ref[i : i + 256, HD : 2 * HD], dm_ref[...], across, preferred_element_type=F32
        )
        dlogits = jnp.where(
            allowed, dattn * inverse * slope(logits, sigma) * HD ** (-0.5), 0.0
        ).astype(BF)
        dvalues = jnp.dot(attn, dm_ref[...], preferred_element_type=F32)
        dkeys = jnp.dot(dlogits, act_ref[:, 2 * HD : 3 * HD], preferred_element_type=F32)
        dq_ref[...] += lax.dot_general(
            dlogits, keys, (((0,), (0,)), ((), ())), preferred_element_type=F32
        )
        for j, grad in ((1, dvalues), (3, dkeys)):
            pre = pre_ref[i : i + 256, HD * j : HD * j + HD]
            dpre_ref[i : i + 256, HD * j : HD * j + HD] = (
                grad * slope(pre, jax.nn.sigmoid(pre))
            ).astype(BF)
    for j, ref in ((0, du_ref), (2, dq_ref)):
        pre = pre_ref[:, HD * j : HD * j + HD]
        dpre_ref[:, HD * j : HD * j + HD] = (
            ref[...].astype(F32) * slope(pre, jax.nn.sigmoid(pre))
        ).astype(BF)
    near_ref[...] = dpre_ref[: near_ref.shape[0], :]
    far_ref[...] = dpre_ref[near_ref.shape[0] :, :]


def part_kernel(near_ref, far_ref, w_ref, far_w_ref, cand_ref, far_cand_ref, *outs):
    across = (((1,), (1,)), ((), ()))
    for h in range(2):
        rows = slice(256 * h, 256 * h + 256)
        part = lax.dot_general(near_ref[rows, :], w_ref[...], across, preferred_element_type=F32)
        part = part + lax.dot_general(
            far_ref[rows, :], far_w_ref[...], across, preferred_element_type=F32
        )
        part = part.astype(BF)
        outs[2 * h][0:128, :] = part[:128, :]
        outs[2 * h + 1][0:128, :] = part[128:, :]
    for k in range(NX):
        outs[k][128:, :] = (cand_ref[k].astype(F32) + far_cand_ref[k].astype(F32)).astype(BF)


def weight_kernel(near_ref, far_ref, normed_ref, a_ref, b_ref, grads_ref):
    half = a_ref.shape[1]
    count = near_ref.shape[0]
    turned = (((0,), (0,)), ((), ()))
    left = (a_ref[...].astype(F32) + b_ref[...].astype(F32)).astype(BF)
    right = lax.dot_general(
        normed_ref[:count, :], near_ref[...], turned, preferred_element_type=F32
    )
    right = right + lax.dot_general(
        normed_ref[count:, :], far_ref[...], turned, preferred_element_type=F32
    )
    right = right.astype(BF)
    for y in range(NY):
        for z in range(NZ):
            rows = slice(32 * (NZ * y + z), 32 * (NZ * y + z) + 32)
            grads_ref[z, 32 * y : 32 * y + 32, :half] = left[rows, :]
            grads_ref[z, 32 * y : 32 * y + 32, half:] = right[rows, :]


def meta_kernel(place_ref, history_ref, cands_ref, loss_ref, meta_ref):
    owner = 2 * place_ref[0] + place_ref[1]

    def digits(values, wanted):
        row = lax.broadcasted_iota(jnp.int32, (16, values.shape[1]), 0)
        upper, lower = values // 128, jnp.bitwise_and(values, 127)
        both = jnp.where(row == 0, upper, jnp.where(row == 2, lower, 0)).astype(F32).astype(BF)
        source = lax.broadcasted_iota(jnp.int32, (values.shape[1], 128), 0)
        hot = (source == wanted).astype(F32).astype(BF)
        return jnp.dot(both, hot, preferred_element_type=F32)

    lane = lax.broadcasted_iota(jnp.int32, (16, 128), 1)
    row = lax.broadcasted_iota(jnp.int32, (16, 128), 0)
    events = digits(history_ref[...], event_slots(owner, (1, 128), 1))
    wanted = cand_slots(owner, (1, 128), 1)
    wanted = jnp.where(lax.broadcasted_iota(jnp.int32, (1, 128), 1) < 64, wanted, -1)
    cands = pltpu.roll(digits(cands_ref[...], wanted), 1, 0)
    meta = events + cands + loss_ref[...].astype(F32)
    for where, value in ((64, place_ref[2]), (65, place_ref[3])):
        for r, part in ((1, value // 128), (3, jnp.bitwise_and(value, 127))):
            part = jnp.full((16, 128), part, jnp.int32).astype(F32)
            meta = jnp.where((lane == where) & (row == r), part, meta)
    meta_ref[...] = meta.astype(BF)


def pack_kernel(a_ref, b_ref, c_ref, d_ref, rows_ref, dhidden_ref, meta_ref, out_ref):
    refs = (a_ref, b_ref, c_ref, d_ref)
    block = rows_ref.shape[0]
    dnormed = sum(ref[:block, :].astype(F32) for ref in refs)
    rows = rows_ref[...].astype(F32)
    scale = lax.rsqrt(jnp.mean(rows * rows, axis=-1, keepdims=True) + 1e-06)
    normed = rows * scale
    drows = dhidden_ref[...].astype(F32) + scale * (
        dnormed - normed * jnp.mean(dnormed * normed, axis=-1, keepdims=True)
    )
    drows = drows.astype(BF)
    dcand = sum(ref[block:, :].astype(F32) for ref in refs).astype(BF)
    meta = meta_ref[...]
    for d in range(out_ref.shape[0]):
        out_ref[d, 0:32, :] = jnp.concatenate(
            [drows[32 * g : 32 * g + 32, 32 * d : 32 * d + 32] for g in range(4)], axis=1
        )
        out_ref[d, 32:48, :] = jnp.concatenate(
            [dcand[16 * g : 16 * g + 16, 32 * d : 32 * d + 32] for g in range(4)], axis=1
        )
        out_ref[d, 48:64, :] = meta


def scatter_kernel(ids_ref, place_ref, data_ref, own_ref, other_ref, rows_ref, acc_ref, more_ref):
    users = data_ref.shape[0]
    total = acc_ref.shape[0]
    chunk = 512
    owner = 2 * place_ref[0] + place_ref[1]

    def clear(i, carry):
        here = pl.ds(pl.multiple_of(i * chunk, chunk), chunk)
        acc_ref[here, :] = jnp.zeros((chunk, 128), F32)
        more_ref[here, :] = jnp.zeros((chunk, 128), F32)
        return carry

    lax.fori_loop(0, total // chunk, clear, 0)
    for u in range(users):
        rows_ref[48 * u : 48 * u + 48, :] = data_ref[u, 0:48, :].astype(F32)
    lane = lax.broadcasted_iota(jnp.int32, (1, 128), 1) // 32
    masks = [lane == g for g in range(4)]

    def add(first_id, pitch, first_row, count):
        def step(i, carry):
            for j in range(2):
                work = []
                for half, ref in ((0, acc_ref), (1, more_ref)):
                    p = i * 4 + j * 2 + half
                    row = rows_ref[pl.ds(first_row + p, 1), :]
                    ids = [ids_ref[first_id + g * pitch + p] for g in range(4)]
                    work.append((ref, row, ids, [ref[pl.ds(ids[g], 1), :] for g in range(4)]))
                for ref, row, ids, held in work:
                    for g in range(4):
                        pltpu.store(ref.at[pl.ds(ids[g], 1), :], held[g] + row, mask=masks[g])
            return carry

        lax.fori_loop(0, (count + 3) // 4, step, 0)

    def user(u, carry):
        base = u * 256
        events = jnp.clip((ids_ref[base + 192] - owner + 31) // 32, 0, 32)
        cands = jnp.clip((ids_ref[base + 193] - owner + 31) // 32, 0, 16)
        add(base, 32, u * 48, events)
        add(base + 128, 16, u * 48 + 32, cands)
        return carry

    lax.fori_loop(0, users, user, 0)
    wide = lax.broadcasted_iota(jnp.int32, (512, 128), 1) // 32
    for cc in range(2):
        for k in range(4):
            item = item_of(place_ref, cc * NX + k)
            result = jnp.zeros((512, 128), F32)
            for q in range(4):
                here = pl.ds(pl.multiple_of(item * 2048 + q * 512, 512), 512)
                part = acc_ref[here, :] + more_ref[here, :]
                part = part + pltpu.roll(part, 64, 1)
                part = part + pltpu.roll(part, 32, 1)
                result = jnp.where(wide == q, part, result)
            (own_ref, other_ref)[cc][k] = result.astype(BF)


def final_pair_kernel(a_ref, b_ref, grads_ref, *outs):
    for k, out in enumerate(outs):
        out[:512, :] = (a_ref[k].astype(F32) + b_ref[k].astype(F32)).astype(BF)
        out[512:, :] = grads_ref[:, HD * k : HD * k + HD]


def unpack_kernel(a_ref, b_ref, c_ref, d_ref, grads_ref, out_ref, proj_ref, in_ref):
    refs = (a_ref, b_ref, c_ref, d_ref)
    proj_ref[...] = sum(ref[512:, :].astype(F32) for ref in refs)
    turned = sum(ref[:512, :].astype(F32) for ref in refs).T
    for q in range(4):
        out_ref[:, q * 512 : (q + 1) * 512] = turned[32 * q : 32 * q + 32, :]
    in_ref[...] = grads_ref[:, NX * HD :].astype(F32)


def whole(count, smem=0):
    specs = [pl.BlockSpec(memory_space=pltpu.SMEM)] * smem
    return specs + [pl.BlockSpec(memory_space=pltpu.VMEM)] * count


def call(kernel, name, outs, *args, smem=0, scratch=(), limit=32, far=(), far_outs=(), cost=1.0):
    outs = tuple(jax.ShapeDtypeStruct(shape, dtype) for shape, dtype in outs)
    hbm = pl.BlockSpec(memory_space=pltpu.HBM)
    specs = [hbm if i in far_outs else whole(1)[0] for i in range(len(outs))]
    in_specs = [hbm if i in far else spec for i, spec in enumerate(whole(len(args) - smem, smem))]
    return pl.pallas_call(
        kernel,
        out_shape=outs if len(outs) > 1 else outs[0],
        in_specs=in_specs,
        out_specs=tuple(specs) if len(outs) > 1 else specs[0],
        scratch_shapes=list(scratch),
        compiler_params=pltpu.CompilerParams(vmem_limit_bytes=int(limit * 1024 * 1024)),
        cost_estimate=pl.CostEstimate(
            flops=int(cost * 1.1e9), bytes_accessed=int(cost * 3.6e6), transcendentals=0
        ),
        name=name,
    )(*args)


def on_device(table, w_uvqk, w_out, history, lengths, candidates, counts, actions, targets):
    rows_total, width = table.shape
    seq = history.shape[1]
    ncand = candidates.shape[1]
    users = NY * NZ
    parts = NX * NC
    block = seq // parts
    cblock = ncand // parts
    x, c = lax.axis_index("x"), lax.axis_index("c")
    length = lengths[0]

    place = jnp.stack([x, c, length, counts[0], lax.axis_index("y")]).astype(jnp.int32)

    def along_x(own):
        return [own] + [swap_x(own, k) for k in range(1, NX)]

    size = block + cblock

    def pick(half):
        return call(
            functools.partial(pick_kernel, half),
            "pick",
            [((NX, size, width), BF)],
            place,
            history,
            candidates,
            table,
            smem=1,
            scratch=[pltpu.VMEM((NX * size, rows_total), BF)],
            limit=20,
            cost=5.0 if half else 0.05,
        )

    picked_other = swap_core(pick(1))
    weights_out = lax.all_gather(w_out, ("x", "c"), axis=0, tiled=False)
    picked_own = pick(0)
    line = list(call(pair_kernel, "pair", [((size, width), BF)] * NX, picked_other, picked_own, limit=8))
    line = [line[0]] + [swap_x(line[k], k) for k in range(1, NX)]
    w_uvqk, line[0] = lax.optimization_barrier((w_uvqk, line[0]))
    local_w = w_uvqk.reshape(width, -1)
    normed, crow = call(
        norm_kernel,
        "norm",
        [((block, width), BF), ((cblock, width), BF)],
        *line,
        limit=50,
    )
    own_other = swap_core(normed)
    far_w = swap_core(local_w)
    line[0], normed = lax.optimization_barrier((line[0], normed))
    rows = call(rows_kernel, "rows", [((block, width), BF)], *line, limit=50, cost=0.5)
    *normed_line, local_w, far_w, rows = lax.optimization_barrier(
        (*along_x(normed), crow, local_w, far_w, rows)
    )
    spread_rows = normed_line[:NX] + [own_other] + [swap_core(part) for part in normed_line[1:NX]]
    crows = lax.all_gather(normed_line[NX], ("x", "c"), axis=0, tiled=True)
    normed, pre, act, sent = call(
        attend_kernel,
        "attend",
        [((seq, width), BF), ((seq, 4 * HD), F32), ((seq, 4 * HD), BF), ((parts, block, 3 * HD), BF)],
        place,
        *spread_rows,
        local_w,
        smem=1,
        limit=52,
        far_outs=(0, 1, 2),
        scratch=[
            pltpu.VMEM((seq, width), BF),
            pltpu.VMEM((seq, 4 * HD), F32),
            pltpu.VMEM((seq, 4 * HD), BF),
            pltpu.SemaphoreType.DMA((3,)),
        ],
        cost=4.0,
    )
    sent = lax.all_to_all(sent, ("x", "c"), 0, 0)

    half = NX * HD
    back, dhidden, cand_own, cand_other, out_own, out_other = call(
        event_kernel,
        "event",
        [
            ((parts, block + 16, 2 * HD), BF),
            ((block, width), BF),
            ((NX, cblock, width), BF),
            ((NX, cblock, width), BF),
            ((width, half), BF),
            ((width, half), BF),
        ],
        place,
        sent,
        rows,
        weights_out,
        crows,
        actions,
        targets,
        smem=1,
        limit=60,
        far=(3, 4),
        scratch=[
            pltpu.VMEM((ncand, width), BF),
            pltpu.VMEM((width, width), BF),
            pltpu.VMEM((ncand, width), BF),
            pltpu.SemaphoreType.DMA((parts + 1,)),
        ],
        cost=4.0,
    )
    back = lax.all_to_all(back, ("x", "c"), 0, 0)
    out_other = swap_core(out_other)

    back, cand_other = lax.optimization_barrier((back, swap_core(cand_other)))
    near, far, loss_meta = call(
        backward_kernel,
        "backward",
        [((seq // 2, 4 * HD), BF), ((seq // 2, 4 * HD), BF), ((16, 128), BF)],
        place,
        back,
        act,
        pre,
        smem=1,
        scratch=[
            pltpu.VMEM((seq, HD), BF),
            pltpu.VMEM((seq, HD), BF),
            pltpu.VMEM((seq, HD), F32),
            pltpu.VMEM((seq, 4 * HD), BF),
            pltpu.VMEM((seq, 4 * HD), BF),
            pltpu.VMEM((seq, 4 * HD), F32),
            pltpu.SemaphoreType.DMA((2,)),
        ],
        limit=60,
        far=(2, 3),
        cost=6.0,
    )
    far_got = swap_core(far)
    grads = call(
        weight_kernel,
        "weight",
        [((NZ, width // NZ, half + 4 * HD), BF)],
        near,
        far,
        normed,
        out_own,
        out_other,
        limit=60,
        cost=2.5,
    )
    line = list(
        call(
            part_kernel,
            "part",
            [((size, width), BF)] * NX,
            near,
            far_got,
            local_w,
            far_w,
            cand_own,
            cand_other,
            limit=50,
            cost=2.0,
        )
    )
    grads = lax.psum_scatter(grads, "z", scatter_dimension=0, tiled=False)
    loss_meta, line[0] = lax.optimization_barrier((loss_meta, line[0]))
    meta = call(
        meta_kernel, "meta", [((16, 128), BF)], place, history, candidates, loss_meta, smem=1, limit=40
    )
    line = [line[0]] + [swap_x(line[k], k) for k in range(1, NX)]

    packed = call(
        pack_kernel,
        "pack",
        [((users, 64, 128), BF)],
        *line,
        rows,
        dhidden,
        meta,
        limit=50,
    )
    arrived = lax.all_to_all(packed, ("y", "z"), 0, 0)
    _, grads = lax.optimization_barrier((arrived, grads))
    grads = lax.psum_scatter(grads.reshape(NY, 32, -1), "y", scatter_dimension=0, tiled=False)
    got = arrived[:, 48:53].astype(F32)
    all_ids = (got[:, 0:2] * 128.0 + got[:, 2:4]).astype(jnp.int32).reshape(-1)
    own, other = call(
        scatter_kernel,
        "scatter",
        [((NX, 512, 128), BF)] * 2,
        all_ids,
        place,
        arrived,
        smem=2,
        scratch=[
            pltpu.VMEM((users * 48, 128), F32),
            pltpu.VMEM((parts * rows_total, 128), F32),
            pltpu.VMEM((parts * rows_total, 128), F32),
        ],
        limit=24,
        cost=12.0,
    )
    other, grads = lax.optimization_barrier((other, grads))
    line = call(
        final_pair_kernel, "final_pair", [((512 + 32, 128), BF)] * NX, swap_core(other), own, grads, limit=8
    )
    line = [line[0]] + [swap_x(line[k], k) for k in range(1, NX)]
    shard_t, proj_t, grad_in = call(
        unpack_kernel,
        "unpack",
        [((32, rows_total), F32), ((32, HD), F32), ((32, 4 * HD), F32)],
        *line,
        grads,
        limit=8,
    )
    grad_in = grad_in.reshape(-1, 4, HD)
    loss = jnp.sum(got[:, 4, 0:3])
    return (loss, grad_in, proj_t.T, shard_t.T)


def solution(mesh):
    fine = Mesh(mesh.devices.reshape(NY, NZ, NX, NC), ("y", "z", "x", "c"))
    dp, item = ("y", "z"), ("x", "c")
    placed = (
        P(item, None),
        P(None, None, item),
        P(item, None),
        P(dp, None),
        P(dp),
        P(dp, None),
        P(dp),
        P(dp, None),
        P(dp, None),
    )
    return jax.shard_map(
        on_device,
        mesh=fine,
        in_specs=placed,
        out_specs=(P(), P(dp, None, item), P(item, dp), P(item, dp)),
        check_vma=False,
    )
```

```python
import functools

import jax
import jax.numpy as jnp
from jax import lax
from jax.experimental import pallas as pl
from jax.experimental.pallas import tpu as pltpu
from jax.sharding import Mesh, PartitionSpec as P

HD = 128
NX, NC, NY, NZ = 4, 2, 4, 8
CQL_WEIGHT = 0.5
BF = jnp.bfloat16
F32 = jnp.float32


def swap_x(value, k):
    return lax.ppermute(value, "x", [(i, i ^ k) for i in range(NX)])


def swap_core(value):
    return lax.ppermute(value, "c", [(0, 1), (1, 0)])


def event_slots(item, shape, axis):
    row = lax.broadcasted_iota(jnp.int32, shape, axis)
    return 32 * jnp.bitwise_and(row, 31) + 8 * (row // 32) + item


def cand_slots(item, shape, axis):
    row = lax.broadcasted_iota(jnp.int32, shape, axis)
    return 32 * jnp.bitwise_and(row, 15) + 8 * (row // 16) + item


def chosen(values, slots):
    cols = lax.broadcasted_iota(jnp.int32, (1, values.shape[1]), 1)
    return jnp.sum(jnp.where(cols == slots, values.astype(F32), 0.0), axis=1, keepdims=True)


def pick_kernel(half, place_ref, history_ref, cand_ref, table_ref, out_ref, hot_ref):
    total = table_ref.shape[0]
    first_row = (2 * place_ref[0] + place_ref[1]) * total
    size = out_ref.shape[1]
    for k in range(NX):
        item = item_of(place_ref, half * NX + k)
        events = chosen(history_ref[...], event_slots(item, (128, 1), 0))
        cands = chosen(cand_ref[...], cand_slots(item, (size - 128, 1), 0))
        for first, ids in ((0, events), (128, cands)):
            local = ids.astype(jnp.int32) - first_row
            count = ids.shape[0]
            for i in range(0, total, 512):
                cols = lax.broadcasted_iota(jnp.int32, (1, 512), 1) + i
                hot_ref[size * k + first : size * k + first + count, i : i + 512] = (
                    (local == cols).astype(F32).astype(BF)
                )
    for i in range(0, out_ref.shape[2], 256):
        found = jnp.dot(hot_ref[...], table_ref[:, i : i + 256], preferred_element_type=F32).astype(BF)
        for k in range(NX):
            out_ref[k, :, i : i + 256] = found[size * k : size * k + size, :]


def pair_kernel(a_ref, b_ref, *outs):
    for k, out in enumerate(outs):
        out[...] = (a_ref[k].astype(F32) + b_ref[k].astype(F32)).astype(BF)


def norm_kernel(a_ref, b_ref, c_ref, d_ref, normed_ref, crow_ref):
    refs = (a_ref, b_ref, c_ref, d_ref)
    block = normed_ref.shape[0]
    rows = sum(ref[:block, :].astype(F32) for ref in refs)
    scale = lax.rsqrt(jnp.mean(rows * rows, axis=-1, keepdims=True) + 1e-06)
    normed_ref[...] = (rows * scale).astype(BF)
    crow_ref[...] = sum(ref[block:, :].astype(F32) for ref in refs).astype(BF)


def rows_kernel(a_ref, b_ref, c_ref, d_ref, rows_ref):
    block = rows_ref.shape[0]
    rows_ref[...] = sum(ref[:block, :].astype(F32) for ref in (a_ref, b_ref, c_ref, d_ref)).astype(BF)


def sigmoid(value):
    return 0.5 * jnp.tanh(0.5 * value) + 0.5


def item_of(place_ref, b):
    return 2 * jnp.bitwise_xor(place_ref[0], b % NX) + jnp.bitwise_xor(place_ref[1], b // NX)


def places_of(place_ref, shape, axis, first=0):
    row = lax.broadcasted_iota(jnp.int32, shape, axis) + first
    line = jnp.bitwise_and(row, 511)
    item = 2 * jnp.bitwise_xor(place_ref[0], line // 128) + jnp.bitwise_xor(place_ref[1], row // 512)
    inside = jnp.bitwise_and(row, 127)
    return 32 * jnp.bitwise_and(inside, 31) + 8 * (inside // 32) + item


def attend_kernel(
    place_ref, b0, b1, b2, b3, b4, b5, b6, b7, w_ref,
    normed_out, pre_out, act_out, sent_ref, normed_ref, pre_ref, act_ref, sems,
):
    for b, ref in enumerate((b0, b1, b2, b3, b4, b5, b6, b7)):
        normed_ref[128 * b : 128 * b + 128, :] = ref[...]
    copies = [pltpu.make_async_copy(normed_ref, normed_out, sems.at[0])]
    copies[0].start()
    seq = normed_ref.shape[0]
    for i in range(0, seq, 256):
        pre = jnp.dot(normed_ref[i : i + 256, :], w_ref[...], preferred_element_type=F32)
        pre_ref[i : i + 256, :] = pre
        act_ref[i : i + 256, :] = (pre * sigmoid(pre)).astype(BF)
    for i, (source, target) in enumerate(((pre_ref, pre_out), (act_ref, act_out))):
        copies.append(pltpu.make_async_copy(source, target, sems.at[i + 1]))
        copies[-1].start()
    length = place_ref[2]
    inverse = 1.0 / jnp.full((1, 1), length, jnp.int32).astype(F32)
    cols = places_of(place_ref, (1, seq), 1)
    cols = jnp.where(cols < length, cols, seq)
    for i in range(0, seq, 256):
        queries = act_ref[i : i + 256, 2 * HD : 3 * HD]
        logits = lax.dot_general(
            queries, act_ref[:, 3 * HD :], (((1,), (1,)), ((), ())), preferred_element_type=F32
        ) * HD ** (-0.5)
        rows = places_of(place_ref, (256, 1), 0, i)
        attn = jnp.where(cols <= rows, logits * sigmoid(logits) * inverse, 0.0).astype(BF)
        mixed = jnp.dot(attn, act_ref[:, HD : 2 * HD], preferred_element_type=F32)
        top = mixed.astype(BF)
        rest = (mixed - top.astype(F32)).astype(BF)
        for h in range(2):
            b = i // 128 + h
            item = item_of(place_ref, b)
            sent_ref[item, :, 0:HD] = top[128 * h : 128 * h + 128, :]
            sent_ref[item, :, HD : 2 * HD] = rest[128 * h : 128 * h + 128, :]
            sent_ref[item, :, 2 * HD :] = act_ref[128 * b : 128 * b + 128, 0:HD]
    for copy in copies:
        copy.wait()


def split_loss(value, shape, row):
    value = jnp.broadcast_to(value, shape)
    top = value.astype(BF).astype(F32)
    middle = (value - top).astype(BF).astype(F32)
    low = value - top - middle
    lane = lax.broadcasted_iota(jnp.int32, shape, 1)
    picked = jnp.where(lane == 0, top, jnp.where(lane == 1, middle, jnp.where(lane == 2, low, 0.0)))
    return jnp.where(lax.broadcasted_iota(jnp.int32, shape, 0) == row, picked, 0.0).astype(BF)


def event_kernel(
    place_ref, sent_ref, rows_ref, w_ref, crows_ref, action_ref, target_ref,
    back_ref, dhidden_ref, cand_own_ref, cand_other_ref, out_own_ref, out_other_ref,
    dcand_ref, weight_ref, crow_ref, sems,
):
    copies = [
        pltpu.make_async_copy(
            w_ref.at[item_of(place_ref, b)], weight_ref.at[HD * b : HD * b + HD, :], sems.at[b]
        )
        for b in range(NX * NC)
    ]
    copies.append(pltpu.make_async_copy(crows_ref, crow_ref, sems.at[NX * NC]))
    for copy in copies:
        copy.start()
    owner = 2 * place_ref[0] + place_ref[1]
    length, count = place_ref[2], place_ref[3]
    block, width = rows_ref.shape
    seq = block * NX * NC
    items = [item_of(place_ref, b) for b in range(NX * NC)]
    mixed = jnp.concatenate(
        [sent_ref[i, :, 0:HD].astype(F32) + sent_ref[i, :, HD : 2 * HD].astype(F32) for i in items], axis=1
    )
    gate = jnp.concatenate([sent_ref[i, :, 2 * HD :] for i in items], axis=1).astype(F32)
    center = jnp.mean(mixed, axis=-1, keepdims=True)
    rstd = lax.rsqrt(jnp.mean(mixed * mixed, axis=-1, keepdims=True) - center * center + 1e-05)
    normo = (mixed - center) * rstd
    gated = (normo * gate).astype(BF)
    for copy in copies:
        copy.wait()
    weights = weight_ref[...]
    out = rows_ref[...].astype(F32) + jnp.dot(gated, weights, preferred_element_type=F32)
    hidden = out.astype(BF)
    crows = crow_ref[...]
    scores = lax.dot_general(hidden, crows, (((1,), (1,)), ((), ())), preferred_element_type=F32)
    col = lax.broadcasted_iota(jnp.int32, (1, crows.shape[0]), 1)
    inside = jnp.bitwise_and(col, 63)
    slots = 32 * jnp.bitwise_and(inside, 15) + 8 * (inside // 16) + col // 64
    masked = jnp.where(slots < count, scores, -jnp.inf)
    top = jnp.max(masked, axis=-1, keepdims=True)
    expo = jnp.exp(masked - top)
    total = jnp.sum(expo, axis=-1, keepdims=True)
    soft = expo / total
    lse = top + jnp.log(total)
    places = event_slots(owner, (block, 1), 0)
    actions = chosen(action_ref[...], places).astype(jnp.int32)
    onehot = (slots == actions).astype(F32)
    taken = jnp.sum(scores * onehot, axis=-1, keepdims=True)
    live = jnp.where(places < length, 1.0 / seq, 0.0)
    miss = taken - chosen(target_ref[...], places)
    loss = jnp.sum(live * (CQL_WEIGHT * (lse - taken) + 0.5 * miss * miss), axis=0, keepdims=True)
    loss = split_loss(loss, (16, 2 * HD), 0)
    dscore = (live * (CQL_WEIGHT * soft + (miss - CQL_WEIGHT) * onehot)).astype(BF)
    dhidden = jnp.dot(dscore, crows, preferred_element_type=F32).astype(BF)
    dhidden_ref[...] = dhidden
    dgated = lax.dot_general(
        dhidden, weights, (((1,), (1,)), ((), ())), preferred_element_type=F32
    )
    dnormo = dgated * gate
    first = jnp.mean(dnormo, axis=-1, keepdims=True)
    second = jnp.mean(dnormo * normo, axis=-1, keepdims=True)
    dmixed = (rstd * (dnormo - first - normo * second)).astype(BF)
    du = (dgated * normo).astype(BF)
    for b, i in enumerate(items):
        back_ref[i, 0:block, 0:HD] = dmixed[:, HD * b : HD * b + HD]
        back_ref[i, 0:block, HD:] = du[:, HD * b : HD * b + HD]
        back_ref[i, block:, :] = loss
    turned = (((0,), (0,)), ((), ()))
    half = NX * HD
    out_other_ref[...] = lax.dot_general(
        dhidden, gated[:, half:], turned, preferred_element_type=F32
    ).astype(BF)
    out_own_ref[...] = lax.dot_general(
        dhidden, gated[:, :half], turned, preferred_element_type=F32
    ).astype(BF)
    dcand_ref[...] = lax.dot_general(dscore, hidden, turned, preferred_element_type=F32).astype(BF)
    size = cand_own_ref.shape[1]
    for k in range(NX):
        cand_own_ref[k] = dcand_ref[pl.ds(pl.multiple_of(items[k] * size, size), size), :]
        cand_other_ref[k] = dcand_ref[pl.ds(pl.multiple_of(items[NX + k] * size, size), size), :]


def backward_kernel(
    place_ref, back_ref, act_in, pre_in, near_ref, far_ref, loss_ref,
    dm_ref, du_ref, dq_ref, dpre_ref, act_ref, pre_ref, sems,
):
    copies = [
        pltpu.make_async_copy(source, target, sems.at[i])
        for i, (source, target) in enumerate(((act_in, act_ref), (pre_in, pre_ref)))
    ]
    for copy in copies:
        copy.start()
    seq = act_ref.shape[0]
    loss = jnp.zeros((16, 2 * HD), F32)
    for b in range(8):
        item = item_of(place_ref, b)
        dm_ref[128 * b : 128 * b + 128, :] = back_ref[item, 0:128, 0:HD]
        du_ref[128 * b : 128 * b + 128, :] = back_ref[item, 0:128, HD:]
        loss = loss + back_ref[item, 128:144, :].astype(F32)
    loss = jnp.sum(jnp.sum(loss, axis=1, keepdims=True), axis=0, keepdims=True)
    loss_ref[...] = split_loss(loss, (16, 128), 4)
    length = place_ref[2]
    inverse = 1.0 / jnp.full((1, 1), length, jnp.int32).astype(F32)
    cols = places_of(place_ref, (1, seq), 1)
    across = (((1,), (1,)), ((), ()))
    dq_ref[...] = jnp.zeros(dq_ref.shape, F32)

    def slope(value, sigma):
        return sigma * (1.0 + value * (1.0 - sigma))

    for copy in copies:
        copy.wait()
    for i in range(0, seq, 256):
        keys = act_ref[i : i + 256, 3 * HD :]
        logits = lax.dot_general(
            keys, act_ref[:, 2 * HD : 3 * HD], across, preferred_element_type=F32
        ) * HD ** (-0.5)
        rows = places_of(place_ref, (256, 1), 0, i)
        rows = jnp.where(rows < length, rows, seq)
        allowed = rows <= cols
        sigma = sigmoid(logits)
        attn = jnp.where(allowed, logits * sigma * inverse, 0.0).astype(BF)
        dattn = lax.dot_general(
            act_ref[i : i + 256, HD : 2 * HD], dm_ref[...], across, preferred_element_type=F32
        )
        dlogits = jnp.where(
            allowed, dattn * inverse * slope(logits, sigma) * HD ** (-0.5), 0.0
        ).astype(BF)
        dvalues = jnp.dot(attn, dm_ref[...], preferred_element_type=F32)
        dkeys = jnp.dot(dlogits, act_ref[:, 2 * HD : 3 * HD], preferred_element_type=F32)
        dq_ref[...] += lax.dot_general(
            dlogits, keys, (((0,), (0,)), ((), ())), preferred_element_type=F32
        )
        for j, grad in ((1, dvalues), (3, dkeys)):
            pre = pre_ref[i : i + 256, HD * j : HD * j + HD]
            dpre_ref[i : i + 256, HD * j : HD * j + HD] = (
                grad * slope(pre, sigmoid(pre))
            ).astype(BF)
    for j, ref in ((0, du_ref), (2, dq_ref)):
        pre = pre_ref[:, HD * j : HD * j + HD]
        dpre_ref[:, HD * j : HD * j + HD] = (
            ref[...].astype(F32) * slope(pre, sigmoid(pre))
        ).astype(BF)
    near_ref[...] = dpre_ref[: near_ref.shape[0], :]
    far_ref[...] = dpre_ref[near_ref.shape[0] :, :]


def part_kernel(near_ref, far_ref, w_ref, far_w_ref, cand_ref, far_cand_ref, *outs):
    across = (((1,), (1,)), ((), ()))
    for h in range(2):
        rows = slice(256 * h, 256 * h + 256)
        part = lax.dot_general(near_ref[rows, :], w_ref[...], across, preferred_element_type=F32)
        part = part + lax.dot_general(
            far_ref[rows, :], far_w_ref[...], across, preferred_element_type=F32
        )
        part = part.astype(BF)
        outs[2 * h][0:128, :] = part[:128, :]
        outs[2 * h + 1][0:128, :] = part[128:, :]
    for k in range(NX):
        outs[k][128:, :] = (cand_ref[k].astype(F32) + far_cand_ref[k].astype(F32)).astype(BF)


def weight_kernel(near_ref, far_ref, normed_ref, a_ref, b_ref, grads_ref):
    half = a_ref.shape[1]
    count = near_ref.shape[0]
    turned = (((0,), (0,)), ((), ()))
    left = (a_ref[...].astype(F32) + b_ref[...].astype(F32)).astype(BF)
    right = lax.dot_general(
        normed_ref[:count, :], near_ref[...], turned, preferred_element_type=F32
    )
    right = right + lax.dot_general(
        normed_ref[count:, :], far_ref[...], turned, preferred_element_type=F32
    )
    right = right.astype(BF)
    for y in range(NY):
        for z in range(NZ):
            rows = slice(32 * (NZ * y + z), 32 * (NZ * y + z) + 32)
            grads_ref[z, 32 * y : 32 * y + 32, :half] = left[rows, :]
            grads_ref[z, 32 * y : 32 * y + 32, half:] = right[rows, :]


def meta_kernel(place_ref, history_ref, cands_ref, loss_ref, meta_ref):
    owner = 2 * place_ref[0] + place_ref[1]

    def digits(values, wanted):
        row = lax.broadcasted_iota(jnp.int32, (16, values.shape[1]), 0)
        upper, lower = values // 128, jnp.bitwise_and(values, 127)
        both = jnp.where(row == 0, upper, jnp.where(row == 2, lower, 0)).astype(F32).astype(BF)
        source = lax.broadcasted_iota(jnp.int32, (values.shape[1], 128), 0)
        hot = (source == wanted).astype(F32).astype(BF)
        return jnp.dot(both, hot, preferred_element_type=F32)

    lane = lax.broadcasted_iota(jnp.int32, (16, 128), 1)
    row = lax.broadcasted_iota(jnp.int32, (16, 128), 0)
    events = digits(history_ref[...], event_slots(owner, (1, 128), 1))
    wanted = cand_slots(owner, (1, 128), 1)
    wanted = jnp.where(lax.broadcasted_iota(jnp.int32, (1, 128), 1) < 64, wanted, -1)
    cands = pltpu.roll(digits(cands_ref[...], wanted), 1, 0)
    meta = events + cands + loss_ref[...].astype(F32)
    for where, value in ((64, place_ref[2]), (65, place_ref[3])):
        for r, part in ((1, value // 128), (3, jnp.bitwise_and(value, 127))):
            part = jnp.full((16, 128), part, jnp.int32).astype(F32)
            meta = jnp.where((lane == where) & (row == r), part, meta)
    meta_ref[...] = meta.astype(BF)


def pack_kernel(a_ref, b_ref, c_ref, d_ref, rows_ref, dhidden_ref, meta_ref, out_ref):
    refs = (a_ref, b_ref, c_ref, d_ref)
    block = rows_ref.shape[0]
    dnormed = sum(ref[:block, :].astype(F32) for ref in refs)
    rows = rows_ref[...].astype(F32)
    scale = lax.rsqrt(jnp.mean(rows * rows, axis=-1, keepdims=True) + 1e-06)
    normed = rows * scale
    drows = dhidden_ref[...].astype(F32) + scale * (
        dnormed - normed * jnp.mean(dnormed * normed, axis=-1, keepdims=True)
    )
    drows = drows.astype(BF)
    dcand = sum(ref[block:, :].astype(F32) for ref in refs).astype(BF)
    meta = meta_ref[...]
    for d in range(out_ref.shape[0]):
        out_ref[d, 0:32, :] = jnp.concatenate(
            [drows[32 * g : 32 * g + 32, 32 * d : 32 * d + 32] for g in range(4)], axis=1
        )
        out_ref[d, 32:48, :] = jnp.concatenate(
            [dcand[16 * g : 16 * g + 16, 32 * d : 32 * d + 32] for g in range(4)], axis=1
        )
        out_ref[d, 48:64, :] = meta


def scatter_kernel(ids_ref, place_ref, data_ref, own_ref, other_ref, rows_ref, acc_ref, more_ref):
    users = data_ref.shape[0]
    total = acc_ref.shape[0]
    chunk = 512
    owner = 2 * place_ref[0] + place_ref[1]

    def clear(i, carry):
        here = pl.ds(pl.multiple_of(i * chunk, chunk), chunk)
        acc_ref[here, :] = jnp.zeros((chunk, 128), F32)
        more_ref[here, :] = jnp.zeros((chunk, 128), F32)
        return carry

    lax.fori_loop(0, total // chunk, clear, 0)
    for u in range(users):
        rows_ref[48 * u : 48 * u + 48, :] = data_ref[u, 0:48, :].astype(F32)
    lane = lax.broadcasted_iota(jnp.int32, (1, 128), 1) // 32
    masks = [lane == g for g in range(4)]

    def add(first_id, pitch, first_row, count):
        def step(i, carry):
            for j in range(2):
                work = []
                for half, ref in ((0, acc_ref), (1, more_ref)):
                    p = i * 4 + j * 2 + half
                    row = rows_ref[pl.ds(first_row + p, 1), :]
                    ids = [ids_ref[first_id + g * pitch + p] for g in range(4)]
                    work.append((ref, row, ids, [ref[pl.ds(ids[g], 1), :] for g in range(4)]))
                for ref, row, ids, held in work:
                    for g in range(4):
                        pltpu.store(ref.at[pl.ds(ids[g], 1), :], held[g] + row, mask=masks[g])
            return carry

        lax.fori_loop(0, (count + 3) // 4, step, 0)

    def user(u, carry):
        base = u * 256
        events = jnp.clip((ids_ref[base + 192] - owner + 31) // 32, 0, 32)
        cands = jnp.clip((ids_ref[base + 193] - owner + 31) // 32, 0, 16)
        add(base, 32, u * 48, events)
        add(base + 128, 16, u * 48 + 32, cands)
        return carry

    lax.fori_loop(0, users, user, 0)
    wide = lax.broadcasted_iota(jnp.int32, (512, 128), 1) // 32
    for cc in range(2):
        for k in range(4):
            item = item_of(place_ref, cc * NX + k)
            result = jnp.zeros((512, 128), F32)
            for q in range(4):
                here = pl.ds(pl.multiple_of(item * 2048 + q * 512, 512), 512)
                part = acc_ref[here, :] + more_ref[here, :]
                part = part + pltpu.roll(part, 64, 1)
                part = part + pltpu.roll(part, 32, 1)
                result = jnp.where(wide == q, part, result)
            (own_ref, other_ref)[cc][k] = result.astype(BF)


def turn_kernel(place_ref, grads_ref, *outs):
    for k, out in enumerate(outs):
        start = jnp.bitwise_xor(place_ref[4], k) * 32
        out[...] = grads_ref[pl.ds(pl.multiple_of(start, 32), 32), :]


def split_kernel(g0, g1, g2, g3, in_ref, *outs):
    total = sum(ref[...].astype(F32) for ref in (g0, g1, g2, g3))
    in_ref[...] = total[:, NX * HD :]
    for k, out in enumerate(outs):
        out[...] = total[:, HD * k : HD * k + HD].astype(BF)


def unpack_kernel(a_ref, b_ref, c_ref, d_ref, p0, p1, p2, p3, out_ref, proj_ref):
    proj_ref[...] = sum(ref[...].astype(F32) for ref in (p0, p1, p2, p3))
    turned = sum(ref[...].astype(F32) for ref in (a_ref, b_ref, c_ref, d_ref)).T
    for q in range(4):
        out_ref[:, q * 512 : (q + 1) * 512] = turned[32 * q : 32 * q + 32, :]


def whole(count, smem=0):
    specs = [pl.BlockSpec(memory_space=pltpu.SMEM)] * smem
    return specs + [pl.BlockSpec(memory_space=pltpu.VMEM)] * count


def call(kernel, name, outs, *args, smem=0, scratch=(), limit=32, far=(), far_outs=(), cost=1.0):
    outs = tuple(jax.ShapeDtypeStruct(shape, dtype) for shape, dtype in outs)
    hbm = pl.BlockSpec(memory_space=pltpu.HBM)
    specs = [hbm if i in far_outs else whole(1)[0] for i in range(len(outs))]
    in_specs = [hbm if i in far else spec for i, spec in enumerate(whole(len(args) - smem, smem))]
    return pl.pallas_call(
        kernel,
        out_shape=outs if len(outs) > 1 else outs[0],
        in_specs=in_specs,
        out_specs=tuple(specs) if len(outs) > 1 else specs[0],
        scratch_shapes=list(scratch),
        compiler_params=pltpu.CompilerParams(vmem_limit_bytes=int(limit * 1024 * 1024)),
        cost_estimate=pl.CostEstimate(
            flops=int(cost * 1.1e9), bytes_accessed=int(cost * 3.6e6), transcendentals=0
        ),
        name=name,
    )(*args)


def on_device(table, w_uvqk, w_out, history, lengths, candidates, counts, actions, targets):
    rows_total, width = table.shape
    seq = history.shape[1]
    ncand = candidates.shape[1]
    users = NY * NZ
    parts = NX * NC
    block = seq // parts
    cblock = ncand // parts
    x, c = lax.axis_index("x"), lax.axis_index("c")
    length = lengths[0]

    place = jnp.stack([x, c, length, counts[0], lax.axis_index("y")]).astype(jnp.int32)

    def along_x(own):
        return [own] + [swap_x(own, k) for k in range(1, NX)]

    size = block + cblock

    def pick(half):
        return call(
            functools.partial(pick_kernel, half),
            "pick",
            [((NX, size, width), BF)],
            place,
            history,
            candidates,
            table,
            smem=1,
            scratch=[pltpu.VMEM((NX * size, rows_total), BF)],
            limit=20,
            cost=5.0 if half else 0.05,
        )

    picked_other = swap_core(pick(1))
    weights_out = lax.all_gather(w_out, ("x", "c"), axis=0, tiled=False)
    picked_own = pick(0)
    line = list(call(pair_kernel, "pair", [((size, width), BF)] * NX, picked_other, picked_own, limit=8))
    line = [line[0]] + [swap_x(line[k], k) for k in range(1, NX)]
    w_uvqk, line[0] = lax.optimization_barrier((w_uvqk, line[0]))
    local_w = w_uvqk.reshape(width, -1)
    normed, crow = call(
        norm_kernel,
        "norm",
        [((block, width), BF), ((cblock, width), BF)],
        *line,
        limit=50,
    )
    own_other = swap_core(normed)
    far_w = swap_core(local_w)
    line[0], normed = lax.optimization_barrier((line[0], normed))
    rows = call(rows_kernel, "rows", [((block, width), BF)], *line, limit=50, cost=0.5)
    *normed_line, local_w, far_w, rows = lax.optimization_barrier(
        (*along_x(normed), crow, local_w, far_w, rows)
    )
    spread_rows = normed_line[:NX] + [own_other] + [swap_core(part) for part in normed_line[1:NX]]
    crows = lax.all_gather(normed_line[NX], ("x", "c"), axis=0, tiled=True)
    normed, pre, act, sent = call(
        attend_kernel,
        "attend",
        [((seq, width), BF), ((seq, 4 * HD), F32), ((seq, 4 * HD), BF), ((parts, block, 3 * HD), BF)],
        place,
        *spread_rows,
        local_w,
        smem=1,
        limit=52,
        far_outs=(0, 1, 2),
        scratch=[
            pltpu.VMEM((seq, width), BF),
            pltpu.VMEM((seq, 4 * HD), F32),
            pltpu.VMEM((seq, 4 * HD), BF),
            pltpu.SemaphoreType.DMA((3,)),
        ],
        cost=4.0,
    )
    sent = lax.all_to_all(sent, ("x", "c"), 0, 0)

    half = NX * HD
    back, dhidden, cand_own, cand_other, out_own, out_other = call(
        event_kernel,
        "event",
        [
            ((parts, block + 16, 2 * HD), BF),
            ((block, width), BF),
            ((NX, cblock, width), BF),
            ((NX, cblock, width), BF),
            ((width, half), BF),
            ((width, half), BF),
        ],
        place,
        sent,
        rows,
        weights_out,
        crows,
        actions,
        targets,
        smem=1,
        limit=60,
        far=(3, 4),
        scratch=[
            pltpu.VMEM((ncand, width), BF),
            pltpu.VMEM((width, width), BF),
            pltpu.VMEM((ncand, width), BF),
            pltpu.SemaphoreType.DMA((parts + 1,)),
        ],
        cost=4.0,
    )
    back = lax.all_to_all(back, ("x", "c"), 0, 0)
    out_other = swap_core(out_other)

    back, cand_other = lax.optimization_barrier((back, swap_core(cand_other)))
    near, far, loss_meta = call(
        backward_kernel,
        "backward",
        [((seq // 2, 4 * HD), BF), ((seq // 2, 4 * HD), BF), ((16, 128), BF)],
        place,
        back,
        act,
        pre,
        smem=1,
        scratch=[
            pltpu.VMEM((seq, HD), BF),
            pltpu.VMEM((seq, HD), BF),
            pltpu.VMEM((seq, HD), F32),
            pltpu.VMEM((seq, 4 * HD), BF),
            pltpu.VMEM((seq, 4 * HD), BF),
            pltpu.VMEM((seq, 4 * HD), F32),
            pltpu.SemaphoreType.DMA((2,)),
        ],
        limit=60,
        far=(2, 3),
        cost=6.0,
    )
    far_got = swap_core(far)
    line = list(
        call(
            part_kernel,
            "part",
            [((size, width), BF)] * NX,
            near,
            far_got,
            local_w,
            far_w,
            cand_own,
            cand_other,
            limit=50,
            cost=2.0,
        )
    )
    near, line[0] = lax.optimization_barrier((near, line[0]))
    grads = call(
        weight_kernel,
        "weight",
        [((NZ, width // NZ, half + 4 * HD), BF)],
        near,
        far,
        normed,
        out_own,
        out_other,
        limit=60,
        cost=2.5,
    )
    grads = lax.psum_scatter(grads, "z", scatter_dimension=0, tiled=False)
    loss_meta, line[0] = lax.optimization_barrier((loss_meta, line[0]))
    meta = call(
        meta_kernel, "meta", [((16, 128), BF)], place, history, candidates, loss_meta, smem=1, limit=40
    )
    line = [line[0]] + [swap_x(line[k], k) for k in range(1, NX)]

    packed = call(
        pack_kernel,
        "pack",
        [((users, 64, 128), BF)],
        *line,
        rows,
        dhidden,
        meta,
        limit=50,
    )
    arrived = lax.all_to_all(packed, ("y", "z"), 0, 0)
    _, grads = lax.optimization_barrier((arrived, grads))
    grads = call(
        turn_kernel, "turn", [((32, half + 4 * HD), BF)] * NY, place, grads, smem=1, limit=8, cost=0.5
    )
    grads = [grads[0]] + [
        lax.ppermute(grads[k], "y", [(i, i ^ k) for i in range(NY)]) for k in range(1, NY)
    ]
    got = arrived[:, 48:53].astype(F32)
    all_ids = (got[:, 0:2] * 128.0 + got[:, 2:4]).astype(jnp.int32).reshape(-1)
    own, other = call(
        scatter_kernel,
        "scatter",
        [((NX, 512, 128), BF)] * 2,
        all_ids,
        place,
        arrived,
        smem=2,
        scratch=[
            pltpu.VMEM((users * 48, 128), F32),
            pltpu.VMEM((parts * rows_total, 128), F32),
            pltpu.VMEM((parts * rows_total, 128), F32),
        ],
        limit=24,
        cost=12.0,
    )
    line = call(pair_kernel, "final_pair", [((512, 128), BF)] * NX, swap_core(other), own, limit=8, cost=0.5)
    line = [line[0]] + [swap_x(line[k], k) for k in range(1, NX)]
    grad_in, *proj = call(
        split_kernel, "split", [((32, 4 * HD), F32)] + [((32, HD), BF)] * NX, *grads, limit=8, cost=0.5
    )
    proj = [proj[0]] + [swap_x(proj[k], k) for k in range(1, NX)]
    shard_t, proj_t = call(
        unpack_kernel,
        "unpack",
        [((32, rows_total), F32), ((32, HD), F32)],
        *line,
        *proj,
        limit=8,
    )
    grad_in = grad_in.reshape(-1, 4, HD)
    loss = jnp.sum(got[:, 4, 0:3])
    return (loss, grad_in, proj_t.T, shard_t.T)


def solution(mesh):
    fine = Mesh(mesh.devices.reshape(NY, NZ, NX, NC), ("y", "z", "x", "c"))
    dp, item = ("y", "z"), ("x", "c")
    placed = (
        P(item, None),
        P(None, None, item),
        P(item, None),
        P(dp, None),
        P(dp),
        P(dp, None),
        P(dp),
        P(dp, None),
        P(dp, None),
    )
    return jax.shard_map(
        on_device,
        mesh=fine,
        in_specs=placed,
        out_specs=(P(), P(dp, None, item), P(item, dp), P(item, dp)),
        check_vma=False,
    )
```

```python
import functools

import jax
import jax.numpy as jnp
from jax import lax
from jax.experimental import pallas as pl
from jax.experimental.pallas import tpu as pltpu
from jax.sharding import Mesh, PartitionSpec as P

HD = 128
NX, NC, NY, NZ = 4, 2, 4, 8
CQL_WEIGHT = 0.5
BF = jnp.bfloat16
F32 = jnp.float32


def swap_x(value, k):
    return lax.ppermute(value, "x", [(i, i ^ k) for i in range(NX)])


def swap_core(value):
    return lax.ppermute(value, "c", [(0, 1), (1, 0)])


def event_slots(item, shape, axis):
    row = lax.broadcasted_iota(jnp.int32, shape, axis)
    return 32 * jnp.bitwise_and(row, 31) + 8 * (row // 32) + item


def cand_slots(item, shape, axis):
    row = lax.broadcasted_iota(jnp.int32, shape, axis)
    return 32 * jnp.bitwise_and(row, 15) + 8 * (row // 16) + item


def chosen(values, slots):
    cols = lax.broadcasted_iota(jnp.int32, (1, values.shape[1]), 1)
    return jnp.sum(jnp.where(cols == slots, values.astype(F32), 0.0), axis=1, keepdims=True)


def pick_kernel(half, place_ref, history_ref, cand_ref, table_ref, out_ref, hot_ref):
    total = table_ref.shape[0]
    first_row = (2 * place_ref[0] + place_ref[1]) * total
    size = out_ref.shape[1]
    for k in range(NX):
        item = item_of(place_ref, half * NX + k)
        events = chosen(history_ref[...], event_slots(item, (128, 1), 0))
        cands = chosen(cand_ref[...], cand_slots(item, (size - 128, 1), 0))
        for first, ids in ((0, events), (128, cands)):
            local = ids.astype(jnp.int32) - first_row
            count = ids.shape[0]
            for i in range(0, total, 512):
                cols = lax.broadcasted_iota(jnp.int32, (1, 512), 1) + i
                hot_ref[size * k + first : size * k + first + count, i : i + 512] = (
                    (local == cols).astype(F32).astype(BF)
                )
    for i in range(0, out_ref.shape[2], 256):
        found = jnp.dot(hot_ref[...], table_ref[:, i : i + 256], preferred_element_type=F32).astype(BF)
        for k in range(NX):
            out_ref[k, :, i : i + 256] = found[size * k : size * k + size, :]


def pair_kernel(a_ref, b_ref, *outs):
    for k, out in enumerate(outs):
        out[...] = (a_ref[k].astype(F32) + b_ref[k].astype(F32)).astype(BF)


def norm_kernel(a_ref, b_ref, c_ref, d_ref, normed_ref, crow_ref):
    refs = (a_ref, b_ref, c_ref, d_ref)
    block = normed_ref.shape[0]
    rows = sum(ref[:block, :].astype(F32) for ref in refs)
    scale = lax.rsqrt(jnp.mean(rows * rows, axis=-1, keepdims=True) + 1e-06)
    normed_ref[...] = (rows * scale).astype(BF)
    crow_ref[...] = sum(ref[block:, :].astype(F32) for ref in refs).astype(BF)


def rows_kernel(a_ref, b_ref, c_ref, d_ref, rows_ref):
    block = rows_ref.shape[0]
    rows_ref[...] = sum(ref[:block, :].astype(F32) for ref in (a_ref, b_ref, c_ref, d_ref)).astype(BF)


def item_of(place_ref, b):
    return 2 * jnp.bitwise_xor(place_ref[0], b % NX) + jnp.bitwise_xor(place_ref[1], b // NX)


def places_of(place_ref, shape, axis, first=0):
    row = lax.broadcasted_iota(jnp.int32, shape, axis) + first
    line = jnp.bitwise_and(row, 511)
    item = 2 * jnp.bitwise_xor(place_ref[0], line // 128) + jnp.bitwise_xor(place_ref[1], row // 512)
    inside = jnp.bitwise_and(row, 127)
    return 32 * jnp.bitwise_and(inside, 31) + 8 * (inside // 32) + item


def attend_kernel(
    place_ref, b0, b1, b2, b3, b4, b5, b6, b7, w_ref,
    normed_out, pre_out, act_out, sent_ref, normed_ref, pre_ref, act_ref, sems,
):
    for b, ref in enumerate((b0, b1, b2, b3, b4, b5, b6, b7)):
        normed_ref[128 * b : 128 * b + 128, :] = ref[...]
    copies = [pltpu.make_async_copy(normed_ref, normed_out, sems.at[0])]
    copies[0].start()
    seq = normed_ref.shape[0]
    for i in range(0, seq, 256):
        pre = jnp.dot(normed_ref[i : i + 256, :], w_ref[...], preferred_element_type=F32)
        pre_ref[i : i + 256, :] = pre
        act_ref[i : i + 256, :] = (pre * jax.nn.sigmoid(pre)).astype(BF)
    for i, (source, target) in enumerate(((pre_ref, pre_out), (act_ref, act_out))):
        copies.append(pltpu.make_async_copy(source, target, sems.at[i + 1]))
        copies[-1].start()
    length = place_ref[2]
    inverse = 1.0 / jnp.full((1, 1), length, jnp.int32).astype(F32)
    cols = places_of(place_ref, (1, seq), 1)
    cols = jnp.where(cols < length, cols, seq)
    for i in range(0, seq, 256):
        queries = act_ref[i : i + 256, 2 * HD : 3 * HD]
        logits = lax.dot_general(
            queries, act_ref[:, 3 * HD :], (((1,), (1,)), ((), ())), preferred_element_type=F32
        ) * HD ** (-0.5)
        rows = places_of(place_ref, (256, 1), 0, i)
        attn = jnp.where(cols <= rows, logits * jax.nn.sigmoid(logits) * inverse, 0.0).astype(BF)
        mixed = jnp.dot(attn, act_ref[:, HD : 2 * HD], preferred_element_type=F32)
        top = mixed.astype(BF)
        rest = (mixed - top.astype(F32)).astype(BF)
        for h in range(2):
            b = i // 128 + h
            item = item_of(place_ref, b)
            sent_ref[item, :, 0:HD] = top[128 * h : 128 * h + 128, :]
            sent_ref[item, :, HD : 2 * HD] = rest[128 * h : 128 * h + 128, :]
            sent_ref[item, :, 2 * HD :] = act_ref[128 * b : 128 * b + 128, 0:HD]
    for copy in copies:
        copy.wait()


def split_loss(value, shape, row):
    value = jnp.broadcast_to(value, shape)
    top = value.astype(BF).astype(F32)
    middle = (value - top).astype(BF).astype(F32)
    low = value - top - middle
    lane = lax.broadcasted_iota(jnp.int32, shape, 1)
    picked = jnp.where(lane == 0, top, jnp.where(lane == 1, middle, jnp.where(lane == 2, low, 0.0)))
    return jnp.where(lax.broadcasted_iota(jnp.int32, shape, 0) == row, picked, 0.0).astype(BF)


def event_kernel(
    place_ref, sent_ref, rows_ref, w_ref, crows_ref, action_ref, target_ref,
    back_ref, dhidden_ref, cand_own_ref, cand_other_ref, out_own_ref, out_other_ref,
    dcand_ref, weight_ref, crow_ref, sems,
):
    copies = [
        pltpu.make_async_copy(
            w_ref.at[item_of(place_ref, b)], weight_ref.at[HD * b : HD * b + HD, :], sems.at[b]
        )
        for b in range(NX * NC)
    ]
    copies.append(pltpu.make_async_copy(crows_ref, crow_ref, sems.at[NX * NC]))
    for copy in copies:
        copy.start()
    owner = 2 * place_ref[0] + place_ref[1]
    length, count = place_ref[2], place_ref[3]
    block, width = rows_ref.shape
    seq = block * NX * NC
    items = [item_of(place_ref, b) for b in range(NX * NC)]
    mixed = jnp.concatenate(
        [sent_ref[i, :, 0:HD].astype(F32) + sent_ref[i, :, HD : 2 * HD].astype(F32) for i in items], axis=1
    )
    gate = jnp.concatenate([sent_ref[i, :, 2 * HD :] for i in items], axis=1).astype(F32)
    center = jnp.mean(mixed, axis=-1, keepdims=True)
    rstd = lax.rsqrt(jnp.mean(mixed * mixed, axis=-1, keepdims=True) - center * center + 1e-05)
    normo = (mixed - center) * rstd
    gated = (normo * gate).astype(BF)
    for copy in copies:
        copy.wait()
    weights = weight_ref[...]
    out = rows_ref[...].astype(F32) + jnp.dot(gated, weights, preferred_element_type=F32)
    hidden = out.astype(BF)
    crows = crow_ref[...]
    scores = lax.dot_general(hidden, crows, (((1,), (1,)), ((), ())), preferred_element_type=F32)
    col = lax.broadcasted_iota(jnp.int32, (1, crows.shape[0]), 1)
    inside = jnp.bitwise_and(col, 63)
    slots = 32 * jnp.bitwise_and(inside, 15) + 8 * (inside // 16) + col // 64
    masked = jnp.where(slots < count, scores, -jnp.inf)
    top = jnp.max(masked, axis=-1, keepdims=True)
    expo = jnp.exp(masked - top)
    total = jnp.sum(expo, axis=-1, keepdims=True)
    soft = expo / total
    lse = top + jnp.log(total)
    places = event_slots(owner, (block, 1), 0)
    actions = chosen(action_ref[...], places).astype(jnp.int32)
    onehot = (slots == actions).astype(F32)
    taken = jnp.sum(scores * onehot, axis=-1, keepdims=True)
    live = jnp.where(places < length, 1.0 / seq, 0.0)
    miss = taken - chosen(target_ref[...], places)
    loss = jnp.sum(live * (CQL_WEIGHT * (lse - taken) + 0.5 * miss * miss), axis=0, keepdims=True)
    loss = split_loss(loss, (16, 2 * HD), 0)
    dscore = (live * (CQL_WEIGHT * soft + (miss - CQL_WEIGHT) * onehot)).astype(BF)
    dhidden = jnp.dot(dscore, crows, preferred_element_type=F32).astype(BF)
    dhidden_ref[...] = dhidden
    dgated = lax.dot_general(
        dhidden, weights, (((1,), (1,)), ((), ())), preferred_element_type=F32
    )
    dnormo = dgated * gate
    first = jnp.mean(dnormo, axis=-1, keepdims=True)
    second = jnp.mean(dnormo * normo, axis=-1, keepdims=True)
    dmixed = (rstd * (dnormo - first - normo * second)).astype(BF)
    du = (dgated * normo).astype(BF)
    for b, i in enumerate(items):
        back_ref[i, 0:block, 0:HD] = dmixed[:, HD * b : HD * b + HD]
        back_ref[i, 0:block, HD:] = du[:, HD * b : HD * b + HD]
        back_ref[i, block:, :] = loss
    turned = (((0,), (0,)), ((), ()))
    half = NX * HD
    out_other_ref[...] = lax.dot_general(
        dhidden, gated[:, half:], turned, preferred_element_type=F32
    ).astype(BF)
    out_own_ref[...] = lax.dot_general(
        dhidden, gated[:, :half], turned, preferred_element_type=F32
    ).astype(BF)
    dcand_ref[...] = lax.dot_general(dscore, hidden, turned, preferred_element_type=F32).astype(BF)
    size = cand_own_ref.shape[1]
    for k in range(NX):
        cand_own_ref[k] = dcand_ref[pl.ds(pl.multiple_of(items[k] * size, size), size), :]
        cand_other_ref[k] = dcand_ref[pl.ds(pl.multiple_of(items[NX + k] * size, size), size), :]


def backward_kernel(
    place_ref, back_ref, act_in, pre_in, normed_in, out_own_in, out_other_in,
    near_ref, far_ref, loss_ref, grads_ref,
    dm_ref, du_ref, dq_ref, dpre_ref, act_ref, pre_ref, normed_ref, own_ref, other_ref, sems,
):
    copies = [
        pltpu.make_async_copy(source, target, sems.at[i])
        for i, (source, target) in enumerate(
            (
                (act_in, act_ref),
                (pre_in, pre_ref),
                (normed_in, normed_ref),
                (out_own_in, own_ref),
                (out_other_in, other_ref),
            )
        )
    ]
    for copy in copies:
        copy.start()
    seq = act_ref.shape[0]
    loss = jnp.zeros((16, 2 * HD), F32)
    for b in range(8):
        item = item_of(place_ref, b)
        dm_ref[128 * b : 128 * b + 128, :] = back_ref[item, 0:128, 0:HD]
        du_ref[128 * b : 128 * b + 128, :] = back_ref[item, 0:128, HD:]
        loss = loss + back_ref[item, 128:144, :].astype(F32)
    loss = jnp.sum(jnp.sum(loss, axis=1, keepdims=True), axis=0, keepdims=True)
    loss_ref[...] = split_loss(loss, (16, 128), 4)
    length = place_ref[2]
    inverse = 1.0 / jnp.full((1, 1), length, jnp.int32).astype(F32)
    cols = places_of(place_ref, (1, seq), 1)
    across = (((1,), (1,)), ((), ()))
    dq_ref[...] = jnp.zeros(dq_ref.shape, F32)

    def slope(value, sigma):
        return sigma * (1.0 + value * (1.0 - sigma))

    copies[0].wait()
    for i in range(0, seq, 256):
        keys = act_ref[i : i + 256, 3 * HD :]
        logits = lax.dot_general(
            keys, act_ref[:, 2 * HD : 3 * HD], across, preferred_element_type=F32
        ) * HD ** (-0.5)
        rows = places_of(place_ref, (256, 1), 0, i)
        rows = jnp.where(rows < length, rows, seq)
        allowed = rows <= cols
        sigma = jax.nn.sigmoid(logits)
        attn = jnp.where(allowed, logits * sigma * inverse, 0.0).astype(BF)
        dattn = lax.dot_general(
            act_ref[i : i + 256, HD : 2 * HD], dm_ref[...], across, preferred_element_type=F32
        )
        dlogits = jnp.where(
            allowed, dattn * inverse * slope(logits, sigma) * HD ** (-0.5), 0.0
        ).astype(BF)
        dvalues = jnp.dot(attn, dm_ref[...], preferred_element_type=F32)
        dkeys = jnp.dot(dlogits, act_ref[:, 2 * HD : 3 * HD], preferred_element_type=F32)
        dq_ref[...] += lax.dot_general(
            dlogits, keys, (((0,), (0,)), ((), ())), preferred_element_type=F32
        )
        if i == 0:
            copies[1].wait()
        for j, grad in ((1, dvalues), (3, dkeys)):
            pre = pre_ref[i : i + 256, HD * j : HD * j + HD]
            dpre_ref[i : i + 256, HD * j : HD * j + HD] = (
                grad * slope(pre, jax.nn.sigmoid(pre))
            ).astype(BF)
    for j, ref in ((0, du_ref), (2, dq_ref)):
        pre = pre_ref[:, HD * j : HD * j + HD]
        dpre_ref[:, HD * j : HD * j + HD] = (
            ref[...].astype(F32) * slope(pre, jax.nn.sigmoid(pre))
        ).astype(BF)
    near_ref[...] = dpre_ref[: near_ref.shape[0], :]
    far_ref[...] = dpre_ref[near_ref.shape[0] :, :]
    for copy in copies[2:]:
        copy.wait()
    half = own_ref.shape[1]
    left = (own_ref[...].astype(F32) + other_ref[...].astype(F32)).astype(BF)
    right = lax.dot_general(
        normed_ref[...], dpre_ref[...], (((0,), (0,)), ((), ())), preferred_element_type=F32
    ).astype(BF)
    for y in range(NY):
        for z in range(NZ):
            rows = slice(32 * (NZ * y + z), 32 * (NZ * y + z) + 32)
            grads_ref[z, 32 * y : 32 * y + 32, :half] = left[rows, :]
            grads_ref[z, 32 * y : 32 * y + 32, half:] = right[rows, :]


def part_kernel(near_ref, far_ref, w_ref, far_w_ref, cand_ref, far_cand_ref, *outs):
    across = (((1,), (1,)), ((), ()))
    for h in range(2):
        rows = slice(256 * h, 256 * h + 256)
        part = lax.dot_general(near_ref[rows, :], w_ref[...], across, preferred_element_type=F32)
        part = part + lax.dot_general(
            far_ref[rows, :], far_w_ref[...], across, preferred_element_type=F32
        )
        part = part.astype(BF)
        outs[2 * h][0:128, :] = part[:128, :]
        outs[2 * h + 1][0:128, :] = part[128:, :]
    for k in range(NX):
        outs[k][128:, :] = (cand_ref[k].astype(F32) + far_cand_ref[k].astype(F32)).astype(BF)


def meta_kernel(place_ref, history_ref, cands_ref, loss_ref, meta_ref):
    owner = 2 * place_ref[0] + place_ref[1]

    def digits(values, wanted):
        row = lax.broadcasted_iota(jnp.int32, (16, values.shape[1]), 0)
        upper, lower = values // 128, jnp.bitwise_and(values, 127)
        both = jnp.where(row == 0, upper, jnp.where(row == 2, lower, 0)).astype(F32).astype(BF)
        source = lax.broadcasted_iota(jnp.int32, (values.shape[1], 128), 0)
        hot = (source == wanted).astype(F32).astype(BF)
        return jnp.dot(both, hot, preferred_element_type=F32)

    lane = lax.broadcasted_iota(jnp.int32, (16, 128), 1)
    row = lax.broadcasted_iota(jnp.int32, (16, 128), 0)
    events = digits(history_ref[...], event_slots(owner, (1, 128), 1))
    wanted = cand_slots(owner, (1, 128), 1)
    wanted = jnp.where(lax.broadcasted_iota(jnp.int32, (1, 128), 1) < 64, wanted, -1)
    cands = pltpu.roll(digits(cands_ref[...], wanted), 1, 0)
    meta = events + cands + loss_ref[...].astype(F32)
    for where, value in ((64, place_ref[2]), (65, place_ref[3])):
        for r, part in ((1, value // 128), (3, jnp.bitwise_and(value, 127))):
            part = jnp.full((16, 128), part, jnp.int32).astype(F32)
            meta = jnp.where((lane == where) & (row == r), part, meta)
    meta_ref[...] = meta.astype(BF)


def pack_kernel(a_ref, b_ref, c_ref, d_ref, rows_ref, dhidden_ref, meta_ref, out_ref):
    refs = (a_ref, b_ref, c_ref, d_ref)
    block = rows_ref.shape[0]
    dnormed = sum(ref[:block, :].astype(F32) for ref in refs)
    rows = rows_ref[...].astype(F32)
    scale = lax.rsqrt(jnp.mean(rows * rows, axis=-1, keepdims=True) + 1e-06)
    normed = rows * scale
    drows = dhidden_ref[...].astype(F32) + scale * (
        dnormed - normed * jnp.mean(dnormed * normed, axis=-1, keepdims=True)
    )
    drows = drows.astype(BF)
    dcand = sum(ref[block:, :].astype(F32) for ref in refs).astype(BF)
    meta = meta_ref[...]
    for d in range(out_ref.shape[0]):
        out_ref[d, 0:32, :] = jnp.concatenate(
            [drows[32 * g : 32 * g + 32, 32 * d : 32 * d + 32] for g in range(4)], axis=1
        )
        out_ref[d, 32:48, :] = jnp.concatenate(
            [dcand[16 * g : 16 * g + 16, 32 * d : 32 * d + 32] for g in range(4)], axis=1
        )
        out_ref[d, 48:64, :] = meta


def scatter_kernel(ids_ref, place_ref, data_ref, own_ref, other_ref, rows_ref, acc_ref, more_ref):
    users = data_ref.shape[0]
    total = acc_ref.shape[0]
    chunk = 512
    owner = 2 * place_ref[0] + place_ref[1]

    def clear(i, carry):
        here = pl.ds(pl.multiple_of(i * chunk, chunk), chunk)
        acc_ref[here, :] = jnp.zeros((chunk, 128), F32)
        more_ref[here, :] = jnp.zeros((chunk, 128), F32)
        return carry

    lax.fori_loop(0, total // chunk, clear, 0)
    for u in range(users):
        rows_ref[48 * u : 48 * u + 48, :] = data_ref[u, 0:48, :].astype(F32)
    lane = lax.broadcasted_iota(jnp.int32, (1, 128), 1) // 32
    masks = [lane == g for g in range(4)]

    def add(first_id, pitch, first_row, count):
        def step(i, carry):
            for j in range(2):
                work = []
                for half, ref in ((0, acc_ref), (1, more_ref)):
                    p = i * 4 + j * 2 + half
                    row = rows_ref[pl.ds(first_row + p, 1), :]
                    ids = [ids_ref[first_id + g * pitch + p] for g in range(4)]
                    work.append((ref, row, ids, [ref[pl.ds(ids[g], 1), :] for g in range(4)]))
                for ref, row, ids, held in work:
                    for g in range(4):
                        pltpu.store(ref.at[pl.ds(ids[g], 1), :], held[g] + row, mask=masks[g])
            return carry

        lax.fori_loop(0, (count + 3) // 4, step, 0)

    def user(u, carry):
        base = u * 256
        events = jnp.clip((ids_ref[base + 192] - owner + 31) // 32, 0, 32)
        cands = jnp.clip((ids_ref[base + 193] - owner + 31) // 32, 0, 16)
        add(base, 32, u * 48, events)
        add(base + 128, 16, u * 48 + 32, cands)
        return carry

    lax.fori_loop(0, users, user, 0)
    wide = lax.broadcasted_iota(jnp.int32, (512, 128), 1) // 32
    for cc in range(2):
        for k in range(4):
            item = item_of(place_ref, cc * NX + k)
            result = jnp.zeros((512, 128), F32)
            for q in range(4):
                here = pl.ds(pl.multiple_of(item * 2048 + q * 512, 512), 512)
                part = acc_ref[here, :] + more_ref[here, :]
                part = part + pltpu.roll(part, 64, 1)
                part = part + pltpu.roll(part, 32, 1)
                result = jnp.where(wide == q, part, result)
            (own_ref, other_ref)[cc][k] = result.astype(BF)


def turn_kernel(place_ref, grads_ref, *outs):
    for k, out in enumerate(outs):
        start = jnp.bitwise_xor(place_ref[4], k) * 32
        out[...] = grads_ref[pl.ds(pl.multiple_of(start, 32), 32), :]


def split_kernel(g0, g1, g2, g3, in_ref, *outs):
    total = sum(ref[...].astype(F32) for ref in (g0, g1, g2, g3))
    in_ref[...] = total[:, NX * HD :]
    for k, out in enumerate(outs):
        out[...] = total[:, HD * k : HD * k + HD].astype(BF)


def unpack_kernel(a_ref, b_ref, c_ref, d_ref, p0, p1, p2, p3, out_ref, proj_ref):
    proj_ref[...] = sum(ref[...].astype(F32) for ref in (p0, p1, p2, p3))
    turned = sum(ref[...].astype(F32) for ref in (a_ref, b_ref, c_ref, d_ref)).T
    for q in range(4):
        out_ref[:, q * 512 : (q + 1) * 512] = turned[32 * q : 32 * q + 32, :]


def whole(count, smem=0):
    specs = [pl.BlockSpec(memory_space=pltpu.SMEM)] * smem
    return specs + [pl.BlockSpec(memory_space=pltpu.VMEM)] * count


def call(kernel, name, outs, *args, smem=0, scratch=(), limit=32, far=(), far_outs=(), cost=1.0):
    outs = tuple(jax.ShapeDtypeStruct(shape, dtype) for shape, dtype in outs)
    hbm = pl.BlockSpec(memory_space=pltpu.HBM)
    specs = [hbm if i in far_outs else whole(1)[0] for i in range(len(outs))]
    in_specs = [hbm if i in far else spec for i, spec in enumerate(whole(len(args) - smem, smem))]
    return pl.pallas_call(
        kernel,
        out_shape=outs if len(outs) > 1 else outs[0],
        in_specs=in_specs,
        out_specs=tuple(specs) if len(outs) > 1 else specs[0],
        scratch_shapes=list(scratch),
        compiler_params=pltpu.CompilerParams(vmem_limit_bytes=int(limit * 1024 * 1024)),
        cost_estimate=pl.CostEstimate(
            flops=int(cost * 1.1e9), bytes_accessed=int(cost * 3.6e6), transcendentals=0
        ),
        name=name,
    )(*args)


def on_device(table, w_uvqk, w_out, history, lengths, candidates, counts, actions, targets):
    rows_total, width = table.shape
    seq = history.shape[1]
    ncand = candidates.shape[1]
    users = NY * NZ
    parts = NX * NC
    block = seq // parts
    cblock = ncand // parts
    x, c = lax.axis_index("x"), lax.axis_index("c")
    length = lengths[0]

    place = jnp.stack([x, c, length, counts[0], lax.axis_index("y")]).astype(jnp.int32)

    def along_x(own):
        return [own] + [swap_x(own, k) for k in range(1, NX)]

    size = block + cblock

    def pick(half):
        return call(
            functools.partial(pick_kernel, half),
            "pick",
            [((NX, size, width), BF)],
            place,
            history,
            candidates,
            table,
            smem=1,
            scratch=[pltpu.VMEM((NX * size, rows_total), BF)],
            limit=20,
            cost=5.0 if half else 0.05,
        )

    picked_other = swap_core(pick(1))
    weights_out = lax.all_gather(w_out, ("x", "c"), axis=0, tiled=False)
    picked_own = pick(0)
    line = list(call(pair_kernel, "pair", [((size, width), BF)] * NX, picked_other, picked_own, limit=8))
    line = [line[0]] + [swap_x(line[k], k) for k in range(1, NX)]
    w_uvqk, line[0] = lax.optimization_barrier((w_uvqk, line[0]))
    local_w = w_uvqk.reshape(width, -1)
    normed, crow = call(
        norm_kernel,
        "norm",
        [((block, width), BF), ((cblock, width), BF)],
        *line,
        limit=50,
    )
    own_other = swap_core(normed)
    far_w = swap_core(local_w)
    line[0], normed = lax.optimization_barrier((line[0], normed))
    rows = call(rows_kernel, "rows", [((block, width), BF)], *line, limit=50, cost=0.5)
    *normed_line, local_w, far_w, rows = lax.optimization_barrier(
        (*along_x(normed), crow, local_w, far_w, rows)
    )
    spread_rows = normed_line[:NX] + [own_other] + [swap_core(part) for part in normed_line[1:NX]]
    crows = lax.all_gather(normed_line[NX], ("x", "c"), axis=0, tiled=True)
    normed, pre, act, sent = call(
        attend_kernel,
        "attend",
        [((seq, width), BF), ((seq, 4 * HD), F32), ((seq, 4 * HD), BF), ((parts, block, 3 * HD), BF)],
        place,
        *spread_rows,
        local_w,
        smem=1,
        limit=52,
        far_outs=(0, 1, 2),
        scratch=[
            pltpu.VMEM((seq, width), BF),
            pltpu.VMEM((seq, 4 * HD), F32),
            pltpu.VMEM((seq, 4 * HD), BF),
            pltpu.SemaphoreType.DMA((3,)),
        ],
        cost=4.0,
    )
    sent = lax.all_to_all(sent, ("x", "c"), 0, 0)

    half = NX * HD
    back, dhidden, cand_own, cand_other, out_own, out_other = call(
        event_kernel,
        "event",
        [
            ((parts, block + 16, 2 * HD), BF),
            ((block, width), BF),
            ((NX, cblock, width), BF),
            ((NX, cblock, width), BF),
            ((width, half), BF),
            ((width, half), BF),
        ],
        place,
        sent,
        rows,
        weights_out,
        crows,
        actions,
        targets,
        smem=1,
        limit=60,
        far=(3, 4),
        scratch=[
            pltpu.VMEM((ncand, width), BF),
            pltpu.VMEM((width, width), BF),
            pltpu.VMEM((ncand, width), BF),
            pltpu.SemaphoreType.DMA((parts + 1,)),
        ],
        cost=4.0,
    )
    back = lax.all_to_all(back, ("x", "c"), 0, 0)
    out_other = swap_core(out_other)

    back, cand_other = lax.optimization_barrier((back, swap_core(cand_other)))
    near, far, loss_meta, grads = call(
        backward_kernel,
        "backward",
        [
            ((seq // 2, 4 * HD), BF),
            ((seq // 2, 4 * HD), BF),
            ((16, 128), BF),
            ((NZ, width // NZ, half + 4 * HD), BF),
        ],
        place,
        back,
        act,
        pre,
        normed,
        out_own,
        out_other,
        smem=1,
        scratch=[
            pltpu.VMEM((seq, HD), BF),
            pltpu.VMEM((seq, HD), BF),
            pltpu.VMEM((seq, HD), F32),
            pltpu.VMEM((seq, 4 * HD), BF),
            pltpu.VMEM((seq, 4 * HD), BF),
            pltpu.VMEM((seq, 4 * HD), F32),
            pltpu.VMEM((seq, width), BF),
            pltpu.VMEM((width, half), BF),
            pltpu.VMEM((width, half), BF),
            pltpu.SemaphoreType.DMA((5,)),
        ],
        limit=60,
        far=(2, 3, 4, 5, 6),
        cost=6.0,
    )
    far_got = swap_core(far)
    line = list(
        call(
            part_kernel,
            "part",
            [((size, width), BF)] * NX,
            near,
            far_got,
            local_w,
            far_w,
            cand_own,
            cand_other,
            limit=50,
            cost=2.0,
        )
    )
    grads = lax.psum_scatter(grads, "z", scatter_dimension=0, tiled=False)
    loss_meta, line[0] = lax.optimization_barrier((loss_meta, line[0]))
    meta = call(
        meta_kernel, "meta", [((16, 128), BF)], place, history, candidates, loss_meta, smem=1, limit=40
    )
    line = [line[0]] + [swap_x(line[k], k) for k in range(1, NX)]

    packed = call(
        pack_kernel,
        "pack",
        [((users, 64, 128), BF)],
        *line,
        rows,
        dhidden,
        meta,
        limit=50,
    )
    arrived = lax.all_to_all(packed, ("y", "z"), 0, 0)
    _, grads = lax.optimization_barrier((arrived, grads))
    grads = call(
        turn_kernel, "turn", [((32, half + 4 * HD), BF)] * NY, place, grads, smem=1, limit=8, cost=0.5
    )
    grads = [grads[0]] + [
        lax.ppermute(grads[k], "y", [(i, i ^ k) for i in range(NY)]) for k in range(1, NY)
    ]
    got = arrived[:, 48:53].astype(F32)
    all_ids = (got[:, 0:2] * 128.0 + got[:, 2:4]).astype(jnp.int32).reshape(-1)
    own, other = call(
        scatter_kernel,
        "scatter",
        [((NX, 512, 128), BF)] * 2,
        all_ids,
        place,
        arrived,
        smem=2,
        scratch=[
            pltpu.VMEM((users * 48, 128), F32),
            pltpu.VMEM((parts * rows_total, 128), F32),
            pltpu.VMEM((parts * rows_total, 128), F32),
        ],
        limit=24,
        cost=12.0,
    )
    line = call(pair_kernel, "final_pair", [((512, 128), BF)] * NX, swap_core(other), own, limit=8, cost=0.5)
    line = [line[0]] + [swap_x(line[k], k) for k in range(1, NX)]
    grad_in, *proj = call(
        split_kernel, "split", [((32, 4 * HD), F32)] + [((32, HD), BF)] * NX, *grads, limit=8, cost=0.5
    )
    proj = [proj[0]] + [swap_x(proj[k], k) for k in range(1, NX)]
    shard_t, proj_t = call(
        unpack_kernel,
        "unpack",
        [((32, rows_total), F32), ((32, HD), F32)],
        *line,
        *proj,
        limit=8,
    )
    grad_in = grad_in.reshape(-1, 4, HD)
    loss = jnp.sum(got[:, 4, 0:3])
    return (loss, grad_in, proj_t.T, shard_t.T)


def solution(mesh):
    fine = Mesh(mesh.devices.reshape(NY, NZ, NX, NC), ("y", "z", "x", "c"))
    dp, item = ("y", "z"), ("x", "c")
    placed = (
        P(item, None),
        P(None, None, item),
        P(item, None),
        P(dp, None),
        P(dp),
        P(dp, None),
        P(dp),
        P(dp, None),
        P(dp, None),
    )
    return jax.shard_map(
        on_device,
        mesh=fine,
        in_specs=placed,
        out_specs=(P(), P(dp, None, item), P(item, dp), P(item, dp)),
        check_vma=False,
    )
```

```python
import functools

import jax
import jax.numpy as jnp
from jax import lax
from jax.experimental import pallas as pl
from jax.experimental.pallas import tpu as pltpu
from jax.sharding import Mesh, PartitionSpec as P

HD = 128
NX, NC, NY, NZ = 4, 2, 4, 8
CQL_WEIGHT = 0.5
BF = jnp.bfloat16
F32 = jnp.float32


def swap_x(value, k):
    return lax.ppermute(value, "x", [(i, i ^ k) for i in range(NX)])


def swap_core(value):
    return lax.ppermute(value, "c", [(0, 1), (1, 0)])


def event_slots(item, shape, axis):
    row = lax.broadcasted_iota(jnp.int32, shape, axis)
    return 32 * jnp.bitwise_and(row, 31) + 8 * (row // 32) + item


def cand_slots(item, shape, axis):
    row = lax.broadcasted_iota(jnp.int32, shape, axis)
    return 32 * jnp.bitwise_and(row, 15) + 8 * (row // 16) + item


def chosen(values, slots):
    cols = lax.broadcasted_iota(jnp.int32, (1, values.shape[1]), 1)
    return jnp.sum(jnp.where(cols == slots, values.astype(F32), 0.0), axis=1, keepdims=True)


def pick_kernel(half, place_ref, history_ref, cand_ref, table_ref, out_ref, hot_ref):
    total = table_ref.shape[0]
    first_row = (2 * place_ref[0] + place_ref[1]) * total
    size = out_ref.shape[1]
    for k in range(NX):
        item = item_of(place_ref, half * NX + k)
        events = chosen(history_ref[...], event_slots(item, (128, 1), 0))
        cands = chosen(cand_ref[...], cand_slots(item, (size - 128, 1), 0))
        for first, ids in ((0, events), (128, cands)):
            local = ids.astype(jnp.int32) - first_row
            count = ids.shape[0]
            for i in range(0, total, 512):
                cols = lax.broadcasted_iota(jnp.int32, (1, 512), 1) + i
                hot_ref[size * k + first : size * k + first + count, i : i + 512] = (
                    (local == cols).astype(F32).astype(BF)
                )
    for i in range(0, out_ref.shape[2], 256):
        found = jnp.dot(hot_ref[...], table_ref[:, i : i + 256], preferred_element_type=F32).astype(BF)
        for k in range(NX):
            out_ref[k, :, i : i + 256] = found[size * k : size * k + size, :]


def pair_kernel(a_ref, b_ref, *outs):
    for k, out in enumerate(outs):
        out[...] = (a_ref[k].astype(F32) + b_ref[k].astype(F32)).astype(BF)


def norm_kernel(a_ref, b_ref, c_ref, d_ref, normed_ref, crow_ref):
    refs = (a_ref, b_ref, c_ref, d_ref)
    block = normed_ref.shape[0]
    rows = sum(ref[:block, :].astype(F32) for ref in refs)
    scale = lax.rsqrt(jnp.mean(rows * rows, axis=-1, keepdims=True) + 1e-06)
    normed_ref[...] = (rows * scale).astype(BF)
    crow_ref[...] = sum(ref[block:, :].astype(F32) for ref in refs).astype(BF)


def rows_kernel(a_ref, b_ref, c_ref, d_ref, rows_ref):
    block = rows_ref.shape[0]
    rows_ref[...] = sum(ref[:block, :].astype(F32) for ref in (a_ref, b_ref, c_ref, d_ref)).astype(BF)


def item_of(place_ref, b):
    return 2 * jnp.bitwise_xor(place_ref[0], b % NX) + jnp.bitwise_xor(place_ref[1], b // NX)


def places_of(place_ref, shape, axis, first=0):
    row = lax.broadcasted_iota(jnp.int32, shape, axis) + first
    line = jnp.bitwise_and(row, 511)
    item = 2 * jnp.bitwise_xor(place_ref[0], line // 128) + jnp.bitwise_xor(place_ref[1], row // 512)
    inside = jnp.bitwise_and(row, 127)
    return 32 * jnp.bitwise_and(inside, 31) + 8 * (inside // 32) + item


def attend_kernel(
    place_ref, b0, b1, b2, b3, b4, b5, b6, b7, w_ref,
    normed_out, pre_out, act_out, sent_ref, normed_ref, pre_ref, act_ref, sems,
):
    for b, ref in enumerate((b0, b1, b2, b3, b4, b5, b6, b7)):
        normed_ref[128 * b : 128 * b + 128, :] = ref[...]
    copies = [pltpu.make_async_copy(normed_ref, normed_out, sems.at[0])]
    copies[0].start()
    seq = normed_ref.shape[0]
    for i in range(0, seq, 256):
        pre = jnp.dot(normed_ref[i : i + 256, :], w_ref[...], preferred_element_type=F32)
        pre_ref[i : i + 256, :] = pre
        act_ref[i : i + 256, :] = (pre * jax.nn.sigmoid(pre)).astype(BF)
    for i, (source, target) in enumerate(((pre_ref, pre_out), (act_ref, act_out))):
        copies.append(pltpu.make_async_copy(source, target, sems.at[i + 1]))
        copies[-1].start()
    length = place_ref[2]
    inverse = 1.0 / jnp.full((1, 1), length, jnp.int32).astype(F32)
    cols = places_of(place_ref, (1, seq), 1)
    cols = jnp.where(cols < length, cols, seq)
    for i in range(0, seq, 256):
        queries = act_ref[i : i + 256, 2 * HD : 3 * HD]
        logits = lax.dot_general(
            queries, act_ref[:, 3 * HD :], (((1,), (1,)), ((), ())), preferred_element_type=F32
        ) * HD ** (-0.5)
        rows = places_of(place_ref, (256, 1), 0, i)
        attn = jnp.where(cols <= rows, logits * jax.nn.sigmoid(logits), 0.0).astype(BF)
        mixed = jnp.dot(attn, act_ref[:, HD : 2 * HD], preferred_element_type=F32) * inverse
        top = mixed.astype(BF)
        rest = (mixed - top.astype(F32)).astype(BF)
        for h in range(2):
            b = i // 128 + h
            item = item_of(place_ref, b)
            sent_ref[item, :, 0:HD] = top[128 * h : 128 * h + 128, :]
            sent_ref[item, :, HD : 2 * HD] = rest[128 * h : 128 * h + 128, :]
            sent_ref[item, :, 2 * HD :] = act_ref[128 * b : 128 * b + 128, 0:HD]
    for copy in copies:
        copy.wait()


def split_loss(value, shape, row):
    value = jnp.broadcast_to(value, shape)
    top = value.astype(BF).astype(F32)
    middle = (value - top).astype(BF).astype(F32)
    low = value - top - middle
    lane = lax.broadcasted_iota(jnp.int32, shape, 1)
    picked = jnp.where(lane == 0, top, jnp.where(lane == 1, middle, jnp.where(lane == 2, low, 0.0)))
    return jnp.where(lax.broadcasted_iota(jnp.int32, shape, 0) == row, picked, 0.0).astype(BF)


def event_kernel(
    place_ref, sent_ref, rows_ref, w_ref, crows_ref, action_ref, target_ref,
    back_ref, dhidden_ref, dcand_ref, out_own_ref, out_other_ref,
    weight_ref, crow_ref, sems,
):
    copies = [
        pltpu.make_async_copy(
            w_ref.at[item_of(place_ref, b)], weight_ref.at[HD * b : HD * b + HD, :], sems.at[b]
        )
        for b in range(NX * NC)
    ]
    copies.append(pltpu.make_async_copy(crows_ref, crow_ref, sems.at[NX * NC]))
    for copy in copies:
        copy.start()
    owner = 2 * place_ref[0] + place_ref[1]
    length, count = place_ref[2], place_ref[3]
    block, width = rows_ref.shape
    seq = block * NX * NC
    items = [item_of(place_ref, b) for b in range(NX * NC)]
    mixed = jnp.concatenate(
        [sent_ref[i, :, 0:HD].astype(F32) + sent_ref[i, :, HD : 2 * HD].astype(F32) for i in items], axis=1
    )
    gate = jnp.concatenate([sent_ref[i, :, 2 * HD :] for i in items], axis=1).astype(F32)
    center = jnp.mean(mixed, axis=-1, keepdims=True)
    rstd = lax.rsqrt(jnp.mean(mixed * mixed, axis=-1, keepdims=True) - center * center + 1e-05)
    normo = (mixed - center) * rstd
    gated = (normo * gate).astype(BF)
    for copy in copies:
        copy.wait()
    weights = weight_ref[...]
    out = rows_ref[...].astype(F32) + jnp.dot(gated, weights, preferred_element_type=F32)
    hidden = out.astype(BF)
    crows = crow_ref[...]
    scores = lax.dot_general(hidden, crows, (((1,), (1,)), ((), ())), preferred_element_type=F32)
    col = lax.broadcasted_iota(jnp.int32, (1, crows.shape[0]), 1)
    inside = jnp.bitwise_and(col, 63)
    slots = 32 * jnp.bitwise_and(inside, 15) + 8 * (inside // 16) + col // 64
    masked = jnp.where(slots < count, scores, -jnp.inf)
    top = jnp.max(masked, axis=-1, keepdims=True)
    expo = jnp.exp(masked - top)
    total = jnp.sum(expo, axis=-1, keepdims=True)
    soft = expo / total
    lse = top + jnp.log(total)
    places = event_slots(owner, (block, 1), 0)
    actions = chosen(action_ref[...], places).astype(jnp.int32)
    onehot = (slots == actions).astype(F32)
    taken = jnp.sum(scores * onehot, axis=-1, keepdims=True)
    live = jnp.where(places < length, 1.0 / seq, 0.0)
    miss = taken - chosen(target_ref[...], places)
    loss = jnp.sum(live * (CQL_WEIGHT * (lse - taken) + 0.5 * miss * miss), axis=0, keepdims=True)
    loss = split_loss(loss, (16, 2 * HD), 0)
    dscore = (live * (CQL_WEIGHT * soft + (miss - CQL_WEIGHT) * onehot)).astype(BF)
    dhidden = jnp.dot(dscore, crows, preferred_element_type=F32).astype(BF)
    dhidden_ref[...] = dhidden
    dgated = lax.dot_general(
        dhidden, weights, (((1,), (1,)), ((), ())), preferred_element_type=F32
    )
    dnormo = dgated * gate
    first = jnp.mean(dnormo, axis=-1, keepdims=True)
    second = jnp.mean(dnormo * normo, axis=-1, keepdims=True)
    dmixed = (rstd * (dnormo - first - normo * second)).astype(BF)
    du = (dgated * normo).astype(BF)
    for b, i in enumerate(items):
        back_ref[i, 0:block, 0:HD] = dmixed[:, HD * b : HD * b + HD]
        back_ref[i, 0:block, HD:] = du[:, HD * b : HD * b + HD]
        back_ref[i, block:, :] = loss
    turned = (((0,), (0,)), ((), ()))
    half = NX * HD
    out_other_ref[...] = lax.dot_general(
        dhidden, gated[:, half:], turned, preferred_element_type=F32
    ).astype(BF)
    out_own_ref[...] = lax.dot_general(
        dhidden, gated[:, :half], turned, preferred_element_type=F32
    ).astype(BF)
    dcand_ref[...] = lax.dot_general(dscore, hidden, turned, preferred_element_type=F32).astype(BF)


def backward_kernel(
    place_ref, back_ref, act_in, pre_in, normed_in, out_own_in, out_other_in,
    near_ref, far_ref, loss_ref, grads_ref,
    dm_ref, du_ref, dq_ref, dpre_ref, act_ref, pre_ref, normed_ref, own_ref, other_ref, sems,
):
    copies = [
        pltpu.make_async_copy(source, target, sems.at[i])
        for i, (source, target) in enumerate(
            (
                (act_in, act_ref),
                (pre_in, pre_ref),
                (normed_in, normed_ref),
                (out_own_in, own_ref),
                (out_other_in, other_ref),
            )
        )
    ]
    for copy in copies:
        copy.start()
    seq = act_ref.shape[0]
    loss = jnp.zeros((16, 2 * HD), F32)
    for b in range(8):
        item = item_of(place_ref, b)
        dm_ref[128 * b : 128 * b + 128, :] = back_ref[item, 0:128, 0:HD]
        du_ref[128 * b : 128 * b + 128, :] = back_ref[item, 0:128, HD:]
        loss = loss + back_ref[item, 128:144, :].astype(F32)
    loss = jnp.sum(jnp.sum(loss, axis=1, keepdims=True), axis=0, keepdims=True)
    loss_ref[...] = split_loss(loss, (16, 128), 4)
    length = place_ref[2]
    inverse = 1.0 / jnp.full((1, 1), length, jnp.int32).astype(F32)
    cols = places_of(place_ref, (1, seq), 1)
    across = (((1,), (1,)), ((), ()))
    dq_ref[...] = jnp.zeros(dq_ref.shape, F32)

    def slope(value, sigma):
        return sigma * (1.0 + value * (1.0 - sigma))

    copies[0].wait()
    for i in range(0, seq, 256):
        keys = act_ref[i : i + 256, 3 * HD :]
        logits = lax.dot_general(
            keys, act_ref[:, 2 * HD : 3 * HD], across, preferred_element_type=F32
        ) * HD ** (-0.5)
        rows = places_of(place_ref, (256, 1), 0, i)
        rows = jnp.where(rows < length, rows, seq)
        sigma = jnp.where(rows <= cols, jax.nn.sigmoid(logits), 0.0)
        swish = logits * sigma
        attn = swish.astype(BF)
        dattn = lax.dot_general(
            act_ref[i : i + 256, HD : 2 * HD], dm_ref[...], across, preferred_element_type=F32
        )
        dlogits = (dattn * (sigma + swish * (1.0 - sigma))).astype(BF)
        dvalues = jnp.dot(attn, dm_ref[...], preferred_element_type=F32) * inverse
        dkeys = jnp.dot(dlogits, act_ref[:, 2 * HD : 3 * HD], preferred_element_type=F32) * (
            inverse * HD ** (-0.5)
        )
        dq_ref[...] += lax.dot_general(
            dlogits, keys, (((0,), (0,)), ((), ())), preferred_element_type=F32
        )
        if i == 0:
            copies[1].wait()
        for j, grad in ((1, dvalues), (3, dkeys)):
            pre = pre_ref[i : i + 256, HD * j : HD * j + HD]
            dpre_ref[i : i + 256, HD * j : HD * j + HD] = (
                grad * slope(pre, jax.nn.sigmoid(pre))
            ).astype(BF)
    dq_ref[...] = dq_ref[...] * (inverse * HD ** (-0.5))
    for j, ref in ((0, du_ref), (2, dq_ref)):
        pre = pre_ref[:, HD * j : HD * j + HD]
        dpre_ref[:, HD * j : HD * j + HD] = (
            ref[...].astype(F32) * slope(pre, jax.nn.sigmoid(pre))
        ).astype(BF)
    near_ref[...] = dpre_ref[: near_ref.shape[0], :]
    far_ref[...] = dpre_ref[near_ref.shape[0] :, :]
    for copy in copies[2:]:
        copy.wait()
    half = own_ref.shape[1]
    left = (own_ref[...].astype(F32) + other_ref[...].astype(F32)).astype(BF)
    right = lax.dot_general(
        normed_ref[...], dpre_ref[...], (((0,), (0,)), ((), ())), preferred_element_type=F32
    ).astype(BF)
    for y in range(NY):
        for z in range(NZ):
            rows = slice(32 * (NZ * y + z), 32 * (NZ * y + z) + 32)
            grads_ref[z, 32 * y : 32 * y + 32, :half] = left[rows, :]
            grads_ref[z, 32 * y : 32 * y + 32, half:] = right[rows, :]


def part_kernel(near_ref, far_ref, w_ref, far_w_ref, *outs):
    across = (((1,), (1,)), ((), ()))
    for h in range(2):
        rows = slice(256 * h, 256 * h + 256)
        part = lax.dot_general(near_ref[rows, :], w_ref[...], across, preferred_element_type=F32)
        part = part + lax.dot_general(
            far_ref[rows, :], far_w_ref[...], across, preferred_element_type=F32
        )
        part = part.astype(BF)
        outs[2 * h][...] = part[:128, :]
        outs[2 * h + 1][...] = part[128:, :]


def meta_kernel(place_ref, history_ref, cands_ref, loss_ref, meta_ref):
    owner = 2 * place_ref[0] + place_ref[1]

    def digits(values, wanted):
        row = lax.broadcasted_iota(jnp.int32, (16, values.shape[1]), 0)
        upper, lower = values // 128, jnp.bitwise_and(values, 127)
        both = jnp.where(row == 0, upper, jnp.where(row == 2, lower, 0)).astype(F32).astype(BF)
        source = lax.broadcasted_iota(jnp.int32, (values.shape[1], 128), 0)
        hot = (source == wanted).astype(F32).astype(BF)
        return jnp.dot(both, hot, preferred_element_type=F32)

    lane = lax.broadcasted_iota(jnp.int32, (16, 128), 1)
    row = lax.broadcasted_iota(jnp.int32, (16, 128), 0)
    events = digits(history_ref[...], event_slots(owner, (1, 128), 1))
    wanted = cand_slots(owner, (1, 128), 1)
    wanted = jnp.where(lax.broadcasted_iota(jnp.int32, (1, 128), 1) < 64, wanted, -1)
    cands = pltpu.roll(digits(cands_ref[...], wanted), 1, 0)
    meta = events + cands + loss_ref[...].astype(F32)
    for where, value in ((64, place_ref[2]), (65, place_ref[3])):
        for r, part in ((1, value // 128), (3, jnp.bitwise_and(value, 127))):
            part = jnp.full((16, 128), part, jnp.int32).astype(F32)
            meta = jnp.where((lane == where) & (row == r), part, meta)
    meta_ref[...] = meta.astype(BF)


def pack_kernel(a_ref, b_ref, c_ref, d_ref, dcand_ref, rows_ref, dhidden_ref, meta_ref, out_ref):
    refs = (a_ref, b_ref, c_ref, d_ref)
    dnormed = sum(ref[...].astype(F32) for ref in refs)
    rows = rows_ref[...].astype(F32)
    scale = lax.rsqrt(jnp.mean(rows * rows, axis=-1, keepdims=True) + 1e-06)
    normed = rows * scale
    drows = dhidden_ref[...].astype(F32) + scale * (
        dnormed - normed * jnp.mean(dnormed * normed, axis=-1, keepdims=True)
    )
    drows = drows.astype(BF)
    dcand = dcand_ref[...]
    meta = meta_ref[...]
    for d in range(out_ref.shape[0]):
        out_ref[d, 0:32, :] = jnp.concatenate(
            [drows[32 * g : 32 * g + 32, 32 * d : 32 * d + 32] for g in range(4)], axis=1
        )
        out_ref[d, 32:48, :] = jnp.concatenate(
            [dcand[16 * g : 16 * g + 16, 32 * d : 32 * d + 32] for g in range(4)], axis=1
        )
        out_ref[d, 48:64, :] = meta


def scatter_kernel(ids_ref, place_ref, data_ref, own_ref, other_ref, rows_ref, acc_ref, more_ref):
    users = data_ref.shape[0]
    total = acc_ref.shape[0]
    chunk = 512
    owner = 2 * place_ref[0] + place_ref[1]

    def clear(i, carry):
        here = pl.ds(pl.multiple_of(i * chunk, chunk), chunk)
        acc_ref[here, :] = jnp.zeros((chunk, 128), F32)
        more_ref[here, :] = jnp.zeros((chunk, 128), F32)
        return carry

    lax.fori_loop(0, total // chunk, clear, 0)
    for u in range(users):
        rows_ref[48 * u : 48 * u + 48, :] = data_ref[u, 0:48, :].astype(F32)
    lane = lax.broadcasted_iota(jnp.int32, (1, 128), 1) // 32
    masks = [lane == g for g in range(4)]

    def add(first_id, pitch, first_row, count):
        def step(i, carry):
            for j in range(2):
                work = []
                for half, ref in ((0, acc_ref), (1, more_ref)):
                    p = i * 4 + j * 2 + half
                    row = rows_ref[pl.ds(first_row + p, 1), :]
                    ids = [ids_ref[first_id + g * pitch + p] for g in range(4)]
                    work.append((ref, row, ids, [ref[pl.ds(ids[g], 1), :] for g in range(4)]))
                for ref, row, ids, held in work:
                    for g in range(4):
                        pltpu.store(ref.at[pl.ds(ids[g], 1), :], held[g] + row, mask=masks[g])
            return carry

        lax.fori_loop(0, (count + 3) // 4, step, 0)

    def user(u, carry):
        base = u * 256
        events = jnp.clip((ids_ref[base + 192] - owner + 31) // 32, 0, 32)
        cands = jnp.clip((ids_ref[base + 193] - owner + 31) // 32, 0, 16)
        add(base, 32, u * 48, events)
        add(base + 128, 16, u * 48 + 32, cands)
        return carry

    lax.fori_loop(0, users, user, 0)
    wide = lax.broadcasted_iota(jnp.int32, (512, 128), 1) // 32
    for cc in range(2):
        for k in range(4):
            item = item_of(place_ref, cc * NX + k)
            result = jnp.zeros((512, 128), F32)
            for q in range(4):
                here = pl.ds(pl.multiple_of(item * 2048 + q * 512, 512), 512)
                part = acc_ref[here, :] + more_ref[here, :]
                part = part + pltpu.roll(part, 64, 1)
                part = part + pltpu.roll(part, 32, 1)
                result = jnp.where(wide == q, part, result)
            (own_ref, other_ref)[cc][k] = result.astype(BF)


def turn_kernel(place_ref, grads_ref, *outs):
    for k, out in enumerate(outs):
        start = jnp.bitwise_xor(place_ref[4], k) * 32
        out[...] = grads_ref[pl.ds(pl.multiple_of(start, 32), 32), :]


def split_kernel(g0, g1, g2, g3, in_ref, *outs):
    total = sum(ref[...].astype(F32) for ref in (g0, g1, g2, g3))
    in_ref[...] = total[:, NX * HD :]
    for k, out in enumerate(outs):
        out[...] = total[:, HD * k : HD * k + HD].astype(BF)


def unpack_kernel(a_ref, b_ref, c_ref, d_ref, p0, p1, p2, p3, out_ref, proj_ref):
    proj_ref[...] = sum(ref[...].astype(F32) for ref in (p0, p1, p2, p3))
    turned = sum(ref[...].astype(F32) for ref in (a_ref, b_ref, c_ref, d_ref)).T
    for q in range(4):
        out_ref[:, q * 512 : (q + 1) * 512] = turned[32 * q : 32 * q + 32, :]


def whole(count, smem=0):
    specs = [pl.BlockSpec(memory_space=pltpu.SMEM)] * smem
    return specs + [pl.BlockSpec(memory_space=pltpu.VMEM)] * count


def call(kernel, name, outs, *args, smem=0, scratch=(), limit=32, far=(), far_outs=(), cost=1.0):
    outs = tuple(jax.ShapeDtypeStruct(shape, dtype) for shape, dtype in outs)
    hbm = pl.BlockSpec(memory_space=pltpu.HBM)
    specs = [hbm if i in far_outs else whole(1)[0] for i in range(len(outs))]
    in_specs = [hbm if i in far else spec for i, spec in enumerate(whole(len(args) - smem, smem))]
    return pl.pallas_call(
        kernel,
        out_shape=outs if len(outs) > 1 else outs[0],
        in_specs=in_specs,
        out_specs=tuple(specs) if len(outs) > 1 else specs[0],
        scratch_shapes=list(scratch),
        compiler_params=pltpu.CompilerParams(vmem_limit_bytes=int(limit * 1024 * 1024)),
        cost_estimate=pl.CostEstimate(
            flops=int(cost * 1.1e9), bytes_accessed=int(cost * 3.6e6), transcendentals=0
        ),
        name=name,
    )(*args)


def on_device(table, w_uvqk, w_out, history, lengths, candidates, counts, actions, targets):
    rows_total, width = table.shape
    seq = history.shape[1]
    ncand = candidates.shape[1]
    users = NY * NZ
    parts = NX * NC
    block = seq // parts
    cblock = ncand // parts
    x, c = lax.axis_index("x"), lax.axis_index("c")
    length = lengths[0]

    place = jnp.stack([x, c, length, counts[0], lax.axis_index("y")]).astype(jnp.int32)

    def along_x(own):
        return [own] + [swap_x(own, k) for k in range(1, NX)]

    size = block + cblock

    def pick(half):
        return call(
            functools.partial(pick_kernel, half),
            "pick",
            [((NX, size, width), BF)],
            place,
            history,
            candidates,
            table,
            smem=1,
            scratch=[pltpu.VMEM((NX * size, rows_total), BF)],
            limit=20,
            cost=5.0 if half else 0.05,
        )

    picked_other = swap_core(pick(1))
    weights_out = lax.all_gather(w_out, ("x", "c"), axis=0, tiled=False)
    picked_own = pick(0)
    line = list(call(pair_kernel, "pair", [((size, width), BF)] * NX, picked_other, picked_own, limit=8))
    line = [line[0]] + [swap_x(line[k], k) for k in range(1, NX)]
    w_uvqk, line[0] = lax.optimization_barrier((w_uvqk, line[0]))
    local_w = w_uvqk.reshape(width, -1)
    normed, crow = call(
        norm_kernel,
        "norm",
        [((block, width), BF), ((cblock, width), BF)],
        *line,
        limit=50,
    )
    own_other = swap_core(normed)
    far_w = swap_core(local_w)
    line[0], normed = lax.optimization_barrier((line[0], normed))
    rows = call(rows_kernel, "rows", [((block, width), BF)], *line, limit=50, cost=0.5)
    *normed_line, local_w, far_w, rows = lax.optimization_barrier(
        (*along_x(normed), crow, local_w, far_w, rows)
    )
    spread_rows = normed_line[:NX] + [own_other] + [swap_core(part) for part in normed_line[1:NX]]
    crows = lax.all_gather(normed_line[NX], ("x", "c"), axis=0, tiled=True)
    normed, pre, act, sent = call(
        attend_kernel,
        "attend",
        [((seq, width), BF), ((seq, 4 * HD), F32), ((seq, 4 * HD), BF), ((parts, block, 3 * HD), BF)],
        place,
        *spread_rows,
        local_w,
        smem=1,
        limit=52,
        far_outs=(0, 1, 2),
        scratch=[
            pltpu.VMEM((seq, width), BF),
            pltpu.VMEM((seq, 4 * HD), F32),
            pltpu.VMEM((seq, 4 * HD), BF),
            pltpu.SemaphoreType.DMA((3,)),
        ],
        cost=4.0,
    )
    sent = lax.all_to_all(sent, ("x", "c"), 0, 0)

    half = NX * HD
    back, dhidden, dcand, out_own, out_other = call(
        event_kernel,
        "event",
        [
            ((parts, block + 16, 2 * HD), BF),
            ((block, width), BF),
            ((ncand, width), BF),
            ((width, half), BF),
            ((width, half), BF),
        ],
        place,
        sent,
        rows,
        weights_out,
        crows,
        actions,
        targets,
        smem=1,
        limit=60,
        far=(3, 4),
        scratch=[
            pltpu.VMEM((width, width), BF),
            pltpu.VMEM((ncand, width), BF),
            pltpu.SemaphoreType.DMA((parts + 1,)),
        ],
        cost=4.0,
    )
    back = lax.all_to_all(back, ("x", "c"), 0, 0)
    out_other = swap_core(out_other)

    dcand = lax.psum_scatter(dcand, ("x", "c"), scatter_dimension=0, tiled=True)
    near, far, loss_meta, grads = call(
        backward_kernel,
        "backward",
        [
            ((seq // 2, 4 * HD), BF),
            ((seq // 2, 4 * HD), BF),
            ((16, 128), BF),
            ((NZ, width // NZ, half + 4 * HD), BF),
        ],
        place,
        back,
        act,
        pre,
        normed,
        out_own,
        out_other,
        smem=1,
        scratch=[
            pltpu.VMEM((seq, HD), BF),
            pltpu.VMEM((seq, HD), BF),
            pltpu.VMEM((seq, HD), F32),
            pltpu.VMEM((seq, 4 * HD), BF),
            pltpu.VMEM((seq, 4 * HD), BF),
            pltpu.VMEM((seq, 4 * HD), F32),
            pltpu.VMEM((seq, width), BF),
            pltpu.VMEM((width, half), BF),
            pltpu.VMEM((width, half), BF),
            pltpu.SemaphoreType.DMA((5,)),
        ],
        limit=60,
        far=(2, 3, 4, 5, 6),
        cost=6.0,
    )
    far_got = swap_core(far)
    line = list(
        call(
            part_kernel,
            "part",
            [((block, width), BF)] * NX,
            near,
            far_got,
            local_w,
            far_w,
            limit=50,
            cost=2.0,
        )
    )
    grads = lax.psum_scatter(grads, "z", scatter_dimension=0, tiled=False)
    loss_meta, line[0] = lax.optimization_barrier((loss_meta, line[0]))
    meta = call(
        meta_kernel, "meta", [((16, 128), BF)], place, history, candidates, loss_meta, smem=1, limit=40
    )
    line = [line[0]] + [swap_x(line[k], k) for k in range(1, NX)]

    packed = call(
        pack_kernel,
        "pack",
        [((users, 64, 128), BF)],
        *line,
        dcand,
        rows,
        dhidden,
        meta,
        limit=50,
    )
    arrived = lax.all_to_all(packed, ("y", "z"), 0, 0)
    _, grads = lax.optimization_barrier((arrived, grads))
    grads = call(
        turn_kernel, "turn", [((32, half + 4 * HD), BF)] * NY, place, grads, smem=1, limit=8, cost=0.5
    )
    grads = [grads[0]] + [
        lax.ppermute(grads[k], "y", [(i, i ^ k) for i in range(NY)]) for k in range(1, NY)
    ]
    got = arrived[:, 48:53].astype(F32)
    all_ids = (got[:, 0:2] * 128.0 + got[:, 2:4]).astype(jnp.int32).reshape(-1)
    own, other = call(
        scatter_kernel,
        "scatter",
        [((NX, 512, 128), BF)] * 2,
        all_ids,
        place,
        arrived,
        smem=2,
        scratch=[
            pltpu.VMEM((users * 48, 128), F32),
            pltpu.VMEM((parts * rows_total, 128), F32),
            pltpu.VMEM((parts * rows_total, 128), F32),
        ],
        limit=24,
        cost=12.0,
    )
    line = call(pair_kernel, "final_pair", [((512, 128), BF)] * NX, swap_core(other), own, limit=8, cost=0.5)
    line = [line[0]] + [swap_x(line[k], k) for k in range(1, NX)]
    grad_in, *proj = call(
        split_kernel, "split", [((32, 4 * HD), F32)] + [((32, HD), BF)] * NX, *grads, limit=8, cost=0.5
    )
    proj = [proj[0]] + [swap_x(proj[k], k) for k in range(1, NX)]
    shard_t, proj_t = call(
        unpack_kernel,
        "unpack",
        [((32, rows_total), F32), ((32, HD), F32)],
        *line,
        *proj,
        limit=8,
    )
    grad_in = grad_in.reshape(-1, 4, HD)
    loss = jnp.sum(got[:, 4, 0:3])
    return (loss, grad_in, proj_t.T, shard_t.T)


def solution(mesh):
    fine = Mesh(mesh.devices.reshape(NY, NZ, NX, NC), ("y", "z", "x", "c"))
    dp, item = ("y", "z"), ("x", "c")
    placed = (
        P(item, None),
        P(None, None, item),
        P(item, None),
        P(dp, None),
        P(dp),
        P(dp, None),
        P(dp),
        P(dp, None),
        P(dp, None),
    )
    return jax.shard_map(
        on_device,
        mesh=fine,
        in_specs=placed,
        out_specs=(P(), P(dp, None, item), P(item, dp), P(item, dp)),
        check_vma=False,
    )
```

```python
import functools

import jax
import jax.numpy as jnp
from jax import lax
from jax.experimental import pallas as pl
from jax.experimental.pallas import tpu as pltpu
from jax.sharding import Mesh, PartitionSpec as P

HD = 128
NX, NC, NY, NZ = 4, 2, 4, 8
CQL_WEIGHT = 0.5
BF = jnp.bfloat16
F32 = jnp.float32


def swap_x(value, k):
    return lax.ppermute(value, "x", [(i, i ^ k) for i in range(NX)])


def swap_core(value):
    return lax.ppermute(value, "c", [(0, 1), (1, 0)])


def event_slots(item, shape, axis):
    row = lax.broadcasted_iota(jnp.int32, shape, axis)
    return 32 * jnp.bitwise_and(row, 31) + 8 * (row // 32) + item


def cand_slots(item, shape, axis):
    row = lax.broadcasted_iota(jnp.int32, shape, axis)
    return 32 * jnp.bitwise_and(row, 15) + 8 * (row // 16) + item


def chosen(values, slots):
    cols = lax.broadcasted_iota(jnp.int32, (1, values.shape[1]), 1)
    return jnp.sum(jnp.where(cols == slots, values.astype(F32), 0.0), axis=1, keepdims=True)


def pick_kernel(half, place_ref, history_ref, cand_ref, table_ref, out_ref, hot_ref):
    total = table_ref.shape[0]
    first_row = (2 * place_ref[0] + place_ref[1]) * total
    size = out_ref.shape[1]
    for k in range(NX):
        item = item_of(place_ref, half * NX + k)
        events = chosen(history_ref[...], event_slots(item, (128, 1), 0))
        cands = chosen(cand_ref[...], cand_slots(item, (size - 128, 1), 0))
        for first, ids in ((0, events), (128, cands)):
            local = ids.astype(jnp.int32) - first_row
            count = ids.shape[0]
            for i in range(0, total, 512):
                cols = lax.broadcasted_iota(jnp.int32, (1, 512), 1) + i
                hot_ref[size * k + first : size * k + first + count, i : i + 512] = (
                    (local == cols).astype(F32).astype(BF)
                )
    for i in range(0, out_ref.shape[2], 256):
        found = jnp.dot(hot_ref[...], table_ref[:, i : i + 256], preferred_element_type=F32).astype(BF)
        for k in range(NX):
            out_ref[k, :, i : i + 256] = found[size * k : size * k + size, :]


def pair_kernel(a_ref, b_ref, *outs):
    for k, out in enumerate(outs):
        out[...] = (a_ref[k].astype(F32) + b_ref[k].astype(F32)).astype(BF)


def norm_kernel(a_ref, b_ref, c_ref, d_ref, normed_ref, crow_ref):
    refs = (a_ref, b_ref, c_ref, d_ref)
    block = normed_ref.shape[0]
    rows = sum(ref[:block, :].astype(F32) for ref in refs)
    scale = lax.rsqrt(jnp.mean(rows * rows, axis=-1, keepdims=True) + 1e-06)
    normed_ref[...] = (rows * scale).astype(BF)
    crow_ref[...] = sum(ref[block:, :].astype(F32) for ref in refs).astype(BF)


def rows_kernel(a_ref, b_ref, c_ref, d_ref, rows_ref):
    block = rows_ref.shape[0]
    rows_ref[...] = sum(ref[:block, :].astype(F32) for ref in (a_ref, b_ref, c_ref, d_ref)).astype(BF)


def item_of(place_ref, b):
    return 2 * jnp.bitwise_xor(place_ref[0], b % NX) + jnp.bitwise_xor(place_ref[1], b // NX)


def places_of(place_ref, shape, axis, first=0):
    row = lax.broadcasted_iota(jnp.int32, shape, axis) + first
    line = jnp.bitwise_and(row, 511)
    item = 2 * jnp.bitwise_xor(place_ref[0], line // 128) + jnp.bitwise_xor(place_ref[1], row // 512)
    inside = jnp.bitwise_and(row, 127)
    return 32 * jnp.bitwise_and(inside, 31) + 8 * (inside // 32) + item


def attend_kernel(
    place_ref, b0, b1, b2, b3, b4, b5, b6, b7, w_ref,
    normed_out, pre_out, act_out, sent_ref, normed_ref, pre_ref, act_ref, sems,
):
    for b, ref in enumerate((b0, b1, b2, b3, b4, b5, b6, b7)):
        normed_ref[128 * b : 128 * b + 128, :] = ref[...]
    copies = [pltpu.make_async_copy(normed_ref, normed_out, sems.at[0])]
    copies[0].start()
    seq = normed_ref.shape[0]
    for i in range(0, seq, 256):
        pre = jnp.dot(normed_ref[i : i + 256, :], w_ref[...], preferred_element_type=F32)
        pre_ref[i : i + 256, :] = pre
        act_ref[i : i + 256, :] = (pre * jax.nn.sigmoid(pre)).astype(BF)
    for i, (source, target) in enumerate(((pre_ref, pre_out), (act_ref, act_out))):
        copies.append(pltpu.make_async_copy(source, target, sems.at[i + 1]))
        copies[-1].start()
    length = place_ref[2]
    inverse = 1.0 / jnp.full((1, 1), length, jnp.int32).astype(F32)
    cols = places_of(place_ref, (1, seq), 1)
    cols = jnp.where(cols < length, cols, seq)
    for i in range(0, seq, 256):
        queries = act_ref[i : i + 256, 2 * HD : 3 * HD]
        logits = lax.dot_general(
            queries, act_ref[:, 3 * HD :], (((1,), (1,)), ((), ())), preferred_element_type=F32
        ) * HD ** (-0.5)
        rows = places_of(place_ref, (256, 1), 0, i)
        attn = jnp.where(cols <= rows, logits * jax.nn.sigmoid(logits), 0.0).astype(BF)
        mixed = jnp.dot(attn, act_ref[:, HD : 2 * HD], preferred_element_type=F32) * inverse
        top = mixed.astype(BF)
        rest = (mixed - top.astype(F32)).astype(BF)
        for h in range(2):
            b = i // 128 + h
            item = item_of(place_ref, b)
            sent_ref[item, :, 0:HD] = top[128 * h : 128 * h + 128, :]
            sent_ref[item, :, HD : 2 * HD] = rest[128 * h : 128 * h + 128, :]
            sent_ref[item, :, 2 * HD :] = act_ref[128 * b : 128 * b + 128, 0:HD]
    for copy in copies:
        copy.wait()


def split_loss(value, shape, row):
    value = jnp.broadcast_to(value, shape)
    top = value.astype(BF).astype(F32)
    middle = (value - top).astype(BF).astype(F32)
    low = value - top - middle
    lane = lax.broadcasted_iota(jnp.int32, shape, 1)
    picked = jnp.where(lane == 0, top, jnp.where(lane == 1, middle, jnp.where(lane == 2, low, 0.0)))
    return jnp.where(lax.broadcasted_iota(jnp.int32, shape, 0) == row, picked, 0.0).astype(BF)


def event_kernel(
    place_ref, sent_ref, rows_ref, w_ref, crows_ref, action_ref, target_ref,
    back_ref, dhidden_ref, dcand_ref, out_own_ref, out_other_ref,
    weight_ref, crow_ref, sems,
):
    copies = [
        pltpu.make_async_copy(
            w_ref.at[item_of(place_ref, b)], weight_ref.at[HD * b : HD * b + HD, :], sems.at[b]
        )
        for b in range(NX * NC)
    ]
    copies.append(pltpu.make_async_copy(crows_ref, crow_ref, sems.at[NX * NC]))
    for copy in copies:
        copy.start()
    owner = 2 * place_ref[0] + place_ref[1]
    length, count = place_ref[2], place_ref[3]
    block, width = rows_ref.shape
    seq = block * NX * NC
    items = [item_of(place_ref, b) for b in range(NX * NC)]
    mixed = jnp.concatenate(
        [sent_ref[i, :, 0:HD].astype(F32) + sent_ref[i, :, HD : 2 * HD].astype(F32) for i in items], axis=1
    )
    gate = jnp.concatenate([sent_ref[i, :, 2 * HD :] for i in items], axis=1).astype(F32)
    center = jnp.mean(mixed, axis=-1, keepdims=True)
    rstd = lax.rsqrt(jnp.mean(mixed * mixed, axis=-1, keepdims=True) - center * center + 1e-05)
    normo = (mixed - center) * rstd
    gated = (normo * gate).astype(BF)
    for copy in copies:
        copy.wait()
    weights = weight_ref[...]
    out = rows_ref[...].astype(F32) + jnp.dot(gated, weights, preferred_element_type=F32)
    hidden = out.astype(BF)
    crows = crow_ref[...]
    scores = lax.dot_general(hidden, crows, (((1,), (1,)), ((), ())), preferred_element_type=F32)
    col = lax.broadcasted_iota(jnp.int32, (1, crows.shape[0]), 1)
    inside = jnp.bitwise_and(col, 63)
    slots = 32 * jnp.bitwise_and(inside, 15) + 8 * (inside // 16) + col // 64
    masked = jnp.where(slots < count, scores, -jnp.inf)
    top = jnp.max(masked, axis=-1, keepdims=True)
    expo = jnp.exp(masked - top)
    total = jnp.sum(expo, axis=-1, keepdims=True)
    soft = expo / total
    lse = top + jnp.log(total)
    places = event_slots(owner, (block, 1), 0)
    actions = chosen(action_ref[...], places).astype(jnp.int32)
    onehot = (slots == actions).astype(F32)
    taken = jnp.sum(scores * onehot, axis=-1, keepdims=True)
    live = jnp.where(places < length, 1.0 / seq, 0.0)
    miss = taken - chosen(target_ref[...], places)
    loss = jnp.sum(live * (CQL_WEIGHT * (lse - taken) + 0.5 * miss * miss), axis=0, keepdims=True)
    loss = split_loss(loss, (16, 2 * HD), 0)
    dscore = (live * (CQL_WEIGHT * soft + (miss - CQL_WEIGHT) * onehot)).astype(BF)
    dhidden = jnp.dot(dscore, crows, preferred_element_type=F32).astype(BF)
    dhidden_ref[...] = dhidden
    dgated = lax.dot_general(
        dhidden, weights, (((1,), (1,)), ((), ())), preferred_element_type=F32
    )
    dnormo = dgated * gate
    first = jnp.mean(dnormo, axis=-1, keepdims=True)
    second = jnp.mean(dnormo * normo, axis=-1, keepdims=True)
    dmixed = (rstd * (dnormo - first - normo * second)).astype(BF)
    du = (dgated * normo).astype(BF)
    for b, i in enumerate(items):
        back_ref[i, 0:block, 0:HD] = dmixed[:, HD * b : HD * b + HD]
        back_ref[i, 0:block, HD:] = du[:, HD * b : HD * b + HD]
        back_ref[i, block:, :] = loss
    turned = (((0,), (0,)), ((), ()))
    half = NX * HD
    out_other_ref[...] = lax.dot_general(
        dhidden, gated[:, half:], turned, preferred_element_type=F32
    ).astype(BF)
    out_own_ref[...] = lax.dot_general(
        dhidden, gated[:, :half], turned, preferred_element_type=F32
    ).astype(BF)
    dcand_ref[...] = lax.dot_general(dscore, hidden, turned, preferred_element_type=F32).astype(BF)


def backward_kernel(
    place_ref, back_ref, act_in, pre_in, normed_in, out_own_in, out_other_in,
    near_ref, far_ref, loss_ref, g0, g1, g2, g3,
    dm_ref, du_ref, dq_ref, dpre_ref, act_ref, pre_ref, normed_ref, own_ref, other_ref, grads_ref, sems,
):
    copies = [
        pltpu.make_async_copy(source, target, sems.at[i])
        for i, (source, target) in enumerate(
            (
                (act_in, act_ref),
                (pre_in, pre_ref),
                (normed_in, normed_ref),
                (out_own_in, own_ref),
                (out_other_in, other_ref),
            )
        )
    ]
    for copy in copies:
        copy.start()
    seq = act_ref.shape[0]
    loss = jnp.zeros((16, 2 * HD), F32)
    for b in range(8):
        item = item_of(place_ref, b)
        dm_ref[128 * b : 128 * b + 128, :] = back_ref[item, 0:128, 0:HD]
        du_ref[128 * b : 128 * b + 128, :] = back_ref[item, 0:128, HD:]
        loss = loss + back_ref[item, 128:144, :].astype(F32)
    loss = jnp.sum(jnp.sum(loss, axis=1, keepdims=True), axis=0, keepdims=True)
    loss_ref[...] = split_loss(loss, (16, 128), 4)
    length = place_ref[2]
    inverse = 1.0 / jnp.full((1, 1), length, jnp.int32).astype(F32)
    cols = places_of(place_ref, (1, seq), 1)
    across = (((1,), (1,)), ((), ()))
    dq_ref[...] = jnp.zeros(dq_ref.shape, F32)

    def slope(value, sigma):
        return sigma * (1.0 + value * (1.0 - sigma))

    copies[0].wait()
    for i in range(0, seq, 256):
        keys = act_ref[i : i + 256, 3 * HD :]
        logits = lax.dot_general(
            keys, act_ref[:, 2 * HD : 3 * HD], across, preferred_element_type=F32
        ) * HD ** (-0.5)
        rows = places_of(place_ref, (256, 1), 0, i)
        rows = jnp.where(rows < length, rows, seq)
        sigma = jnp.where(rows <= cols, jax.nn.sigmoid(logits), 0.0)
        swish = logits * sigma
        attn = swish.astype(BF)
        dattn = lax.dot_general(
            act_ref[i : i + 256, HD : 2 * HD], dm_ref[...], across, preferred_element_type=F32
        )
        dlogits = (dattn * (sigma + swish * (1.0 - sigma))).astype(BF)
        dvalues = jnp.dot(attn, dm_ref[...], preferred_element_type=F32) * inverse
        dkeys = jnp.dot(dlogits, act_ref[:, 2 * HD : 3 * HD], preferred_element_type=F32) * (
            inverse * HD ** (-0.5)
        )
        dq_ref[...] += lax.dot_general(
            dlogits, keys, (((0,), (0,)), ((), ())), preferred_element_type=F32
        )
        if i == 0:
            copies[1].wait()
        for j, grad in ((1, dvalues), (3, dkeys)):
            pre = pre_ref[i : i + 256, HD * j : HD * j + HD]
            dpre_ref[i : i + 256, HD * j : HD * j + HD] = (
                grad * slope(pre, jax.nn.sigmoid(pre))
            ).astype(BF)
    dq_ref[...] = dq_ref[...] * (inverse * HD ** (-0.5))
    for j, ref in ((0, du_ref), (2, dq_ref)):
        pre = pre_ref[:, HD * j : HD * j + HD]
        dpre_ref[:, HD * j : HD * j + HD] = (
            ref[...].astype(F32) * slope(pre, jax.nn.sigmoid(pre))
        ).astype(BF)
    near_ref[...] = dpre_ref[: near_ref.shape[0], :]
    far_ref[...] = dpre_ref[near_ref.shape[0] :, :]
    for copy in copies[2:]:
        copy.wait()
    half = own_ref.shape[1]
    grads_ref[:, :half] = (own_ref[...].astype(F32) + other_ref[...].astype(F32)).astype(BF)
    grads_ref[:, half:] = lax.dot_general(
        normed_ref[...], dpre_ref[...], (((0,), (0,)), ((), ())), preferred_element_type=F32
    ).astype(BF)
    size = g0.shape[0]
    for k, ref in enumerate((g0, g1, g2, g3)):
        start = jnp.bitwise_xor(place_ref[4], k) * size
        ref[...] = grads_ref[pl.ds(pl.multiple_of(start, size), size), :]


def part_kernel(near_ref, far_ref, w_ref, far_w_ref, *outs):
    across = (((1,), (1,)), ((), ()))
    for h in range(2):
        rows = slice(256 * h, 256 * h + 256)
        part = lax.dot_general(near_ref[rows, :], w_ref[...], across, preferred_element_type=F32)
        part = part + lax.dot_general(
            far_ref[rows, :], far_w_ref[...], across, preferred_element_type=F32
        )
        part = part.astype(BF)
        outs[2 * h][...] = part[:128, :]
        outs[2 * h + 1][...] = part[128:, :]


def meta_kernel(place_ref, history_ref, cands_ref, loss_ref, meta_ref):
    owner = 2 * place_ref[0] + place_ref[1]

    def digits(values, wanted):
        row = lax.broadcasted_iota(jnp.int32, (16, values.shape[1]), 0)
        upper, lower = values // 128, jnp.bitwise_and(values, 127)
        both = jnp.where(row == 0, upper, jnp.where(row == 2, lower, 0)).astype(F32).astype(BF)
        source = lax.broadcasted_iota(jnp.int32, (values.shape[1], 128), 0)
        hot = (source == wanted).astype(F32).astype(BF)
        return jnp.dot(both, hot, preferred_element_type=F32)

    lane = lax.broadcasted_iota(jnp.int32, (16, 128), 1)
    row = lax.broadcasted_iota(jnp.int32, (16, 128), 0)
    events = digits(history_ref[...], event_slots(owner, (1, 128), 1))
    wanted = cand_slots(owner, (1, 128), 1)
    wanted = jnp.where(lax.broadcasted_iota(jnp.int32, (1, 128), 1) < 64, wanted, -1)
    cands = pltpu.roll(digits(cands_ref[...], wanted), 1, 0)
    meta = events + cands + loss_ref[...].astype(F32)
    for where, value in ((64, place_ref[2]), (65, place_ref[3])):
        for r, part in ((1, value // 128), (3, jnp.bitwise_and(value, 127))):
            part = jnp.full((16, 128), part, jnp.int32).astype(F32)
            meta = jnp.where((lane == where) & (row == r), part, meta)
    meta_ref[...] = meta.astype(BF)


def pack_kernel(a_ref, b_ref, c_ref, d_ref, dcand_ref, rows_ref, dhidden_ref, meta_ref, out_ref):
    refs = (a_ref, b_ref, c_ref, d_ref)
    dnormed = sum(ref[...].astype(F32) for ref in refs)
    rows = rows_ref[...].astype(F32)
    scale = lax.rsqrt(jnp.mean(rows * rows, axis=-1, keepdims=True) + 1e-06)
    normed = rows * scale
    drows = dhidden_ref[...].astype(F32) + scale * (
        dnormed - normed * jnp.mean(dnormed * normed, axis=-1, keepdims=True)
    )
    drows = drows.astype(BF)
    dcand = dcand_ref[...]
    meta = meta_ref[...]
    for d in range(out_ref.shape[0]):
        out_ref[d, 0:32, :] = jnp.concatenate(
            [drows[32 * g : 32 * g + 32, 32 * d : 32 * d + 32] for g in range(4)], axis=1
        )
        out_ref[d, 32:48, :] = jnp.concatenate(
            [dcand[16 * g : 16 * g + 16, 32 * d : 32 * d + 32] for g in range(4)], axis=1
        )
        out_ref[d, 48:64, :] = meta


def scatter_kernel(ids_ref, place_ref, data_ref, own_ref, other_ref, rows_ref, acc_ref, more_ref):
    users = data_ref.shape[0]
    total = acc_ref.shape[0]
    chunk = 512
    owner = 2 * place_ref[0] + place_ref[1]

    def clear(i, carry):
        here = pl.ds(pl.multiple_of(i * chunk, chunk), chunk)
        acc_ref[here, :] = jnp.zeros((chunk, 128), F32)
        more_ref[here, :] = jnp.zeros((chunk, 128), F32)
        return carry

    lax.fori_loop(0, total // chunk, clear, 0)
    for u in range(users):
        rows_ref[48 * u : 48 * u + 48, :] = data_ref[u, 0:48, :].astype(F32)
    lane = lax.broadcasted_iota(jnp.int32, (1, 128), 1) // 32
    masks = [lane == g for g in range(4)]

    def add(first_id, pitch, first_row, count):
        def step(i, carry):
            for j in range(2):
                work = []
                for half, ref in ((0, acc_ref), (1, more_ref)):
                    p = i * 4 + j * 2 + half
                    row = rows_ref[pl.ds(first_row + p, 1), :]
                    ids = [ids_ref[first_id + g * pitch + p] for g in range(4)]
                    work.append((ref, row, ids, [ref[pl.ds(ids[g], 1), :] for g in range(4)]))
                for ref, row, ids, held in work:
                    for g in range(4):
                        pltpu.store(ref.at[pl.ds(ids[g], 1), :], held[g] + row, mask=masks[g])
            return carry

        lax.fori_loop(0, (count + 3) // 4, step, 0)

    def user(u, carry):
        base = u * 256
        events = jnp.clip((ids_ref[base + 192] - owner + 31) // 32, 0, 32)
        cands = jnp.clip((ids_ref[base + 193] - owner + 31) // 32, 0, 16)
        add(base, 32, u * 48, events)
        add(base + 128, 16, u * 48 + 32, cands)
        return carry

    lax.fori_loop(0, users, user, 0)
    wide = lax.broadcasted_iota(jnp.int32, (512, 128), 1) // 32
    for cc in range(2):
        for k in range(4):
            item = item_of(place_ref, cc * NX + k)
            result = jnp.zeros((512, 128), F32)
            for q in range(4):
                here = pl.ds(pl.multiple_of(item * 2048 + q * 512, 512), 512)
                part = acc_ref[here, :] + more_ref[here, :]
                part = part + pltpu.roll(part, 64, 1)
                part = part + pltpu.roll(part, 32, 1)
                result = jnp.where(wide == q, part, result)
            (own_ref, other_ref)[cc][k] = result.astype(BF)


def sum_kernel(a_ref, b_ref, c_ref, d_ref, out_ref):
    out_ref[...] = sum(ref[...].astype(F32) for ref in (a_ref, b_ref, c_ref, d_ref)).astype(BF)


def final_pair_kernel(a_ref, b_ref, grads_ref, *outs):
    for k, out in enumerate(outs):
        out[:512, :] = (a_ref[k].astype(F32) + b_ref[k].astype(F32)).astype(BF)
        out[512:, :] = grads_ref[:, HD * k : HD * k + HD]


def unpack_kernel(a_ref, b_ref, c_ref, d_ref, grads_ref, out_ref, proj_ref, in_ref):
    refs = (a_ref, b_ref, c_ref, d_ref)
    proj_ref[...] = sum(ref[512:, :].astype(F32) for ref in refs)
    turned = sum(ref[:512, :].astype(F32) for ref in refs).T
    for q in range(4):
        out_ref[:, q * 512 : (q + 1) * 512] = turned[32 * q : 32 * q + 32, :]
    in_ref[...] = grads_ref[:, NX * HD :].astype(F32)


def whole(count, smem=0):
    specs = [pl.BlockSpec(memory_space=pltpu.SMEM)] * smem
    return specs + [pl.BlockSpec(memory_space=pltpu.VMEM)] * count


def call(kernel, name, outs, *args, smem=0, scratch=(), limit=32, far=(), far_outs=(), cost=1.0):
    outs = tuple(jax.ShapeDtypeStruct(shape, dtype) for shape, dtype in outs)
    hbm = pl.BlockSpec(memory_space=pltpu.HBM)
    specs = [hbm if i in far_outs else whole(1)[0] for i in range(len(outs))]
    in_specs = [hbm if i in far else spec for i, spec in enumerate(whole(len(args) - smem, smem))]
    return pl.pallas_call(
        kernel,
        out_shape=outs if len(outs) > 1 else outs[0],
        in_specs=in_specs,
        out_specs=tuple(specs) if len(outs) > 1 else specs[0],
        scratch_shapes=list(scratch),
        compiler_params=pltpu.CompilerParams(vmem_limit_bytes=int(limit * 1024 * 1024)),
        cost_estimate=pl.CostEstimate(
            flops=int(cost * 1.1e9), bytes_accessed=int(cost * 3.6e6), transcendentals=0
        ),
        name=name,
    )(*args)


def on_device(table, w_uvqk, w_out, history, lengths, candidates, counts, actions, targets):
    rows_total, width = table.shape
    seq = history.shape[1]
    ncand = candidates.shape[1]
    users = NY * NZ
    parts = NX * NC
    block = seq // parts
    cblock = ncand // parts
    x, c = lax.axis_index("x"), lax.axis_index("c")
    length = lengths[0]

    place = jnp.stack([x, c, length, counts[0], lax.axis_index("y")]).astype(jnp.int32)

    def along_x(own):
        return [own] + [swap_x(own, k) for k in range(1, NX)]

    size = block + cblock

    def pick(half):
        return call(
            functools.partial(pick_kernel, half),
            "pick",
            [((NX, size, width), BF)],
            place,
            history,
            candidates,
            table,
            smem=1,
            scratch=[pltpu.VMEM((NX * size, rows_total), BF)],
            limit=20,
            cost=5.0 if half else 0.05,
        )

    picked_other = swap_core(pick(1))
    weights_out = lax.all_gather(w_out, ("x", "c"), axis=0, tiled=False)
    picked_own = pick(0)
    line = list(call(pair_kernel, "pair", [((size, width), BF)] * NX, picked_other, picked_own, limit=8))
    line = [line[0]] + [swap_x(line[k], k) for k in range(1, NX)]
    w_uvqk, line[0] = lax.optimization_barrier((w_uvqk, line[0]))
    local_w = w_uvqk.reshape(width, -1)
    normed, crow = call(
        norm_kernel,
        "norm",
        [((block, width), BF), ((cblock, width), BF)],
        *line,
        limit=50,
    )
    own_other = swap_core(normed)
    far_w = swap_core(local_w)
    line[0], normed = lax.optimization_barrier((line[0], normed))
    rows = call(rows_kernel, "rows", [((block, width), BF)], *line, limit=50, cost=0.5)
    *normed_line, local_w, far_w, rows = lax.optimization_barrier(
        (*along_x(normed), crow, local_w, far_w, rows)
    )
    spread_rows = normed_line[:NX] + [own_other] + [swap_core(part) for part in normed_line[1:NX]]
    crows = lax.all_gather(normed_line[NX], ("x", "c"), axis=0, tiled=True)
    normed, pre, act, sent = call(
        attend_kernel,
        "attend",
        [((seq, width), BF), ((seq, 4 * HD), F32), ((seq, 4 * HD), BF), ((parts, block, 3 * HD), BF)],
        place,
        *spread_rows,
        local_w,
        smem=1,
        limit=52,
        far_outs=(0, 1, 2),
        scratch=[
            pltpu.VMEM((seq, width), BF),
            pltpu.VMEM((seq, 4 * HD), F32),
            pltpu.VMEM((seq, 4 * HD), BF),
            pltpu.SemaphoreType.DMA((3,)),
        ],
        cost=4.0,
    )
    sent = lax.all_to_all(sent, ("x", "c"), 0, 0)

    half = NX * HD
    back, dhidden, dcand, out_own, out_other = call(
        event_kernel,
        "event",
        [
            ((parts, block + 16, 2 * HD), BF),
            ((block, width), BF),
            ((ncand, width), BF),
            ((width, half), BF),
            ((width, half), BF),
        ],
        place,
        sent,
        rows,
        weights_out,
        crows,
        actions,
        targets,
        smem=1,
        limit=60,
        far=(3, 4),
        scratch=[
            pltpu.VMEM((width, width), BF),
            pltpu.VMEM((ncand, width), BF),
            pltpu.SemaphoreType.DMA((parts + 1,)),
        ],
        cost=4.0,
    )
    back = lax.all_to_all(back, ("x", "c"), 0, 0)
    out_other = swap_core(out_other)

    dcand = lax.psum_scatter(dcand, ("x", "c"), scatter_dimension=0, tiled=True)
    near, far, loss_meta, *grads = call(
        backward_kernel,
        "backward",
        [
            ((seq // 2, 4 * HD), BF),
            ((seq // 2, 4 * HD), BF),
            ((16, 128), BF),
            *[((width // NY, half + 4 * HD), BF)] * NY,
        ],
        place,
        back,
        act,
        pre,
        normed,
        out_own,
        out_other,
        smem=1,
        scratch=[
            pltpu.VMEM((seq, HD), BF),
            pltpu.VMEM((seq, HD), BF),
            pltpu.VMEM((seq, HD), F32),
            pltpu.VMEM((seq, 4 * HD), BF),
            pltpu.VMEM((seq, 4 * HD), BF),
            pltpu.VMEM((seq, 4 * HD), F32),
            pltpu.VMEM((seq, width), BF),
            pltpu.VMEM((width, half), BF),
            pltpu.VMEM((width, half), BF),
            pltpu.VMEM((width, half + 4 * HD), BF),
            pltpu.SemaphoreType.DMA((5,)),
        ],
        limit=60,
        far=(2, 3, 4, 5, 6),
        cost=6.0,
    )
    far_got = swap_core(far)
    grads = [grads[0]] + [
        lax.ppermute(grads[k], "y", [(i, i ^ k) for i in range(NY)]) for k in range(1, NY)
    ]
    line = list(
        call(
            part_kernel,
            "part",
            [((block, width), BF)] * NX,
            near,
            far_got,
            local_w,
            far_w,
            limit=50,
            cost=2.0,
        )
    )
    loss_meta, line[0] = lax.optimization_barrier((loss_meta, line[0]))
    meta = call(
        meta_kernel, "meta", [((16, 128), BF)], place, history, candidates, loss_meta, smem=1, limit=40
    )
    line = [line[0]] + [swap_x(line[k], k) for k in range(1, NX)]
    *line, grads[1] = lax.optimization_barrier((*line, grads[1]))
    grads = call(sum_kernel, "sum", [((width // NY, half + 4 * HD), BF)], *grads, limit=50, cost=1.0)
    line[0], grads = lax.optimization_barrier((line[0], grads))
    grads = lax.psum_scatter(grads.reshape(NZ, 32, -1), "z", scatter_dimension=0, tiled=False)

    packed = call(
        pack_kernel,
        "pack",
        [((users, 64, 128), BF)],
        *line,
        dcand,
        rows,
        dhidden,
        meta,
        limit=50,
    )
    arrived = lax.all_to_all(packed, ("y", "z"), 0, 0)
    got = arrived[:, 48:53].astype(F32)
    all_ids = (got[:, 0:2] * 128.0 + got[:, 2:4]).astype(jnp.int32).reshape(-1)
    own, other = call(
        scatter_kernel,
        "scatter",
        [((NX, 512, 128), BF)] * 2,
        all_ids,
        place,
        arrived,
        smem=2,
        scratch=[
            pltpu.VMEM((users * 48, 128), F32),
            pltpu.VMEM((parts * rows_total, 128), F32),
            pltpu.VMEM((parts * rows_total, 128), F32),
        ],
        limit=24,
        cost=12.0,
    )
    line = call(
        final_pair_kernel,
        "final_pair",
        [((512 + 32, 128), BF)] * NX,
        swap_core(other),
        own,
        grads,
        limit=8,
        cost=0.5,
    )
    line = [line[0]] + [swap_x(line[k], k) for k in range(1, NX)]
    shard_t, proj_t, grad_in = call(
        unpack_kernel,
        "unpack",
        [((32, rows_total), F32), ((32, HD), F32), ((32, 4 * HD), F32)],
        *line,
        grads,
        limit=8,
    )
    grad_in = grad_in.reshape(-1, 4, HD)
    loss = jnp.sum(got[:, 4, 0:3])
    return (loss, grad_in, proj_t.T, shard_t.T)


def solution(mesh):
    fine = Mesh(mesh.devices.reshape(NY, NZ, NX, NC), ("y", "z", "x", "c"))
    dp, item = ("y", "z"), ("x", "c")
    placed = (
        P(item, None),
        P(None, None, item),
        P(item, None),
        P(dp, None),
        P(dp),
        P(dp, None),
        P(dp),
        P(dp, None),
        P(dp, None),
    )
    return jax.shard_map(
        on_device,
        mesh=fine,
        in_specs=placed,
        out_specs=(P(), P(dp, None, item), P(item, dp), P(item, dp)),
        check_vma=False,
    )
```

```python
import functools

import jax
import jax.numpy as jnp
from jax import lax
from jax.experimental import pallas as pl
from jax.experimental.pallas import tpu as pltpu
from jax.sharding import Mesh, PartitionSpec as P

HD = 128
NX, NC, NY, NZ = 4, 2, 4, 8
CQL_WEIGHT = 0.5
BF = jnp.bfloat16
F32 = jnp.float32


def swap_x(value, k):
    return lax.ppermute(value, "x", [(i, i ^ k) for i in range(NX)])


def swap_core(value):
    return lax.ppermute(value, "c", [(0, 1), (1, 0)])


def event_slots(item, shape, axis):
    row = lax.broadcasted_iota(jnp.int32, shape, axis)
    return 32 * jnp.bitwise_and(row, 31) + 8 * (row // 32) + item


def cand_slots(item, shape, axis):
    row = lax.broadcasted_iota(jnp.int32, shape, axis)
    return 32 * jnp.bitwise_and(row, 15) + 8 * (row // 16) + item


def chosen(values, slots):
    cols = lax.broadcasted_iota(jnp.int32, (1, values.shape[1]), 1)
    return jnp.sum(jnp.where(cols == slots, values.astype(F32), 0.0), axis=1, keepdims=True)


def pick_kernel(half, place_ref, history_ref, cand_ref, table_ref, out_ref, hot_ref):
    total = table_ref.shape[0]
    first_row = (2 * place_ref[0] + place_ref[1]) * total
    size = out_ref.shape[1]
    for k in range(NX):
        item = item_of(place_ref, half * NX + k)
        events = chosen(history_ref[...], event_slots(item, (128, 1), 0))
        cands = chosen(cand_ref[...], cand_slots(item, (size - 128, 1), 0))
        for first, ids in ((0, events), (128, cands)):
            local = ids.astype(jnp.int32) - first_row
            count = ids.shape[0]
            for i in range(0, total, 512):
                cols = lax.broadcasted_iota(jnp.int32, (1, 512), 1) + i
                hot_ref[size * k + first : size * k + first + count, i : i + 512] = (
                    (local == cols).astype(F32).astype(BF)
                )
    for i in range(0, out_ref.shape[2], 256):
        found = jnp.dot(hot_ref[...], table_ref[:, i : i + 256], preferred_element_type=F32).astype(BF)
        for k in range(NX):
            out_ref[k, :, i : i + 256] = found[size * k : size * k + size, :]


def pair_kernel(a_ref, b_ref, *outs):
    for k, out in enumerate(outs):
        out[...] = (a_ref[k].astype(F32) + b_ref[k].astype(F32)).astype(BF)


def norm_kernel(a_ref, b_ref, c_ref, d_ref, normed_ref, crow_ref):
    refs = (a_ref, b_ref, c_ref, d_ref)
    block = normed_ref.shape[0]
    rows = sum(ref[:block, :].astype(F32) for ref in refs)
    scale = lax.rsqrt(jnp.mean(rows * rows, axis=-1, keepdims=True) + 1e-06)
    normed_ref[...] = (rows * scale).astype(BF)
    crow_ref[...] = sum(ref[block:, :].astype(F32) for ref in refs).astype(BF)


def rows_kernel(a_ref, b_ref, c_ref, d_ref, rows_ref):
    block = rows_ref.shape[0]
    rows_ref[...] = sum(ref[:block, :].astype(F32) for ref in (a_ref, b_ref, c_ref, d_ref)).astype(BF)


def item_of(place_ref, b):
    return 2 * jnp.bitwise_xor(place_ref[0], b % NX) + jnp.bitwise_xor(place_ref[1], b // NX)


def places_of(place_ref, shape, axis, first=0):
    row = lax.broadcasted_iota(jnp.int32, shape, axis) + first
    line = jnp.bitwise_and(row, 511)
    item = 2 * jnp.bitwise_xor(place_ref[0], line // 128) + jnp.bitwise_xor(place_ref[1], row // 512)
    inside = jnp.bitwise_and(row, 127)
    return 32 * jnp.bitwise_and(inside, 31) + 8 * (inside // 32) + item


def attend_kernel(
    place_ref, b0, b1, b2, b3, b4, b5, b6, b7, w_ref,
    normed_out, pre_out, act_out, sent_ref, normed_ref, pre_ref, act_ref, sems,
):
    for b, ref in enumerate((b0, b1, b2, b3, b4, b5, b6, b7)):
        normed_ref[128 * b : 128 * b + 128, :] = ref[...]
    copies = [pltpu.make_async_copy(normed_ref, normed_out, sems.at[0])]
    copies[0].start()
    seq = normed_ref.shape[0]
    for i in range(0, seq, 256):
        pre = jnp.dot(normed_ref[i : i + 256, :], w_ref[...], preferred_element_type=F32)
        pre_ref[i : i + 256, :] = pre
        act_ref[i : i + 256, :] = (pre * jax.nn.sigmoid(pre)).astype(BF)
    for i, (source, target) in enumerate(((pre_ref, pre_out), (act_ref, act_out))):
        copies.append(pltpu.make_async_copy(source, target, sems.at[i + 1]))
        copies[-1].start()
    length = place_ref[2]
    inverse = 1.0 / jnp.full((1, 1), length, jnp.int32).astype(F32)
    cols = places_of(place_ref, (1, seq), 1)
    cols = jnp.where(cols < length, cols, seq)
    for i in range(0, seq, 256):
        queries = act_ref[i : i + 256, 2 * HD : 3 * HD]
        logits = lax.dot_general(
            queries, act_ref[:, 3 * HD :], (((1,), (1,)), ((), ())), preferred_element_type=F32
        ) * HD ** (-0.5)
        rows = places_of(place_ref, (256, 1), 0, i)
        attn = jnp.where(cols <= rows, logits * jax.nn.sigmoid(logits), 0.0).astype(BF)
        mixed = jnp.dot(attn, act_ref[:, HD : 2 * HD], preferred_element_type=F32) * inverse
        top = mixed.astype(BF)
        rest = (mixed - top.astype(F32)).astype(BF)
        for h in range(2):
            b = i // 128 + h
            item = item_of(place_ref, b)
            sent_ref[item, :, 0:HD] = top[128 * h : 128 * h + 128, :]
            sent_ref[item, :, HD : 2 * HD] = rest[128 * h : 128 * h + 128, :]
            sent_ref[item, :, 2 * HD :] = act_ref[128 * b : 128 * b + 128, 0:HD]
    for copy in copies:
        copy.wait()


def split_loss(value, shape, row):
    value = jnp.broadcast_to(value, shape)
    top = value.astype(BF).astype(F32)
    middle = (value - top).astype(BF).astype(F32)
    low = value - top - middle
    lane = lax.broadcasted_iota(jnp.int32, shape, 1)
    picked = jnp.where(lane == 0, top, jnp.where(lane == 1, middle, jnp.where(lane == 2, low, 0.0)))
    return jnp.where(lax.broadcasted_iota(jnp.int32, shape, 0) == row, picked, 0.0).astype(BF)


def event_kernel(
    place_ref, sent_ref, rows_ref, w_ref, crows_ref, action_ref, target_ref,
    back_ref, dhidden_ref, dcand_ref, out_own_ref, out_other_ref,
    weight_ref, crow_ref, sems,
):
    copies = [
        pltpu.make_async_copy(
            w_ref.at[item_of(place_ref, b)], weight_ref.at[HD * b : HD * b + HD, :], sems.at[b]
        )
        for b in range(NX * NC)
    ]
    copies.append(pltpu.make_async_copy(crows_ref, crow_ref, sems.at[NX * NC]))
    for copy in copies:
        copy.start()
    owner = 2 * place_ref[0] + place_ref[1]
    length, count = place_ref[2], place_ref[3]
    block, width = rows_ref.shape
    seq = block * NX * NC
    items = [item_of(place_ref, b) for b in range(NX * NC)]
    mixed = jnp.concatenate(
        [sent_ref[i, :, 0:HD].astype(F32) + sent_ref[i, :, HD : 2 * HD].astype(F32) for i in items], axis=1
    )
    gate = jnp.concatenate([sent_ref[i, :, 2 * HD :] for i in items], axis=1).astype(F32)
    center = jnp.mean(mixed, axis=-1, keepdims=True)
    rstd = lax.rsqrt(jnp.mean(mixed * mixed, axis=-1, keepdims=True) - center * center + 1e-05)
    normo = (mixed - center) * rstd
    gated = (normo * gate).astype(BF)
    for copy in copies:
        copy.wait()
    weights = weight_ref[...]
    out = rows_ref[...].astype(F32) + jnp.dot(gated, weights, preferred_element_type=F32)
    hidden = out.astype(BF)
    crows = crow_ref[...]
    scores = lax.dot_general(hidden, crows, (((1,), (1,)), ((), ())), preferred_element_type=F32)
    col = lax.broadcasted_iota(jnp.int32, (1, crows.shape[0]), 1)
    inside = jnp.bitwise_and(col, 63)
    slots = 32 * jnp.bitwise_and(inside, 15) + 8 * (inside // 16) + col // 64
    masked = jnp.where(slots < count, scores, -jnp.inf)
    top = jnp.max(masked, axis=-1, keepdims=True)
    expo = jnp.exp(masked - top)
    total = jnp.sum(expo, axis=-1, keepdims=True)
    soft = expo / total
    lse = top + jnp.log(total)
    places = event_slots(owner, (block, 1), 0)
    actions = chosen(action_ref[...], places).astype(jnp.int32)
    onehot = (slots == actions).astype(F32)
    taken = jnp.sum(scores * onehot, axis=-1, keepdims=True)
    live = jnp.where(places < length, 1.0 / seq, 0.0)
    miss = taken - chosen(target_ref[...], places)
    loss = jnp.sum(live * (CQL_WEIGHT * (lse - taken) + 0.5 * miss * miss), axis=0, keepdims=True)
    loss = split_loss(loss, (16, 2 * HD), 0)
    dscore = (live * (CQL_WEIGHT * soft + (miss - CQL_WEIGHT) * onehot)).astype(BF)
    dhidden = jnp.dot(dscore, crows, preferred_element_type=F32).astype(BF)
    dhidden_ref[...] = dhidden
    dgated = lax.dot_general(
        dhidden, weights, (((1,), (1,)), ((), ())), preferred_element_type=F32
    )
    dnormo = dgated * gate
    first = jnp.mean(dnormo, axis=-1, keepdims=True)
    second = jnp.mean(dnormo * normo, axis=-1, keepdims=True)
    dmixed = (rstd * (dnormo - first - normo * second)).astype(BF)
    du = (dgated * normo).astype(BF)
    for b, i in enumerate(items):
        back_ref[i, 0:block, 0:HD] = dmixed[:, HD * b : HD * b + HD]
        back_ref[i, 0:block, HD:] = du[:, HD * b : HD * b + HD]
        back_ref[i, block:, :] = loss
    turned = (((0,), (0,)), ((), ()))
    half = NX * HD
    out_other_ref[...] = lax.dot_general(
        dhidden, gated[:, half:], turned, preferred_element_type=F32
    ).astype(BF)
    out_own_ref[...] = lax.dot_general(
        dhidden, gated[:, :half], turned, preferred_element_type=F32
    ).astype(BF)
    dcand_ref[...] = lax.dot_general(dscore, hidden, turned, preferred_element_type=F32).astype(BF)


def backward_kernel(
    place_ref, back_ref, act_in, pre_in, normed_in, out_own_in, out_other_in,
    near_ref, far_ref, loss_ref, g0, g1, g2, g3,
    dm_ref, du_ref, dq_ref, dpre_ref, act_ref, pre_ref, normed_ref, own_ref, other_ref, grads_ref, sems,
):
    copies = [
        pltpu.make_async_copy(source, target, sems.at[i])
        for i, (source, target) in enumerate(
            (
                (act_in, act_ref),
                (pre_in, pre_ref),
                (normed_in, normed_ref),
                (out_own_in, own_ref),
                (out_other_in, other_ref),
            )
        )
    ]
    for copy in copies:
        copy.start()
    seq = act_ref.shape[0]
    loss = jnp.zeros((16, 2 * HD), F32)
    for b in range(8):
        item = item_of(place_ref, b)
        dm_ref[128 * b : 128 * b + 128, :] = back_ref[item, 0:128, 0:HD]
        du_ref[128 * b : 128 * b + 128, :] = back_ref[item, 0:128, HD:]
        loss = loss + back_ref[item, 128:144, :].astype(F32)
    loss = jnp.sum(jnp.sum(loss, axis=1, keepdims=True), axis=0, keepdims=True)
    loss_ref[...] = split_loss(loss, (16, 128), 4)
    length = place_ref[2]
    inverse = 1.0 / jnp.full((1, 1), length, jnp.int32).astype(F32)
    cols = places_of(place_ref, (1, seq), 1)
    across = (((1,), (1,)), ((), ()))
    dq_ref[...] = jnp.zeros(dq_ref.shape, F32)

    def slope(value, sigma):
        return sigma * (1.0 + value * (1.0 - sigma))

    copies[0].wait()
    for i in range(0, seq, 256):
        keys = act_ref[i : i + 256, 3 * HD :]
        logits = lax.dot_general(
            keys, act_ref[:, 2 * HD : 3 * HD], across, preferred_element_type=F32
        ) * HD ** (-0.5)
        rows = places_of(place_ref, (256, 1), 0, i)
        rows = jnp.where(rows < length, rows, seq)
        sigma = jnp.where(rows <= cols, jax.nn.sigmoid(logits), 0.0)
        swish = logits * sigma
        attn = swish.astype(BF)
        dattn = lax.dot_general(
            act_ref[i : i + 256, HD : 2 * HD], dm_ref[...], across, preferred_element_type=F32
        )
        dlogits = (dattn * (sigma + swish * (1.0 - sigma))).astype(BF)
        dvalues = jnp.dot(attn, dm_ref[...], preferred_element_type=F32) * inverse
        dkeys = jnp.dot(dlogits, act_ref[:, 2 * HD : 3 * HD], preferred_element_type=F32) * (
            inverse * HD ** (-0.5)
        )
        dq_ref[...] += lax.dot_general(
            dlogits, keys, (((0,), (0,)), ((), ())), preferred_element_type=F32
        )
        if i == 0:
            copies[1].wait()
        for j, grad in ((1, dvalues), (3, dkeys)):
            pre = pre_ref[i : i + 256, HD * j : HD * j + HD]
            dpre_ref[i : i + 256, HD * j : HD * j + HD] = (
                grad * slope(pre, jax.nn.sigmoid(pre))
            ).astype(BF)
    dq_ref[...] = dq_ref[...] * (inverse * HD ** (-0.5))
    for j, ref in ((0, du_ref), (2, dq_ref)):
        pre = pre_ref[:, HD * j : HD * j + HD]
        dpre_ref[:, HD * j : HD * j + HD] = (
            ref[...].astype(F32) * slope(pre, jax.nn.sigmoid(pre))
        ).astype(BF)
    near_ref[...] = dpre_ref[: near_ref.shape[0], :]
    far_ref[...] = dpre_ref[near_ref.shape[0] :, :]
    for copy in copies[2:]:
        copy.wait()
    half = own_ref.shape[1]
    grads_ref[:, :half] = (own_ref[...].astype(F32) + other_ref[...].astype(F32)).astype(BF)
    grads_ref[:, half:] = lax.dot_general(
        normed_ref[...], dpre_ref[...], (((0,), (0,)), ((), ())), preferred_element_type=F32
    ).astype(BF)
    size = g0.shape[0]
    for k, ref in enumerate((g0, g1, g2, g3)):
        start = jnp.bitwise_xor(place_ref[4], k) * size
        ref[...] = grads_ref[pl.ds(pl.multiple_of(start, size), size), :]


def part_kernel(near_ref, far_ref, w_ref, far_w_ref, *outs):
    across = (((1,), (1,)), ((), ()))
    for h in range(2):
        rows = slice(256 * h, 256 * h + 256)
        part = lax.dot_general(near_ref[rows, :], w_ref[...], across, preferred_element_type=F32)
        part = part + lax.dot_general(
            far_ref[rows, :], far_w_ref[...], across, preferred_element_type=F32
        )
        part = part.astype(BF)
        outs[2 * h][...] = part[:128, :]
        outs[2 * h + 1][...] = part[128:, :]


def meta_kernel(place_ref, history_ref, cands_ref, loss_ref, meta_ref):
    owner = 2 * place_ref[0] + place_ref[1]

    def digits(values, wanted):
        row = lax.broadcasted_iota(jnp.int32, (16, values.shape[1]), 0)
        upper, lower = values // 128, jnp.bitwise_and(values, 127)
        both = jnp.where(row == 0, upper, jnp.where(row == 2, lower, 0)).astype(F32).astype(BF)
        source = lax.broadcasted_iota(jnp.int32, (values.shape[1], 128), 0)
        hot = (source == wanted).astype(F32).astype(BF)
        return jnp.dot(both, hot, preferred_element_type=F32)

    lane = lax.broadcasted_iota(jnp.int32, (16, 128), 1)
    row = lax.broadcasted_iota(jnp.int32, (16, 128), 0)
    events = digits(history_ref[...], event_slots(owner, (1, 128), 1))
    wanted = cand_slots(owner, (1, 128), 1)
    wanted = jnp.where(lax.broadcasted_iota(jnp.int32, (1, 128), 1) < 64, wanted, -1)
    cands = pltpu.roll(digits(cands_ref[...], wanted), 1, 0)
    meta = events + cands + loss_ref[...].astype(F32)
    for where, value in ((64, place_ref[2]), (65, place_ref[3])):
        for r, part in ((1, value // 128), (3, jnp.bitwise_and(value, 127))):
            part = jnp.full((16, 128), part, jnp.int32).astype(F32)
            meta = jnp.where((lane == where) & (row == r), part, meta)
    meta_ref[...] = meta.astype(BF)


def pack_kernel(a_ref, b_ref, c_ref, d_ref, dcand_ref, rows_ref, dhidden_ref, meta_ref, out_ref):
    refs = (a_ref, b_ref, c_ref, d_ref)
    dnormed = sum(ref[...].astype(F32) for ref in refs)
    rows = rows_ref[...].astype(F32)
    scale = lax.rsqrt(jnp.mean(rows * rows, axis=-1, keepdims=True) + 1e-06)
    normed = rows * scale
    drows = dhidden_ref[...].astype(F32) + scale * (
        dnormed - normed * jnp.mean(dnormed * normed, axis=-1, keepdims=True)
    )
    drows = drows.astype(BF)
    dcand = dcand_ref[...]
    meta = meta_ref[...]
    for d in range(out_ref.shape[0]):
        out_ref[d, 0:32, :] = jnp.concatenate(
            [drows[32 * g : 32 * g + 32, 32 * d : 32 * d + 32] for g in range(4)], axis=1
        )
        out_ref[d, 32:48, :] = jnp.concatenate(
            [dcand[16 * g : 16 * g + 16, 32 * d : 32 * d + 32] for g in range(4)], axis=1
        )
        out_ref[d, 48:64, :] = meta


def scatter_kernel(ids_ref, place_ref, data_ref, own_ref, other_ref, rows_ref, acc_ref, more_ref):
    users = data_ref.shape[0]
    total = acc_ref.shape[0]
    chunk = 512
    owner = 2 * place_ref[0] + place_ref[1]

    def clear(i, carry):
        here = pl.ds(pl.multiple_of(i * chunk, chunk), chunk)
        acc_ref[here, :] = jnp.zeros((chunk, 128), F32)
        more_ref[here, :] = jnp.zeros((chunk, 128), F32)
        return carry

    lax.fori_loop(0, total // chunk, clear, 0)
    for u in range(users):
        rows_ref[48 * u : 48 * u + 48, :] = data_ref[u, 0:48, :].astype(F32)
    lane = lax.broadcasted_iota(jnp.int32, (1, 128), 1) // 32
    masks = [lane == g for g in range(4)]

    def add(first_id, pitch, first_row, count):
        def step(i, carry):
            for j in range(2):
                work = []
                for half, ref in ((0, acc_ref), (1, more_ref)):
                    p = i * 4 + j * 2 + half
                    row = rows_ref[pl.ds(first_row + p, 1), :]
                    ids = [ids_ref[first_id + g * pitch + p] for g in range(4)]
                    work.append((ref, row, ids, [ref[pl.ds(ids[g], 1), :] for g in range(4)]))
                for ref, row, ids, held in work:
                    for g in range(4):
                        pltpu.store(ref.at[pl.ds(ids[g], 1), :], held[g] + row, mask=masks[g])
            return carry

        lax.fori_loop(0, (count + 3) // 4, step, 0)

    def user(u, carry):
        base = u * 256
        events = jnp.clip((ids_ref[base + 192] - owner + 31) // 32, 0, 32)
        cands = jnp.clip((ids_ref[base + 193] - owner + 31) // 32, 0, 16)
        add(base, 32, u * 48, events)
        add(base + 128, 16, u * 48 + 32, cands)
        return carry

    lax.fori_loop(0, users, user, 0)
    wide = lax.broadcasted_iota(jnp.int32, (512, 128), 1) // 32
    for cc in range(2):
        for k in range(4):
            item = item_of(place_ref, cc * NX + k)
            result = jnp.zeros((512, 128), F32)
            for q in range(4):
                here = pl.ds(pl.multiple_of(item * 2048 + q * 512, 512), 512)
                part = acc_ref[here, :] + more_ref[here, :]
                part = part + pltpu.roll(part, 64, 1)
                part = part + pltpu.roll(part, 32, 1)
                result = jnp.where(wide == q, part, result)
            (own_ref, other_ref)[cc][k] = result.astype(BF)


def sum_kernel(a_ref, b_ref, c_ref, d_ref, out_ref):
    out_ref[...] = sum(ref[...].astype(F32) for ref in (a_ref, b_ref, c_ref, d_ref)).astype(BF)


def final_pair_kernel(a_ref, b_ref, grads_ref, *outs):
    for k, out in enumerate(outs):
        out[:512, :] = (a_ref[k].astype(F32) + b_ref[k].astype(F32)).astype(BF)
        out[512:, :] = grads_ref[:, HD * k : HD * k + HD]


def unpack_kernel(a_ref, b_ref, c_ref, d_ref, grads_ref, out_ref, proj_ref, in_ref):
    refs = (a_ref, b_ref, c_ref, d_ref)
    proj_ref[...] = sum(ref[512:, :].astype(F32) for ref in refs)
    turned = sum(ref[:512, :].astype(F32) for ref in refs).T
    for q in range(4):
        out_ref[:, q * 512 : (q + 1) * 512] = turned[32 * q : 32 * q + 32, :]
    in_ref[...] = grads_ref[:, NX * HD :].astype(F32)


def whole(count, smem=0):
    specs = [pl.BlockSpec(memory_space=pltpu.SMEM)] * smem
    return specs + [pl.BlockSpec(memory_space=pltpu.VMEM)] * count


def call(kernel, name, outs, *args, smem=0, scratch=(), limit=32, far=(), far_outs=(), cost=1.0):
    outs = tuple(jax.ShapeDtypeStruct(shape, dtype) for shape, dtype in outs)
    hbm = pl.BlockSpec(memory_space=pltpu.HBM)
    specs = [hbm if i in far_outs else whole(1)[0] for i in range(len(outs))]
    in_specs = [hbm if i in far else spec for i, spec in enumerate(whole(len(args) - smem, smem))]
    return pl.pallas_call(
        kernel,
        out_shape=outs if len(outs) > 1 else outs[0],
        in_specs=in_specs,
        out_specs=tuple(specs) if len(outs) > 1 else specs[0],
        scratch_shapes=list(scratch),
        compiler_params=pltpu.CompilerParams(vmem_limit_bytes=int(limit * 1024 * 1024)),
        cost_estimate=pl.CostEstimate(
            flops=int(cost * 1.1e9), bytes_accessed=int(cost * 3.6e6), transcendentals=0
        ),
        name=name,
    )(*args)


def on_device(table, w_uvqk, w_out, history, lengths, candidates, counts, actions, targets):
    rows_total, width = table.shape
    seq = history.shape[1]
    ncand = candidates.shape[1]
    users = NY * NZ
    parts = NX * NC
    block = seq // parts
    cblock = ncand // parts
    x, c = lax.axis_index("x"), lax.axis_index("c")
    length = lengths[0]

    place = jnp.stack([x, c, length, counts[0], lax.axis_index("y")]).astype(jnp.int32)

    def along_x(own):
        return [own] + [swap_x(own, k) for k in range(1, NX)]

    size = block + cblock

    def pick(half):
        return call(
            functools.partial(pick_kernel, half),
            "pick",
            [((NX, size, width), BF)],
            place,
            history,
            candidates,
            table,
            smem=1,
            scratch=[pltpu.VMEM((NX * size, rows_total), BF)],
            limit=20,
            cost=5.0 if half else 0.05,
        )

    picked_other = swap_core(pick(1))
    weights_out = lax.all_gather(w_out, ("x", "c"), axis=0, tiled=False)
    picked_own = pick(0)
    line = list(call(pair_kernel, "pair", [((size, width), BF)] * NX, picked_other, picked_own, limit=8))
    line = [line[0]] + [swap_x(line[k], k) for k in range(1, NX)]
    w_uvqk, line[0] = lax.optimization_barrier((w_uvqk, line[0]))
    local_w = w_uvqk.reshape(width, -1)
    normed, crow = call(
        norm_kernel,
        "norm",
        [((block, width), BF), ((cblock, width), BF)],
        *line,
        limit=50,
    )
    own_other = swap_core(normed)
    far_w = swap_core(local_w)
    line[0], normed = lax.optimization_barrier((line[0], normed))
    rows = call(rows_kernel, "rows", [((block, width), BF)], *line, limit=50, cost=0.5)
    *normed_line, local_w, far_w, rows = lax.optimization_barrier(
        (*along_x(normed), crow, local_w, far_w, rows)
    )
    spread_rows = normed_line[:NX] + [own_other] + [swap_core(part) for part in normed_line[1:NX]]
    crows = lax.all_gather(normed_line[NX], ("x", "c"), axis=0, tiled=True)
    normed, pre, act, sent = call(
        attend_kernel,
        "attend",
        [((seq, width), BF), ((seq, 4 * HD), F32), ((seq, 4 * HD), BF), ((parts, block, 3 * HD), BF)],
        place,
        *spread_rows,
        local_w,
        smem=1,
        limit=52,
        far_outs=(0, 1, 2),
        scratch=[
            pltpu.VMEM((seq, width), BF),
            pltpu.VMEM((seq, 4 * HD), F32),
            pltpu.VMEM((seq, 4 * HD), BF),
            pltpu.SemaphoreType.DMA((3,)),
        ],
        cost=4.0,
    )
    sent = lax.all_to_all(sent, ("x", "c"), 0, 0)

    half = NX * HD
    back, dhidden, dcand, out_own, out_other = call(
        event_kernel,
        "event",
        [
            ((parts, block + 16, 2 * HD), BF),
            ((block, width), BF),
            ((ncand, width), BF),
            ((width, half), BF),
            ((width, half), BF),
        ],
        place,
        sent,
        rows,
        weights_out,
        crows,
        actions,
        targets,
        smem=1,
        limit=60,
        far=(3, 4),
        scratch=[
            pltpu.VMEM((width, width), BF),
            pltpu.VMEM((ncand, width), BF),
            pltpu.SemaphoreType.DMA((parts + 1,)),
        ],
        cost=4.0,
    )
    back = lax.all_to_all(back, ("x", "c"), 0, 0)
    out_other = swap_core(out_other)

    dcand = lax.psum_scatter(dcand, ("x", "c"), scatter_dimension=0, tiled=True)
    near, far, loss_meta, *grads = call(
        backward_kernel,
        "backward",
        [
            ((seq // 2, 4 * HD), BF),
            ((seq // 2, 4 * HD), BF),
            ((16, 128), BF),
            *[((width // NY, half + 4 * HD), BF)] * NY,
        ],
        place,
        back,
        act,
        pre,
        normed,
        out_own,
        out_other,
        smem=1,
        scratch=[
            pltpu.VMEM((seq, HD), BF),
            pltpu.VMEM((seq, HD), BF),
            pltpu.VMEM((seq, HD), F32),
            pltpu.VMEM((seq, 4 * HD), BF),
            pltpu.VMEM((seq, 4 * HD), BF),
            pltpu.VMEM((seq, 4 * HD), F32),
            pltpu.VMEM((seq, width), BF),
            pltpu.VMEM((width, half), BF),
            pltpu.VMEM((width, half), BF),
            pltpu.VMEM((width, half + 4 * HD), BF),
            pltpu.SemaphoreType.DMA((5,)),
        ],
        limit=60,
        far=(2, 3, 4, 5, 6),
        cost=6.0,
    )
    far_got = swap_core(far)
    grads = [grads[0]] + [
        lax.ppermute(grads[k], "y", [(i, i ^ k) for i in range(NY)]) for k in range(1, NY)
    ]
    grads = call(sum_kernel, "sum", [((width // NY, half + 4 * HD), BF)], *grads, limit=50, cost=1.0)
    line = list(
        call(
            part_kernel,
            "part",
            [((block, width), BF)] * NX,
            near,
            far_got,
            local_w,
            far_w,
            limit=50,
            cost=2.0,
        )
    )
    loss_meta, line[0] = lax.optimization_barrier((loss_meta, line[0]))
    meta = call(
        meta_kernel, "meta", [((16, 128), BF)], place, history, candidates, loss_meta, smem=1, limit=40
    )
    far_first = [swap_x(line[k], k) for k in (3, 2, 1)]
    line = [line[0]] + far_first
    line[0], grads = lax.optimization_barrier((line[0], grads))
    grads = lax.psum_scatter(grads.reshape(NZ, 32, -1), "z", scatter_dimension=0, tiled=False)

    packed = call(
        pack_kernel,
        "pack",
        [((users, 64, 128), BF)],
        *line,
        dcand,
        rows,
        dhidden,
        meta,
        limit=50,
    )
    arrived = lax.all_to_all(packed, ("y", "z"), 0, 0)
    got = arrived[:, 48:53].astype(F32)
    all_ids = (got[:, 0:2] * 128.0 + got[:, 2:4]).astype(jnp.int32).reshape(-1)
    own, other = call(
        scatter_kernel,
        "scatter",
        [((NX, 512, 128), BF)] * 2,
        all_ids,
        place,
        arrived,
        smem=2,
        scratch=[
            pltpu.VMEM((users * 48, 128), F32),
            pltpu.VMEM((parts * rows_total, 128), F32),
            pltpu.VMEM((parts * rows_total, 128), F32),
        ],
        limit=24,
        cost=12.0,
    )
    line = call(
        final_pair_kernel,
        "final_pair",
        [((512 + 32, 128), BF)] * NX,
        swap_core(other),
        own,
        grads,
        limit=8,
        cost=0.5,
    )
    line = [line[0]] + [swap_x(line[k], k) for k in range(1, NX)]
    shard_t, proj_t, grad_in = call(
        unpack_kernel,
        "unpack",
        [((32, rows_total), F32), ((32, HD), F32), ((32, 4 * HD), F32)],
        *line,
        grads,
        limit=8,
    )
    grad_in = grad_in.reshape(-1, 4, HD)
    loss = jnp.sum(got[:, 4, 0:3])
    return (loss, grad_in, proj_t.T, shard_t.T)


def solution(mesh):
    fine = Mesh(mesh.devices.reshape(NY, NZ, NX, NC), ("y", "z", "x", "c"))
    dp, item = ("y", "z"), ("x", "c")
    placed = (
        P(item, None),
        P(None, None, item),
        P(item, None),
        P(dp, None),
        P(dp),
        P(dp, None),
        P(dp),
        P(dp, None),
        P(dp, None),
    )
    return jax.shard_map(
        on_device,
        mesh=fine,
        in_specs=placed,
        out_specs=(P(), P(dp, None, item), P(item, dp), P(item, dp)),
        check_vma=False,
    )
```

```python
import functools

import jax
import jax.numpy as jnp
from jax import lax
from jax.experimental import pallas as pl
from jax.experimental.pallas import tpu as pltpu
from jax.sharding import Mesh, PartitionSpec as P

HD = 128
NX, NC, NY, NZ = 4, 2, 4, 8
CQL_WEIGHT = 0.5
BF = jnp.bfloat16
F32 = jnp.float32


def swap_x(value, k):
    return lax.ppermute(value, "x", [(i, i ^ k) for i in range(NX)])


def swap_core(value):
    return lax.ppermute(value, "c", [(0, 1), (1, 0)])


def event_slots(item, shape, axis):
    row = lax.broadcasted_iota(jnp.int32, shape, axis)
    return 32 * jnp.bitwise_and(row, 31) + 8 * (row // 32) + item


def cand_slots(item, shape, axis):
    row = lax.broadcasted_iota(jnp.int32, shape, axis)
    return 32 * jnp.bitwise_and(row, 15) + 8 * (row // 16) + item


def chosen(values, slots):
    cols = lax.broadcasted_iota(jnp.int32, (1, values.shape[1]), 1)
    return jnp.sum(jnp.where(cols == slots, values.astype(F32), 0.0), axis=1, keepdims=True)


def pick_kernel(half, place_ref, history_ref, cand_ref, table_ref, out_ref, hot_ref):
    total = table_ref.shape[0]
    first_row = (2 * place_ref[0] + place_ref[1]) * total
    size = out_ref.shape[1]
    for k in range(NX):
        item = item_of(place_ref, half * NX + k)
        events = chosen(history_ref[...], event_slots(item, (128, 1), 0))
        cands = chosen(cand_ref[...], cand_slots(item, (size - 128, 1), 0))
        for first, ids in ((0, events), (128, cands)):
            local = ids.astype(jnp.int32) - first_row
            count = ids.shape[0]
            for i in range(0, total, 512):
                cols = lax.broadcasted_iota(jnp.int32, (1, 512), 1) + i
                hot_ref[size * k + first : size * k + first + count, i : i + 512] = (
                    (local == cols).astype(F32).astype(BF)
                )
    for i in range(0, out_ref.shape[2], 256):
        found = jnp.dot(hot_ref[...], table_ref[:, i : i + 256], preferred_element_type=F32).astype(BF)
        for k in range(NX):
            out_ref[k, :, i : i + 256] = found[size * k : size * k + size, :]


def pair_kernel(a_ref, b_ref, *outs):
    for k, out in enumerate(outs):
        out[...] = (a_ref[k].astype(F32) + b_ref[k].astype(F32)).astype(BF)


def norm_kernel(a_ref, b_ref, c_ref, d_ref, normed_ref, crow_ref):
    refs = (a_ref, b_ref, c_ref, d_ref)
    block = normed_ref.shape[0]
    rows = sum(ref[:block, :].astype(F32) for ref in refs)
    scale = lax.rsqrt(jnp.mean(rows * rows, axis=-1, keepdims=True) + 1e-06)
    normed_ref[...] = (rows * scale).astype(BF)
    crow_ref[...] = sum(ref[block:, :].astype(F32) for ref in refs).astype(BF)


def rows_kernel(a_ref, b_ref, c_ref, d_ref, rows_ref):
    block = rows_ref.shape[0]
    rows_ref[...] = sum(ref[:block, :].astype(F32) for ref in (a_ref, b_ref, c_ref, d_ref)).astype(BF)


def item_of(place_ref, b):
    return 2 * jnp.bitwise_xor(place_ref[0], b % NX) + jnp.bitwise_xor(place_ref[1], b // NX)


def places_of(place_ref, shape, axis, first=0):
    row = lax.broadcasted_iota(jnp.int32, shape, axis) + first
    line = jnp.bitwise_and(row, 511)
    item = 2 * jnp.bitwise_xor(place_ref[0], line // 128) + jnp.bitwise_xor(place_ref[1], row // 512)
    inside = jnp.bitwise_and(row, 127)
    return 32 * jnp.bitwise_and(inside, 31) + 8 * (inside // 32) + item


def attend_kernel(
    place_ref, b0, b1, b2, b3, b4, b5, b6, b7, w_ref,
    normed_out, pre_out, act_out, sent_ref, normed_ref, pre_ref, act_ref, sems,
):
    for b, ref in enumerate((b0, b1, b2, b3, b4, b5, b6, b7)):
        normed_ref[128 * b : 128 * b + 128, :] = ref[...]
    copies = [pltpu.make_async_copy(normed_ref, normed_out, sems.at[0])]
    copies[0].start()
    seq = normed_ref.shape[0]
    for i in range(0, seq, 256):
        pre = jnp.dot(normed_ref[i : i + 256, :], w_ref[...], preferred_element_type=F32)
        pre_ref[i : i + 256, :] = pre
        act_ref[i : i + 256, :] = (pre * jax.nn.sigmoid(pre)).astype(BF)
    for i, (source, target) in enumerate(((pre_ref, pre_out), (act_ref, act_out))):
        copies.append(pltpu.make_async_copy(source, target, sems.at[i + 1]))
        copies[-1].start()
    length = place_ref[2]
    inverse = 1.0 / jnp.full((1, 1), length, jnp.int32).astype(F32)
    cols = places_of(place_ref, (1, seq), 1)
    cols = jnp.where(cols < length, cols, seq)
    for i in range(0, seq, 256):
        queries = act_ref[i : i + 256, 2 * HD : 3 * HD]
        logits = lax.dot_general(
            queries, act_ref[:, 3 * HD :], (((1,), (1,)), ((), ())), preferred_element_type=F32
        ) * HD ** (-0.5)
        rows = places_of(place_ref, (256, 1), 0, i)
        attn = jnp.where(cols <= rows, logits * jax.nn.sigmoid(logits), 0.0).astype(BF)
        mixed = jnp.dot(attn, act_ref[:, HD : 2 * HD], preferred_element_type=F32) * inverse
        top = mixed.astype(BF)
        rest = (mixed - top.astype(F32)).astype(BF)
        for h in range(2):
            b = i // 128 + h
            item = item_of(place_ref, b)
            sent_ref[item, :, 0:HD] = top[128 * h : 128 * h + 128, :]
            sent_ref[item, :, HD : 2 * HD] = rest[128 * h : 128 * h + 128, :]
            sent_ref[item, :, 2 * HD :] = act_ref[128 * b : 128 * b + 128, 0:HD]
    for copy in copies:
        copy.wait()


def split_loss(value, shape, row):
    value = jnp.broadcast_to(value, shape)
    top = value.astype(BF).astype(F32)
    middle = (value - top).astype(BF).astype(F32)
    low = value - top - middle
    lane = lax.broadcasted_iota(jnp.int32, shape, 1)
    picked = jnp.where(lane == 0, top, jnp.where(lane == 1, middle, jnp.where(lane == 2, low, 0.0)))
    return jnp.where(lax.broadcasted_iota(jnp.int32, shape, 0) == row, picked, 0.0).astype(BF)


def event_kernel(
    place_ref, sent_ref, rows_ref, w_ref, crows_ref, action_ref, target_ref,
    back_ref, dhidden_ref, dcand_ref, near_ref, far_ref,
    weight_ref, crow_ref, sems,
):
    copies = [
        pltpu.make_async_copy(
            w_ref.at[item_of(place_ref, b)], weight_ref.at[HD * b : HD * b + HD, :], sems.at[b]
        )
        for b in range(NX * NC)
    ]
    copies.append(pltpu.make_async_copy(crows_ref, crow_ref, sems.at[NX * NC]))
    for copy in copies:
        copy.start()
    owner = 2 * place_ref[0] + place_ref[1]
    length, count = place_ref[2], place_ref[3]
    block, width = rows_ref.shape
    seq = block * NX * NC
    items = [item_of(place_ref, b) for b in range(NX * NC)]
    mixed = jnp.concatenate(
        [sent_ref[i, :, 0:HD].astype(F32) + sent_ref[i, :, HD : 2 * HD].astype(F32) for i in items], axis=1
    )
    gate = jnp.concatenate([sent_ref[i, :, 2 * HD :] for i in items], axis=1).astype(F32)
    center = jnp.mean(mixed, axis=-1, keepdims=True)
    rstd = lax.rsqrt(jnp.mean(mixed * mixed, axis=-1, keepdims=True) - center * center + 1e-05)
    normo = (mixed - center) * rstd
    gated = (normo * gate).astype(BF)
    for copy in copies:
        copy.wait()
    weights = weight_ref[...]
    out = rows_ref[...].astype(F32) + jnp.dot(gated, weights, preferred_element_type=F32)
    hidden = out.astype(BF)
    crows = crow_ref[...]
    scores = lax.dot_general(hidden, crows, (((1,), (1,)), ((), ())), preferred_element_type=F32)
    col = lax.broadcasted_iota(jnp.int32, (1, crows.shape[0]), 1)
    inside = jnp.bitwise_and(col, 63)
    slots = 32 * jnp.bitwise_and(inside, 15) + 8 * (inside // 16) + col // 64
    masked = jnp.where(slots < count, scores, -jnp.inf)
    top = jnp.max(masked, axis=-1, keepdims=True)
    expo = jnp.exp(masked - top)
    total = jnp.sum(expo, axis=-1, keepdims=True)
    soft = expo / total
    lse = top + jnp.log(total)
    places = event_slots(owner, (block, 1), 0)
    actions = chosen(action_ref[...], places).astype(jnp.int32)
    onehot = (slots == actions).astype(F32)
    taken = jnp.sum(scores * onehot, axis=-1, keepdims=True)
    live = jnp.where(places < length, 1.0 / seq, 0.0)
    miss = taken - chosen(target_ref[...], places)
    loss = jnp.sum(live * (CQL_WEIGHT * (lse - taken) + 0.5 * miss * miss), axis=0, keepdims=True)
    loss = split_loss(loss, (16, 2 * HD), 0)
    dscore = (live * (CQL_WEIGHT * soft + (miss - CQL_WEIGHT) * onehot)).astype(BF)
    dhidden = jnp.dot(dscore, crows, preferred_element_type=F32).astype(BF)
    dhidden_ref[...] = dhidden
    dgated = lax.dot_general(
        dhidden, weights, (((1,), (1,)), ((), ())), preferred_element_type=F32
    )
    dnormo = dgated * gate
    first = jnp.mean(dnormo, axis=-1, keepdims=True)
    second = jnp.mean(dnormo * normo, axis=-1, keepdims=True)
    dmixed = (rstd * (dnormo - first - normo * second)).astype(BF)
    du = (dgated * normo).astype(BF)
    for b, i in enumerate(items):
        back_ref[i, 0:block, 0:HD] = dmixed[:, HD * b : HD * b + HD]
        back_ref[i, 0:block, HD:] = du[:, HD * b : HD * b + HD]
        back_ref[i, block:, :] = loss
    turned = (((0,), (0,)), ((), ()))
    half = NX * HD
    near_ref[...] = gated[:, :half]
    far_ref[:, :width] = dhidden
    far_ref[:, width:] = gated[:, half:]
    dcand_ref[...] = lax.dot_general(dscore, hidden, turned, preferred_element_type=F32).astype(BF)


def backward_kernel(
    place_ref, back_ref, act_in, pre_in, normed_in, dhidden_in, own_in, other_in,
    near_ref, far_ref, loss_ref, grads_ref,
    dm_ref, du_ref, dq_ref, dpre_ref, act_ref, pre_ref, normed_ref, dhidden_ref, own_ref, other_ref, sems,
):
    copies = [
        pltpu.make_async_copy(source, target, sems.at[i])
        for i, (source, target) in enumerate(
            (
                (act_in, act_ref),
                (pre_in, pre_ref),
                (normed_in, normed_ref),
                (dhidden_in, dhidden_ref),
                (own_in, own_ref),
                (other_in, other_ref),
            )
        )
    ]
    for copy in copies:
        copy.start()
    seq = act_ref.shape[0]
    loss = jnp.zeros((16, 2 * HD), F32)
    for b in range(8):
        item = item_of(place_ref, b)
        dm_ref[128 * b : 128 * b + 128, :] = back_ref[item, 0:128, 0:HD]
        du_ref[128 * b : 128 * b + 128, :] = back_ref[item, 0:128, HD:]
        loss = loss + back_ref[item, 128:144, :].astype(F32)
    loss = jnp.sum(jnp.sum(loss, axis=1, keepdims=True), axis=0, keepdims=True)
    loss_ref[...] = split_loss(loss, (16, 128), 4)
    length = place_ref[2]
    inverse = 1.0 / jnp.full((1, 1), length, jnp.int32).astype(F32)
    cols = places_of(place_ref, (1, seq), 1)
    across = (((1,), (1,)), ((), ()))
    dq_ref[...] = jnp.zeros(dq_ref.shape, F32)

    def slope(value, sigma):
        return sigma * (1.0 + value * (1.0 - sigma))

    copies[0].wait()
    for i in range(0, seq, 256):
        keys = act_ref[i : i + 256, 3 * HD :]
        logits = lax.dot_general(
            keys, act_ref[:, 2 * HD : 3 * HD], across, preferred_element_type=F32
        ) * HD ** (-0.5)
        rows = places_of(place_ref, (256, 1), 0, i)
        rows = jnp.where(rows < length, rows, seq)
        sigma = jnp.where(rows <= cols, jax.nn.sigmoid(logits), 0.0)
        swish = logits * sigma
        attn = swish.astype(BF)
        dattn = lax.dot_general(
            act_ref[i : i + 256, HD : 2 * HD], dm_ref[...], across, preferred_element_type=F32
        )
        dlogits = (dattn * (sigma + swish * (1.0 - sigma))).astype(BF)
        dvalues = jnp.dot(attn, dm_ref[...], preferred_element_type=F32) * inverse
        dkeys = jnp.dot(dlogits, act_ref[:, 2 * HD : 3 * HD], preferred_element_type=F32) * (
            inverse * HD ** (-0.5)
        )
        dq_ref[...] += lax.dot_general(
            dlogits, keys, (((0,), (0,)), ((), ())), preferred_element_type=F32
        )
        if i == 0:
            copies[1].wait()
        for j, grad in ((1, dvalues), (3, dkeys)):
            pre = pre_ref[i : i + 256, HD * j : HD * j + HD]
            dpre_ref[i : i + 256, HD * j : HD * j + HD] = (
                grad * slope(pre, jax.nn.sigmoid(pre))
            ).astype(BF)
    dq_ref[...] = dq_ref[...] * (inverse * HD ** (-0.5))
    for j, ref in ((0, du_ref), (2, dq_ref)):
        pre = pre_ref[:, HD * j : HD * j + HD]
        dpre_ref[:, HD * j : HD * j + HD] = (
            ref[...].astype(F32) * slope(pre, jax.nn.sigmoid(pre))
        ).astype(BF)
    near_ref[...] = dpre_ref[: near_ref.shape[0], :]
    far_ref[...] = dpre_ref[near_ref.shape[0] :, :]
    for copy in copies[2:]:
        copy.wait()
    half = own_ref.shape[1]
    turned = (((0,), (0,)), ((), ()))
    width = dhidden_ref.shape[1]
    left = lax.dot_general(dhidden_ref[...], own_ref[...], turned, preferred_element_type=F32)
    left = left + lax.dot_general(
        other_ref[:, :width], other_ref[:, width:], turned, preferred_element_type=F32
    )
    left = left.astype(BF)
    right = lax.dot_general(
        normed_ref[...], dpre_ref[...], (((0,), (0,)), ((), ())), preferred_element_type=F32
    ).astype(BF)
    for y in range(NY):
        for z in range(NZ):
            rows = slice(32 * (NZ * y + z), 32 * (NZ * y + z) + 32)
            grads_ref[z, 32 * y : 32 * y + 32, :half] = left[rows, :]
            grads_ref[z, 32 * y : 32 * y + 32, half:] = right[rows, :]


def part_kernel(near_ref, far_ref, w_ref, far_w_ref, *outs):
    across = (((1,), (1,)), ((), ()))
    for h in range(2):
        rows = slice(256 * h, 256 * h + 256)
        part = lax.dot_general(near_ref[rows, :], w_ref[...], across, preferred_element_type=F32)
        part = part + lax.dot_general(
            far_ref[rows, :], far_w_ref[...], across, preferred_element_type=F32
        )
        part = part.astype(BF)
        outs[2 * h][...] = part[:128, :]
        outs[2 * h + 1][...] = part[128:, :]


def meta_kernel(place_ref, history_ref, cands_ref, loss_ref, meta_ref):
    owner = 2 * place_ref[0] + place_ref[1]

    def digits(values, wanted):
        row = lax.broadcasted_iota(jnp.int32, (16, values.shape[1]), 0)
        upper, lower = values // 128, jnp.bitwise_and(values, 127)
        both = jnp.where(row == 0, upper, jnp.where(row == 2, lower, 0)).astype(F32).astype(BF)
        source = lax.broadcasted_iota(jnp.int32, (values.shape[1], 128), 0)
        hot = (source == wanted).astype(F32).astype(BF)
        return jnp.dot(both, hot, preferred_element_type=F32)

    lane = lax.broadcasted_iota(jnp.int32, (16, 128), 1)
    row = lax.broadcasted_iota(jnp.int32, (16, 128), 0)
    events = digits(history_ref[...], event_slots(owner, (1, 128), 1))
    wanted = cand_slots(owner, (1, 128), 1)
    wanted = jnp.where(lax.broadcasted_iota(jnp.int32, (1, 128), 1) < 64, wanted, -1)
    cands = pltpu.roll(digits(cands_ref[...], wanted), 1, 0)
    meta = events + cands + loss_ref[...].astype(F32)
    for where, value in ((64, place_ref[2]), (65, place_ref[3])):
        for r, part in ((1, value // 128), (3, jnp.bitwise_and(value, 127))):
            part = jnp.full((16, 128), part, jnp.int32).astype(F32)
            meta = jnp.where((lane == where) & (row == r), part, meta)
    meta_ref[...] = meta.astype(BF)


def pack_kernel(a_ref, b_ref, c_ref, d_ref, dcand_ref, rows_ref, dhidden_ref, meta_ref, out_ref):
    refs = (a_ref, b_ref, c_ref, d_ref)
    dnormed = sum(ref[...].astype(F32) for ref in refs)
    rows = rows_ref[...].astype(F32)
    scale = lax.rsqrt(jnp.mean(rows * rows, axis=-1, keepdims=True) + 1e-06)
    normed = rows * scale
    drows = dhidden_ref[...].astype(F32) + scale * (
        dnormed - normed * jnp.mean(dnormed * normed, axis=-1, keepdims=True)
    )
    drows = drows.astype(BF)
    dcand = dcand_ref[...]
    meta = meta_ref[...]
    for d in range(out_ref.shape[0]):
        out_ref[d, 0:32, :] = jnp.concatenate(
            [drows[32 * g : 32 * g + 32, 32 * d : 32 * d + 32] for g in range(4)], axis=1
        )
        out_ref[d, 32:48, :] = jnp.concatenate(
            [dcand[16 * g : 16 * g + 16, 32 * d : 32 * d + 32] for g in range(4)], axis=1
        )
        out_ref[d, 48:64, :] = meta


def scatter_kernel(ids_ref, place_ref, data_ref, own_ref, other_ref, rows_ref, acc_ref, more_ref):
    users = data_ref.shape[0]
    total = acc_ref.shape[0]
    chunk = 512
    owner = 2 * place_ref[0] + place_ref[1]

    def clear(i, carry):
        here = pl.ds(pl.multiple_of(i * chunk, chunk), chunk)
        acc_ref[here, :] = jnp.zeros((chunk, 128), F32)
        more_ref[here, :] = jnp.zeros((chunk, 128), F32)
        return carry

    lax.fori_loop(0, total // chunk, clear, 0)
    for u in range(users):
        rows_ref[48 * u : 48 * u + 48, :] = data_ref[u, 0:48, :].astype(F32)
    lane = lax.broadcasted_iota(jnp.int32, (1, 128), 1) // 32
    masks = [lane == g for g in range(4)]

    def add(first_id, pitch, first_row, count):
        def step(i, carry):
            for j in range(2):
                work = []
                for half, ref in ((0, acc_ref), (1, more_ref)):
                    p = i * 4 + j * 2 + half
                    row = rows_ref[pl.ds(first_row + p, 1), :]
                    ids = [ids_ref[first_id + g * pitch + p] for g in range(4)]
                    work.append((ref, row, ids, [ref[pl.ds(ids[g], 1), :] for g in range(4)]))
                for ref, row, ids, held in work:
                    for g in range(4):
                        pltpu.store(ref.at[pl.ds(ids[g], 1), :], held[g] + row, mask=masks[g])
            return carry

        lax.fori_loop(0, (count + 3) // 4, step, 0)

    def user(u, carry):
        base = u * 256
        events = jnp.clip((ids_ref[base + 192] - owner + 31) // 32, 0, 32)
        cands = jnp.clip((ids_ref[base + 193] - owner + 31) // 32, 0, 16)
        add(base, 32, u * 48, events)
        add(base + 128, 16, u * 48 + 32, cands)
        return carry

    lax.fori_loop(0, users, user, 0)
    wide = lax.broadcasted_iota(jnp.int32, (512, 128), 1) // 32
    for cc in range(2):
        for k in range(4):
            item = item_of(place_ref, cc * NX + k)
            result = jnp.zeros((512, 128), F32)
            for q in range(4):
                here = pl.ds(pl.multiple_of(item * 2048 + q * 512, 512), 512)
                part = acc_ref[here, :] + more_ref[here, :]
                part = part + pltpu.roll(part, 64, 1)
                part = part + pltpu.roll(part, 32, 1)
                result = jnp.where(wide == q, part, result)
            (own_ref, other_ref)[cc][k] = result.astype(BF)


def turn_kernel(place_ref, grads_ref, *outs):
    for k, out in enumerate(outs):
        start = jnp.bitwise_xor(place_ref[4], k) * 32
        out[...] = grads_ref[pl.ds(pl.multiple_of(start, 32), 32), :]


def split_kernel(g0, g1, g2, g3, in_ref, *outs):
    total = sum(ref[...].astype(F32) for ref in (g0, g1, g2, g3))
    in_ref[...] = total[:, NX * HD :]
    for k, out in enumerate(outs):
        out[...] = total[:, HD * k : HD * k + HD].astype(BF)


def unpack_kernel(a_ref, b_ref, c_ref, d_ref, p0, p1, p2, p3, out_ref, proj_ref):
    proj_ref[...] = sum(ref[...].astype(F32) for ref in (p0, p1, p2, p3))
    turned = sum(ref[...].astype(F32) for ref in (a_ref, b_ref, c_ref, d_ref)).T
    for q in range(4):
        out_ref[:, q * 512 : (q + 1) * 512] = turned[32 * q : 32 * q + 32, :]


def whole(count, smem=0):
    specs = [pl.BlockSpec(memory_space=pltpu.SMEM)] * smem
    return specs + [pl.BlockSpec(memory_space=pltpu.VMEM)] * count


def call(kernel, name, outs, *args, smem=0, scratch=(), limit=32, far=(), far_outs=(), cost=1.0):
    outs = tuple(jax.ShapeDtypeStruct(shape, dtype) for shape, dtype in outs)
    hbm = pl.BlockSpec(memory_space=pltpu.HBM)
    specs = [hbm if i in far_outs else whole(1)[0] for i in range(len(outs))]
    in_specs = [hbm if i in far else spec for i, spec in enumerate(whole(len(args) - smem, smem))]
    return pl.pallas_call(
        kernel,
        out_shape=outs if len(outs) > 1 else outs[0],
        in_specs=in_specs,
        out_specs=tuple(specs) if len(outs) > 1 else specs[0],
        scratch_shapes=list(scratch),
        compiler_params=pltpu.CompilerParams(vmem_limit_bytes=int(limit * 1024 * 1024)),
        cost_estimate=pl.CostEstimate(
            flops=int(cost * 1.1e9), bytes_accessed=int(cost * 3.6e6), transcendentals=0
        ),
        name=name,
    )(*args)


def on_device(table, w_uvqk, w_out, history, lengths, candidates, counts, actions, targets):
    rows_total, width = table.shape
    seq = history.shape[1]
    ncand = candidates.shape[1]
    users = NY * NZ
    parts = NX * NC
    block = seq // parts
    cblock = ncand // parts
    x, c = lax.axis_index("x"), lax.axis_index("c")
    length = lengths[0]

    place = jnp.stack([x, c, length, counts[0], lax.axis_index("y")]).astype(jnp.int32)

    def along_x(own):
        return [own] + [swap_x(own, k) for k in range(1, NX)]

    size = block + cblock

    def pick(half):
        return call(
            functools.partial(pick_kernel, half),
            "pick",
            [((NX, size, width), BF)],
            place,
            history,
            candidates,
            table,
            smem=1,
            scratch=[pltpu.VMEM((NX * size, rows_total), BF)],
            limit=20,
            cost=5.0 if half else 0.05,
        )

    picked_other = swap_core(pick(1))
    weights_out = lax.all_gather(w_out, ("x", "c"), axis=0, tiled=False)
    picked_own = pick(0)
    line = list(call(pair_kernel, "pair", [((size, width), BF)] * NX, picked_other, picked_own, limit=8))
    line = [line[0]] + [swap_x(line[k], k) for k in range(1, NX)]
    w_uvqk, line[0] = lax.optimization_barrier((w_uvqk, line[0]))
    local_w = w_uvqk.reshape(width, -1)
    normed, crow = call(
        norm_kernel,
        "norm",
        [((block, width), BF), ((cblock, width), BF)],
        *line,
        limit=50,
    )
    own_other = swap_core(normed)
    far_w = swap_core(local_w)
    line[0], normed = lax.optimization_barrier((line[0], normed))
    rows = call(rows_kernel, "rows", [((block, width), BF)], *line, limit=50, cost=0.5)
    *normed_line, local_w, far_w, rows = lax.optimization_barrier(
        (*along_x(normed), crow, local_w, far_w, rows)
    )
    spread_rows = normed_line[:NX] + [own_other] + [swap_core(part) for part in normed_line[1:NX]]
    crows = lax.all_gather(normed_line[NX], ("x", "c"), axis=0, tiled=True)
    normed, pre, act, sent = call(
        attend_kernel,
        "attend",
        [((seq, width), BF), ((seq, 4 * HD), F32), ((seq, 4 * HD), BF), ((parts, block, 3 * HD), BF)],
        place,
        *spread_rows,
        local_w,
        smem=1,
        limit=52,
        far_outs=(0, 1, 2),
        scratch=[
            pltpu.VMEM((seq, width), BF),
            pltpu.VMEM((seq, 4 * HD), F32),
            pltpu.VMEM((seq, 4 * HD), BF),
            pltpu.SemaphoreType.DMA((3,)),
        ],
        cost=4.0,
    )
    sent = lax.all_to_all(sent, ("x", "c"), 0, 0)

    half = NX * HD
    back, dhidden, dcand, gated_near, gated_far = call(
        event_kernel,
        "event",
        [
            ((parts, block + 16, 2 * HD), BF),
            ((block, width), BF),
            ((ncand, width), BF),
            ((block, half), BF),
            ((block, width + half), BF),
        ],
        place,
        sent,
        rows,
        weights_out,
        crows,
        actions,
        targets,
        smem=1,
        limit=60,
        far=(3, 4),
        scratch=[
            pltpu.VMEM((width, width), BF),
            pltpu.VMEM((ncand, width), BF),
            pltpu.SemaphoreType.DMA((parts + 1,)),
        ],
        cost=4.0,
    )
    back = lax.all_to_all(back, ("x", "c"), 0, 0)
    gated_far = swap_core(gated_far)

    dcand = lax.psum_scatter(dcand, ("x", "c"), scatter_dimension=0, tiled=True)
    near, far, loss_meta, grads = call(
        backward_kernel,
        "backward",
        [
            ((seq // 2, 4 * HD), BF),
            ((seq // 2, 4 * HD), BF),
            ((16, 128), BF),
            ((NZ, width // NZ, half + 4 * HD), BF),
        ],
        place,
        back,
        act,
        pre,
        normed,
        dhidden,
        gated_near,
        gated_far,
        smem=1,
        scratch=[
            pltpu.VMEM((seq, HD), BF),
            pltpu.VMEM((seq, HD), BF),
            pltpu.VMEM((seq, HD), F32),
            pltpu.VMEM((seq, 4 * HD), BF),
            pltpu.VMEM((seq, 4 * HD), BF),
            pltpu.VMEM((seq, 4 * HD), F32),
            pltpu.VMEM((seq, width), BF),
            pltpu.VMEM((block, width), BF),
            pltpu.VMEM((block, half), BF),
            pltpu.VMEM((block, width + half), BF),
            pltpu.SemaphoreType.DMA((6,)),
        ],
        limit=60,
        far=(2, 3, 4, 5, 6, 7),
        cost=6.0,
    )
    far_got = swap_core(far)
    line = list(
        call(
            part_kernel,
            "part",
            [((block, width), BF)] * NX,
            near,
            far_got,
            local_w,
            far_w,
            limit=50,
            cost=2.0,
        )
    )
    grads = lax.psum_scatter(grads, "z", scatter_dimension=0, tiled=False)
    loss_meta, line[0] = lax.optimization_barrier((loss_meta, line[0]))
    meta = call(
        meta_kernel, "meta", [((16, 128), BF)], place, history, candidates, loss_meta, smem=1, limit=40
    )
    line = [line[0]] + [swap_x(line[k], k) for k in range(1, NX)]

    packed = call(
        pack_kernel,
        "pack",
        [((users, 64, 128), BF)],
        *line,
        dcand,
        rows,
        dhidden,
        meta,
        limit=50,
    )
    arrived = lax.all_to_all(packed, ("y", "z"), 0, 0)
    _, grads = lax.optimization_barrier((arrived, grads))
    grads = call(
        turn_kernel, "turn", [((32, half + 4 * HD), BF)] * NY, place, grads, smem=1, limit=8, cost=0.5
    )
    grads = [grads[0]] + [
        lax.ppermute(grads[k], "y", [(i, i ^ k) for i in range(NY)]) for k in range(1, NY)
    ]
    got = arrived[:, 48:53].astype(F32)
    all_ids = (got[:, 0:2] * 128.0 + got[:, 2:4]).astype(jnp.int32).reshape(-1)
    own, other = call(
        scatter_kernel,
        "scatter",
        [((NX, 512, 128), BF)] * 2,
        all_ids,
        place,
        arrived,
        smem=2,
        scratch=[
            pltpu.VMEM((users * 48, 128), F32),
            pltpu.VMEM((parts * rows_total, 128), F32),
            pltpu.VMEM((parts * rows_total, 128), F32),
        ],
        limit=24,
        cost=12.0,
    )
    line = call(pair_kernel, "final_pair", [((512, 128), BF)] * NX, swap_core(other), own, limit=8, cost=0.5)
    line = [line[0]] + [swap_x(line[k], k) for k in range(1, NX)]
    grad_in, *proj = call(
        split_kernel, "split", [((32, 4 * HD), F32)] + [((32, HD), BF)] * NX, *grads, limit=8, cost=0.5
    )
    proj = [proj[0]] + [swap_x(proj[k], k) for k in range(1, NX)]
    shard_t, proj_t = call(
        unpack_kernel,
        "unpack",
        [((32, rows_total), F32), ((32, HD), F32)],
        *line,
        *proj,
        limit=8,
    )
    grad_in = grad_in.reshape(-1, 4, HD)
    loss = jnp.sum(got[:, 4, 0:3])
    return (loss, grad_in, proj_t.T, shard_t.T)


def solution(mesh):
    fine = Mesh(mesh.devices.reshape(NY, NZ, NX, NC), ("y", "z", "x", "c"))
    dp, item = ("y", "z"), ("x", "c")
    placed = (
        P(item, None),
        P(None, None, item),
        P(item, None),
        P(dp, None),
        P(dp),
        P(dp, None),
        P(dp),
        P(dp, None),
        P(dp, None),
    )
    return jax.shard_map(
        on_device,
        mesh=fine,
        in_specs=placed,
        out_specs=(P(), P(dp, None, item), P(item, dp), P(item, dp)),
        check_vma=False,
    )
```

```python
import functools

import jax
import jax.numpy as jnp
from jax import lax
from jax.experimental import pallas as pl
from jax.experimental.pallas import tpu as pltpu
from jax.sharding import Mesh, PartitionSpec as P

HD = 128
NX, NC, NY, NZ = 4, 2, 4, 8
CQL_WEIGHT = 0.5
BF = jnp.bfloat16
F32 = jnp.float32


def swap_x(value, k):
    return lax.ppermute(value, "x", [(i, i ^ k) for i in range(NX)])


def swap_core(value):
    return lax.ppermute(value, "c", [(0, 1), (1, 0)])


def event_slots(item, shape, axis):
    row = lax.broadcasted_iota(jnp.int32, shape, axis)
    return 32 * jnp.bitwise_and(row, 31) + 8 * (row // 32) + item


def cand_slots(item, shape, axis):
    row = lax.broadcasted_iota(jnp.int32, shape, axis)
    return 32 * jnp.bitwise_and(row, 15) + 8 * (row // 16) + item


def chosen(values, slots):
    cols = lax.broadcasted_iota(jnp.int32, (1, values.shape[1]), 1)
    return jnp.sum(jnp.where(cols == slots, values.astype(F32), 0.0), axis=1, keepdims=True)


def pick_kernel(half, place_ref, history_ref, cand_ref, table_ref, out_ref, hot_ref):
    total = table_ref.shape[0]
    first_row = (2 * place_ref[0] + place_ref[1]) * total
    size = out_ref.shape[1]
    for k in range(NX):
        item = item_of(place_ref, half * NX + k)
        events = chosen(history_ref[...], event_slots(item, (128, 1), 0))
        cands = chosen(cand_ref[...], cand_slots(item, (size - 128, 1), 0))
        for first, ids in ((0, events), (128, cands)):
            local = ids.astype(jnp.int32) - first_row
            count = ids.shape[0]
            for i in range(0, total, 512):
                cols = lax.broadcasted_iota(jnp.int32, (1, 512), 1) + i
                hot_ref[size * k + first : size * k + first + count, i : i + 512] = (
                    (local == cols).astype(F32).astype(BF)
                )
    for i in range(0, out_ref.shape[2], 256):
        found = jnp.dot(hot_ref[...], table_ref[:, i : i + 256], preferred_element_type=F32).astype(BF)
        for k in range(NX):
            out_ref[k, :, i : i + 256] = found[size * k : size * k + size, :]


def pair_kernel(a_ref, b_ref, *outs):
    for k, out in enumerate(outs):
        out[...] = (a_ref[k].astype(F32) + b_ref[k].astype(F32)).astype(BF)


def norm_kernel(a_ref, b_ref, c_ref, d_ref, normed_ref, crow_ref):
    refs = (a_ref, b_ref, c_ref, d_ref)
    block = normed_ref.shape[0]
    rows = sum(ref[:block, :].astype(F32) for ref in refs)
    scale = lax.rsqrt(jnp.mean(rows * rows, axis=-1, keepdims=True) + 1e-06)
    normed_ref[...] = (rows * scale).astype(BF)
    crow_ref[...] = sum(ref[block:, :].astype(F32) for ref in refs).astype(BF)


def rows_kernel(a_ref, b_ref, c_ref, d_ref, rows_ref):
    block = rows_ref.shape[0]
    rows_ref[...] = sum(ref[:block, :].astype(F32) for ref in (a_ref, b_ref, c_ref, d_ref)).astype(BF)


def item_of(place_ref, b):
    return 2 * jnp.bitwise_xor(place_ref[0], b % NX) + jnp.bitwise_xor(place_ref[1], b // NX)


def places_of(place_ref, shape, axis, first=0):
    row = lax.broadcasted_iota(jnp.int32, shape, axis) + first
    line = jnp.bitwise_and(row, 511)
    item = 2 * jnp.bitwise_xor(place_ref[0], line // 128) + jnp.bitwise_xor(place_ref[1], row // 512)
    inside = jnp.bitwise_and(row, 127)
    return 32 * jnp.bitwise_and(inside, 31) + 8 * (inside // 32) + item


def attend_kernel(
    place_ref, b0, b1, b2, b3, b4, b5, b6, b7, w_ref,
    normed_out, pre_out, act_out, sent_ref, normed_ref, pre_ref, act_ref, sems,
):
    for b, ref in enumerate((b0, b1, b2, b3, b4, b5, b6, b7)):
        normed_ref[128 * b : 128 * b + 128, :] = ref[...]
    copies = [pltpu.make_async_copy(normed_ref, normed_out, sems.at[0])]
    copies[0].start()
    seq = normed_ref.shape[0]
    for i in range(0, seq, 256):
        pre = jnp.dot(normed_ref[i : i + 256, :], w_ref[...], preferred_element_type=F32)
        pre_ref[i : i + 256, :] = pre
        act_ref[i : i + 256, :] = (pre * jax.nn.sigmoid(pre)).astype(BF)
    for i, (source, target) in enumerate(((pre_ref, pre_out), (act_ref, act_out))):
        copies.append(pltpu.make_async_copy(source, target, sems.at[i + 1]))
        copies[-1].start()
    length = place_ref[2]
    inverse = 1.0 / jnp.full((1, 1), length, jnp.int32).astype(F32)
    cols = places_of(place_ref, (1, seq), 1)
    cols = jnp.where(cols < length, cols, seq)
    for i in range(0, seq, 256):
        queries = act_ref[i : i + 256, 2 * HD : 3 * HD]
        logits = lax.dot_general(
            queries, act_ref[:, 3 * HD :], (((1,), (1,)), ((), ())), preferred_element_type=F32
        ) * HD ** (-0.5)
        rows = places_of(place_ref, (256, 1), 0, i)
        attn = jnp.where(cols <= rows, logits * jax.nn.sigmoid(logits), 0.0).astype(BF)
        mixed = jnp.dot(attn, act_ref[:, HD : 2 * HD], preferred_element_type=F32) * inverse
        top = mixed.astype(BF)
        rest = (mixed - top.astype(F32)).astype(BF)
        for h in range(2):
            b = i // 128 + h
            item = item_of(place_ref, b)
            sent_ref[item, :, 0:HD] = top[128 * h : 128 * h + 128, :]
            sent_ref[item, :, HD : 2 * HD] = rest[128 * h : 128 * h + 128, :]
            sent_ref[item, :, 2 * HD :] = act_ref[128 * b : 128 * b + 128, 0:HD]
    for copy in copies:
        copy.wait()


def split_loss(value, shape, row):
    value = jnp.broadcast_to(value, shape)
    top = value.astype(BF).astype(F32)
    middle = (value - top).astype(BF).astype(F32)
    low = value - top - middle
    lane = lax.broadcasted_iota(jnp.int32, shape, 1)
    picked = jnp.where(lane == 0, top, jnp.where(lane == 1, middle, jnp.where(lane == 2, low, 0.0)))
    return jnp.where(lax.broadcasted_iota(jnp.int32, shape, 0) == row, picked, 0.0).astype(BF)


def event_kernel(
    place_ref, sent_ref, rows_ref, w_ref, crows_ref, action_ref, target_ref,
    back_ref, dhidden_ref, dcand_ref, near_ref, far_ref,
    weight_ref, crow_ref, sems,
):
    copies = [
        pltpu.make_async_copy(
            w_ref.at[item_of(place_ref, b)], weight_ref.at[HD * b : HD * b + HD, :], sems.at[b]
        )
        for b in range(NX * NC)
    ]
    copies.append(pltpu.make_async_copy(crows_ref, crow_ref, sems.at[NX * NC]))
    for copy in copies:
        copy.start()
    owner = 2 * place_ref[0] + place_ref[1]
    length, count = place_ref[2], place_ref[3]
    block, width = rows_ref.shape
    seq = block * NX * NC
    items = [item_of(place_ref, b) for b in range(NX * NC)]
    mixed = jnp.concatenate(
        [sent_ref[i, :, 0:HD].astype(F32) + sent_ref[i, :, HD : 2 * HD].astype(F32) for i in items], axis=1
    )
    gate = jnp.concatenate([sent_ref[i, :, 2 * HD :] for i in items], axis=1).astype(F32)
    center = jnp.mean(mixed, axis=-1, keepdims=True)
    rstd = lax.rsqrt(jnp.mean(mixed * mixed, axis=-1, keepdims=True) - center * center + 1e-05)
    normo = (mixed - center) * rstd
    gated = (normo * gate).astype(BF)
    for copy in copies:
        copy.wait()
    weights = weight_ref[...]
    out = rows_ref[...].astype(F32) + jnp.dot(gated, weights, preferred_element_type=F32)
    hidden = out.astype(BF)
    crows = crow_ref[...]
    scores = lax.dot_general(hidden, crows, (((1,), (1,)), ((), ())), preferred_element_type=F32)
    col = lax.broadcasted_iota(jnp.int32, (1, crows.shape[0]), 1)
    inside = jnp.bitwise_and(col, 63)
    slots = 32 * jnp.bitwise_and(inside, 15) + 8 * (inside // 16) + col // 64
    masked = jnp.where(slots < count, scores, -jnp.inf)
    top = jnp.max(masked, axis=-1, keepdims=True)
    expo = jnp.exp(masked - top)
    total = jnp.sum(expo, axis=-1, keepdims=True)
    soft = expo / total
    lse = top + jnp.log(total)
    places = event_slots(owner, (block, 1), 0)
    actions = chosen(action_ref[...], places).astype(jnp.int32)
    onehot = (slots == actions).astype(F32)
    taken = jnp.sum(scores * onehot, axis=-1, keepdims=True)
    live = jnp.where(places < length, 1.0 / seq, 0.0)
    miss = taken - chosen(target_ref[...], places)
    loss = jnp.sum(live * (CQL_WEIGHT * (lse - taken) + 0.5 * miss * miss), axis=0, keepdims=True)
    loss = split_loss(loss, (16, 2 * HD), 0)
    dscore = (live * (CQL_WEIGHT * soft + (miss - CQL_WEIGHT) * onehot)).astype(BF)
    dhidden = jnp.dot(dscore, crows, preferred_element_type=F32).astype(BF)
    dhidden_ref[...] = dhidden
    dgated = lax.dot_general(
        dhidden, weights, (((1,), (1,)), ((), ())), preferred_element_type=F32
    )
    dnormo = dgated * gate
    first = jnp.mean(dnormo, axis=-1, keepdims=True)
    second = jnp.mean(dnormo * normo, axis=-1, keepdims=True)
    dmixed = (rstd * (dnormo - first - normo * second)).astype(BF)
    du = (dgated * normo).astype(BF)
    for b, i in enumerate(items):
        back_ref[i, 0:block, 0:HD] = dmixed[:, HD * b : HD * b + HD]
        back_ref[i, 0:block, HD:] = du[:, HD * b : HD * b + HD]
        back_ref[i, block:, :] = loss
    turned = (((0,), (0,)), ((), ()))
    half = NX * HD
    near_ref[...] = gated[:, :half]
    far_ref[:, :width] = dhidden
    far_ref[:, width:] = gated[:, half:]
    dcand_ref[...] = lax.dot_general(dscore, hidden, turned, preferred_element_type=F32).astype(BF)


def backward_kernel(
    place_ref, back_ref, act_in, pre_in, normed_in, dhidden_in, own_in, other_in,
    near_ref, far_ref, loss_ref, grads_ref,
    dm_ref, du_ref, dq_ref, dpre_ref, act_ref, pre_ref, normed_ref, dhidden_ref, own_ref, other_ref, sems,
):
    copies = [
        pltpu.make_async_copy(source, target, sems.at[i])
        for i, (source, target) in enumerate(
            (
                (act_in, act_ref),
                (pre_in, pre_ref),
                (normed_in, normed_ref),
                (dhidden_in, dhidden_ref),
                (own_in, own_ref),
                (other_in, other_ref),
            )
        )
    ]
    for copy in copies:
        copy.start()
    seq = act_ref.shape[0]
    loss = jnp.zeros((16, 2 * HD), F32)
    for b in range(8):
        item = item_of(place_ref, b)
        dm_ref[128 * b : 128 * b + 128, :] = back_ref[item, 0:128, 0:HD]
        du_ref[128 * b : 128 * b + 128, :] = back_ref[item, 0:128, HD:]
        loss = loss + back_ref[item, 128:144, :].astype(F32)
    loss = jnp.sum(jnp.sum(loss, axis=1, keepdims=True), axis=0, keepdims=True)
    loss_ref[...] = split_loss(loss, (16, 128), 4)
    length = place_ref[2]
    inverse = 1.0 / jnp.full((1, 1), length, jnp.int32).astype(F32)
    cols = places_of(place_ref, (1, seq), 1)
    across = (((1,), (1,)), ((), ()))
    dq_ref[...] = jnp.zeros(dq_ref.shape, F32)

    def slope(value, sigma):
        return sigma * (1.0 + value * (1.0 - sigma))

    copies[0].wait()
    for i in range(0, seq, 256):
        keys = act_ref[i : i + 256, 3 * HD :]
        logits = lax.dot_general(
            keys, act_ref[:, 2 * HD : 3 * HD], across, preferred_element_type=F32
        ) * HD ** (-0.5)
        rows = places_of(place_ref, (256, 1), 0, i)
        rows = jnp.where(rows < length, rows, seq)
        sigma = jnp.where(rows <= cols, jax.nn.sigmoid(logits), 0.0)
        swish = logits * sigma
        attn = swish.astype(BF)
        dattn = lax.dot_general(
            act_ref[i : i + 256, HD : 2 * HD], dm_ref[...], across, preferred_element_type=F32
        )
        dlogits = (dattn * (sigma + swish * (1.0 - sigma))).astype(BF)
        dvalues = jnp.dot(attn, dm_ref[...], preferred_element_type=F32) * inverse
        dkeys = jnp.dot(dlogits, act_ref[:, 2 * HD : 3 * HD], preferred_element_type=F32) * (
            inverse * HD ** (-0.5)
        )
        dq_ref[...] += lax.dot_general(
            dlogits, keys, (((0,), (0,)), ((), ())), preferred_element_type=F32
        )
        if i == 0:
            copies[1].wait()
        for j, grad in ((1, dvalues), (3, dkeys)):
            pre = pre_ref[i : i + 256, HD * j : HD * j + HD]
            dpre_ref[i : i + 256, HD * j : HD * j + HD] = (
                grad * slope(pre, jax.nn.sigmoid(pre))
            ).astype(BF)
    dq_ref[...] = dq_ref[...] * (inverse * HD ** (-0.5))
    for j, ref in ((0, du_ref), (2, dq_ref)):
        pre = pre_ref[:, HD * j : HD * j + HD]
        dpre_ref[:, HD * j : HD * j + HD] = (
            ref[...].astype(F32) * slope(pre, jax.nn.sigmoid(pre))
        ).astype(BF)
    near_ref[...] = dpre_ref[: near_ref.shape[0], :]
    far_ref[...] = dpre_ref[near_ref.shape[0] :, :]
    for copy in copies[2:]:
        copy.wait()
    half = own_ref.shape[1]
    turned = (((0,), (0,)), ((), ()))
    width = dhidden_ref.shape[1]
    left = lax.dot_general(dhidden_ref[...], own_ref[...], turned, preferred_element_type=F32)
    left = left + lax.dot_general(
        other_ref[:, :width], other_ref[:, width:], turned, preferred_element_type=F32
    )
    left = left.astype(BF)
    right = lax.dot_general(
        normed_ref[...], dpre_ref[...], (((0,), (0,)), ((), ())), preferred_element_type=F32
    ).astype(BF)
    for y in range(NY):
        for z in range(NZ):
            rows = slice(32 * (NZ * y + z), 32 * (NZ * y + z) + 32)
            grads_ref[z, 32 * y : 32 * y + 32, :half] = left[rows, :]
            grads_ref[z, 32 * y : 32 * y + 32, half:] = right[rows, :]


def part_kernel(near_ref, far_ref, w_ref, far_w_ref, *outs):
    across = (((1,), (1,)), ((), ()))
    for h in range(2):
        rows = slice(256 * h, 256 * h + 256)
        part = lax.dot_general(near_ref[rows, :], w_ref[...], across, preferred_element_type=F32)
        part = part + lax.dot_general(
            far_ref[rows, :], far_w_ref[...], across, preferred_element_type=F32
        )
        part = part.astype(BF)
        outs[2 * h][...] = part[:128, :]
        outs[2 * h + 1][...] = part[128:, :]


def meta_kernel(place_ref, history_ref, cands_ref, loss_ref, meta_ref):
    owner = 2 * place_ref[0] + place_ref[1]

    def digits(values, wanted):
        row = lax.broadcasted_iota(jnp.int32, (16, values.shape[1]), 0)
        upper, lower = values // 128, jnp.bitwise_and(values, 127)
        both = jnp.where(row == 0, upper, jnp.where(row == 2, lower, 0)).astype(F32).astype(BF)
        source = lax.broadcasted_iota(jnp.int32, (values.shape[1], 128), 0)
        hot = (source == wanted).astype(F32).astype(BF)
        return jnp.dot(both, hot, preferred_element_type=F32)

    lane = lax.broadcasted_iota(jnp.int32, (16, 128), 1)
    row = lax.broadcasted_iota(jnp.int32, (16, 128), 0)
    events = digits(history_ref[...], event_slots(owner, (1, 128), 1))
    wanted = cand_slots(owner, (1, 128), 1)
    wanted = jnp.where(lax.broadcasted_iota(jnp.int32, (1, 128), 1) < 64, wanted, -1)
    cands = pltpu.roll(digits(cands_ref[...], wanted), 1, 0)
    meta = events + cands + loss_ref[...].astype(F32)
    for where, value in ((64, place_ref[2]), (65, place_ref[3])):
        for r, part in ((1, value // 128), (3, jnp.bitwise_and(value, 127))):
            part = jnp.full((16, 128), part, jnp.int32).astype(F32)
            meta = jnp.where((lane == where) & (row == r), part, meta)
    meta_ref[...] = meta.astype(BF)


def pack_kernel(a_ref, b_ref, c_ref, d_ref, dcand_ref, rows_ref, dhidden_ref, meta_ref, out_ref):
    refs = (a_ref, b_ref, c_ref, d_ref)
    dnormed = sum(ref[...].astype(F32) for ref in refs)
    rows = rows_ref[...].astype(F32)
    scale = lax.rsqrt(jnp.mean(rows * rows, axis=-1, keepdims=True) + 1e-06)
    normed = rows * scale
    drows = dhidden_ref[...].astype(F32) + scale * (
        dnormed - normed * jnp.mean(dnormed * normed, axis=-1, keepdims=True)
    )
    drows = drows.astype(BF)
    dcand = dcand_ref[...]
    meta = meta_ref[...]
    for d in range(out_ref.shape[0]):
        out_ref[d, 0:32, :] = jnp.concatenate(
            [drows[32 * g : 32 * g + 32, 32 * d : 32 * d + 32] for g in range(4)], axis=1
        )
        out_ref[d, 32:48, :] = jnp.concatenate(
            [dcand[16 * g : 16 * g + 16, 32 * d : 32 * d + 32] for g in range(4)], axis=1
        )
        out_ref[d, 48:64, :] = meta


def scatter_kernel(ids_ref, place_ref, data_ref, own_ref, other_ref, rows_ref, acc_ref, more_ref):
    users = data_ref.shape[0]
    total = acc_ref.shape[0]
    chunk = 512
    owner = 2 * place_ref[0] + place_ref[1]

    def clear(i, carry):
        here = pl.ds(pl.multiple_of(i * chunk, chunk), chunk)
        acc_ref[here, :] = jnp.zeros((chunk, 128), F32)
        more_ref[here, :] = jnp.zeros((chunk, 128), F32)
        return carry

    lax.fori_loop(0, total // chunk, clear, 0)
    for u in range(users):
        rows_ref[48 * u : 48 * u + 48, :] = data_ref[u, 0:48, :].astype(F32)
    lane = lax.broadcasted_iota(jnp.int32, (1, 128), 1) // 32
    masks = [lane == g for g in range(4)]

    def add(first_id, pitch, first_row, count):
        def step(i, carry):
            for j in range(2):
                work = []
                for half, ref in ((0, acc_ref), (1, more_ref)):
                    p = i * 4 + j * 2 + half
                    row = rows_ref[pl.ds(first_row + p, 1), :]
                    ids = [ids_ref[first_id + g * pitch + p] for g in range(4)]
                    work.append((ref, row, ids, [ref[pl.ds(ids[g], 1), :] for g in range(4)]))
                for ref, row, ids, held in work:
                    for g in range(4):
                        pltpu.store(ref.at[pl.ds(ids[g], 1), :], held[g] + row, mask=masks[g])
            return carry

        lax.fori_loop(0, (count + 3) // 4, step, 0)

    def user(u, carry):
        base = u * 256
        events = jnp.clip((ids_ref[base + 192] - owner + 31) // 32, 0, 32)
        cands = jnp.clip((ids_ref[base + 193] - owner + 31) // 32, 0, 16)
        add(base, 32, u * 48, events)
        add(base + 128, 16, u * 48 + 32, cands)
        return carry

    lax.fori_loop(0, users, user, 0)
    wide = lax.broadcasted_iota(jnp.int32, (512, 128), 1) // 32
    for cc in range(2):
        for k in range(4):
            item = item_of(place_ref, cc * NX + k)
            result = jnp.zeros((512, 128), F32)
            for q in range(4):
                here = pl.ds(pl.multiple_of(item * 2048 + q * 512, 512), 512)
                part = acc_ref[here, :] + more_ref[here, :]
                part = part + pltpu.roll(part, 64, 1)
                part = part + pltpu.roll(part, 32, 1)
                result = jnp.where(wide == q, part, result)
            (own_ref, other_ref)[cc][k] = result.astype(BF)


def turn_kernel(place_ref, grads_ref, *outs):
    for k, out in enumerate(outs):
        start = jnp.bitwise_xor(place_ref[4], k) * 32
        out[...] = grads_ref[pl.ds(pl.multiple_of(start, 32), 32), :]


def split_kernel(g0, g1, g2, g3, in_ref, *outs):
    total = sum(ref[...].astype(F32) for ref in (g0, g1, g2, g3))
    in_ref[...] = total[:, NX * HD :]
    for k, out in enumerate(outs):
        out[...] = total[:, HD * k : HD * k + HD].astype(BF)


def unpack_kernel(a_ref, b_ref, c_ref, d_ref, p0, p1, p2, p3, out_ref, proj_ref):
    proj_ref[...] = sum(ref[...].astype(F32) for ref in (p0, p1, p2, p3))
    turned = sum(ref[...].astype(F32) for ref in (a_ref, b_ref, c_ref, d_ref)).T
    for q in range(4):
        out_ref[:, q * 512 : (q + 1) * 512] = turned[32 * q : 32 * q + 32, :]


def whole(count, smem=0):
    specs = [pl.BlockSpec(memory_space=pltpu.SMEM)] * smem
    return specs + [pl.BlockSpec(memory_space=pltpu.VMEM)] * count


def call(kernel, name, outs, *args, smem=0, scratch=(), limit=32, far=(), far_outs=(), cost=1.0):
    outs = tuple(jax.ShapeDtypeStruct(shape, dtype) for shape, dtype in outs)
    hbm = pl.BlockSpec(memory_space=pltpu.HBM)
    specs = [hbm if i in far_outs else whole(1)[0] for i in range(len(outs))]
    in_specs = [hbm if i in far else spec for i, spec in enumerate(whole(len(args) - smem, smem))]
    return pl.pallas_call(
        kernel,
        out_shape=outs if len(outs) > 1 else outs[0],
        in_specs=in_specs,
        out_specs=tuple(specs) if len(outs) > 1 else specs[0],
        scratch_shapes=list(scratch),
        compiler_params=pltpu.CompilerParams(vmem_limit_bytes=int(limit * 1024 * 1024)),
        cost_estimate=pl.CostEstimate(
            flops=int(cost * 1.1e9), bytes_accessed=int(cost * 3.6e6), transcendentals=0
        ),
        name=name,
    )(*args)


def on_device(table, w_uvqk, w_out, history, lengths, candidates, counts, actions, targets):
    rows_total, width = table.shape
    seq = history.shape[1]
    ncand = candidates.shape[1]
    users = NY * NZ
    parts = NX * NC
    block = seq // parts
    cblock = ncand // parts
    x, c = lax.axis_index("x"), lax.axis_index("c")
    length = lengths[0]

    place = jnp.stack([x, c, length, counts[0], lax.axis_index("y")]).astype(jnp.int32)

    def along_x(own):
        return [own] + [swap_x(own, k) for k in range(1, NX)]

    size = block + cblock

    def pick(half):
        return call(
            functools.partial(pick_kernel, half),
            "pick",
            [((NX, size, width), BF)],
            place,
            history,
            candidates,
            table,
            smem=1,
            scratch=[pltpu.VMEM((NX * size, rows_total), BF)],
            limit=20,
            cost=5.0 if half else 0.05,
        )

    picked_other = swap_core(pick(1))
    weights_out = lax.all_gather(w_out, ("x", "c"), axis=0, tiled=False)
    picked_own = pick(0)
    line = list(call(pair_kernel, "pair", [((size, width), BF)] * NX, picked_other, picked_own, limit=8))
    line = [line[0]] + [swap_x(line[k], k) for k in range(1, NX)]
    w_uvqk, line[0] = lax.optimization_barrier((w_uvqk, line[0]))
    local_w = w_uvqk.reshape(width, -1)
    normed, crow = call(
        norm_kernel,
        "norm",
        [((block, width), BF), ((cblock, width), BF)],
        *line,
        limit=50,
    )
    own_other = swap_core(normed)
    far_w = swap_core(local_w)
    line[0], normed = lax.optimization_barrier((line[0], normed))
    rows = call(rows_kernel, "rows", [((block, width), BF)], *line, limit=50, cost=0.5)
    *normed_line, local_w, far_w, rows = lax.optimization_barrier(
        (*along_x(normed), crow, local_w, far_w, rows)
    )
    spread_rows = normed_line[:NX] + [own_other] + [swap_core(part) for part in normed_line[1:NX]]
    crows = lax.all_gather(normed_line[NX], ("x", "c"), axis=0, tiled=True)
    normed, pre, act, sent = call(
        attend_kernel,
        "attend",
        [((seq, width), BF), ((seq, 4 * HD), F32), ((seq, 4 * HD), BF), ((parts, block, 3 * HD), BF)],
        place,
        *spread_rows,
        local_w,
        smem=1,
        limit=52,
        far_outs=(0, 1, 2),
        scratch=[
            pltpu.VMEM((seq, width), BF),
            pltpu.VMEM((seq, 4 * HD), F32),
            pltpu.VMEM((seq, 4 * HD), BF),
            pltpu.SemaphoreType.DMA((3,)),
        ],
        cost=4.0,
    )
    sent = lax.all_to_all(sent, ("x", "c"), 0, 0)

    half = NX * HD
    back, dhidden, dcand, gated_near, gated_far = call(
        event_kernel,
        "event",
        [
            ((parts, block + 16, 2 * HD), BF),
            ((block, width), BF),
            ((ncand, width), BF),
            ((block, half), BF),
            ((block, width + half), BF),
        ],
        place,
        sent,
        rows,
        weights_out,
        crows,
        actions,
        targets,
        smem=1,
        limit=60,
        far=(3, 4),
        scratch=[
            pltpu.VMEM((width, width), BF),
            pltpu.VMEM((ncand, width), BF),
            pltpu.SemaphoreType.DMA((parts + 1,)),
        ],
        cost=4.0,
    )
    back = lax.all_to_all(back, ("x", "c"), 0, 0)
    gated_far = swap_core(gated_far)

    dcand = lax.psum_scatter(dcand, ("x", "c"), scatter_dimension=0, tiled=True)
    near, far, loss_meta, grads = call(
        backward_kernel,
        "backward",
        [
            ((seq // 2, 4 * HD), BF),
            ((seq // 2, 4 * HD), BF),
            ((16, 128), BF),
            ((NZ, width // NZ, half + 4 * HD), BF),
        ],
        place,
        back,
        act,
        pre,
        normed,
        dhidden,
        gated_near,
        gated_far,
        smem=1,
        scratch=[
            pltpu.VMEM((seq, HD), BF),
            pltpu.VMEM((seq, HD), BF),
            pltpu.VMEM((seq, HD), F32),
            pltpu.VMEM((seq, 4 * HD), BF),
            pltpu.VMEM((seq, 4 * HD), BF),
            pltpu.VMEM((seq, 4 * HD), F32),
            pltpu.VMEM((seq, width), BF),
            pltpu.VMEM((block, width), BF),
            pltpu.VMEM((block, half), BF),
            pltpu.VMEM((block, width + half), BF),
            pltpu.SemaphoreType.DMA((6,)),
        ],
        limit=60,
        far=(2, 3, 4, 5, 6, 7),
        cost=6.0,
    )
    far_got = swap_core(far)
    line = list(
        call(
            part_kernel,
            "part",
            [((block, width), BF)] * NX,
            near,
            far_got,
            local_w,
            far_w,
            limit=50,
            cost=2.0,
        )
    )
    grads = lax.psum_scatter(grads, "z", scatter_dimension=0, tiled=False)
    loss_meta, line[0], dcand = lax.optimization_barrier((loss_meta, line[0], dcand))
    meta = call(
        meta_kernel, "meta", [((16, 128), BF)], place, history, candidates, loss_meta, smem=1, limit=40
    )
    line = [line[0]] + [swap_x(line[k], k) for k in range(1, NX)]

    packed = call(
        pack_kernel,
        "pack",
        [((users, 64, 128), BF)],
        *line,
        dcand,
        rows,
        dhidden,
        meta,
        limit=50,
    )
    arrived = lax.all_to_all(packed, ("y", "z"), 0, 0)
    _, grads = lax.optimization_barrier((arrived, grads))
    grads = call(
        turn_kernel, "turn", [((32, half + 4 * HD), BF)] * NY, place, grads, smem=1, limit=8, cost=0.5
    )
    grads = [grads[0]] + [
        lax.ppermute(grads[k], "y", [(i, i ^ k) for i in range(NY)]) for k in range(1, NY)
    ]
    got = arrived[:, 48:53].astype(F32)
    all_ids = (got[:, 0:2] * 128.0 + got[:, 2:4]).astype(jnp.int32).reshape(-1)
    own, other = call(
        scatter_kernel,
        "scatter",
        [((NX, 512, 128), BF)] * 2,
        all_ids,
        place,
        arrived,
        smem=2,
        scratch=[
            pltpu.VMEM((users * 48, 128), F32),
            pltpu.VMEM((parts * rows_total, 128), F32),
            pltpu.VMEM((parts * rows_total, 128), F32),
        ],
        limit=24,
        cost=12.0,
    )
    line = call(pair_kernel, "final_pair", [((512, 128), BF)] * NX, swap_core(other), own, limit=8, cost=0.5)
    line = [line[0]] + [swap_x(line[k], k) for k in range(1, NX)]
    grad_in, *proj = call(
        split_kernel, "split", [((32, 4 * HD), F32)] + [((32, HD), BF)] * NX, *grads, limit=8, cost=0.5
    )
    proj = [proj[0]] + [swap_x(proj[k], k) for k in range(1, NX)]
    shard_t, proj_t = call(
        unpack_kernel,
        "unpack",
        [((32, rows_total), F32), ((32, HD), F32)],
        *line,
        *proj,
        limit=8,
    )
    grad_in = grad_in.reshape(-1, 4, HD)
    loss = jnp.sum(got[:, 4, 0:3])
    return (loss, grad_in, proj_t.T, shard_t.T)


def solution(mesh):
    fine = Mesh(mesh.devices.reshape(NY, NZ, NX, NC), ("y", "z", "x", "c"))
    dp, item = ("y", "z"), ("x", "c")
    placed = (
        P(item, None),
        P(None, None, item),
        P(item, None),
        P(dp, None),
        P(dp),
        P(dp, None),
        P(dp),
        P(dp, None),
        P(dp, None),
    )
    return jax.shard_map(
        on_device,
        mesh=fine,
        in_specs=placed,
        out_specs=(P(), P(dp, None, item), P(item, dp), P(item, dp)),
        check_vma=False,
    )
```

```python
import functools

import jax
import jax.numpy as jnp
from jax import lax
from jax.experimental import pallas as pl
from jax.experimental.pallas import tpu as pltpu
from jax.sharding import Mesh, PartitionSpec as P

HD = 128
NX, NC, NY, NZ = 4, 2, 4, 8
CQL_WEIGHT = 0.5
BF = jnp.bfloat16
F32 = jnp.float32


def swap_x(value, k):
    return lax.ppermute(value, "x", [(i, i ^ k) for i in range(NX)])


def swap_core(value):
    return lax.ppermute(value, "c", [(0, 1), (1, 0)])


def event_slots(item, shape, axis):
    row = lax.broadcasted_iota(jnp.int32, shape, axis)
    return 32 * jnp.bitwise_and(row, 31) + 8 * (row // 32) + item


def cand_slots(item, shape, axis):
    row = lax.broadcasted_iota(jnp.int32, shape, axis)
    return 32 * jnp.bitwise_and(row, 15) + 8 * (row // 16) + item


def chosen(values, slots):
    cols = lax.broadcasted_iota(jnp.int32, (1, values.shape[1]), 1)
    return jnp.sum(jnp.where(cols == slots, values.astype(F32), 0.0), axis=1, keepdims=True)


def pick_kernel(half, place_ref, history_ref, cand_ref, table_ref, out_ref, hot_ref):
    total = table_ref.shape[0]
    first_row = (2 * place_ref[0] + place_ref[1]) * total
    size = out_ref.shape[1]
    for k in range(NX):
        item = item_of(place_ref, half * NX + k)
        events = chosen(history_ref[...], event_slots(item, (128, 1), 0))
        cands = chosen(cand_ref[...], cand_slots(item, (size - 128, 1), 0))
        for first, ids in ((0, events), (128, cands)):
            local = ids.astype(jnp.int32) - first_row
            count = ids.shape[0]
            for i in range(0, total, 512):
                cols = lax.broadcasted_iota(jnp.int32, (1, 512), 1) + i
                hot_ref[size * k + first : size * k + first + count, i : i + 512] = (
                    (local == cols).astype(F32).astype(BF)
                )
    for i in range(0, out_ref.shape[2], 256):
        found = jnp.dot(hot_ref[...], table_ref[:, i : i + 256], preferred_element_type=F32).astype(BF)
        for k in range(NX):
            out_ref[k, :, i : i + 256] = found[size * k : size * k + size, :]


def pair_kernel(a_ref, b_ref, *outs):
    for k, out in enumerate(outs):
        out[...] = (a_ref[k].astype(F32) + b_ref[k].astype(F32)).astype(BF)


def norm_kernel(a_ref, b_ref, c_ref, d_ref, normed_ref, crow_ref):
    refs = (a_ref, b_ref, c_ref, d_ref)
    block = normed_ref.shape[0]
    rows = sum(ref[:block, :].astype(F32) for ref in refs)
    scale = lax.rsqrt(jnp.mean(rows * rows, axis=-1, keepdims=True) + 1e-06)
    normed_ref[...] = (rows * scale).astype(BF)
    crow_ref[...] = sum(ref[block:, :].astype(F32) for ref in refs).astype(BF)


def rows_kernel(a_ref, b_ref, c_ref, d_ref, rows_ref):
    block = rows_ref.shape[0]
    rows_ref[...] = sum(ref[:block, :].astype(F32) for ref in (a_ref, b_ref, c_ref, d_ref)).astype(BF)


def item_of(place_ref, b):
    return 2 * jnp.bitwise_xor(place_ref[0], b % NX) + jnp.bitwise_xor(place_ref[1], b // NX)


def places_of(place_ref, shape, axis, first=0):
    row = lax.broadcasted_iota(jnp.int32, shape, axis) + first
    line = jnp.bitwise_and(row, 511)
    item = 2 * jnp.bitwise_xor(place_ref[0], line // 128) + jnp.bitwise_xor(place_ref[1], row // 512)
    inside = jnp.bitwise_and(row, 127)
    return 32 * jnp.bitwise_and(inside, 31) + 8 * (inside // 32) + item


def attend_kernel(
    place_ref, b0, b1, b2, b3, b4, b5, b6, b7, w_ref,
    normed_out, pre_out, act_out, sent_ref, normed_ref, pre_ref, act_ref, sems,
):
    for b, ref in enumerate((b0, b1, b2, b3, b4, b5, b6, b7)):
        normed_ref[128 * b : 128 * b + 128, :] = ref[...]
    copies = [pltpu.make_async_copy(normed_ref, normed_out, sems.at[0])]
    copies[0].start()
    seq = normed_ref.shape[0]
    for i in range(0, seq, 256):
        pre = jnp.dot(normed_ref[i : i + 256, :], w_ref[...], preferred_element_type=F32)
        pre_ref[i : i + 256, :] = pre
        act_ref[i : i + 256, :] = (pre * jax.nn.sigmoid(pre)).astype(BF)
    for i, (source, target) in enumerate(((pre_ref, pre_out), (act_ref, act_out))):
        copies.append(pltpu.make_async_copy(source, target, sems.at[i + 1]))
        copies[-1].start()
    length = place_ref[2]
    inverse = 1.0 / jnp.full((1, 1), length, jnp.int32).astype(F32)
    cols = places_of(place_ref, (1, seq), 1)
    cols = jnp.where(cols < length, cols, seq)
    for i in range(0, seq, 256):
        queries = act_ref[i : i + 256, 2 * HD : 3 * HD]
        logits = lax.dot_general(
            queries, act_ref[:, 3 * HD :], (((1,), (1,)), ((), ())), preferred_element_type=F32
        ) * HD ** (-0.5)
        rows = places_of(place_ref, (256, 1), 0, i)
        attn = jnp.where(cols <= rows, logits * jax.nn.sigmoid(logits), 0.0).astype(BF)
        mixed = jnp.dot(attn, act_ref[:, HD : 2 * HD], preferred_element_type=F32) * inverse
        top = mixed.astype(BF)
        rest = (mixed - top.astype(F32)).astype(BF)
        for h in range(2):
            b = i // 128 + h
            item = item_of(place_ref, b)
            sent_ref[item, :, 0:HD] = top[128 * h : 128 * h + 128, :]
            sent_ref[item, :, HD : 2 * HD] = rest[128 * h : 128 * h + 128, :]
            sent_ref[item, :, 2 * HD :] = act_ref[128 * b : 128 * b + 128, 0:HD]
    for copy in copies:
        copy.wait()


def split_loss(value, shape, row):
    value = jnp.broadcast_to(value, shape)
    top = value.astype(BF).astype(F32)
    middle = (value - top).astype(BF).astype(F32)
    low = value - top - middle
    lane = lax.broadcasted_iota(jnp.int32, shape, 1)
    picked = jnp.where(lane == 0, top, jnp.where(lane == 1, middle, jnp.where(lane == 2, low, 0.0)))
    return jnp.where(lax.broadcasted_iota(jnp.int32, shape, 0) == row, picked, 0.0).astype(BF)


def event_kernel(
    place_ref, sent_ref, rows_ref, w_ref, crows_ref, action_ref, target_ref,
    back_ref, dhidden_ref, dcand_ref, near_ref, far_ref,
    weight_ref, crow_ref, sems,
):
    copies = [
        pltpu.make_async_copy(
            w_ref.at[item_of(place_ref, b)], weight_ref.at[HD * b : HD * b + HD, :], sems.at[b]
        )
        for b in range(NX * NC)
    ]
    copies.append(pltpu.make_async_copy(crows_ref, crow_ref, sems.at[NX * NC]))
    for copy in copies:
        copy.start()
    owner = 2 * place_ref[0] + place_ref[1]
    length, count = place_ref[2], place_ref[3]
    block, width = rows_ref.shape
    seq = block * NX * NC
    items = [item_of(place_ref, b) for b in range(NX * NC)]
    mixed = jnp.concatenate(
        [sent_ref[i, :, 0:HD].astype(F32) + sent_ref[i, :, HD : 2 * HD].astype(F32) for i in items], axis=1
    )
    gate = jnp.concatenate([sent_ref[i, :, 2 * HD :] for i in items], axis=1).astype(F32)
    center = jnp.mean(mixed, axis=-1, keepdims=True)
    rstd = lax.rsqrt(jnp.mean(mixed * mixed, axis=-1, keepdims=True) - center * center + 1e-05)
    normo = (mixed - center) * rstd
    gated = (normo * gate).astype(BF)
    for copy in copies:
        copy.wait()
    weights = weight_ref[...]
    out = rows_ref[...].astype(F32) + jnp.dot(gated, weights, preferred_element_type=F32)
    hidden = out.astype(BF)
    crows = crow_ref[...]
    scores = lax.dot_general(hidden, crows, (((1,), (1,)), ((), ())), preferred_element_type=F32)
    col = lax.broadcasted_iota(jnp.int32, (1, crows.shape[0]), 1)
    inside = jnp.bitwise_and(col, 63)
    slots = 32 * jnp.bitwise_and(inside, 15) + 8 * (inside // 16) + col // 64
    masked = jnp.where(slots < count, scores, -jnp.inf)
    top = jnp.max(masked, axis=-1, keepdims=True)
    expo = jnp.exp(masked - top)
    total = jnp.sum(expo, axis=-1, keepdims=True)
    soft = expo / total
    lse = top + jnp.log(total)
    places = event_slots(owner, (block, 1), 0)
    actions = chosen(action_ref[...], places).astype(jnp.int32)
    onehot = (slots == actions).astype(F32)
    taken = jnp.sum(scores * onehot, axis=-1, keepdims=True)
    live = jnp.where(places < length, 1.0 / seq, 0.0)
    miss = taken - chosen(target_ref[...], places)
    loss = jnp.sum(live * (CQL_WEIGHT * (lse - taken) + 0.5 * miss * miss), axis=0, keepdims=True)
    loss = split_loss(loss, (16, 2 * HD), 0)
    dscore = (live * (CQL_WEIGHT * soft + (miss - CQL_WEIGHT) * onehot)).astype(BF)
    dhidden = jnp.dot(dscore, crows, preferred_element_type=F32).astype(BF)
    dhidden_ref[...] = dhidden
    dgated = lax.dot_general(
        dhidden, weights, (((1,), (1,)), ((), ())), preferred_element_type=F32
    )
    dnormo = dgated * gate
    first = jnp.mean(dnormo, axis=-1, keepdims=True)
    second = jnp.mean(dnormo * normo, axis=-1, keepdims=True)
    dmixed = (rstd * (dnormo - first - normo * second)).astype(BF)
    du = (dgated * normo).astype(BF)
    for b, i in enumerate(items):
        back_ref[i, 0:block, 0:HD] = dmixed[:, HD * b : HD * b + HD]
        back_ref[i, 0:block, HD:] = du[:, HD * b : HD * b + HD]
        back_ref[i, block:, :] = loss
    turned = (((0,), (0,)), ((), ()))
    half = NX * HD
    near_ref[...] = gated[:, :half]
    far_ref[:, :width] = dhidden
    far_ref[:, width:] = gated[:, half:]
    dcand_ref[...] = lax.dot_general(dscore, hidden, turned, preferred_element_type=F32).astype(BF)


def backward_kernel(
    place_ref, back_ref, act_in, pre_in, normed_in, dhidden_in, own_in, other_in,
    near_ref, far_ref, loss_ref, grads_ref,
    dm_ref, du_ref, dq_ref, dpre_ref, act_ref, pre_ref, normed_ref, dhidden_ref, own_ref, other_ref, sems,
):
    copies = [
        pltpu.make_async_copy(source, target, sems.at[i])
        for i, (source, target) in enumerate(
            (
                (act_in, act_ref),
                (pre_in, pre_ref),
                (normed_in, normed_ref),
                (dhidden_in, dhidden_ref),
                (own_in, own_ref),
                (other_in, other_ref),
            )
        )
    ]
    for copy in copies:
        copy.start()
    seq = act_ref.shape[0]
    loss = jnp.zeros((16, 2 * HD), F32)
    for b in range(8):
        item = item_of(place_ref, b)
        dm_ref[128 * b : 128 * b + 128, :] = back_ref[item, 0:128, 0:HD]
        du_ref[128 * b : 128 * b + 128, :] = back_ref[item, 0:128, HD:]
        loss = loss + back_ref[item, 128:144, :].astype(F32)
    loss = jnp.sum(jnp.sum(loss, axis=1, keepdims=True), axis=0, keepdims=True)
    loss_ref[...] = split_loss(loss, (16, 128), 4)
    length = place_ref[2]
    inverse = 1.0 / jnp.full((1, 1), length, jnp.int32).astype(F32)
    cols = places_of(place_ref, (1, seq), 1)
    across = (((1,), (1,)), ((), ()))
    dq_ref[...] = jnp.zeros(dq_ref.shape, F32)

    def slope(value, sigma):
        return sigma * (1.0 + value * (1.0 - sigma))

    copies[0].wait()
    for i in range(0, seq, 256):
        keys = act_ref[i : i + 256, 3 * HD :]
        logits = lax.dot_general(
            keys, act_ref[:, 2 * HD : 3 * HD], across, preferred_element_type=F32
        ) * HD ** (-0.5)
        rows = places_of(place_ref, (256, 1), 0, i)
        rows = jnp.where(rows < length, rows, seq)
        sigma = jnp.where(rows <= cols, jax.nn.sigmoid(logits), 0.0)
        swish = logits * sigma
        attn = swish.astype(BF)
        dattn = lax.dot_general(
            act_ref[i : i + 256, HD : 2 * HD], dm_ref[...], across, preferred_element_type=F32
        )
        dlogits = (dattn * (sigma + swish * (1.0 - sigma))).astype(BF)
        dvalues = jnp.dot(attn, dm_ref[...], preferred_element_type=F32) * inverse
        dkeys = jnp.dot(dlogits, act_ref[:, 2 * HD : 3 * HD], preferred_element_type=F32) * (
            inverse * HD ** (-0.5)
        )
        dq_ref[...] += lax.dot_general(
            dlogits, keys, (((0,), (0,)), ((), ())), preferred_element_type=F32
        )
        if i == 0:
            copies[1].wait()
        for j, grad in ((1, dvalues), (3, dkeys)):
            pre = pre_ref[i : i + 256, HD * j : HD * j + HD]
            dpre_ref[i : i + 256, HD * j : HD * j + HD] = (
                grad * slope(pre, jax.nn.sigmoid(pre))
            ).astype(BF)
    dq_ref[...] = dq_ref[...] * (inverse * HD ** (-0.5))
    for j, ref in ((0, du_ref), (2, dq_ref)):
        pre = pre_ref[:, HD * j : HD * j + HD]
        dpre_ref[:, HD * j : HD * j + HD] = (
            ref[...].astype(F32) * slope(pre, jax.nn.sigmoid(pre))
        ).astype(BF)
    near_ref[...] = dpre_ref[: near_ref.shape[0], :]
    far_ref[...] = dpre_ref[near_ref.shape[0] :, :]
    for copy in copies[2:]:
        copy.wait()
    half = own_ref.shape[1]
    turned = (((0,), (0,)), ((), ()))
    width = dhidden_ref.shape[1]
    left = lax.dot_general(dhidden_ref[...], own_ref[...], turned, preferred_element_type=F32)
    left = left + lax.dot_general(
        other_ref[:, :width], other_ref[:, width:], turned, preferred_element_type=F32
    )
    left = left.astype(BF)
    right = lax.dot_general(
        normed_ref[...], dpre_ref[...], (((0,), (0,)), ((), ())), preferred_element_type=F32
    ).astype(BF)
    for y in range(NY):
        for z in range(NZ):
            rows = slice(32 * (NZ * y + z), 32 * (NZ * y + z) + 32)
            grads_ref[z, 32 * y : 32 * y + 32, :half] = left[rows, :]
            grads_ref[z, 32 * y : 32 * y + 32, half:] = right[rows, :]


def part_kernel(near_ref, far_ref, w_ref, far_w_ref, *outs):
    across = (((1,), (1,)), ((), ()))
    for h in range(2):
        rows = slice(256 * h, 256 * h + 256)
        part = lax.dot_general(near_ref[rows, :], w_ref[...], across, preferred_element_type=F32)
        part = part + lax.dot_general(
            far_ref[rows, :], far_w_ref[...], across, preferred_element_type=F32
        )
        part = part.astype(BF)
        outs[2 * h][...] = part[:128, :]
        outs[2 * h + 1][...] = part[128:, :]


def meta_kernel(place_ref, history_ref, cands_ref, loss_ref, meta_ref):
    owner = 2 * place_ref[0] + place_ref[1]

    def digits(values, wanted):
        row = lax.broadcasted_iota(jnp.int32, (16, values.shape[1]), 0)
        upper, lower = values // 128, jnp.bitwise_and(values, 127)
        both = jnp.where(row == 0, upper, jnp.where(row == 2, lower, 0)).astype(F32).astype(BF)
        source = lax.broadcasted_iota(jnp.int32, (values.shape[1], 128), 0)
        hot = (source == wanted).astype(F32).astype(BF)
        return jnp.dot(both, hot, preferred_element_type=F32)

    lane = lax.broadcasted_iota(jnp.int32, (16, 128), 1)
    row = lax.broadcasted_iota(jnp.int32, (16, 128), 0)
    events = digits(history_ref[...], event_slots(owner, (1, 128), 1))
    wanted = cand_slots(owner, (1, 128), 1)
    wanted = jnp.where(lax.broadcasted_iota(jnp.int32, (1, 128), 1) < 64, wanted, -1)
    cands = pltpu.roll(digits(cands_ref[...], wanted), 1, 0)
    meta = events + cands + loss_ref[...].astype(F32)
    for where, value in ((64, place_ref[2]), (65, place_ref[3])):
        for r, part in ((1, value // 128), (3, jnp.bitwise_and(value, 127))):
            part = jnp.full((16, 128), part, jnp.int32).astype(F32)
            meta = jnp.where((lane == where) & (row == r), part, meta)
    meta_ref[...] = meta.astype(BF)


def pack_kernel(a_ref, b_ref, c_ref, d_ref, dcand_ref, rows_ref, dhidden_ref, meta_ref, out_ref):
    refs = (a_ref, b_ref, c_ref, d_ref)
    dnormed = sum(ref[...].astype(F32) for ref in refs)
    rows = rows_ref[...].astype(F32)
    scale = lax.rsqrt(jnp.mean(rows * rows, axis=-1, keepdims=True) + 1e-06)
    normed = rows * scale
    drows = dhidden_ref[...].astype(F32) + scale * (
        dnormed - normed * jnp.mean(dnormed * normed, axis=-1, keepdims=True)
    )
    drows = drows.astype(BF)
    dcand = dcand_ref[...]
    meta = meta_ref[...]
    for d in range(out_ref.shape[0]):
        out_ref[d, 0:32, :] = jnp.concatenate(
            [drows[32 * g : 32 * g + 32, 32 * d : 32 * d + 32] for g in range(4)], axis=1
        )
        out_ref[d, 32:48, :] = jnp.concatenate(
            [dcand[16 * g : 16 * g + 16, 32 * d : 32 * d + 32] for g in range(4)], axis=1
        )
        out_ref[d, 48:64, :] = meta


def scatter_kernel(ids_ref, place_ref, data_ref, own_ref, other_ref, rows_ref, acc_ref, more_ref):
    users = data_ref.shape[0]
    total = acc_ref.shape[0]
    chunk = 512
    owner = 2 * place_ref[0] + place_ref[1]

    def clear(i, carry):
        here = pl.ds(pl.multiple_of(i * chunk, chunk), chunk)
        acc_ref[here, :] = jnp.zeros((chunk, 128), F32)
        more_ref[here, :] = jnp.zeros((chunk, 128), F32)
        return carry

    lax.fori_loop(0, total // chunk, clear, 0)
    for u in range(users):
        rows_ref[48 * u : 48 * u + 48, :] = data_ref[u, 0:48, :].astype(F32)
    lane = lax.broadcasted_iota(jnp.int32, (1, 128), 1) // 32
    masks = [lane == g for g in range(4)]

    def add(first_id, pitch, first_row, count):
        def step(i, carry):
            for j in range(2):
                work = []
                for half, ref in ((0, acc_ref), (1, more_ref)):
                    p = i * 4 + j * 2 + half
                    row = rows_ref[pl.ds(first_row + p, 1), :]
                    ids = [ids_ref[first_id + g * pitch + p] for g in range(4)]
                    work.append((ref, row, ids, [ref[pl.ds(ids[g], 1), :] for g in range(4)]))
                for ref, row, ids, held in work:
                    for g in range(4):
                        pltpu.store(ref.at[pl.ds(ids[g], 1), :], held[g] + row, mask=masks[g])
            return carry

        lax.fori_loop(0, (count + 3) // 4, step, 0)

    def user(u, carry):
        base = u * 256
        events = jnp.clip((ids_ref[base + 192] - owner + 31) // 32, 0, 32)
        cands = jnp.clip((ids_ref[base + 193] - owner + 31) // 32, 0, 16)
        add(base, 32, u * 48, events)
        add(base + 128, 16, u * 48 + 32, cands)
        return carry

    lax.fori_loop(0, users, user, 0)
    wide = lax.broadcasted_iota(jnp.int32, (512, 128), 1) // 32
    for cc in range(2):
        for k in range(4):
            item = item_of(place_ref, cc * NX + k)
            result = jnp.zeros((512, 128), F32)
            for q in range(4):
                here = pl.ds(pl.multiple_of(item * 2048 + q * 512, 512), 512)
                part = acc_ref[here, :] + more_ref[here, :]
                part = part + pltpu.roll(part, 64, 1)
                part = part + pltpu.roll(part, 32, 1)
                result = jnp.where(wide == q, part, result)
            (own_ref, other_ref)[cc][k] = result.astype(BF)


def turn_kernel(place_ref, grads_ref, *outs):
    for k, out in enumerate(outs):
        start = jnp.bitwise_xor(place_ref[4], k) * 32
        out[...] = grads_ref[pl.ds(pl.multiple_of(start, 32), 32), :]


def split_kernel(g0, g1, g2, g3, in_ref, *outs):
    total = sum(ref[...].astype(F32) for ref in (g0, g1, g2, g3))
    in_ref[...] = total[:, NX * HD :]
    for k, out in enumerate(outs):
        out[...] = total[:, HD * k : HD * k + HD].astype(BF)


def unpack_kernel(a_ref, b_ref, c_ref, d_ref, p0, p1, p2, p3, out_ref, proj_ref):
    proj_ref[...] = sum(ref[...].astype(F32) for ref in (p0, p1, p2, p3))
    turned = sum(ref[...].astype(F32) for ref in (a_ref, b_ref, c_ref, d_ref)).T
    for q in range(4):
        out_ref[:, q * 512 : (q + 1) * 512] = turned[32 * q : 32 * q + 32, :]


def whole(count, smem=0):
    specs = [pl.BlockSpec(memory_space=pltpu.SMEM)] * smem
    return specs + [pl.BlockSpec(memory_space=pltpu.VMEM)] * count


def call(kernel, name, outs, *args, smem=0, scratch=(), limit=32, far=(), far_outs=(), cost=1.0):
    outs = tuple(jax.ShapeDtypeStruct(shape, dtype) for shape, dtype in outs)
    hbm = pl.BlockSpec(memory_space=pltpu.HBM)
    specs = [hbm if i in far_outs else whole(1)[0] for i in range(len(outs))]
    in_specs = [hbm if i in far else spec for i, spec in enumerate(whole(len(args) - smem, smem))]
    return pl.pallas_call(
        kernel,
        out_shape=outs if len(outs) > 1 else outs[0],
        in_specs=in_specs,
        out_specs=tuple(specs) if len(outs) > 1 else specs[0],
        scratch_shapes=list(scratch),
        compiler_params=pltpu.CompilerParams(vmem_limit_bytes=int(limit * 1024 * 1024)),
        cost_estimate=pl.CostEstimate(
            flops=int(cost * 1.1e9), bytes_accessed=int(cost * 3.6e6), transcendentals=0
        ),
        name=name,
    )(*args)


def on_device(table, w_uvqk, w_out, history, lengths, candidates, counts, actions, targets):
    rows_total, width = table.shape
    seq = history.shape[1]
    ncand = candidates.shape[1]
    users = NY * NZ
    parts = NX * NC
    block = seq // parts
    cblock = ncand // parts
    x, c = lax.axis_index("x"), lax.axis_index("c")
    length = lengths[0]

    place = jnp.stack([x, c, length, counts[0], lax.axis_index("y")]).astype(jnp.int32)

    def along_x(own):
        return [own] + [swap_x(own, k) for k in range(1, NX)]

    size = block + cblock

    def pick(half):
        return call(
            functools.partial(pick_kernel, half),
            "pick",
            [((NX, size, width), BF)],
            place,
            history,
            candidates,
            table,
            smem=1,
            scratch=[pltpu.VMEM((NX * size, rows_total), BF)],
            limit=20,
            cost=5.0 if half else 0.05,
        )

    picked_other = swap_core(pick(1))
    weights_out = lax.all_gather(w_out, ("x", "c"), axis=0, tiled=False)
    picked_own = pick(0)
    line = list(call(pair_kernel, "pair", [((size, width), BF)] * NX, picked_other, picked_own, limit=8))
    line = [line[0]] + [swap_x(line[k], k) for k in range(1, NX)]
    w_uvqk, line[0] = lax.optimization_barrier((w_uvqk, line[0]))
    local_w = w_uvqk.reshape(width, -1)
    normed, crow = call(
        norm_kernel,
        "norm",
        [((block, width), BF), ((cblock, width), BF)],
        *line,
        limit=50,
    )
    own_other = swap_core(normed)
    far_w = swap_core(local_w)
    line[0], normed = lax.optimization_barrier((line[0], normed))
    rows = call(rows_kernel, "rows", [((block, width), BF)], *line, limit=50, cost=0.5)
    *normed_line, local_w, far_w, rows = lax.optimization_barrier(
        (*along_x(normed), local_w, far_w, rows)
    )
    spread_rows = normed_line[:NX] + [own_other] + [swap_core(part) for part in normed_line[1:NX]]
    crows = lax.all_gather(crow, ("x", "c"), axis=0, tiled=True)
    normed, pre, act, sent = call(
        attend_kernel,
        "attend",
        [((seq, width), BF), ((seq, 4 * HD), F32), ((seq, 4 * HD), BF), ((parts, block, 3 * HD), BF)],
        place,
        *spread_rows,
        local_w,
        smem=1,
        limit=52,
        far_outs=(0, 1, 2),
        scratch=[
            pltpu.VMEM((seq, width), BF),
            pltpu.VMEM((seq, 4 * HD), F32),
            pltpu.VMEM((seq, 4 * HD), BF),
            pltpu.SemaphoreType.DMA((3,)),
        ],
        cost=4.0,
    )
    sent = lax.all_to_all(sent, ("x", "c"), 0, 0)

    half = NX * HD
    back, dhidden, dcand, gated_near, gated_far = call(
        event_kernel,
        "event",
        [
            ((parts, block + 16, 2 * HD), BF),
            ((block, width), BF),
            ((ncand, width), BF),
            ((block, half), BF),
            ((block, width + half), BF),
        ],
        place,
        sent,
        rows,
        weights_out,
        crows,
        actions,
        targets,
        smem=1,
        limit=60,
        far=(3, 4),
        scratch=[
            pltpu.VMEM((width, width), BF),
            pltpu.VMEM((ncand, width), BF),
            pltpu.SemaphoreType.DMA((parts + 1,)),
        ],
        cost=4.0,
    )
    back = lax.all_to_all(back, ("x", "c"), 0, 0)
    gated_far = swap_core(gated_far)

    dcand = lax.psum_scatter(dcand, ("x", "c"), scatter_dimension=0, tiled=True)
    near, far, loss_meta, grads = call(
        backward_kernel,
        "backward",
        [
            ((seq // 2, 4 * HD), BF),
            ((seq // 2, 4 * HD), BF),
            ((16, 128), BF),
            ((NZ, width // NZ, half + 4 * HD), BF),
        ],
        place,
        back,
        act,
        pre,
        normed,
        dhidden,
        gated_near,
        gated_far,
        smem=1,
        scratch=[
            pltpu.VMEM((seq, HD), BF),
            pltpu.VMEM((seq, HD), BF),
            pltpu.VMEM((seq, HD), F32),
            pltpu.VMEM((seq, 4 * HD), BF),
            pltpu.VMEM((seq, 4 * HD), BF),
            pltpu.VMEM((seq, 4 * HD), F32),
            pltpu.VMEM((seq, width), BF),
            pltpu.VMEM((block, width), BF),
            pltpu.VMEM((block, half), BF),
            pltpu.VMEM((block, width + half), BF),
            pltpu.SemaphoreType.DMA((6,)),
        ],
        limit=60,
        far=(2, 3, 4, 5, 6, 7),
        cost=6.0,
    )
    far_got = swap_core(far)
    line = list(
        call(
            part_kernel,
            "part",
            [((block, width), BF)] * NX,
            near,
            far_got,
            local_w,
            far_w,
            limit=50,
            cost=2.0,
        )
    )
    grads = lax.psum_scatter(grads, "z", scatter_dimension=0, tiled=False)
    loss_meta, line[0], dcand = lax.optimization_barrier((loss_meta, line[0], dcand))
    meta = call(
        meta_kernel, "meta", [((16, 128), BF)], place, history, candidates, loss_meta, smem=1, limit=40
    )
    line = [line[0]] + [swap_x(line[k], k) for k in range(1, NX)]

    packed = call(
        pack_kernel,
        "pack",
        [((users, 64, 128), BF)],
        *line,
        dcand,
        rows,
        dhidden,
        meta,
        limit=50,
    )
    arrived = lax.all_to_all(packed, ("y", "z"), 0, 0)
    _, grads = lax.optimization_barrier((arrived, grads))
    grads = call(
        turn_kernel, "turn", [((32, half + 4 * HD), BF)] * NY, place, grads, smem=1, limit=8, cost=0.5
    )
    grads = [grads[0]] + [
        lax.ppermute(grads[k], "y", [(i, i ^ k) for i in range(NY)]) for k in range(1, NY)
    ]
    got = arrived[:, 48:53].astype(F32)
    all_ids = (got[:, 0:2] * 128.0 + got[:, 2:4]).astype(jnp.int32).reshape(-1)
    own, other = call(
        scatter_kernel,
        "scatter",
        [((NX, 512, 128), BF)] * 2,
        all_ids,
        place,
        arrived,
        smem=2,
        scratch=[
            pltpu.VMEM((users * 48, 128), F32),
            pltpu.VMEM((parts * rows_total, 128), F32),
            pltpu.VMEM((parts * rows_total, 128), F32),
        ],
        limit=24,
        cost=12.0,
    )
    line = call(pair_kernel, "final_pair", [((512, 128), BF)] * NX, swap_core(other), own, limit=8, cost=0.5)
    line = [line[0]] + [swap_x(line[k], k) for k in range(1, NX)]
    grad_in, *proj = call(
        split_kernel, "split", [((32, 4 * HD), F32)] + [((32, HD), BF)] * NX, *grads, limit=8, cost=0.5
    )
    proj = [proj[0]] + [swap_x(proj[k], k) for k in range(1, NX)]
    shard_t, proj_t = call(
        unpack_kernel,
        "unpack",
        [((32, rows_total), F32), ((32, HD), F32)],
        *line,
        *proj,
        limit=8,
    )
    grad_in = grad_in.reshape(-1, 4, HD)
    loss = jnp.sum(got[:, 4, 0:3])
    return (loss, grad_in, proj_t.T, shard_t.T)


def solution(mesh):
    fine = Mesh(mesh.devices.reshape(NY, NZ, NX, NC), ("y", "z", "x", "c"))
    dp, item = ("y", "z"), ("x", "c")
    placed = (
        P(item, None),
        P(None, None, item),
        P(item, None),
        P(dp, None),
        P(dp),
        P(dp, None),
        P(dp),
        P(dp, None),
        P(dp, None),
    )
    return jax.shard_map(
        on_device,
        mesh=fine,
        in_specs=placed,
        out_specs=(P(), P(dp, None, item), P(item, dp), P(item, dp)),
        check_vma=False,
    )
```
